32 devices in a mesh: dp: 8 (over z, y), blk: 4 (over x, core).
Axes of the slice: x: 2, y: 2, z: 4, core: 2. Of those that a mesh axis runs over, the one named last changes fastest.
Arguments:
- tokens: bfloat16 [26624, 1024], P(('dp', 'blk')), may hold values from -6 to 6
- cotangent: bfloat16 [26624, 1024], P(('dp', 'blk')), may hold values from -6 to 6
- lengths: int32 [8, 3], P('dp'), may hold values from 1 to 2368, as said below
- qkv_weight: bfloat16 [1024, 3072], replicated, may hold values from -0.1875 to 0.1875
- out_weight: bfloat16 [1024, 1024], replicated, may hold values from -0.1875 to 0.1875
- up_weight: bfloat16 [1024, 4096], replicated, may hold values from -0.1875 to 0.1875
- down_weight: bfloat16 [4096, 1024], replicated, may hold values from -0.09375 to 0.09375
- norm_gain: float32 [4, 1024], replicated, may hold values from 0.5 to 1.5
- norm_bias: float32 [4, 1024], replicated, may hold values from -1.5 to 1.5
- proj_bias: float32 [4, 1024], replicated, may hold values from -1.5 to 1.5
- ffn_bias: float32 [4096], replicated, may hold values from -1.5 to 1.5
Outputs:
- mixed: bfloat16 [26624, 1024], P(('dp', 'blk'))
- token_grad: bfloat16 [26624, 1024], P(('dp', 'blk'))
- qkv_grad: float32 [1024, 3072], P('dp', 'blk')
- out_grad: float32 [1024, 1024], P('dp', 'blk')
- up_grad: float32 [1024, 4096], P('dp', 'blk')
- down_grad: float32 [4096, 1024], P('dp', 'blk')
- gain_grad: float32 [4, 1024], P(None, 'dp')
- norm_bias_grad: float32 [4, 1024], P(None, 'dp')
- proj_bias_grad: float32 [4, 1024], P(None, 'dp')
- ffn_bias_grad: float32 [4096], P('dp')
The draws below stay inside these ranges and needn't reach their ends.
Inputs may be any that keep to these rules, and one draw needn't show every extreme that they name: In each row the three lengths sum to 3328; the middle one is exactly 2368 and its sequence holds a position of the group's first 832 rows and one of its last 832 rows.
All inputs are finite; a program needn't handle non-finite values.
Results may differ from the reference program's by a relative error of at most 0.015.
Values may be sent and summed in bfloat16 or wider, within the bound.
A program may use at most 384 MiB of HBM per device.

```python
import math
import jax
import jax.numpy as jnp
from jax import lax

D = 1024
FF = 4096
HEADS = 16
TOK_DEV = 832
LONG_LEN = 2368
TOKENS = 26624
N_DP = 8
N_BLK = 4


def draw_lengths(key, part):
    key = jax.random.fold_in(key, 11)
    group = TOK_DEV * N_BLK
    lowest = max(1, (N_BLK - 1) * TOK_DEV + 1 - LONG_LEN)
    highest = min(TOK_DEV - 1, group - LONG_LEN - 1)
    leading = jax.random.randint(key, (N_DP,), lowest, highest + 1, dtype=jnp.int32)
    middle = jnp.full((N_DP,), LONG_LEN, jnp.int32)
    return jnp.stack([leading, middle, group - LONG_LEN - leading], axis=1)


def raised(values, own_key, source, target, parts, factor):
    def block_of(dim):
        return (jnp.arange(values.shape[dim]) // (values.shape[dim] // parts)).reshape((-1,) + (1,) * (values.ndim - 1 - dim))

    one_side = jax.random.permutation(own_key, parts)[block_of(target)]
    other_side = (block_of(target) + parts // 2) % parts
    return jnp.where((block_of(source) == one_side) | (block_of(source) == other_side), factor * values, values)


def level_of(own_key, shape, pieces, low, top_value):
    loudness, own = 1.0, jax.random.fold_in(own_key, 6)
    for position, shards_of in pieces:
        steps = jnp.exp(jax.random.uniform(jax.random.fold_in(own, position), (shards_of,), jnp.float32, low / len(pieces), top_value / len(pieces)))
        loudness = loudness * jnp.repeat(steps, shape[position] // shards_of).reshape([-1 if axis == position else 1 for axis in range(len(shape))])
    return loudness


def normal_values(own_key, dims, width, bound, cuts=(), kind=jnp.bfloat16):
    loudness = level_of(own_key, dims, cuts, -0.22, 0.18) if cuts else 1.0
    values = jax.random.normal(own_key, dims, jnp.float32) * width * loudness
    return jnp.minimum(jnp.maximum(values, -bound), bound).astype(kind)


def gaussian_with(rng, extent, scale, bound, cuts, heavy, kind=jnp.bfloat16):
    values = scale * jax.random.normal(rng, extent, jnp.float32)
    if cuts:
        values = values * level_of(rng, extent, cuts, -0.22, 0.18)
    return jnp.clip(raised(values, jax.random.fold_in(rng, 3), *heavy), -bound, bound).astype(kind)


def setup_inputs(seed: int = 0) -> dict:
    streams_of = jax.random.split(jax.random.key(seed), 12)
    tokens = gaussian_with(streams_of[0], (TOKENS, D), 1.0, 6.0, ((0, 32),), (0, 1, 32, 2.75))
    cotangent = normal_values(streams_of[1], (TOKENS, D), 1.0, 6.0, ((0, 32),))
    lengths = draw_lengths(jax.random.fold_in(streams_of[11], 71), 0)
    qkv_weight = normal_values(streams_of[3], (D, 3 * D), D ** -0.5, 0.1875)
    out_weight = normal_values(streams_of[4], (D, D), D ** -0.5, 0.1875)
    up_weight = normal_values(streams_of[5], (D, FF), D ** -0.5, 0.1875)
    down_weight = normal_values(streams_of[6], (FF, D), FF ** -0.5, 0.09375)
    norm_gain = jnp.clip(1.0 + 0.1 * jax.random.normal(streams_of[7], (4, D), jnp.float32), 0.5, 1.5)
    norm_bias = normal_values(streams_of[8], (4, D), 0.3, 1.5, (), jnp.float32)
    proj_bias = normal_values(streams_of[9], (4, D), 0.3, 1.5, (), jnp.float32)
    ffn_bias = normal_values(streams_of[10], (FF,), 0.3, 1.5, (), jnp.float32)
    return dict(tokens=tokens, cotangent=cotangent, lengths=lengths, qkv_weight=qkv_weight, out_weight=out_weight, up_weight=up_weight, down_weight=down_weight, norm_gain=norm_gain, norm_bias=norm_bias, proj_bias=proj_bias, ffn_bias=ffn_bias)


relax_factor = 32.0
epsilon = 1e-05

@jax.custom_vjp
def low(v):
    return lax.optimization_barrier(v.astype(jnp.bfloat16)).astype(jnp.float32)

@jax.custom_vjp
def low_back(v):
    return v

def low_keep(v):
    return (low(v), None)

def low_pass(kept, grad):
    return (grad,)

def back_keep(v):
    return (v, None)

def back_low(kept, grad):
    return (low(grad),)
low.defvjp(low_keep, low_pass)
low_back.defvjp(back_keep, back_low)

def product(left, right):
    return jnp.dot(left, right, precision=lax.Precision.HIGHEST, preferred_element_type=jnp.float32)

def layer_norm(values, gain, shift):
    centre = values - lax.optimization_barrier(jnp.mean(values, -1, keepdims=True))
    spread = lax.optimization_barrier(jnp.mean(centre * centre, -1, keepdims=True))
    return centre * lax.rsqrt(spread + epsilon) * gain + shift

def segment_of(positions, ends):
    return (positions >= ends[0]).astype(jnp.int32) + (positions >= ends[1]).astype(jnp.int32)

def forward(values, weights, allowed):
    qkv_weight, out_weight, up_weight, down_weight, norm_gain, norm_bias, proj_bias, ffn_bias = weights
    group = values.shape[0]
    head_size = D // HEADS
    scale = 1.0 / (relax_factor * math.sqrt(head_size))
    first_normed = low(layer_norm(values, norm_gain[0], norm_bias[0]))
    projected = product(first_normed, qkv_weight)
    queries = low_back(low(projected[:, :D] + proj_bias[0]))
    keys_all = low_back(low(projected[:, D:2 * D]))
    values_all = low_back(low(projected[:, 2 * D:] + proj_bias[1]))

    def attend(query_head, key_head, value_head):
        scores = low_back(product(query_head, key_head.T) * scale)
        masked = jnp.where(allowed, scores, -1e+30)
        top = lax.optimization_barrier(jnp.max(masked, -1, keepdims=True))
        weights_raw = jnp.where(allowed, jnp.exp(relax_factor * (masked - top)), 0.0)
        probs = low(weights_raw / lax.optimization_barrier(jnp.sum(weights_raw, -1, keepdims=True)))
        return product(probs, value_head)
    checked = jax.checkpoint(attend)

    def split_heads(array):
        return array.reshape(group, HEADS, head_size).transpose(1, 0, 2)
    per_head = lax.map(lambda trio: checked(trio[0], trio[1], trio[2]), (split_heads(queries), split_heads(keys_all), split_heads(values_all)))
    attended = low_back(low(per_head.transpose(1, 0, 2).reshape(group, D)))
    attn_branch = low_back(product(attended, out_weight) + proj_bias[2])
    middle = values + layer_norm(attn_branch, norm_gain[1], norm_bias[1])
    second_normed = low(layer_norm(middle, norm_gain[2], norm_bias[2]))
    pre_gelu = low_back(product(second_normed, up_weight) + ffn_bias)
    activated = low(jax.nn.gelu(pre_gelu, approximate=True))
    ffn_branch = low_back(product(activated, down_weight) + proj_bias[3])
    return middle + layer_norm(ffn_branch, norm_gain[3], norm_bias[3])

def reference(tokens, cotangent, lengths, qkv_weight, out_weight, up_weight, down_weight, norm_gain, norm_bias, proj_bias, ffn_bias):
    group = TOK_DEV * N_BLK
    weights = (qkv_weight.astype(jnp.float32), out_weight.astype(jnp.float32), up_weight.astype(jnp.float32), down_weight.astype(jnp.float32), norm_gain, norm_bias, proj_bias, ffn_bias)
    inputs = tokens.astype(jnp.float32).reshape(N_DP, group, D)
    incoming = cotangent.astype(jnp.float32).reshape(N_DP, group, D)
    positions = jnp.arange(group, dtype=jnp.int32)

    def one_group(totals, item):
        values_in, grad_in, sizes = item
        ends = jnp.cumsum(sizes)
        segments = segment_of(positions, ends)
        allowed = (segments[:, None] == segments[None, :]) & (positions[None, :] <= positions[:, None])
        result, pull = jax.vjp(lambda first, *rest: forward(first, rest, allowed), values_in, *weights)
        grads = pull(grad_in)
        totals = tuple((total + grad for total, grad in zip(totals, grads[1:])))
        return (totals, (result.astype(jnp.bfloat16), grads[0].astype(jnp.bfloat16)))
    start = tuple((jnp.zeros(weight.shape, jnp.float32) for weight in weights))
    totals, pair = lax.scan(one_group, start, (inputs, incoming, lengths))
    outputs, input_grads = pair
    return (outputs.reshape(TOKENS, D), input_grads.reshape(TOKENS, D), totals[0], totals[1], totals[2], totals[3], totals[4], totals[5], totals[6], totals[7])
```

```python
import functools

import jax
import jax.numpy as jnp
from jax import lax
from jax.experimental import pallas as pl
from jax.experimental.pallas import tpu as pltpu
from jax.sharding import PartitionSpec as P

HEADS = 16
HD = 64
NT = (((1,), (1,)), ((), ()))
NEG = -1e30

def _bounds(len_ref, qb, tile):
    l0 = len_ref[0, 0]
    e1 = l0 + len_ref[0, 1]
    def start_of(r):
        return jnp.where(r >= e1, e1, jnp.where(r >= l0, l0, 0))
    first = qb * tile
    s_first, s_last = start_of(first), start_of(first + tile - 1)
    kmin = s_first // tile
    kmid = jnp.maximum(kmin, jnp.minimum(qb, (s_last + tile - 1) // tile))
    rows = first + lax.broadcasted_iota(jnp.int32, (1, tile), 1)
    return kmin, kmid, rows, start_of(rows)

def _fill_masked(dst, value, heads):
    lane = lax.broadcasted_iota(jnp.int32, value.shape, 1) // HD
    for h in range(heads):
        dst[pl.ds(h * value.shape[0], value.shape[0]), :] = jnp.where(lane == h, value, jnp.zeros_like(value))

def fwd_kernel(len_ref, q_ref, k_ref, vt_ref, o_ref, lse_ref, qm, acc, ps, *, tile, heads):
    qb = pl.program_id(0)
    kmin, kmid, rows, starts = _bounds(len_ref, qb, tile)
    _fill_masked(qm, q_ref[...] * jnp.bfloat16(0.125), heads)
    acc[...] = jnp.zeros_like(acc)
    def step(kb, carry, masked):
        at = pl.multiple_of(kb * tile, tile)
        kblk = k_ref[pl.ds(at, tile), :]
        if masked:
            kpos = at + lax.broadcasted_iota(jnp.int32, (tile, tile), 0)
            mask = (kpos >= starts) & (kpos <= rows)
        scores = [lax.dot_general(kblk, qm[pl.ds(h * tile, tile), :], NT, preferred_element_type=jnp.float32) for h in range(heads)]
        out, alphas = [], []
        for h in range(heads):
            m, l = carry[h]
            s = scores[h]
            if masked:
                s = jnp.where(mask, s, NEG)
            mn = jnp.maximum(m, jnp.max(s, 0, keepdims=True))
            p = jnp.exp(s - mn)
            if masked:
                p = jnp.where(mask, p, 0.0)
            alpha = jnp.exp(m - mn)
            l = l * alpha + jnp.sum(p, 0, keepdims=True)
            ps[:, pl.ds(h * tile, tile)] = p.astype(jnp.bfloat16)
            out.append((mn, l))
            alphas.append(alpha)
        for h in range(heads):
            part = jnp.dot(vt_ref[pl.ds(h * HD, HD), pl.ds(at, tile)], ps[:, pl.ds(h * tile, tile)], preferred_element_type=jnp.float32)
            acc[pl.ds(h * HD, HD), :] = acc[pl.ds(h * HD, HD), :] * alphas[h] + part
        return tuple(out)
    carry = tuple((jnp.full((1, tile), NEG, jnp.float32), jnp.zeros((1, tile), jnp.float32)) for _ in range(heads))
    carry = lax.fori_loop(kmin, kmid, functools.partial(step, masked=True), carry)
    carry = lax.fori_loop(kmid, qb, functools.partial(step, masked=False), carry)
    carry = step(qb, carry, True)
    for h in range(heads):
        m, l = carry[h]
        lse_ref[pl.ds(h, 1), :] = m + jnp.log(l)
        acc[pl.ds(h * HD, HD), :] = acc[pl.ds(h * HD, HD), :] / l
    o_ref[...] = acc[...].T.astype(jnp.bfloat16)

def attn_fwd(lengths, q, k, vt, tile=256):
    n, c = q.shape
    heads = c // HD
    return pl.pallas_call(
        functools.partial(fwd_kernel, tile=tile, heads=heads),
        grid_spec=pltpu.PrefetchScalarGridSpec(
            num_scalar_prefetch=1, grid=(n // tile,),
            in_specs=[pl.BlockSpec((tile, c), lambda i, L: (i, 0)), pl.BlockSpec((n, c), lambda i, L: (0, 0)), pl.BlockSpec((c, n), lambda i, L: (0, 0))],
            out_specs=[pl.BlockSpec((tile, c), lambda i, L: (i, 0)), pl.BlockSpec((heads, tile), lambda i, L: (0, i))],
            scratch_shapes=[pltpu.VMEM((heads * tile, c), jnp.bfloat16), pltpu.VMEM((c, tile), jnp.float32), pltpu.VMEM((tile, heads * tile), jnp.bfloat16)]),
        out_shape=[jax.ShapeDtypeStruct((n, c), jnp.bfloat16), jax.ShapeDtypeStruct((heads, n), jnp.float32)],
        compiler_params=pltpu.CompilerParams(vmem_limit_bytes=40 * 2**20),
        name="attn_fwd",
    )(lengths, q, k, vt)

def bwd_kernel(len_ref, q_ref, do_ref, o_ref, lse_ref, k_ref, v_ref, kt_ref, d_ref, qm, dom, ps, ds, dqt, dk, dv, *, tile, heads):
    qb = pl.program_id(0)
    c = heads * HD
    kmin, kmid, rows, starts = _bounds(len_ref, qb, tile)
    @pl.when(qb == 0)
    def _():
        dk[...] = jnp.zeros_like(dk)
        dv[...] = jnp.zeros_like(dv)
    _fill_masked(qm, q_ref[...] * jnp.bfloat16(0.125), heads)
    _fill_masked(dom, do_ref[...], heads)
    prod = (do_ref[...].astype(jnp.float32) * o_ref[...].astype(jnp.float32)).T
    delta = [jnp.sum(prod[h * HD:(h + 1) * HD], 0, keepdims=True) for h in range(heads)]
    dqt[...] = jnp.zeros_like(dqt)
    def step(kb, carry, masked):
        at = pl.multiple_of(kb * tile, tile)
        kblk = k_ref[pl.ds(at, tile), :]
        vblk = v_ref[pl.ds(at, tile), :]
        if masked:
            kpos = at + lax.broadcasted_iota(jnp.int32, (tile, tile), 0)
            mask = (kpos >= starts) & (kpos <= rows)
        for h in range(heads):
            mine = pl.ds(h * tile, tile)
            s = lax.dot_general(kblk, qm[mine, :], NT, preferred_element_type=jnp.float32)
            p = jnp.exp(s - lse_ref[pl.ds(h, 1), :])
            if masked:
                p = jnp.where(mask, p, 0.0)
            dp = lax.dot_general(vblk, dom[mine, :], NT, preferred_element_type=jnp.float32)
            g = (p * (dp - delta[h])).astype(jnp.bfloat16)
            ps[:, mine] = p.astype(jnp.bfloat16)
            ds[:, mine] = g
        dv[pl.ds(at, tile), :] += jnp.dot(ps[...], dom[...], preferred_element_type=jnp.float32)
        dk[pl.ds(at, tile), :] += jnp.dot(ds[...], qm[...], preferred_element_type=jnp.float32)
        for h in range(heads):
            lanes = pl.ds(h * HD, HD)
            dqt[lanes, :] += jnp.dot(kt_ref[lanes, pl.ds(at, tile)], ds[:, pl.ds(h * tile, tile)], preferred_element_type=jnp.float32)
        return carry
    lax.fori_loop(kmin, kmid, functools.partial(step, masked=True), 0)
    lax.fori_loop(kmid, qb, functools.partial(step, masked=False), 0)
    step(qb, 0, True)
    d_ref[pl.ds(pl.multiple_of(qb * tile, tile), tile), pl.ds(0, c)] = (dqt[...] * 0.125).T.astype(jnp.bfloat16)
    @pl.when(qb == pl.num_programs(0) - 1)
    def _():
        d_ref[:, pl.ds(c, c)] = dk[...].astype(jnp.bfloat16)
        d_ref[:, pl.ds(2 * c, c)] = dv[...].astype(jnp.bfloat16)

def attn_bwd(lengths, q, do, o, lse, k, v, kt, tile=256):
    n, c = q.shape
    heads = c // HD
    row = pl.BlockSpec((tile, c), lambda i, L: (i, 0))
    whole = pl.BlockSpec((n, c), lambda i, L: (0, 0))
    return pl.pallas_call(
        functools.partial(bwd_kernel, tile=tile, heads=heads),
        grid_spec=pltpu.PrefetchScalarGridSpec(
            num_scalar_prefetch=1, grid=(n // tile,),
            in_specs=[row, row, row, pl.BlockSpec((heads, tile), lambda i, L: (0, i)), whole, whole, pl.BlockSpec((c, n), lambda i, L: (0, 0))],
            out_specs=pl.BlockSpec((n, 3 * c), lambda i, L: (0, 0)),
            scratch_shapes=[pltpu.VMEM((heads * tile, c), jnp.bfloat16), pltpu.VMEM((heads * tile, c), jnp.bfloat16),
                            pltpu.VMEM((tile, heads * tile), jnp.bfloat16), pltpu.VMEM((tile, heads * tile), jnp.bfloat16),
                            pltpu.VMEM((c, tile), jnp.float32), pltpu.VMEM((n, c), jnp.float32), pltpu.VMEM((n, c), jnp.float32)]),
        out_shape=jax.ShapeDtypeStruct((n, 3 * c), jnp.bfloat16),
        compiler_params=pltpu.CompilerParams(vmem_limit_bytes=56 * 2**20),
        name="attn_bwd",
    )(lengths, q, do, o, lse, k, v, kt)

epsilon = 1e-05


def layer_norm(values, gain, shift):
    centre = values - jnp.mean(values, -1, keepdims=True)
    spread = jnp.mean(centre * centre, -1, keepdims=True)
    return centre * lax.rsqrt(spread + epsilon) * gain + shift


def gelu_tanh(values):
    return jax.nn.gelu(values, approximate=True)


def outer_sum(left, right):
    return lax.dot_general(left, right, (((0,), (0,)), ((), ())), preferred_element_type=jnp.float32)


def times_transposed(left, right):
    return lax.dot_general(left, right, NT, preferred_element_type=jnp.float32)


def column_sums(values):
    return jnp.sum(values.astype(jnp.float32), 0)


def exchange(values, axis, bit):
    return lax.ppermute(values, axis, [(i, i ^ bit) for i in range(lax.axis_size(axis))])


def columns_for(values, order, blocks):
    width = values.shape[1] // blocks
    return jnp.concatenate([lax.dynamic_slice_in_dim(values, b * width, width, 1) for b in order], 1)


def reduced_outer(left, right, me, blocks):
    low = lambda t: t.astype(jnp.bfloat16)
    away = low(outer_sum(left, columns_for(right, (me ^ 3, me ^ 1), blocks)))
    stay = outer_sum(left, columns_for(right, (me ^ 2, me), blocks))
    half = low(stay + exchange(away, "blk", 1).astype(jnp.float32))
    width = half.shape[1] // 2
    quarter = half[:, width:] + exchange(half[:, :width], "blk", 2)
    return lax.psum_scatter(quarter, "dp", scatter_dimension=0, tiled=True).astype(jnp.float32)


def local(tokens, cotangent, lengths, qkv_weight, out_weight, up_weight, down_weight, norm_gain, norm_bias, proj_bias, ffn_bias):
    rows, width = tokens.shape
    blocks = lax.axis_size("blk")
    me = lax.axis_index("blk")
    own = width // blocks
    inputs = tokens.astype(jnp.float32)
    normed_in, pull_first = jax.vjp(layer_norm, inputs, norm_gain[0], norm_bias[0])
    first_normed = normed_in.astype(jnp.bfloat16)
    first_all = lax.all_gather(first_normed, "blk", axis=0, tiled=True)

    def own_columns(values, third):
        return lax.dynamic_slice_in_dim(values, third * width + me * own, own, values.ndim - 1)

    own_weight = jnp.concatenate([own_columns(qkv_weight, third) for third in range(3)], 1)
    query_bias = lax.dynamic_slice_in_dim(proj_bias[0], me * own, own)
    value_bias = lax.dynamic_slice_in_dim(proj_bias[1], me * own, own)
    projected = jnp.dot(first_all, own_weight, preferred_element_type=jnp.float32)
    queries = (projected[:, :own] + query_bias).astype(jnp.bfloat16)
    keys = projected[:, own : 2 * own].astype(jnp.bfloat16)
    values = (projected[:, 2 * own :] + value_bias).astype(jnp.bfloat16)
    attended_own, log_total = attn_fwd(lengths, queries, keys, values.T)
    attended = lax.all_to_all(attended_own, "blk", split_axis=0, concat_axis=1, tiled=True)
    attn_branch = jnp.dot(attended, out_weight, preferred_element_type=jnp.float32) + proj_bias[2]
    attn_normed, pull_attn = jax.vjp(layer_norm, attn_branch, norm_gain[1], norm_bias[1])
    middle = inputs + attn_normed
    second_full, pull_second = jax.vjp(layer_norm, middle, norm_gain[2], norm_bias[2])
    second_normed = second_full.astype(jnp.bfloat16)
    pre_gelu = jnp.dot(second_normed, up_weight, preferred_element_type=jnp.float32) + ffn_bias
    activated_full, pull_gelu = jax.vjp(gelu_tanh, pre_gelu)
    activated = activated_full.astype(jnp.bfloat16)
    ffn_branch = jnp.dot(activated, down_weight, preferred_element_type=jnp.float32) + proj_bias[3]
    ffn_normed, pull_ffn = jax.vjp(layer_norm, ffn_branch, norm_gain[3], norm_bias[3])
    mixed = (middle + ffn_normed).astype(jnp.bfloat16)
    incoming = cotangent.astype(jnp.float32)
    grad_ffn, gain_three, shift_three = pull_ffn(incoming)
    grad_ffn_low = grad_ffn.astype(jnp.bfloat16)
    down_grad = reduced_outer(activated, grad_ffn_low, me, blocks)
    bias_three = column_sums(grad_ffn_low)
    (grad_pre,) = pull_gelu(times_transposed(grad_ffn_low, down_weight))
    grad_pre_low = grad_pre.astype(jnp.bfloat16)
    up_grad = reduced_outer(second_normed, grad_pre_low, me, blocks)
    hidden_bias = column_sums(grad_pre_low)
    grad_from_ffn, gain_two, shift_two = pull_second(times_transposed(grad_pre_low, up_weight))
    grad_middle = incoming + grad_from_ffn
    grad_attn, gain_one, shift_one = pull_attn(grad_middle)
    grad_attn_low = grad_attn.astype(jnp.bfloat16)
    out_grad = reduced_outer(attended, grad_attn_low, me, blocks)
    bias_two = column_sums(grad_attn_low)
    grad_attended = times_transposed(grad_attn_low, out_weight).astype(jnp.bfloat16)
    grad_own = lax.all_to_all(grad_attended, "blk", split_axis=1, concat_axis=0, tiled=True)
    grad_projected = attn_bwd(lengths, queries, grad_own, attended_own, log_total, keys, values, keys.T)

    qkv_term = lax.psum_scatter(outer_sum(first_all, grad_projected).astype(jnp.bfloat16), "dp", scatter_dimension=0, tiled=True)
    qkv_blocks = lax.all_gather(qkv_term, "blk", axis=0)
    qkv_rows = qkv_blocks.reshape(blocks, -1, 3, own).transpose(1, 2, 0, 3).reshape(-1, 3 * width)
    qkv_grad = lax.dynamic_slice_in_dim(qkv_rows, me * 3 * own, 3 * own, 1).astype(jnp.float32)
    bias_query = lax.dynamic_update_slice_in_dim(jnp.zeros((width,), jnp.float32), column_sums(grad_projected[:, :own]), me * own, 0)
    bias_value = lax.dynamic_update_slice_in_dim(jnp.zeros((width,), jnp.float32), column_sums(grad_projected[:, 2 * own :]), me * own, 0)
    partial = times_transposed(grad_projected, own_weight)
    by_block = partial.astype(jnp.bfloat16).reshape(2, 2, rows, width)
    core, chip = me % 2, me // 2
    away = lax.dynamic_index_in_dim(by_block, 1 - core, 1, False)
    stay = lax.dynamic_index_in_dim(by_block, core, 1, False)
    half = stay + exchange(away, "blk", 1)
    grad_from_attn = lax.dynamic_index_in_dim(half, chip, 0, False).astype(jnp.float32) + exchange(
        lax.dynamic_index_in_dim(half, 1 - chip, 0, False), "blk", 2
    ).astype(jnp.float32)
    grad_first, gain_zero, shift_zero = pull_first(grad_from_attn)
    token_grad = (grad_middle + grad_first).astype(jnp.bfloat16)
    small = jnp.stack(
        [gain_zero, gain_one, gain_two, gain_three, shift_zero, shift_one, shift_two, shift_three, bias_query, bias_value, bias_two, bias_three]
    )
    parts = lax.axis_size("dp")
    packed = jnp.concatenate(
        [small.reshape(12, parts, -1).transpose(1, 0, 2).reshape(parts, -1), hidden_bias.reshape(parts, -1)], 1
    )
    packed = lax.psum(lax.psum_scatter(packed, "dp", scatter_dimension=0, tiled=True), "blk")[0]
    small = packed[: 12 * width // parts].reshape(12, -1)
    return (
        mixed,
        token_grad,
        qkv_grad,
        out_grad,
        up_grad,
        down_grad,
        small[:4],
        small[4:8],
        small[8:],
        packed[12 * width // parts :],
    )


def solution(mesh):
    return jax.shard_map(
        local,
        mesh=mesh,
        in_specs=(P(("dp", "blk"), None), P(("dp", "blk"), None), P("dp", None)) + (P(),) * 8,
        out_specs=(P(("dp", "blk"), None), P(("dp", "blk"), None))
        + (P("dp", "blk"),) * 4
        + (P(None, "dp"),) * 3
        + (P("dp"),),
        check_vma=False,
    )
```

```python
import functools

import jax
import jax.numpy as jnp
from jax import lax
from jax.experimental import pallas as pl
from jax.experimental.pallas import tpu as pltpu
from jax.sharding import PartitionSpec as P

epsilon = 1e-05
HD = 64
NT = (((1,), (1,)), ((), ()))
NEG = -1e30
TILE = 256


def _bounds(len_ref, qb):
    l0 = len_ref[0, 0]
    e1 = l0 + len_ref[0, 1]

    def start_of(r):
        return jnp.where(r >= e1, e1, jnp.where(r >= l0, l0, 0))

    first = qb * TILE
    s_first, s_last = start_of(first), start_of(first + TILE - 1)
    kmin = s_first // TILE
    kmid = jnp.maximum(kmin, jnp.minimum(qb, (s_last + TILE - 1) // TILE))
    rows = first + lax.broadcasted_iota(jnp.int32, (1, TILE), 1)
    return kmin, kmid, rows, start_of(rows)


def _walk(len_ref, qb, step, carry, wide):
    kmin, kmid, rows, starts = _bounds(len_ref, qb)

    def masked(kb, carry):
        at = pl.multiple_of(kb * TILE, TILE)
        kpos = at + lax.broadcasted_iota(jnp.int32, (TILE, TILE), 0)
        return step(at, TILE, (kpos >= starts) & (kpos <= rows), carry)

    def plain(size):
        def run(kb, carry):
            return step(pl.multiple_of(kb * TILE, TILE), size * TILE, None, carry)

        return run

    carry = lax.fori_loop(kmin, kmid, masked, carry)
    at, left = kmid, qb - kmid
    for size in wide:
        count = left // size
        base = at
        carry = lax.fori_loop(0, count, lambda i, c, base=base, size=size: plain(size)(base + i * size, c), carry)
        at, left = at + count * size, left - count * size
    return masked(qb, carry)


def _fill_masked(dst, value, heads):
    lane = lax.broadcasted_iota(jnp.int32, value.shape, 1) // HD
    for h in range(heads):
        dst[pl.ds(h * TILE, TILE), :] = jnp.where(lane == h, value, jnp.zeros_like(value))


def fwd_kernel(len_ref, q_ref, k_ref, v_ref, o_ref, lse_ref, qm, acc, ps, vt, *, heads, wide):
    qb = pl.program_id(0)

    @pl.when(qb == 0)
    def _():
        vt[...] = v_ref[...].T

    _fill_masked(qm, q_ref[...] * jnp.bfloat16(0.125), heads)
    acc[...] = jnp.zeros_like(acc)

    def step(at, size, mask, carry):
        keys = pl.ds(at, size)
        scores = [
            lax.dot_general(k_ref[keys, :], qm[pl.ds(h * TILE, TILE), :], NT, preferred_element_type=jnp.float32)
            for h in range(heads)
        ]
        out, fades = [], []
        for h in range(heads):
            m, l = carry[h]
            s = scores[h]
            if mask is not None:
                s = jnp.where(mask, s, NEG)
            top = jnp.maximum(m, jnp.max(s, 0, keepdims=True))
            p = jnp.exp(s - top)
            if mask is not None:
                p = jnp.where(mask, p, 0.0)
            fade = jnp.exp(m - top)
            ps[pl.ds(0, size), pl.ds(h * TILE, TILE)] = p.astype(jnp.bfloat16)
            out.append((top, l * fade + jnp.sum(p, 0, keepdims=True)))
            fades.append(fade)
        for h in range(heads):
            lanes = pl.ds(h * HD, HD)
            part = jnp.dot(vt[lanes, keys], ps[pl.ds(0, size), pl.ds(h * TILE, TILE)], preferred_element_type=jnp.float32)
            acc[lanes, :] = acc[lanes, :] * fades[h] + part
        return tuple(out)

    carry = tuple((jnp.full((1, TILE), NEG, jnp.float32), jnp.zeros((1, TILE), jnp.float32)) for _ in range(heads))
    carry = _walk(len_ref, qb, step, carry, wide)
    for h in range(heads):
        m, l = carry[h]
        lse_ref[pl.ds(h, 1), :] = m + jnp.log(l)
        acc[pl.ds(h * HD, HD), :] = acc[pl.ds(h * HD, HD), :] / l
    o_ref[...] = acc[...].T.astype(jnp.bfloat16)


def attn_fwd(lengths, qkv, pair=0, lane=256, wide=(1,)):
    n = qkv.shape[0]
    heads = lane // HD
    return pl.pallas_call(
        functools.partial(fwd_kernel, heads=heads, wide=wide),
        grid_spec=pltpu.PrefetchScalarGridSpec(
            num_scalar_prefetch=1,
            grid=(n // TILE,),
            in_specs=[
                pl.BlockSpec((TILE, lane), lambda i, L: (i, 3 * pair)),
                pl.BlockSpec((n, lane), lambda i, L: (0, 3 * pair + 1)),
                pl.BlockSpec((n, lane), lambda i, L: (0, 3 * pair + 2)),
            ],
            out_specs=[pl.BlockSpec((TILE, lane), lambda i, L: (i, 0)), pl.BlockSpec((heads, TILE), lambda i, L: (0, i))],
            scratch_shapes=[
                pltpu.VMEM((heads * TILE, lane), jnp.bfloat16),
                pltpu.VMEM((lane, TILE), jnp.float32),
                pltpu.VMEM((wide[0] * TILE, heads * TILE), jnp.bfloat16),
                pltpu.VMEM((lane, n), jnp.bfloat16),
            ],
        ),
        out_shape=[jax.ShapeDtypeStruct((n, lane), jnp.bfloat16), jax.ShapeDtypeStruct((heads, n), jnp.float32)],
        compiler_params=pltpu.CompilerParams(vmem_limit_bytes=40 * 2**20),
        cost_estimate=pl.CostEstimate(flops=n * n * lane * 9, bytes_accessed=10 * n * lane, transcendentals=n * n * heads // 2),
        name="attn_fwd",
    )(lengths, qkv, qkv, qkv)


def bwd_kernel(len_ref, q_ref, do_ref, o_ref, lse_ref, k_ref, v_ref, d_ref, qm, dom, ps, ds, dqt, dk, dv, kt, *, heads, wide):
    qb = pl.program_id(0)
    c = heads * HD

    @pl.when(qb == 0)
    def _():
        dk[...] = jnp.zeros_like(dk)
        dv[...] = jnp.zeros_like(dv)
        kt[...] = k_ref[...].T

    _fill_masked(qm, q_ref[...] * jnp.bfloat16(0.125), heads)
    _fill_masked(dom, do_ref[...], heads)
    prod = (do_ref[...].astype(jnp.float32) * o_ref[...].astype(jnp.float32)).T
    delta = [jnp.sum(prod[h * HD : (h + 1) * HD], 0, keepdims=True) for h in range(heads)]
    dqt[...] = jnp.zeros_like(dqt)

    def step(at, size, mask, carry):
        keys = pl.ds(at, size)
        used = pl.ds(0, size)
        for h in range(heads):
            mine = pl.ds(h * TILE, TILE)
            s = lax.dot_general(k_ref[keys, :], qm[mine, :], NT, preferred_element_type=jnp.float32)
            p = jnp.exp(s - lse_ref[pl.ds(h, 1), :])
            if mask is not None:
                p = jnp.where(mask, p, 0.0)
            dp = lax.dot_general(v_ref[keys, :], dom[mine, :], NT, preferred_element_type=jnp.float32)
            ps[used, mine] = p.astype(jnp.bfloat16)
            ds[used, mine] = (p * (dp - delta[h])).astype(jnp.bfloat16)
        dv[keys, :] += jnp.dot(ps[used, :], dom[...], preferred_element_type=jnp.float32)
        dk[keys, :] += jnp.dot(ds[used, :], qm[...], preferred_element_type=jnp.float32)
        for h in range(heads):
            lanes = pl.ds(h * HD, HD)
            dqt[lanes, :] += jnp.dot(kt[lanes, keys], ds[used, pl.ds(h * TILE, TILE)], preferred_element_type=jnp.float32)
        return carry

    _walk(len_ref, qb, step, 0, wide)
    d_ref[pl.ds(pl.multiple_of(qb * TILE, TILE), TILE), pl.ds(0, c)] = (dqt[...] * 0.125).T.astype(jnp.bfloat16)

    @pl.when(qb == pl.num_programs(0) - 1)
    def _():
        d_ref[:, pl.ds(c, c)] = dk[...].astype(jnp.bfloat16)
        d_ref[:, pl.ds(2 * c, c)] = dv[...].astype(jnp.bfloat16)


def attn_bwd(lengths, qkv, do, o, lse, pair=0, lane=256, wide=(1,)):
    n = qkv.shape[0]
    heads = lane // HD
    row = lambda col: pl.BlockSpec((TILE, lane), lambda i, L: (i, col))
    whole = lambda col: pl.BlockSpec((n, lane), lambda i, L: (0, col))
    return pl.pallas_call(
        functools.partial(bwd_kernel, heads=heads, wide=wide),
        grid_spec=pltpu.PrefetchScalarGridSpec(
            num_scalar_prefetch=1,
            grid=(n // TILE,),
            in_specs=[
                row(3 * pair), row(pair), row(0), pl.BlockSpec((heads, TILE), lambda i, L: (0, i)),
                whole(3 * pair + 1), whole(3 * pair + 2),
            ],
            out_specs=pl.BlockSpec((n, 3 * lane), lambda i, L: (0, pair)),
            scratch_shapes=[
                pltpu.VMEM((heads * TILE, lane), jnp.bfloat16),
                pltpu.VMEM((heads * TILE, lane), jnp.bfloat16),
                pltpu.VMEM((wide[0] * TILE, heads * TILE), jnp.bfloat16),
                pltpu.VMEM((wide[0] * TILE, heads * TILE), jnp.bfloat16),
                pltpu.VMEM((lane, TILE), jnp.float32),
                pltpu.VMEM((n, lane), jnp.float32),
                pltpu.VMEM((n, lane), jnp.float32),
                pltpu.VMEM((lane, n), jnp.bfloat16),
            ],
        ),
        out_shape=jax.ShapeDtypeStruct(qkv.shape, jnp.bfloat16),
        compiler_params=pltpu.CompilerParams(vmem_limit_bytes=40 * 2**20),
        cost_estimate=pl.CostEstimate(flops=n * n * lane * 11, bytes_accessed=20 * n * lane, transcendentals=n * n * heads // 2),
        name="attn_bwd",
    )(lengths, qkv, do, o, lse, qkv, qkv)


def _stats(v):
    c = v - jnp.mean(v, -1, keepdims=True)
    r = lax.rsqrt(jnp.mean(c * c, -1, keepdims=True) + epsilon)
    return c * r, r


def _pull(n, r, e):
    return r * (e - jnp.mean(e, -1, keepdims=True) - n * jnp.mean(e * n, -1, keepdims=True))


def _fold(v):
    return jnp.sum(v.reshape(-1, 8, v.shape[-1]), 0)


def _each(total, size, fn):
    def body(i, carry):
        fn(pl.ds(pl.multiple_of(i * size, size), size))
        return carry

    lax.fori_loop(0, total // size, body, 0)


def ffn_kernel(
    order, places,
    x_ref, cot_ref, att_ref, wo_ref, up_ref, down_ref, gain_ref, shift_ref, bias_ref, fb_ref,
    mixed_ref, gmid_ref, gatt_ref, out_away, out_stay, up_away, up_stay, down_away, down_stay, small_ref, hid_ref,
    act, slope, second, second_t, turned, branch, ffn,
    sums, *, tiles, cut, strip,
):
    s = pl.program_id(0)
    rows, width = x_ref.shape
    own = width // 4
    f32 = jnp.float32
    hid = up_ref.shape[1]
    row = lambda ref, i: ref[pl.ds(i, 1), :]

    def turn_into(dst, value):
        flipped = value.T
        for b in range(4):
            dst[pl.ds(b * own, own), :] = dst_rows(flipped, b)

    def dst_rows(flipped, b):
        return flipped[b * own : (b + 1) * own, :]

    @pl.when(s == 0)
    def _():
        sums[...] = jnp.zeros_like(sums)
        for i in range(rows // cut):
            at = pl.ds(i * cut, cut)
            branch[at, :] = jnp.dot(att_ref[at, :], wo_ref[...], preferred_element_type=f32) + row(bias_ref, 2)

        def normed(at):
            n, _ = _stats(branch[at, :])
            m = x_ref[at, :].astype(f32) + n * row(gain_ref, 1) + row(shift_ref, 1)
            gmid_ref[at, :] = m
            n, _ = _stats(m)
            second[at, :] = (n * row(gain_ref, 2) + row(shift_ref, 2)).astype(jnp.bfloat16)

        _each(rows, strip, normed)
        second_t[...] = second[...].T

    @pl.when(s < tiles)
    def _():
        at_hid = pl.ds(pl.multiple_of(s * hid, hid), hid)
        for i in range(rows // cut):
            at = pl.ds(i * cut, cut)
            u = jnp.dot(second[at, :], up_ref[...], preferred_element_type=f32) + fb_ref[...]
            c1, c3 = 0.7978845608028654, 0.7978845608028654 * 0.044715
            sq = u * u
            t = jnp.tanh(u * (c1 + c3 * sq))
            half = 0.5 + 0.5 * t
            a = (u * half).astype(jnp.bfloat16)
            act[at, at_hid] = a
            slope[at, at_hid] = (half + (0.5 * u) * (1.0 - t * t) * (c1 + 3.0 * c3 * sq)).astype(jnp.bfloat16)
            part = jnp.dot(a, down_ref[...], preferred_element_type=f32)

            @pl.when(s == 0)
            def _():
                ffn[at, :] = part + row(bias_ref, 3)

            @pl.when(s > 0)
            def _():
                ffn[at, :] += part

    @pl.when(s == tiles - 1)
    def _():
        def normed(at):
            n, r = _stats(ffn[at, :])
            y = cot_ref[at, :].astype(f32)
            mixed_ref[at, :] = (gmid_ref[at, :] + n * row(gain_ref, 3) + row(shift_ref, 3)).astype(jnp.bfloat16)
            g = _pull(n, r, y * row(gain_ref, 3)).astype(jnp.bfloat16)
            second[at, :] = g
            sums[pl.ds(16, 8), :] += _fold(y * n)
            sums[pl.ds(40, 8), :] += _fold(y)
            sums[pl.ds(56, 8), :] += _fold(g.astype(f32))

        _each(rows, strip, normed)
        flipped = second[...].T
        for b in range(4):
            ffn_rows = pl.ds(pl.multiple_of(places[b] * own, own), own)
            turned[ffn_rows, :] = flipped[b * own : (b + 1) * own, :]

    @pl.when(s >= tiles)
    def _():
        at_hid = pl.ds(pl.multiple_of((s - tiles) * hid, hid), hid)
        pre = []
        for i in range(rows // cut):
            at = pl.ds(i * cut, cut)
            g = lax.dot_general(second[at, :], down_ref[...], NT, preferred_element_type=f32) * slope[at, at_hid].astype(f32)
            g = g.astype(jnp.bfloat16)
            slope[at, at_hid] = g
            pre.append(_fold(g.astype(f32)))
            part = lax.dot_general(g, up_ref[...], NT, preferred_element_type=f32)

            @pl.when(s == tiles)
            def _():
                ffn[at, :] = part

            @pl.when(s > tiles)
            def _():
                ffn[at, :] += part

        hid_ref[0] = jnp.sum(sum(pre), 0, keepdims=True)
        down_grad = jnp.dot(turned[...], act[:, at_hid], preferred_element_type=f32).astype(jnp.bfloat16)
        down_away[0] = down_grad[: width // 2]
        down_stay[0] = down_grad[width // 2 :]
        up_grad = jnp.dot(second_t[...], slope[:, at_hid], preferred_element_type=f32).astype(jnp.bfloat16)

        @pl.when(s < tiles + tiles // 2)
        def _():
            up_away[...] = up_grad.reshape(up_away.shape)

        @pl.when(s >= tiles + tiles // 2)
        def _():
            up_stay[...] = up_grad.reshape(up_stay.shape)

    @pl.when(s == 2 * tiles - 1)
    def _():
        def normed(at):
            n, r = _stats(gmid_ref[at, :])
            y = ffn[at, :]
            gm = cot_ref[at, :].astype(f32) + _pull(n, r, y * row(gain_ref, 2))
            gmid_ref[at, :] = gm
            sums[pl.ds(8, 8), :] += _fold(y * n)
            sums[pl.ds(32, 8), :] += _fold(y)
            n, r = _stats(branch[at, :])
            g = _pull(n, r, gm * row(gain_ref, 1)).astype(jnp.bfloat16)
            second[at, :] = g
            sums[pl.ds(0, 8), :] += _fold(gm * n)
            sums[pl.ds(24, 8), :] += _fold(gm)
            sums[pl.ds(48, 8), :] += _fold(g.astype(f32))

        _each(rows, strip, normed)
        flipped = second[...].T
        for b in range(4):
            at = pl.ds(pl.multiple_of(places[b] * own, own), own)
            turned[at, :] = flipped[b * own : (b + 1) * own, :]
        for i in range(rows // cut):
            at = pl.ds(i * cut, cut)
            gatt_ref[at, :] = lax.dot_general(second[at, :], wo_ref[...], NT, preferred_element_type=f32).astype(jnp.bfloat16)
        grad = jnp.dot(turned[...], att_ref[...], preferred_element_type=f32).astype(jnp.bfloat16)
        out_away[...] = grad[: width // 2]
        out_stay[...] = grad[width // 2 :]
        for i in range(8):
            small_ref[pl.ds(i, 1), :] = jnp.sum(sums[pl.ds(8 * i, 8), :], 0, keepdims=True)


def ffn_both(me, tokens, cotangent, attended, out_weight, up_weight, down_weight, norm_gain, norm_bias, proj_bias, ffn_bias):
    rows, width = tokens.shape
    hidden = up_weight.shape[1]
    tiles = 8
    hid = hidden // tiles
    half = tiles // 2
    bf16, f32 = jnp.bfloat16, jnp.float32
    blocks = jnp.stack([me ^ 3, me ^ 1, me ^ 2, me])
    order = (blocks[:, None] * 2 + jnp.arange(2)[None]).reshape(-1).astype(jnp.int32)
    spot = jnp.arange(4) ^ me
    places = jnp.where(spot == 3, 0, jnp.where(spot == 1, 1, jnp.where(spot == 2, 2, 3))).astype(jnp.int32)
    tile_of = lambda s: lax.rem(s, tiles)
    late = lambda s: jnp.maximum(s - tiles, 0)
    whole = lambda *shape: pl.BlockSpec(shape, lambda s, o, p: (0,) * len(shape))
    once = lambda *shape: pl.BlockSpec(shape, lambda s, o, p: (0,) * len(shape), pipeline_mode=pl.Buffered(1))
    return pl.pallas_call(
        functools.partial(ffn_kernel, tiles=tiles, cut=rows, strip=rows // 4),
        grid_spec=pltpu.PrefetchScalarGridSpec(
            num_scalar_prefetch=2,
            grid=(2 * tiles,),
            in_specs=[
                once(rows, width), once(rows, width), once(rows, width), once(width, width),
                pl.BlockSpec((width, hid), lambda s, o, p: (0, o[tile_of(s)])),
                pl.BlockSpec((hid, width), lambda s, o, p: (o[tile_of(s)], 0)),
                once(4, width), once(4, width), once(4, width),
                pl.BlockSpec((1, hid), lambda s, o, p: (0, o[tile_of(s)])),
            ],
            out_specs=[
                once(rows, width), once(rows, width), once(rows, width),
                once(width // 2, width), once(width // 2, width),
                pl.BlockSpec((8, 1, width // 8, hid), lambda s, o, p: (0, jnp.minimum(late(s), half - 1), 0, 0)),
                pl.BlockSpec((8, 1, width // 8, hid), lambda s, o, p: (0, jnp.maximum(late(s) - half, 0), 0, 0)),
                pl.BlockSpec((1, width // 2, hid), lambda s, o, p: (o[late(s)], 0, 0)),
                pl.BlockSpec((1, width // 2, hid), lambda s, o, p: (o[late(s)], 0, 0)),
                once(8, width),
                pl.BlockSpec((1, 1, hid), lambda s, o, p: (o[late(s)], 0, 0)),
            ],
            scratch_shapes=[
                pltpu.VMEM((rows, hidden), bf16), pltpu.VMEM((rows, hidden), bf16),
                pltpu.VMEM((rows, width), bf16), pltpu.VMEM((width, rows), bf16), pltpu.VMEM((width, rows), bf16),
                pltpu.VMEM((rows, width), f32), pltpu.VMEM((rows, width), f32),
                pltpu.VMEM((64, width), f32),
            ],
        ),
        out_shape=[
            jax.ShapeDtypeStruct((rows, width), bf16), jax.ShapeDtypeStruct((rows, width), f32), jax.ShapeDtypeStruct((rows, width), bf16),
            jax.ShapeDtypeStruct((width // 2, width), bf16), jax.ShapeDtypeStruct((width // 2, width), bf16),
            jax.ShapeDtypeStruct((8, half, width // 8, hid), bf16), jax.ShapeDtypeStruct((8, half, width // 8, hid), bf16),
            jax.ShapeDtypeStruct((tiles, width // 2, hid), bf16), jax.ShapeDtypeStruct((tiles, width // 2, hid), bf16),
            jax.ShapeDtypeStruct((8, width), f32), jax.ShapeDtypeStruct((tiles, 1, hid), f32),
        ],
        compiler_params=pltpu.CompilerParams(vmem_limit_bytes=60 * 2**20),
        cost_estimate=pl.CostEstimate(flops=50 * rows * width * width, bytes_accessed=80 * 2**20, transcendentals=rows * hidden),
        name="ffn_both",
    )(order, places, tokens, cotangent, attended, out_weight, up_weight, down_weight, norm_gain, norm_bias, proj_bias, ffn_bias.reshape(1, -1))


def project_kernel(x_ref, w_hbm, gain_ref, shift_ref, bias_ref, all_ref, qkv_ref, w_ref, w_sems, chip_send, chip_recv, core_send, core_recv, pass_send, pass_recv, *, pieces):
    me = lax.axis_index("blk")
    core = lax.rem(me, 2)
    twin, other, last = me + 1 - 2 * core, lax.rem(me + 2, 4), 3 - me
    rows, width = x_ref.shape
    own = width // 4
    size = rows // pieces
    barrier = pltpu.get_barrier_semaphore()
    for target in (twin, other):
        pl.semaphore_signal(barrier, inc=1, device_id={"blk": target}, device_id_type=pl.DeviceIdType.MESH)
    loads = []
    for third in range(3):
        columns = pl.ds(pl.multiple_of(third * width + me * own, own), own)
        load = pltpu.make_async_copy(w_hbm.at[:, columns], w_ref.at[:, pl.ds(third * own, own)], w_sems.at[third])
        load.start()
        loads.append(load)

    def at(block, i):
        return pl.ds(pl.multiple_of(block * rows + i * size, size), size)

    def send(block, i, target, sends, recvs):
        piece = all_ref.at[at(block, i), :]
        copy = pltpu.make_async_remote_copy(
            src_ref=piece, dst_ref=piece, send_sem=sends.at[i], recv_sem=recvs.at[i],
            device_id={"blk": target}, device_id_type=pl.DeviceIdType.MESH,
        )
        return copy

    def project(block, i):
        where = at(block, i)
        got = jnp.dot(all_ref[where, :], w_ref[...], preferred_element_type=jnp.float32) + bias_ref[...]
        qkv_ref[where, :] = got.astype(jnp.bfloat16)

    sent = []
    for i in range(pieces):
        n, _ = _stats(x_ref[pl.ds(i * size, size), :].astype(jnp.float32))
        all_ref[at(me, i), :] = (n * gain_ref[pl.ds(0, 1), :] + shift_ref[pl.ds(0, 1), :]).astype(jnp.bfloat16)
        if i == 0:
            pl.semaphore_wait(barrier, 2)
        for target, sends, recvs in ((other, chip_send, chip_recv), (twin, core_send, core_recv)):
            copy = send(me, i, target, sends, recvs)
            copy.start()
            sent.append(copy)
    for load in loads:
        load.wait()
    for i in range(pieces):
        project(me, i)
    for i in range(pieces):
        send(twin, i, twin, core_send, core_recv).wait_recv()
        project(twin, i)
    for i in range(pieces):
        send(other, i, other, chip_send, chip_recv).wait_recv()
        copy = send(other, i, twin, pass_send, pass_recv)
        copy.start()
        sent.append(copy)
        project(other, i)
        if i > 0:
            send(last, i - 1, twin, pass_send, pass_recv).wait_recv()
            project(last, i - 1)
    send(last, pieces - 1, twin, pass_send, pass_recv).wait_recv()
    project(last, pieces - 1)
    for copy in sent:
        copy.wait_send()


def gather_project(tokens, qkv_weight, norm_gain, norm_bias, bias):
    rows, width = tokens.shape
    pieces = 4
    vmem = pl.BlockSpec(memory_space=pltpu.VMEM)
    dma = pltpu.SemaphoreType.DMA((pieces,))
    return pl.pallas_call(
        functools.partial(project_kernel, pieces=pieces),
        in_specs=[vmem, pl.BlockSpec(memory_space=pl.ANY), vmem, vmem, vmem],
        out_specs=[vmem, vmem],
        out_shape=[jax.ShapeDtypeStruct((4 * rows, width), jnp.bfloat16), jax.ShapeDtypeStruct((4 * rows, 3 * width // 4), jnp.bfloat16)],
        scratch_shapes=[pltpu.VMEM((width, 3 * width // 4), jnp.bfloat16), pltpu.SemaphoreType.DMA((3,))] + [dma] * 6,
        compiler_params=pltpu.CompilerParams(collective_id=0, has_side_effects=True, vmem_limit_bytes=48 * 2**20),
        name="gather_project",
    )(tokens, qkv_weight, norm_gain, norm_bias, bias)


def outer_sum(left, right):
    return lax.dot_general(left, right, (((0,), (0,)), ((), ())), preferred_element_type=jnp.float32)


def times_transposed(left, right):
    return lax.dot_general(left, right, NT, preferred_element_type=jnp.float32)


def column_sums(values):
    return jnp.sum(values.astype(jnp.float32), 0)


def exchange(values, axis, bit):
    return lax.ppermute(values, axis, [(i, i ^ bit) for i in range(lax.axis_size(axis))])


def plus(left, right):
    return (left.astype(jnp.float32) + right.astype(jnp.float32)).astype(jnp.bfloat16)


def pick(values, index, axis):
    return lax.dynamic_index_in_dim(values, index, axis, False)


def sum_everywhere(values):
    for axis in ("blk", "dp"):
        bit = 1
        while bit < lax.axis_size(axis):
            values = values + exchange(values, axis, bit)
            bit *= 2
    return values


def far_sum(half):
    line = lax.axis_index("dp") // 2
    parts = lax.axis_size("dp")
    if parts > 8:
        groups = [[d for d in range(parts) if d % 2 == b] for b in range(2)]
        return jnp.sum(lax.all_to_all(half, "dp", 0, 0, axis_index_groups=groups).astype(jnp.float32), 0)
    got = [exchange(pick(half, line ^ step, 0), "dp", 2 * step) for step in range(1, parts // 2)]
    return pick(half, line, 0).astype(jnp.float32) + sum(piece.astype(jnp.float32) for piece in got)


def weight_sums(up, down, out):
    parts = lax.axis_size("dp")
    width, hidden = out.shape[1], down.shape[0] * down.shape[2]
    own = width // 4
    if parts == 8:
        thin = own // 4
        pieces = [
            up.reshape(8, 2, -1, hidden // 8),
            down.reshape(8, 2, -1, hidden // 8),
            out.reshape(2, 4, thin, 8, width // 8).transpose(3, 0, 2, 1, 4).reshape(8, 2, thin, width // 2),
        ]
        got = lax.psum_scatter(jnp.concatenate(pieces, 2), "dp", scatter_dimension=0, tiled=False)
        total = got[1].astype(jnp.float32) + exchange(got[0], "blk", 2).astype(jnp.float32)
        up_grad = total[:own].reshape(2, width // 8, -1).transpose(1, 0, 2).reshape(width // 8, -1)
        out_grad = total[2 * own :].reshape(thin, 4, -1).transpose(1, 0, 2).reshape(own, -1)
        return up_grad, total[own : 2 * own].T, out_grad.T
    pieces = [
        up.reshape(8, 2, 2, width // 8, -1).transpose(1, 0, 3, 2, 4).reshape(2, parts, -1),
        down.reshape(8, 2, own, -1).transpose(1, 2, 0, 3).reshape(2, own, parts, -1).transpose(0, 2, 1, 3).reshape(2, parts, -1),
        out.reshape(2, own, parts, -1).transpose(0, 2, 1, 3).reshape(2, parts, -1),
    ]
    ends = [pieces[0].shape[2], pieces[0].shape[2] + pieces[1].shape[2]]
    got = lax.psum_scatter(jnp.concatenate(pieces, 2).transpose(1, 0, 2), "dp", scatter_dimension=0, tiled=False)
    total = got[1].astype(jnp.float32) + exchange(got[0], "blk", 2).astype(jnp.float32)
    up_grad, down_grad, out_grad = total[: ends[0]], total[ends[0] : ends[1]], total[ends[1] :]
    return up_grad.reshape(width // parts, -1), down_grad.reshape(own, -1).T, out_grad.reshape(own, -1).T


def local(tokens, cotangent, lengths, qkv_weight, out_weight, up_weight, down_weight, norm_gain, norm_bias, proj_bias, ffn_bias):
    rows, width = tokens.shape
    blocks = lax.axis_size("blk")
    parts = lax.axis_size("dp")
    me = lax.axis_index("blk")
    core, chip = me % 2, me // 2
    own = width // blocks

    def own_columns(values, third):
        return lax.dynamic_slice_in_dim(values, third * width + me * own, own, values.ndim - 1)

    own_weight = jnp.concatenate([own_columns(qkv_weight, third) for third in range(3)], 1)
    query_bias = lax.dynamic_slice_in_dim(proj_bias[0], me * own, own)
    value_bias = lax.dynamic_slice_in_dim(proj_bias[1], me * own, own)
    own_bias = jnp.concatenate([query_bias, jnp.zeros_like(query_bias), value_bias]).reshape(1, -1)
    first_all, qkv = gather_project(tokens, qkv_weight, norm_gain, norm_bias, own_bias)
    attended_own, log_total = attn_fwd(lengths, qkv)
    attended = lax.all_to_all(attended_own, "blk", split_axis=0, concat_axis=1, tiled=True)

    (mixed, grad_middle, grad_attended, out_away, out_stay, up_away, up_stay, down_away, down_stay, sums, hidden_bias) = ffn_both(
        me, tokens, cotangent, attended, out_weight, up_weight, down_weight, norm_gain, norm_bias, proj_bias, ffn_bias
    )
    grad_own = lax.all_to_all(grad_attended, "blk", split_axis=1, concat_axis=0, tiled=True)
    up_half = plus(up_stay, exchange(up_away, "blk", 1))
    down_half = plus(down_stay, exchange(down_away, "blk", 1))
    out_half = plus(out_stay, exchange(out_away, "blk", 1))
    grad_own, up_half, down_half, out_half = lax.optimization_barrier((grad_own, up_half, down_half, out_half))
    up_grad, down_grad, out_grad = weight_sums(up_half, down_half, out_half)
    grads = attn_bwd(lengths, qkv, grad_own, attended_own, log_total)

    by_block = grads.reshape(2, 2, rows, 3 * own)
    away = times_transposed(pick(by_block, 1 - core, 1).reshape(2 * rows, 3 * own), own_weight).astype(jnp.bfloat16)
    got = exchange(away, "blk", 1)
    stay = times_transposed(pick(by_block, core, 1).reshape(2 * rows, 3 * own), own_weight)
    half = plus(stay, got).reshape(2, rows, width)
    half, grads = lax.optimization_barrier((half, grads))
    far = exchange(pick(half, 1 - chip, 0), "blk", 2)

    term = outer_sum(first_all, grads).astype(jnp.bfloat16).reshape(parts // 2, 2, width // parts, 3 * own)
    near = lax.rem(lax.axis_index("dp"), 2)
    term = plus(pick(term, near, 1), exchange(pick(term, 1 - near, 1), "dp", 1))
    qkv_term = far_sum(term).astype(jnp.bfloat16)
    qkv_blocks = lax.all_gather(qkv_term, "blk", axis=0)
    qkv_rows = qkv_blocks.reshape(blocks, -1, 3, own).transpose(1, 2, 0, 3).reshape(-1, 3 * width)
    qkv_grad = lax.dynamic_slice_in_dim(qkv_rows, me * 3 * own, 3 * own, 1).astype(jnp.float32)

    def spread(values):
        return lax.dynamic_update_slice_in_dim(jnp.zeros((width,), jnp.float32), values, me * own, 0)

    y = pick(half, chip, 0).astype(jnp.float32) + far.astype(jnp.float32)
    n, r = _stats(tokens.astype(jnp.float32))
    token_grad = (grad_middle + _pull(n, r, y * norm_gain[0])).astype(jnp.bfloat16)
    small = jnp.stack(
        [
            jnp.sum(y * n, 0), *sums[:3], jnp.sum(y, 0), *sums[3:6],
            spread(column_sums(grads[:, :own])), spread(column_sums(grads[:, 2 * own :])), *sums[6:],
            *hidden_bias.reshape(-1, width),
        ]
    )
    small = sum_everywhere(small)
    place = lax.axis_index("dp")
    chunk = width // parts
    small_own = lax.dynamic_slice_in_dim(small[:12], place * chunk, chunk, 1)
    hidden = lax.dynamic_slice_in_dim(small[12:].reshape(-1), place * 4 * chunk, 4 * chunk, 0)
    return (mixed, token_grad, qkv_grad, out_grad, up_grad, down_grad, small_own[:4], small_own[4:8], small_own[8:], hidden)


def solution(mesh):
    return jax.shard_map(
        local,
        mesh=mesh,
        in_specs=(P(("dp", "blk"), None), P(("dp", "blk"), None), P("dp", None)) + (P(),) * 8,
        out_specs=(P(("dp", "blk"), None), P(("dp", "blk"), None))
        + (P("dp", "blk"),) * 4
        + (P(None, "dp"),) * 3
        + (P("dp"),),
        check_vma=False,
    )
```

```python
import functools

import jax
import jax.numpy as jnp
from jax import lax
from jax.experimental import pallas as pl
from jax.experimental.pallas import tpu as pltpu
from jax.sharding import PartitionSpec as P

epsilon = 1e-05
HD = 64
NT = (((1,), (1,)), ((), ()))
NEG = -1e30
TILE = 256


def _bounds(len_ref, qb):
    l0 = len_ref[0, 0]
    e1 = l0 + len_ref[0, 1]

    def start_of(r):
        return jnp.where(r >= e1, e1, jnp.where(r >= l0, l0, 0))

    first = qb * TILE
    s_first, s_last = start_of(first), start_of(first + TILE - 1)
    kmin = s_first // TILE
    kmid = jnp.maximum(kmin, jnp.minimum(qb, (s_last + TILE - 1) // TILE))
    rows = first + lax.broadcasted_iota(jnp.int32, (1, TILE), 1)
    return kmin, kmid, rows, start_of(rows)


def _walk(len_ref, qb, step, carry, wide):
    kmin, kmid, rows, starts = _bounds(len_ref, qb)

    def masked(kb, carry):
        at = pl.multiple_of(kb * TILE, TILE)
        kpos = at + lax.broadcasted_iota(jnp.int32, (TILE, TILE), 0)
        return step(at, TILE, (kpos >= starts) & (kpos <= rows), carry)

    def plain(size):
        def run(kb, carry):
            return step(pl.multiple_of(kb * TILE, TILE), size * TILE, None, carry)

        return run

    carry = lax.fori_loop(kmin, kmid, masked, carry)
    at, left = kmid, qb - kmid
    for size in wide:
        count = left // size
        base = at
        carry = lax.fori_loop(0, count, lambda i, c, base=base, size=size: plain(size)(base + i * size, c), carry)
        at, left = at + count * size, left - count * size
    return masked(qb, carry)


def _fill_masked(dst, value, heads):
    lane = lax.broadcasted_iota(jnp.int32, value.shape, 1) // HD
    for h in range(heads):
        dst[pl.ds(h * TILE, TILE), :] = jnp.where(lane == h, value, jnp.zeros_like(value))


def fwd_kernel(len_ref, q_ref, k_ref, v_ref, o_ref, lse_ref, qm, acc, ps, vt, *, heads, wide):
    qb = pl.program_id(0)

    @pl.when(qb == 0)
    def _():
        vt[...] = v_ref[...].T

    _fill_masked(qm, q_ref[...] * jnp.bfloat16(0.125), heads)
    acc[...] = jnp.zeros_like(acc)

    def step(at, size, mask, carry):
        keys = pl.ds(at, size)
        scores = [
            lax.dot_general(k_ref[keys, :], qm[pl.ds(h * TILE, TILE), :], NT, preferred_element_type=jnp.float32)
            for h in range(heads)
        ]
        out, fades = [], []
        for h in range(heads):
            m, l = carry[h]
            s = scores[h]
            if mask is not None:
                s = jnp.where(mask, s, NEG)
            top = jnp.maximum(m, jnp.max(s, 0, keepdims=True))
            p = jnp.exp(s - top)
            if mask is not None:
                p = jnp.where(mask, p, 0.0)
            fade = jnp.exp(m - top)
            ps[pl.ds(0, size), pl.ds(h * TILE, TILE)] = p.astype(jnp.bfloat16)
            out.append((top, l * fade + jnp.sum(p, 0, keepdims=True)))
            fades.append(fade)
        for h in range(heads):
            lanes = pl.ds(h * HD, HD)
            part = jnp.dot(vt[lanes, keys], ps[pl.ds(0, size), pl.ds(h * TILE, TILE)], preferred_element_type=jnp.float32)
            acc[lanes, :] = acc[lanes, :] * fades[h] + part
        return tuple(out)

    carry = tuple((jnp.full((1, TILE), NEG, jnp.float32), jnp.zeros((1, TILE), jnp.float32)) for _ in range(heads))
    carry = _walk(len_ref, qb, step, carry, wide)
    for h in range(heads):
        m, l = carry[h]
        lse_ref[pl.ds(h, 1), :] = m + jnp.log(l)
        acc[pl.ds(h * HD, HD), :] = acc[pl.ds(h * HD, HD), :] / l
    o_ref[...] = acc[...].T.astype(jnp.bfloat16)


def attn_fwd(lengths, qkv, pair=0, lane=256, wide=(1,)):
    n = qkv.shape[0]
    heads = lane // HD
    return pl.pallas_call(
        functools.partial(fwd_kernel, heads=heads, wide=wide),
        grid_spec=pltpu.PrefetchScalarGridSpec(
            num_scalar_prefetch=1,
            grid=(n // TILE,),
            in_specs=[
                pl.BlockSpec((TILE, lane), lambda i, L: (i, 3 * pair)),
                pl.BlockSpec((n, lane), lambda i, L: (0, 3 * pair + 1)),
                pl.BlockSpec((n, lane), lambda i, L: (0, 3 * pair + 2)),
            ],
            out_specs=[pl.BlockSpec((TILE, lane), lambda i, L: (i, 0)), pl.BlockSpec((heads, TILE), lambda i, L: (0, i))],
            scratch_shapes=[
                pltpu.VMEM((heads * TILE, lane), jnp.bfloat16),
                pltpu.VMEM((lane, TILE), jnp.float32),
                pltpu.VMEM((wide[0] * TILE, heads * TILE), jnp.bfloat16),
                pltpu.VMEM((lane, n), jnp.bfloat16),
            ],
        ),
        out_shape=[jax.ShapeDtypeStruct((n, lane), jnp.bfloat16), jax.ShapeDtypeStruct((heads, n), jnp.float32)],
        compiler_params=pltpu.CompilerParams(vmem_limit_bytes=40 * 2**20),
        cost_estimate=pl.CostEstimate(flops=n * n * lane * 9, bytes_accessed=10 * n * lane, transcendentals=n * n * heads // 2),
        name="attn_fwd",
    )(lengths, qkv, qkv, qkv)


def bwd_kernel(len_ref, q_ref, do_ref, o_ref, lse_ref, k_ref, v_ref, d_ref, qm, dom, ps, ds, dqt, dk, dv, kt, *, heads, wide):
    qb = pl.program_id(0)
    c = heads * HD

    @pl.when(qb == 0)
    def _():
        dk[...] = jnp.zeros_like(dk)
        dv[...] = jnp.zeros_like(dv)
        kt[...] = k_ref[...].T

    _fill_masked(qm, q_ref[...] * jnp.bfloat16(0.125), heads)
    _fill_masked(dom, do_ref[...], heads)
    prod = (do_ref[...].astype(jnp.float32) * o_ref[...].astype(jnp.float32)).T
    delta = [jnp.sum(prod[h * HD : (h + 1) * HD], 0, keepdims=True) for h in range(heads)]
    dqt[...] = jnp.zeros_like(dqt)

    def step(at, size, mask, carry):
        keys = pl.ds(at, size)
        used = pl.ds(0, size)
        for h in range(heads):
            mine = pl.ds(h * TILE, TILE)
            s = lax.dot_general(k_ref[keys, :], qm[mine, :], NT, preferred_element_type=jnp.float32)
            p = jnp.exp(s - lse_ref[pl.ds(h, 1), :])
            if mask is not None:
                p = jnp.where(mask, p, 0.0)
            dp = lax.dot_general(v_ref[keys, :], dom[mine, :], NT, preferred_element_type=jnp.float32)
            ps[used, mine] = p.astype(jnp.bfloat16)
            ds[used, mine] = (p * (dp - delta[h])).astype(jnp.bfloat16)
        dv[keys, :] += jnp.dot(ps[used, :], dom[...], preferred_element_type=jnp.float32)
        dk[keys, :] += jnp.dot(ds[used, :], qm[...], preferred_element_type=jnp.float32)
        for h in range(heads):
            lanes = pl.ds(h * HD, HD)
            dqt[lanes, :] += jnp.dot(kt[lanes, keys], ds[used, pl.ds(h * TILE, TILE)], preferred_element_type=jnp.float32)
        return carry

    _walk(len_ref, qb, step, 0, wide)
    d_ref[pl.ds(pl.multiple_of(qb * TILE, TILE), TILE), pl.ds(0, c)] = (dqt[...] * 0.125).T.astype(jnp.bfloat16)

    @pl.when(qb == pl.num_programs(0) - 1)
    def _():
        d_ref[:, pl.ds(c, c)] = dk[...].astype(jnp.bfloat16)
        d_ref[:, pl.ds(2 * c, c)] = dv[...].astype(jnp.bfloat16)


def attn_bwd(lengths, qkv, do, o, lse, pair=0, lane=256, wide=(1,)):
    n = qkv.shape[0]
    heads = lane // HD
    row = lambda col: pl.BlockSpec((TILE, lane), lambda i, L: (i, col))
    whole = lambda col: pl.BlockSpec((n, lane), lambda i, L: (0, col))
    return pl.pallas_call(
        functools.partial(bwd_kernel, heads=heads, wide=wide),
        grid_spec=pltpu.PrefetchScalarGridSpec(
            num_scalar_prefetch=1,
            grid=(n // TILE,),
            in_specs=[
                row(3 * pair), row(pair), row(0), pl.BlockSpec((heads, TILE), lambda i, L: (0, i)),
                whole(3 * pair + 1), whole(3 * pair + 2),
            ],
            out_specs=pl.BlockSpec((n, 3 * lane), lambda i, L: (0, pair)),
            scratch_shapes=[
                pltpu.VMEM((heads * TILE, lane), jnp.bfloat16),
                pltpu.VMEM((heads * TILE, lane), jnp.bfloat16),
                pltpu.VMEM((wide[0] * TILE, heads * TILE), jnp.bfloat16),
                pltpu.VMEM((wide[0] * TILE, heads * TILE), jnp.bfloat16),
                pltpu.VMEM((lane, TILE), jnp.float32),
                pltpu.VMEM((n, lane), jnp.float32),
                pltpu.VMEM((n, lane), jnp.float32),
                pltpu.VMEM((lane, n), jnp.bfloat16),
            ],
        ),
        out_shape=jax.ShapeDtypeStruct(qkv.shape, jnp.bfloat16),
        compiler_params=pltpu.CompilerParams(vmem_limit_bytes=40 * 2**20),
        cost_estimate=pl.CostEstimate(flops=n * n * lane * 11, bytes_accessed=20 * n * lane, transcendentals=n * n * heads // 2),
        name="attn_bwd",
    )(lengths, qkv, do, o, lse, qkv, qkv)


def _stats(v):
    c = v - jnp.mean(v, -1, keepdims=True)
    r = lax.rsqrt(jnp.mean(c * c, -1, keepdims=True) + epsilon)
    return c * r, r


def _pull(n, r, e):
    return r * (e - jnp.mean(e, -1, keepdims=True) - n * jnp.mean(e * n, -1, keepdims=True))


def _fold(v):
    return jnp.sum(v.reshape(-1, 8, v.shape[-1]), 0)


def _row(ref, i):
    return ref[pl.ds(i, 1), :]


def _each(total, size, fn):
    def body(i, carry):
        fn(pl.ds(pl.multiple_of(i * size, size), size))
        return carry

    lax.fori_loop(0, total // size, body, 0)


def _turn_blocks(dst, value, core):
    own = dst.shape[0] // 4
    flipped = value.T
    for b in range(4):
        stays = 1 - lax.rem(core + b % 2, 2)
        dst[pl.ds(pl.multiple_of((2 * stays + b // 2) * own, own), own), :] = flipped[b * own : (b + 1) * own, :]


def ffn_kernel(
    x_ref, cot_ref, att_ref, wo_ref, up_ref, down_ref, gain_ref, shift_ref, bias_ref, fb_ref,
    mixed_ref, mid_ref, n_ref, r_ref, low_ref, turned_ref, second_t, act_ref, slope_ref, small_ref,
    second, branch, ffn, sums, *, tiles, strip,
):
    s = pl.program_id(0)
    rows, width = x_ref.shape
    f32 = jnp.float32

    @pl.when(s == 0)
    def _():
        sums[...] = jnp.zeros_like(sums)
        branch[...] = jnp.dot(att_ref[...], wo_ref[...], preferred_element_type=f32) + _row(bias_ref, 2)

        def normed(at):
            n, r = _stats(branch[at, :])
            n_ref[at, :] = n.astype(jnp.bfloat16)
            r_ref[at, :] = r
            m = x_ref[at, :].astype(f32) + n * _row(gain_ref, 1) + _row(shift_ref, 1)
            mid_ref[at, :] = m
            n, _ = _stats(m)
            second[at, :] = (n * _row(gain_ref, 2) + _row(shift_ref, 2)).astype(jnp.bfloat16)

        _each(rows, strip, normed)
        second_t[...] = second[...].T

    u = jnp.dot(second[...], up_ref[...], preferred_element_type=f32) + fb_ref[...]
    c1, c3 = 0.7978845608028654, 0.7978845608028654 * 0.044715
    sq = u * u
    t = jnp.tanh(u * (c1 + c3 * sq))
    half = 0.5 + 0.5 * t
    a = (u * half).astype(jnp.bfloat16)
    act_ref[...] = a
    slope_ref[...] = (half + (0.5 * u) * (1.0 - t * t) * (c1 + 3.0 * c3 * sq)).astype(jnp.bfloat16)
    part = jnp.dot(a, down_ref[...], preferred_element_type=f32)

    @pl.when(s == 0)
    def _():
        ffn[...] = part + _row(bias_ref, 3)

    @pl.when(s > 0)
    def _():
        ffn[...] += part

    @pl.when(s == tiles - 1)
    def _():
        def normed(at):
            n, r = _stats(ffn[at, :])
            y = cot_ref[at, :].astype(f32)
            mixed_ref[at, :] = (mid_ref[at, :] + n * _row(gain_ref, 3) + _row(shift_ref, 3)).astype(jnp.bfloat16)
            g = _pull(n, r, y * _row(gain_ref, 3)).astype(jnp.bfloat16)
            low_ref[at, :] = g
            sums[pl.ds(0, 8), :] += _fold(y * n)
            sums[pl.ds(8, 8), :] += _fold(y)
            sums[pl.ds(16, 8), :] += _fold(g.astype(f32))

        _each(rows, strip, normed)
        _turn_blocks(turned_ref, low_ref[...], lax.rem(lax.axis_index("blk"), 2))
        for i in range(3):
            small_ref[pl.ds(i, 1), :] = jnp.sum(sums[pl.ds(8 * i, 8), :], 0, keepdims=True)


def _once(*shape):
    return pl.BlockSpec(shape, lambda s: (0,) * len(shape), pipeline_mode=pl.Buffered(1))


def ffn_forward(tokens, cotangent, attended, out_weight, up_weight, down_weight, norm_gain, norm_bias, proj_bias, ffn_bias):
    rows, width = tokens.shape
    hidden = up_weight.shape[1]
    tiles = 8
    hid = hidden // tiles
    bf16, f32 = jnp.bfloat16, jnp.float32
    shape = jax.ShapeDtypeStruct
    return pl.pallas_call(
        functools.partial(ffn_kernel, tiles=tiles, strip=rows // 4),
        grid=(tiles,),
        in_specs=[
            _once(rows, width), _once(rows, width), _once(rows, width), _once(width, width),
            pl.BlockSpec((width, hid), lambda s: (0, s)), pl.BlockSpec((hid, width), lambda s: (s, 0)),
            _once(4, width), _once(4, width), _once(4, width), pl.BlockSpec((1, hid), lambda s: (0, s)),
        ],
        out_specs=[
            _once(rows, width), _once(rows, width), _once(rows, width), _once(rows, 1), _once(rows, width),
            _once(width, rows), _once(width, rows),
            pl.BlockSpec((rows, hid), lambda s: (0, s)), pl.BlockSpec((rows, hid), lambda s: (0, s)), _once(8, width),
        ],
        out_shape=[
            shape((rows, width), bf16), shape((rows, width), f32), shape((rows, width), bf16), shape((rows, 1), f32),
            shape((rows, width), bf16), shape((width, rows), bf16), shape((width, rows), bf16),
            shape((rows, hidden), bf16), shape((rows, hidden), bf16), shape((8, width), f32),
        ],
        scratch_shapes=[pltpu.VMEM((rows, width), bf16), pltpu.VMEM((rows, width), f32), pltpu.VMEM((rows, width), f32), pltpu.VMEM((24, width), f32)],
        compiler_params=pltpu.CompilerParams(vmem_limit_bytes=52 * 2**20),
        cost_estimate=pl.CostEstimate(flops=18 * rows * width * width, bytes_accessed=50 * 2**20, transcendentals=rows * hidden),
        name="ffn_forward",
    )(tokens, cotangent, attended, out_weight, up_weight, down_weight, norm_gain, norm_bias, proj_bias, ffn_bias.reshape(1, -1))


def grads_kernel(
    low_ref, turned_ref, second_t, act_ref, slope_ref, up_ref, down_ref, mid_hbm, n_hbm, r_ref, cot_ref, att_ref, wo_ref, gain_ref,
    gmid_ref, small_ref, hid_ref, up_out, down_out, out_out, gown_out,
    pre, gs, low, turned, gatt, sums, up_buf, up_in, up_y, down_send, down_keep, down_in, down_x,
    up_core, up_core_in, up_far, up_far_in, down_core, down_core_in, down_far, down_far_in, up_done, down_done, own_sems, gatt_sends, gatt_recvs, *, tiles, strip, fold,
):
    s = pl.program_id(0)
    rows, width = low_ref.shape
    own = width // 4
    f32, bf16 = jnp.float32, jnp.bfloat16
    pair, side = s // 2, lax.rem(s, 2)
    me, place = lax.axis_index("blk"), lax.axis_index("dp")
    core, chip, near = lax.rem(me, 2), me // 2, lax.rem(place, 2)
    twin, other, beside = {"blk": me + 1 - 2 * core}, {"blk": lax.rem(me + 2, 4)}, {"dp": place + 1 - 2 * near}
    last = {"blk": 3 - me}
    half = tiles // 2
    mesh_ids = pl.DeviceIdType.MESH

    def remote(src, dst, sends, recvs, i, target):
        return pltpu.make_async_remote_copy(
            src_ref=src, dst_ref=dst, send_sem=sends.at[i], recv_sem=recvs.at[i], device_id=target, device_id_type=mesh_ids
        )

    def up_to_twin(p):
        return remote(up_buf.at[0], up_in.at[p], up_core, up_core_in, p, twin)

    def up_to_beside(p):
        return remote(up_in.at[p, :, 1 - near], up_y.at[p], up_far, up_far_in, p, beside)

    def down_to_twin(u, slot):
        return remote(down_send.at[slot], down_in.at[lax.rem(u, 4)], down_core, down_core_in, u, twin)

    def down_to_other(u):
        return remote(down_keep.at[u, 1 - chip], down_x.at[u], down_far, down_far_in, u, other)

    def up_result(p):
        return pltpu.make_async_copy(up_y.at[p], up_out.at[:, p], up_done.at[p])

    def down_result(u):
        tile = 4 * (u // 4) + 2 * lax.rem(u, 2) + lax.rem(u // 2, 2)
        return pltpu.make_async_copy(down_x.at[u], down_out.at[tile], down_done.at[u])

    def saved(i):
        return pltpu.make_async_copy((mid_hbm, n_hbm)[i], (gmid_ref, low)[i], own_sems.at[i])

    def out_result(i):
        return pltpu.make_async_copy(up_buf.at[i], out_out.at[i], own_sems.at[2 + i])

    def columns_to(i):
        target = (last, other, twin)[i]
        block = target["blk"]
        src = gatt.at[:, pl.ds(pl.multiple_of(block * own, own), own)]
        dst = gown_out.at[pl.ds(pl.multiple_of(me * rows, rows), rows), :]
        return remote(src, dst, gatt_sends, gatt_recvs, i, target)

    def columns_here():
        src = gatt.at[:, pl.ds(pl.multiple_of(me * own, own), own)]
        return pltpu.make_async_copy(src, gown_out.at[pl.ds(pl.multiple_of(me * rows, rows), rows), :], own_sems.at[4])

    def join_up(p):
        up_to_twin(p).wait_recv()
        up_in[p] = (up_in[p].astype(f32) + up_buf[1].astype(f32)).astype(bf16)
        up_to_beside(p).start()

    def join_far_up(p):
        up_to_beside(p).wait_recv()
        up_y[p] = (up_y[p].astype(f32) + up_in[p, :, near].astype(f32)).astype(bf16)
        up_result(p).start()

    def join_cores(p):
        join_up(p)
        for c in range(2):
            u = 2 * p + c
            down_to_twin(u, c).wait_recv()
            down_keep[u] = (down_keep[u].astype(f32) + down_in[lax.rem(u, 4)].astype(f32)).astype(bf16)
            down_to_other(u).start()

    def join_far(p):
        join_far_up(p)
        for c in range(2):
            u = 2 * p + c
            down_to_other(u).wait_recv()
            down_x[u] = (down_x[u].astype(f32) + down_keep[u, chip].astype(f32)).astype(bf16)
            down_result(u).start()

    @pl.when(s == 0)
    def _():
        barrier = pltpu.get_barrier_semaphore()
        for target in (twin, other, beside, last):
            pl.semaphore_signal(barrier, inc=1, device_id=target, device_id_type=mesh_ids)
        sums[...] = jnp.zeros_like(sums)
        saved(0).start()
        saved(1).start()
        pl.semaphore_wait(barrier, 4)

    @pl.when((side == 0) & (s > 0))
    def _():
        join_cores(pair - 1)

    @pl.when(s == 6)
    def _():
        join_far(0)

    g = lax.dot_general(low_ref[...], down_ref[...], NT, preferred_element_type=f32) * slope_ref[...].astype(f32)
    g = g.astype(bf16)
    pre[...] = g
    hid_ref[pl.ds(s, 1)] = jnp.sum(g.astype(f32), 0, keepdims=True)[None]
    part = lax.dot_general(g, up_ref[...], NT, preferred_element_type=f32)

    @pl.when(s == 0)
    def _():
        gs[...] = part

    @pl.when(s > 0)
    def _():
        gs[...] += part

    down_grad = jnp.dot(turned_ref[...], act_ref[...], preferred_element_type=f32).astype(bf16)

    @pl.when(s >= 2)
    def _():
        down_to_twin(s - 2, side).wait_send()

    down_send[side] = down_grad[: width // 2].reshape(2, own, -1)
    down_to_twin(s, side).start()
    down_keep[s] = down_grad[width // 2 :].reshape(2, own, -1)
    up_grad = jnp.dot(second_t[...], pre[...], preferred_element_type=f32).astype(bf16).reshape(up_buf.shape[1:])

    @pl.when(side == core)
    def _():
        up_buf[1] = up_grad

    @pl.when(side != core)
    def _():
        @pl.when(pair > 0)
        def _():
            up_to_twin(pair - 1).wait_send()

        up_buf[0] = up_grad
        up_to_twin(pair).start()

    @pl.when(s == tiles - 1)
    def _():
        def normed(at):
            n, r = _stats(gmid_ref[at, :])
            y = gs[at, :]
            gm = cot_ref[at, :].astype(f32) + _pull(n, r, y * _row(gain_ref, 2))
            gmid_ref[at, :] = gm
            sums[pl.ds(8, 8), :] += _fold(y * n)
            sums[pl.ds(24, 8), :] += _fold(y)
            n, r = low[at, :].astype(f32), r_ref[at, :]
            g = _pull(n, r, gm * _row(gain_ref, 1)).astype(bf16)
            low[at, :] = g
            sums[pl.ds(0, 8), :] += _fold(gm * n)
            sums[pl.ds(16, 8), :] += _fold(gm)
            sums[pl.ds(32, 8), :] += _fold(g.astype(f32))

        join_cores(tiles // 2 - 1)
        saved(0).wait()
        saved(1).wait()
        _each(rows, strip, normed)
        gatt[...] = lax.dot_general(low[...], wo_ref[...], NT, preferred_element_type=f32).astype(bf16)
        for i in range(3):
            columns_to(i).start()
        columns_here().start()
        _turn_blocks(turned, low[...], core)
        grad = jnp.dot(turned[...], att_ref[...], preferred_element_type=f32).astype(bf16)
        up_to_twin(half - 1).wait_send()
        if fold:
            thin = width // 8
            for d in range(8):
                for b in range(8):
                    piece = grad[b * thin : (b + 1) * thin, d * thin : (d + 1) * thin]
                    up_buf[b // 4, d // 2, d % 2, :, pl.ds(b % 4 * thin, thin)] = piece
            up_to_twin(half).start()
        else:
            for i in range(2):
                up_buf[i] = grad[:, i * width // 2 : (i + 1) * width // 2].reshape(up_buf.shape[1:])
                out_result(i).start()
        for i in range(5):
            small_ref[pl.ds(i, 1), :] = jnp.sum(sums[pl.ds(8 * i, 8), :], 0, keepdims=True)
        if fold:
            join_up(half)
        for p in range(1, half):
            join_far(p)
        if fold:
            join_far_up(half)
        down_to_twin(tiles - 2, 0).wait_send()
        down_to_twin(tiles - 1, 1).wait_send()
        if fold:
            up_to_twin(half).wait_send()
        else:
            out_result(0).wait()
            out_result(1).wait()
        for p in range(half + fold):
            up_to_beside(p).wait_send()
            up_result(p).wait()
        for u in range(tiles):
            down_to_other(u).wait_send()
            down_result(u).wait()
        for i in range(3):
            columns_to(i).wait_send()
            columns_to(i).wait_recv()
        columns_here().wait()


def ffn_backward(parts, low, turned, second_t, act, slope, up_weight, down_weight, mid, n_one, r_one, cotangent, attended, out_weight, norm_gain):
    rows, width = low.shape
    hidden = up_weight.shape[1]
    tiles, own = 8, width // 4
    hid = hidden // tiles
    bf16, f32 = jnp.bfloat16, jnp.float32
    shape = jax.ShapeDtypeStruct
    tile_of = lambda s: 4 * (s // 4) + 2 * lax.rem(s, 2) + lax.rem(s // 2, 2)
    thin = (parts // 2, 2, width // parts, hid)
    dma = pltpu.SemaphoreType.DMA
    half = tiles // 2
    fold = int(parts == 8)
    return pl.pallas_call(
        functools.partial(grads_kernel, tiles=tiles, strip=rows // 4, fold=fold),
        grid=(tiles,),
        in_specs=[
            _once(rows, width), _once(width, rows), _once(width, rows),
            pl.BlockSpec((rows, hid), lambda s: (0, tile_of(s))), pl.BlockSpec((rows, hid), lambda s: (0, tile_of(s))),
            pl.BlockSpec((width, hid), lambda s: (0, tile_of(s))), pl.BlockSpec((hid, width), lambda s: (tile_of(s), 0)),
            pl.BlockSpec(memory_space=pl.ANY), pl.BlockSpec(memory_space=pl.ANY), _once(rows, 1), _once(rows, width), _once(rows, width), _once(width, width), _once(4, width),
        ],
        out_specs=[
            _once(rows, width), _once(8, width), _once(tiles, 1, hid),
            pl.BlockSpec(memory_space=pl.ANY), pl.BlockSpec(memory_space=pl.ANY), pl.BlockSpec(memory_space=pl.ANY), pl.BlockSpec(memory_space=pl.ANY),
        ],
        out_shape=[
            shape((rows, width), f32),
            shape((8, width), f32), shape((tiles, 1, hid), f32),
            shape((parts // 2, half + fold, width // parts, hid), bf16), shape((tiles, own, hid), bf16), shape((2,) + thin, bf16),
            shape((4 * rows, own), bf16),
        ],
        scratch_shapes=[
            pltpu.VMEM((rows, hid), bf16), pltpu.VMEM((rows, width), f32), pltpu.VMEM((rows, width), bf16), pltpu.VMEM((width, rows), bf16), pltpu.VMEM((rows, width), bf16),
            pltpu.VMEM((40, width), f32),
            pltpu.VMEM((2,) + thin, bf16), pltpu.VMEM((half + fold,) + thin, bf16), pltpu.VMEM((half + fold, parts // 2, width // parts, hid), bf16),
            pltpu.VMEM((2, 2, own, hid), bf16), pltpu.VMEM((tiles, 2, own, hid), bf16), pltpu.VMEM((4, 2, own, hid), bf16),
            pltpu.VMEM((tiles, own, hid), bf16),
            *[dma((half + fold,))] * 4, *[dma((tiles,))] * 4, dma((half + fold,)), dma((tiles,)), dma((5,)), dma((3,)), dma((3,)),
        ],
        compiler_params=pltpu.CompilerParams(collective_id=1, has_side_effects=True, vmem_limit_bytes=60 * 2**20),
        name="ffn_backward",
    )(low, turned, second_t, act, slope, up_weight, down_weight, mid, n_one, r_one, cotangent, attended, out_weight, norm_gain)


def project_kernel(x_ref, w_hbm, gain_ref, shift_ref, bias_ref, all_ref, qkv_ref, w_ref, w_sems, chip_send, chip_recv, core_send, core_recv, pass_send, pass_recv, *, pieces):
    me = lax.axis_index("blk")
    core = lax.rem(me, 2)
    twin, other, last = me + 1 - 2 * core, lax.rem(me + 2, 4), 3 - me
    rows, width = x_ref.shape
    own = width // 4
    size = rows // pieces
    barrier = pltpu.get_barrier_semaphore()
    for target in (twin, other):
        pl.semaphore_signal(barrier, inc=1, device_id={"blk": target}, device_id_type=pl.DeviceIdType.MESH)
    loads = []
    for third in range(3):
        columns = pl.ds(pl.multiple_of(third * width + me * own, own), own)
        load = pltpu.make_async_copy(w_hbm.at[:, columns], w_ref.at[:, pl.ds(third * own, own)], w_sems.at[third])
        load.start()
        loads.append(load)

    def at(block, i):
        return pl.ds(pl.multiple_of(block * rows + i * size, size), size)

    def send(block, i, target, sends, recvs):
        piece = all_ref.at[at(block, i), :]
        copy = pltpu.make_async_remote_copy(
            src_ref=piece, dst_ref=piece, send_sem=sends.at[i], recv_sem=recvs.at[i],
            device_id={"blk": target}, device_id_type=pl.DeviceIdType.MESH,
        )
        return copy

    def project(block, i):
        where = at(block, i)
        got = jnp.dot(all_ref[where, :], w_ref[...], preferred_element_type=jnp.float32) + bias_ref[...]
        qkv_ref[where, :] = got.astype(jnp.bfloat16)

    sent = []
    for i in range(pieces):
        n, _ = _stats(x_ref[pl.ds(i * size, size), :].astype(jnp.float32))
        all_ref[at(me, i), :] = (n * gain_ref[pl.ds(0, 1), :] + shift_ref[pl.ds(0, 1), :]).astype(jnp.bfloat16)
        if i == 0:
            pl.semaphore_wait(barrier, 2)
        for target, sends, recvs in ((other, chip_send, chip_recv), (twin, core_send, core_recv)):
            copy = send(me, i, target, sends, recvs)
            copy.start()
            sent.append(copy)
    for load in loads:
        load.wait()
    for i in range(pieces):
        project(me, i)
    for i in range(pieces):
        send(twin, i, twin, core_send, core_recv).wait_recv()
        project(twin, i)
    for i in range(pieces):
        send(other, i, other, chip_send, chip_recv).wait_recv()
        copy = send(other, i, twin, pass_send, pass_recv)
        copy.start()
        sent.append(copy)
        project(other, i)
        if i > 0:
            send(last, i - 1, twin, pass_send, pass_recv).wait_recv()
            project(last, i - 1)
    send(last, pieces - 1, twin, pass_send, pass_recv).wait_recv()
    project(last, pieces - 1)
    for copy in sent:
        copy.wait_send()


def gather_project(tokens, qkv_weight, norm_gain, norm_bias, bias):
    rows, width = tokens.shape
    pieces = 4
    vmem = pl.BlockSpec(memory_space=pltpu.VMEM)
    dma = pltpu.SemaphoreType.DMA((pieces,))
    return pl.pallas_call(
        functools.partial(project_kernel, pieces=pieces),
        in_specs=[vmem, pl.BlockSpec(memory_space=pl.ANY), vmem, vmem, vmem],
        out_specs=[vmem, vmem],
        out_shape=[jax.ShapeDtypeStruct((4 * rows, width), jnp.bfloat16), jax.ShapeDtypeStruct((4 * rows, 3 * width // 4), jnp.bfloat16)],
        scratch_shapes=[pltpu.VMEM((width, 3 * width // 4), jnp.bfloat16), pltpu.SemaphoreType.DMA((3,))] + [dma] * 6,
        compiler_params=pltpu.CompilerParams(collective_id=0, has_side_effects=True, vmem_limit_bytes=48 * 2**20),
        name="gather_project",
    )(tokens, qkv_weight, norm_gain, norm_bias, bias)


def outer_sum(left, right):
    return lax.dot_general(left, right, (((0,), (0,)), ((), ())), preferred_element_type=jnp.float32)


def times_transposed(left, right):
    return lax.dot_general(left, right, NT, preferred_element_type=jnp.float32)


def column_sums(values):
    return jnp.sum(values.astype(jnp.float32), 0)


def exchange(values, axis, bit):
    return lax.ppermute(values, axis, [(i, i ^ bit) for i in range(lax.axis_size(axis))])


def plus(left, right):
    return (left.astype(jnp.float32) + right.astype(jnp.float32)).astype(jnp.bfloat16)


def pick(values, index, axis):
    return lax.dynamic_index_in_dim(values, index, axis, False)


def sum_everywhere(values):
    for axis in ("blk", "dp"):
        bit = 1
        while bit < lax.axis_size(axis):
            values = values + exchange(values, axis, bit)
            bit *= 2
    return values


def far_sum(half):
    line = lax.axis_index("dp") // 2
    parts = lax.axis_size("dp")
    if parts > 8:
        groups = [[d for d in range(parts) if d % 2 == b] for b in range(2)]
        return jnp.sum(lax.all_to_all(half, "dp", 0, 0, axis_index_groups=groups).astype(jnp.float32), 0)
    got = [exchange(pick(half, line ^ step, 0), "dp", 2 * step) for step in range(1, parts // 2)]
    return pick(half, line, 0).astype(jnp.float32) + sum(piece.astype(jnp.float32) for piece in got)


def weight_sums(up, down, out, own):
    parts = lax.axis_size("dp")
    chip = lax.axis_index("blk") // 2
    width = 4 * own
    groups = [[d for d in range(parts) if d % 2 == b] for b in range(2)]
    up = lax.psum_scatter(up, "dp", scatter_dimension=0, axis_index_groups=groups, tiled=False)
    halves = up[:4].reshape((2, 2) + up.shape[1:]).transpose(0, 2, 1, 3).reshape(2, up.shape[1], -1)
    if parts == 8:
        thin = up.shape[1]
        halves = jnp.concatenate([halves, up[4].reshape(thin, 2, -1).transpose(1, 0, 2)], 2)
    total = pick(halves, chip, 0).astype(jnp.float32) + exchange(pick(halves, 1 - chip, 0), "blk", 2).astype(jnp.float32)
    if parts == 8:
        out_grad = total[:, width:].reshape(thin, 2, thin).transpose(1, 0, 2).reshape(own, thin).T
        down_grad = lax.psum_scatter(down, "dp", scatter_dimension=0, tiled=False).astype(jnp.float32).T
    else:
        down = down.transpose(1, 0, 2).reshape(own, parts, -1).transpose(1, 0, 2)
        out = out.reshape(own, parts, width // parts).transpose(1, 0, 2)
        both = lax.psum_scatter(jnp.concatenate([down, out], 2), "dp", scatter_dimension=0, tiled=False).astype(jnp.float32)
        down_grad, out_grad = both[:, : down.shape[2]].T, both[:, down.shape[2] :].T
    return total[:, :width], down_grad, out_grad


def local(tokens, cotangent, lengths, qkv_weight, out_weight, up_weight, down_weight, norm_gain, norm_bias, proj_bias, ffn_bias):
    rows, width = tokens.shape
    blocks = lax.axis_size("blk")
    parts = lax.axis_size("dp")
    me = lax.axis_index("blk")
    core, chip = me % 2, me // 2
    own = width // blocks

    def own_columns(values, third):
        return lax.dynamic_slice_in_dim(values, third * width + me * own, own, values.ndim - 1)

    own_weight = jnp.concatenate([own_columns(qkv_weight, third) for third in range(3)], 1)
    query_bias = lax.dynamic_slice_in_dim(proj_bias[0], me * own, own)
    value_bias = lax.dynamic_slice_in_dim(proj_bias[1], me * own, own)
    own_bias = jnp.concatenate([query_bias, jnp.zeros_like(query_bias), value_bias]).reshape(1, -1)
    first_all, qkv = gather_project(tokens, qkv_weight, norm_gain, norm_bias, own_bias)
    attended_own, log_total = attn_fwd(lengths, qkv)
    attended = lax.all_to_all(attended_own, "blk", split_axis=0, concat_axis=1, tiled=True)

    mixed, mid, n_one, r_one, low, turned, second_t, act, slope, sums_three = ffn_forward(
        tokens, cotangent, attended, out_weight, up_weight, down_weight, norm_gain, norm_bias, proj_bias, ffn_bias
    )
    grad_middle, sums, hidden_bias, up_sum, down_sum, out_term, grad_own = ffn_backward(
        parts, low, turned, second_t, act, slope, up_weight, down_weight, mid, n_one, r_one, cotangent, attended, out_weight, norm_gain
    )
    hidden_bias = hidden_bias.reshape(2, 2, 2, -1).transpose(0, 2, 1, 3)
    out_sum = None
    if parts != 8:
        out_term = out_term.reshape(2, 2, width // 2, width // 2).transpose(1, 2, 0, 3).reshape(2, 2, own, width)
        out_half = plus(out_term[1], exchange(out_term[0], "blk", 1))
        out_sum = plus(pick(out_half, chip, 0), exchange(pick(out_half, 1 - chip, 0), "blk", 2))
    up_grad, down_grad, out_grad = weight_sums(up_sum, down_sum, out_sum, own)
    grads = attn_bwd(lengths, qkv, grad_own, attended_own, log_total)

    by_block = grads.reshape(2, 2, rows, 3 * own)
    away = times_transposed(pick(by_block, 1 - core, 1).reshape(2 * rows, 3 * own), own_weight).astype(jnp.bfloat16)
    got = exchange(away, "blk", 1)
    stay = times_transposed(pick(by_block, core, 1).reshape(2 * rows, 3 * own), own_weight)
    half = plus(stay, got).reshape(2, rows, width)
    half, grads = lax.optimization_barrier((half, grads))
    far = exchange(pick(half, 1 - chip, 0), "blk", 2)

    term = outer_sum(first_all, grads).astype(jnp.bfloat16).reshape(parts // 2, 2, width // parts, 3 * own)
    near = lax.rem(lax.axis_index("dp"), 2)
    term = plus(pick(term, near, 1), exchange(pick(term, 1 - near, 1), "dp", 1))
    qkv_term = far_sum(term).astype(jnp.bfloat16)
    qkv_blocks = lax.all_gather(qkv_term, "blk", axis=0)
    qkv_rows = qkv_blocks.reshape(blocks, -1, 3, own).transpose(1, 2, 0, 3).reshape(-1, 3 * width)
    qkv_grad = lax.dynamic_slice_in_dim(qkv_rows, me * 3 * own, 3 * own, 1).astype(jnp.float32)

    def spread(values):
        return lax.dynamic_update_slice_in_dim(jnp.zeros((width,), jnp.float32), values, me * own, 0)

    y = pick(half, chip, 0).astype(jnp.float32) + far.astype(jnp.float32)
    n, r = _stats(tokens.astype(jnp.float32))
    token_grad = (grad_middle + _pull(n, r, y * norm_gain[0])).astype(jnp.bfloat16)
    small = jnp.stack(
        [
            jnp.sum(y * n, 0), sums[0], sums[1], sums_three[0], jnp.sum(y, 0), sums[2], sums[3], sums_three[1],
            spread(column_sums(grads[:, :own])), spread(column_sums(grads[:, 2 * own :])), sums[4], sums_three[2],
            *hidden_bias.reshape(-1, width),
        ]
    )
    small = sum_everywhere(small)
    place = lax.axis_index("dp")
    chunk = width // parts
    small_own = lax.dynamic_slice_in_dim(small[:12], place * chunk, chunk, 1)
    hidden = lax.dynamic_slice_in_dim(small[12:].reshape(-1), place * 4 * chunk, 4 * chunk, 0)
    return (mixed, token_grad, qkv_grad, out_grad, up_grad, down_grad, small_own[:4], small_own[4:8], small_own[8:], hidden)


def solution(mesh):
    return jax.shard_map(
        local,
        mesh=mesh,
        in_specs=(P(("dp", "blk"), None), P(("dp", "blk"), None), P("dp", None)) + (P(),) * 8,
        out_specs=(P(("dp", "blk"), None), P(("dp", "blk"), None))
        + (P("dp", "blk"),) * 4
        + (P(None, "dp"),) * 3
        + (P("dp"),),
        check_vma=False,
    )
```

```python
import functools

import jax
import jax.numpy as jnp
from jax import lax
from jax.experimental import pallas as pl
from jax.experimental.pallas import tpu as pltpu
from jax.sharding import PartitionSpec as P

epsilon = 1e-05
HD = 64
NT = (((1,), (1,)), ((), ()))
NEG = -1e30
TILE = 256


def _bounds(len_ref, qb):
    l0 = len_ref[0, 0]
    e1 = l0 + len_ref[0, 1]

    def start_of(r):
        return jnp.where(r >= e1, e1, jnp.where(r >= l0, l0, 0))

    first = qb * TILE
    s_first, s_last = start_of(first), start_of(first + TILE - 1)
    kmin = s_first // TILE
    kmid = jnp.maximum(kmin, jnp.minimum(qb, (s_last + TILE - 1) // TILE))
    rows = first + lax.broadcasted_iota(jnp.int32, (1, TILE), 1)
    return kmin, kmid, rows, start_of(rows)


def _walk(len_ref, qb, step, carry, wide):
    kmin, kmid, rows, starts = _bounds(len_ref, qb)

    def masked(kb, carry):
        at = pl.multiple_of(kb * TILE, TILE)
        kpos = at + lax.broadcasted_iota(jnp.int32, (TILE, TILE), 0)
        return step(at, TILE, (kpos >= starts) & (kpos <= rows), carry)

    def plain(size):
        def run(kb, carry):
            return step(pl.multiple_of(kb * TILE, TILE), size * TILE, None, carry)

        return run

    carry = lax.fori_loop(kmin, kmid, masked, carry)
    at, left = kmid, qb - kmid
    for size in wide:
        count = left // size
        base = at
        carry = lax.fori_loop(0, count, lambda i, c, base=base, size=size: plain(size)(base + i * size, c), carry)
        at, left = at + count * size, left - count * size
    return masked(qb, carry)


def _fill_masked(dst, value, heads):
    lane = lax.broadcasted_iota(jnp.int32, value.shape, 1) // HD
    for h in range(heads):
        dst[pl.ds(h * TILE, TILE), :] = jnp.where(lane == h, value, jnp.zeros_like(value))


def _span(len_ref, qb):
    l0 = len_ref[0, 0]
    e1 = l0 + len_ref[0, 1]

    def start_of(r):
        return jnp.where(r >= e1, e1, jnp.where(r >= l0, l0, 0))

    rows = qb * TILE + lax.broadcasted_iota(jnp.int32, (1, TILE), 1)
    kmin = start_of(qb * TILE) // TILE
    return kmin, qb + 1 - kmin, rows, start_of(rows)


def _at(kb):
    return pl.ds(pl.multiple_of(kb * TILE, TILE), TILE)


def _mask(kb, rows, starts):
    kpos = kb * TILE + lax.broadcasted_iota(jnp.int32, (TILE, TILE), 0)
    return (kpos >= starts) & (kpos <= rows)


def _pipeline(kmin, count, load, work, use):
    odd = lax.rem(count, 2)
    end = kmin + count - 1

    @pl.when(odd == 1)
    def _():
        load(kmin, 0)
        load(jnp.minimum(kmin + 1, end), 1)
        work(kmin, 0)

    @pl.when(odd == 0)
    def _():
        load(kmin, 1)

    first = kmin + odd

    def two(i, carry):
        kb = first + 2 * i
        load(jnp.minimum(kb + 1, end), 0)
        work(kb, 1)
        use(jnp.maximum(kb - 1, kmin), 0)
        load(jnp.minimum(kb + 2, end), 1)
        work(kb + 1, 0)
        use(kb, 1)
        return carry

    lax.fori_loop(0, count // 2, two, 0)
    use(end, 0)


def fwd_kernel(len_ref, q_ref, k_ref, v_ref, o_ref, lse_ref, qm, acc, s_one, s_two, p_one, p_two, fade_one, fade_two, top, norm, vt, *, heads):
    qb = pl.program_id(0)

    @pl.when(qb == 0)
    def _():
        vt[...] = v_ref[...].T

    _fill_masked(qm, q_ref[...] * jnp.bfloat16(0.125), heads)
    acc[...] = jnp.zeros_like(acc)
    p_one[...] = jnp.zeros_like(p_one)
    fade_one[...] = jnp.zeros_like(fade_one)
    top[...] = jnp.full(top.shape, 0.1 * NEG, jnp.float32)
    norm[...] = jnp.zeros_like(norm)
    kmin, count, rows, starts = _span(len_ref, qb)
    scores, probs, fades = (s_one, s_two), (p_one, p_two), (fade_one, fade_two)

    def load(kb, slot):
        for h in range(heads):
            mine = pl.ds(h * TILE, TILE)
            scores[slot][:, mine] = lax.dot_general(k_ref[_at(kb), :], qm[mine, :], NT, preferred_element_type=jnp.float32)

    def work(kb, slot):
        mask = _mask(kb, rows, starts)
        for h in range(heads):
            mine, row = pl.ds(h * TILE, TILE), pl.ds(h, 1)
            s = jnp.where(mask, scores[slot][:, mine], NEG)
            m = top[row, :]
            new = jnp.maximum(m, jnp.max(s, 0, keepdims=True))
            p = jnp.exp(s - new)
            fade = jnp.exp(m - new)
            top[row, :] = new
            norm[row, :] = norm[row, :] * fade + jnp.sum(p, 0, keepdims=True)
            fades[slot][row, :] = fade
            probs[slot][:, mine] = p.astype(jnp.bfloat16)

    def use(kb, slot):
        for h in range(heads):
            lanes = pl.ds(h * HD, HD)
            part = jnp.dot(vt[lanes, _at(kb)], probs[slot][:, pl.ds(h * TILE, TILE)], preferred_element_type=jnp.float32)
            acc[lanes, :] = acc[lanes, :] * fades[slot][pl.ds(h, 1), :] + part

    _pipeline(kmin, count, load, work, use)
    for h in range(heads):
        row, lanes = pl.ds(h, 1), pl.ds(h * HD, HD)
        lse_ref[row, :] = top[row, :] + jnp.log(norm[row, :])
        acc[lanes, :] = acc[lanes, :] / norm[row, :]
    o_ref[...] = acc[...].T.astype(jnp.bfloat16)


def attn_fwd(lengths, qkv):
    n, lane = qkv.shape[0], qkv.shape[1] // 3
    heads = lane // HD
    wide = heads * TILE
    f32, bf16 = jnp.float32, jnp.bfloat16
    return pl.pallas_call(
        functools.partial(fwd_kernel, heads=heads),
        grid_spec=pltpu.PrefetchScalarGridSpec(
            num_scalar_prefetch=1,
            grid=(n // TILE,),
            in_specs=[
                pl.BlockSpec((TILE, lane), lambda i, L: (i, 0)),
                pl.BlockSpec((n, lane), lambda i, L: (0, 1)),
                pl.BlockSpec((n, lane), lambda i, L: (0, 2)),
            ],
            out_specs=[pl.BlockSpec((TILE, lane), lambda i, L: (i, 0)), pl.BlockSpec((heads, TILE), lambda i, L: (0, i))],
            scratch_shapes=[
                pltpu.VMEM((wide, lane), bf16), pltpu.VMEM((lane, TILE), f32),
                pltpu.VMEM((TILE, wide), f32), pltpu.VMEM((TILE, wide), f32), pltpu.VMEM((TILE, wide), bf16), pltpu.VMEM((TILE, wide), bf16),
                pltpu.VMEM((heads, TILE), f32), pltpu.VMEM((heads, TILE), f32), pltpu.VMEM((heads, TILE), f32), pltpu.VMEM((heads, TILE), f32),
                pltpu.VMEM((lane, n), bf16),
            ],
        ),
        out_shape=[jax.ShapeDtypeStruct((n, lane), bf16), jax.ShapeDtypeStruct((heads, n), f32)],
        compiler_params=pltpu.CompilerParams(vmem_limit_bytes=58 * 2**20),
        cost_estimate=pl.CostEstimate(flops=n * n * lane * 9, bytes_accessed=10 * n * lane, transcendentals=n * n * heads // 2),
        name="attn_fwd",
    )(lengths, qkv, qkv, qkv)


def bwd_kernel(len_ref, q_ref, do_ref, o_ref, lse_ref, k_ref, v_ref, d_ref, qm, dom, ps, ds, dqt, dk, dv, kt, *, heads, wide):
    qb = pl.program_id(0)
    c = heads * HD

    @pl.when(qb == 0)
    def _():
        dk[...] = jnp.zeros_like(dk)
        dv[...] = jnp.zeros_like(dv)
        kt[...] = k_ref[...].T

    _fill_masked(qm, q_ref[...] * jnp.bfloat16(0.125), heads)
    _fill_masked(dom, do_ref[...], heads)
    prod = (do_ref[...].astype(jnp.float32) * o_ref[...].astype(jnp.float32)).T
    delta = [jnp.sum(prod[h * HD : (h + 1) * HD], 0, keepdims=True) for h in range(heads)]
    dqt[...] = jnp.zeros_like(dqt)

    def step(at, size, mask, carry):
        keys = pl.ds(at, size)
        used = pl.ds(0, size)
        for h in range(heads):
            mine = pl.ds(h * TILE, TILE)
            s = lax.dot_general(k_ref[keys, :], qm[mine, :], NT, preferred_element_type=jnp.float32)
            p = jnp.exp(s - lse_ref[pl.ds(h, 1), :])
            if mask is not None:
                p = jnp.where(mask, p, 0.0)
            dp = lax.dot_general(v_ref[keys, :], dom[mine, :], NT, preferred_element_type=jnp.float32)
            ps[used, mine] = p.astype(jnp.bfloat16)
            ds[used, mine] = (p * (dp - delta[h])).astype(jnp.bfloat16)
        dv[keys, :] += jnp.dot(ps[used, :], dom[...], preferred_element_type=jnp.float32)
        dk[keys, :] += jnp.dot(ds[used, :], qm[...], preferred_element_type=jnp.float32)
        for h in range(heads):
            lanes = pl.ds(h * HD, HD)
            dqt[lanes, :] += jnp.dot(kt[lanes, keys], ds[used, pl.ds(h * TILE, TILE)], preferred_element_type=jnp.float32)
        return carry

    _walk(len_ref, qb, step, 0, wide)
    d_ref[pl.ds(pl.multiple_of(qb * TILE, TILE), TILE), pl.ds(0, c)] = (dqt[...] * 0.125).T.astype(jnp.bfloat16)

    @pl.when(qb == pl.num_programs(0) - 1)
    def _():
        d_ref[:, pl.ds(c, c)] = dk[...].astype(jnp.bfloat16)
        d_ref[:, pl.ds(2 * c, c)] = dv[...].astype(jnp.bfloat16)


def attn_bwd(lengths, qkv, do, o, lse, pair=0, lane=256, wide=(1,)):
    n = qkv.shape[0]
    heads = lane // HD
    row = lambda col: pl.BlockSpec((TILE, lane), lambda i, L: (i, col))
    whole = lambda col: pl.BlockSpec((n, lane), lambda i, L: (0, col))
    return pl.pallas_call(
        functools.partial(bwd_kernel, heads=heads, wide=wide),
        grid_spec=pltpu.PrefetchScalarGridSpec(
            num_scalar_prefetch=1,
            grid=(n // TILE,),
            in_specs=[
                row(3 * pair), row(pair), row(0), pl.BlockSpec((heads, TILE), lambda i, L: (0, i)),
                whole(3 * pair + 1), whole(3 * pair + 2),
            ],
            out_specs=pl.BlockSpec((n, 3 * lane), lambda i, L: (0, pair)),
            scratch_shapes=[
                pltpu.VMEM((heads * TILE, lane), jnp.bfloat16),
                pltpu.VMEM((heads * TILE, lane), jnp.bfloat16),
                pltpu.VMEM((wide[0] * TILE, heads * TILE), jnp.bfloat16),
                pltpu.VMEM((wide[0] * TILE, heads * TILE), jnp.bfloat16),
                pltpu.VMEM((lane, TILE), jnp.float32),
                pltpu.VMEM((n, lane), jnp.float32),
                pltpu.VMEM((n, lane), jnp.float32),
                pltpu.VMEM((lane, n), jnp.bfloat16),
            ],
        ),
        out_shape=jax.ShapeDtypeStruct(qkv.shape, jnp.bfloat16),
        compiler_params=pltpu.CompilerParams(vmem_limit_bytes=58 * 2**20),
        cost_estimate=pl.CostEstimate(flops=n * n * lane * 11, bytes_accessed=20 * n * lane, transcendentals=n * n * heads // 2),
        name="attn_bwd",
    )(lengths, qkv, do, o, lse, qkv, qkv)


def _stats(v):
    c = v - jnp.mean(v, -1, keepdims=True)
    r = lax.rsqrt(jnp.mean(c * c, -1, keepdims=True) + epsilon)
    return c * r, r


def _pull(n, r, e):
    return r * (e - jnp.mean(e, -1, keepdims=True) - n * jnp.mean(e * n, -1, keepdims=True))


def _fold(v):
    return jnp.sum(v.reshape(-1, 8, v.shape[-1]), 0)


def _row(ref, i):
    return ref[pl.ds(i, 1), :]


def _each(total, size, fn):
    def body(i, carry):
        fn(pl.ds(pl.multiple_of(i * size, size), size))
        return carry

    lax.fori_loop(0, total // size, body, 0)


def _turn_blocks(dst, value, core):
    own = dst.shape[0] // 4
    flipped = value.T
    for b in range(4):
        stays = 1 - lax.rem(core + b % 2, 2)
        dst[pl.ds(pl.multiple_of((2 * stays + b // 2) * own, own), own), :] = flipped[b * own : (b + 1) * own, :]


def ffn_kernel(
    x_hbm, cot_hbm, own_hbm, wo_hbm, up_ref, down_ref, gain_ref, shift_ref, bias_ref, fb_ref,
    mixed_ref, mid_out, n_out, r_ref, low_ref, turned_ref, second_out, act_ref, slope_ref, small_ref, att_out,
    x_ref, cot_ref, wo_ref, mid_ref, n_ref, second_t, att_ref, second, branch, ffn, sums, sends, recvs, own_sem, load_sems, save_sems, *, tiles, strip,
):
    s = pl.program_id(0)
    rows, width = x_ref.shape
    f32 = jnp.float32

    def loaded(i):
        return pltpu.make_async_copy((x_hbm, cot_hbm, wo_hbm)[i], (x_ref, cot_ref, wo_ref)[i], load_sems.at[i])

    def saved(i):
        pairs = ((mid_ref, mid_out), (n_ref, n_out), (second_t, second_out), (att_ref, att_out))
        return pltpu.make_async_copy(*pairs[i], save_sems.at[i])

    @pl.when(s == 0)
    def _():
        me = lax.axis_index("blk")
        own = width // 4
        peers = (me + 1 - 2 * lax.rem(me, 2), lax.rem(me + 2, 4), 3 - me)
        mesh_ids = pl.DeviceIdType.MESH
        barrier = pltpu.get_barrier_semaphore()
        for block in peers:
            pl.semaphore_signal(barrier, inc=1, device_id={"blk": block}, device_id_type=mesh_ids)
        pl.semaphore_wait(barrier, 3)

        def rows_of(block):
            return own_hbm.at[pl.ds(pl.multiple_of(block * rows, rows), rows), :]

        here = att_ref.at[:, pl.ds(pl.multiple_of(me * own, own), own)]
        copies = [
            pltpu.make_async_remote_copy(
                src_ref=rows_of(block), dst_ref=here, send_sem=sends.at[i], recv_sem=recvs.at[i],
                device_id={"blk": block}, device_id_type=mesh_ids,
            )
            for i, block in enumerate(peers)
        ]
        for copy in copies[::-1]:
            copy.start()
        mine = pltpu.make_async_copy(rows_of(me), here, own_sem)
        mine.start()
        for i in (2, 0, 1):
            loaded(i).start()
        sums[...] = jnp.zeros_like(sums)
        mine.wait()
        for i in range(3):
            loaded(i).wait()
        for copy in copies:
            copy.wait_send()
            copy.wait_recv()
        saved(3).start()
        branch[...] = jnp.dot(att_ref[...], wo_ref[...], preferred_element_type=f32) + _row(bias_ref, 2)

        def normed(at):
            n, r = _stats(branch[at, :])
            n_ref[at, :] = n.astype(jnp.bfloat16)
            r_ref[at, :] = r
            m = x_ref[at, :].astype(f32) + n * _row(gain_ref, 1) + _row(shift_ref, 1)
            mid_ref[at, :] = m
            n, _ = _stats(m)
            second[at, :] = (n * _row(gain_ref, 2) + _row(shift_ref, 2)).astype(jnp.bfloat16)

        _each(rows, strip, normed)
        second_t[...] = second[...].T
        for i in range(3):
            saved(i).start()

    u = jnp.dot(second[...], up_ref[...], preferred_element_type=f32) + fb_ref[...]
    c1, c3 = 0.7978845608028654, 0.7978845608028654 * 0.044715
    sq = u * u
    t = jnp.tanh(u * (c1 + c3 * sq))
    half = 0.5 + 0.5 * t
    a = (u * half).astype(jnp.bfloat16)
    act_ref[...] = a
    slope_ref[...] = (half + (0.5 * u) * (1.0 - t * t) * (c1 + 3.0 * c3 * sq)).astype(jnp.bfloat16)
    part = jnp.dot(a, down_ref[...], preferred_element_type=f32)

    @pl.when(s == 0)
    def _():
        ffn[...] = part + _row(bias_ref, 3)

    @pl.when(s > 0)
    def _():
        ffn[...] += part

    @pl.when(s == tiles - 1)
    def _():
        def normed(at):
            n, r = _stats(ffn[at, :])
            y = cot_ref[at, :].astype(f32)
            mixed_ref[at, :] = (mid_ref[at, :] + n * _row(gain_ref, 3) + _row(shift_ref, 3)).astype(jnp.bfloat16)
            g = _pull(n, r, y * _row(gain_ref, 3)).astype(jnp.bfloat16)
            low_ref[at, :] = g
            sums[pl.ds(0, 8), :] += _fold(y * n)
            sums[pl.ds(8, 8), :] += _fold(y)
            sums[pl.ds(16, 8), :] += _fold(g.astype(f32))

        _each(rows, strip, normed)
        _turn_blocks(turned_ref, low_ref[...], lax.rem(lax.axis_index("blk"), 2))
        for i in range(4):
            saved(i).wait()
        for i in range(3):
            small_ref[pl.ds(i, 1), :] = jnp.sum(sums[pl.ds(8 * i, 8), :], 0, keepdims=True)


def _once(*shape):
    return pl.BlockSpec(shape, lambda s: (0,) * len(shape), pipeline_mode=pl.Buffered(1))


def ffn_forward(tokens, cotangent, attended, out_weight, up_weight, down_weight, norm_gain, norm_bias, proj_bias, ffn_bias):
    rows, width = tokens.shape
    hidden = up_weight.shape[1]
    tiles = 8
    hid = hidden // tiles
    bf16, f32 = jnp.bfloat16, jnp.float32
    shape = jax.ShapeDtypeStruct
    return pl.pallas_call(
        functools.partial(ffn_kernel, tiles=tiles, strip=rows // 4),
        grid=(tiles,),
        in_specs=[
            *[pl.BlockSpec(memory_space=pl.ANY)] * 4,
            pl.BlockSpec((width, hid), lambda s: (0, s)), pl.BlockSpec((hid, width), lambda s: (s, 0)),
            _once(4, width), _once(4, width), _once(4, width), pl.BlockSpec((1, hid), lambda s: (0, s)),
        ],
        out_specs=[
            _once(rows, width), *[pl.BlockSpec(memory_space=pl.ANY)] * 2, _once(rows, 1), _once(rows, width),
            _once(width, rows), pl.BlockSpec(memory_space=pl.ANY),
            pl.BlockSpec((rows, hid), lambda s: (0, s)), pl.BlockSpec((rows, hid), lambda s: (0, s)), _once(8, width), pl.BlockSpec(memory_space=pl.ANY),
        ],
        out_shape=[
            shape((rows, width), bf16), shape((rows, width), f32), shape((rows, width), bf16), shape((rows, 1), f32),
            shape((rows, width), bf16), shape((width, rows), bf16), shape((width, rows), bf16),
            shape((rows, hidden), bf16), shape((rows, hidden), bf16), shape((8, width), f32), shape((rows, width), bf16),
        ],
        scratch_shapes=[
            pltpu.VMEM((rows, width), bf16), pltpu.VMEM((rows, width), bf16), pltpu.VMEM((width, width), bf16), pltpu.VMEM((rows, width), f32),
            pltpu.VMEM((rows, width), bf16), pltpu.VMEM((width, rows), bf16), pltpu.VMEM((rows, width), bf16),
            pltpu.VMEM((rows, width), bf16), pltpu.VMEM((rows, width), f32), pltpu.VMEM((rows, width), f32), pltpu.VMEM((24, width), f32), pltpu.SemaphoreType.DMA((3,)), pltpu.SemaphoreType.DMA((3,)), pltpu.SemaphoreType.DMA(()),
            pltpu.SemaphoreType.DMA((3,)), pltpu.SemaphoreType.DMA((4,)),
        ],
        compiler_params=pltpu.CompilerParams(collective_id=3, has_side_effects=True, vmem_limit_bytes=56 * 2**20),
        cost_estimate=pl.CostEstimate(flops=18 * rows * width * width, bytes_accessed=50 * 2**20, transcendentals=rows * hidden),
        name="ffn_forward",
    )(tokens, cotangent, attended, out_weight, up_weight, down_weight, norm_gain, norm_bias, proj_bias, ffn_bias.reshape(1, -1))


def grads_kernel(
    low_ref, turned_hbm, second_hbm, act_ref, slope_ref, up_ref, down_ref, mid_hbm, n_hbm, r_ref, cot_hbm, att_hbm, wo_hbm, gain_ref,
    gmid_ref, small_ref, hid_ref, up_out, down_out, out_out, gown_out, out_line,
    turned_ref, second_t, cot_ref, att_ref, wo_ref, pre, gs, low, turned, gatt, sums, up_buf, up_in, up_y, down_send, down_keep, down_in, down_x, up_z,
    up_core, up_core_in, up_far, up_far_in, down_core, down_core_in, down_far, down_far_in, up_done, down_done, own_sems, gatt_sends, gatt_recvs, line_sends, line_recvs, save_sems, *, tiles, strip, fold,
):
    s = pl.program_id(0)
    rows, width = low_ref.shape
    own = width // 4
    f32, bf16 = jnp.float32, jnp.bfloat16
    pair, side = s // 2, lax.rem(s, 2)
    me, place = lax.axis_index("blk"), lax.axis_index("dp")
    core, chip, near = lax.rem(me, 2), me // 2, lax.rem(place, 2)
    line = place // 2
    twin, other, beside = {"blk": me + 1 - 2 * core}, {"blk": lax.rem(me + 2, 4)}, {"dp": place + 1 - 2 * near}
    last = {"blk": 3 - me}
    half = tiles // 2
    mesh_ids = pl.DeviceIdType.MESH

    def remote(src, dst, sends, recvs, i, target):
        return pltpu.make_async_remote_copy(
            src_ref=src, dst_ref=dst, send_sem=sends.at[i], recv_sem=recvs.at[i], device_id=target, device_id_type=mesh_ids
        )

    def up_to_twin(p):
        return remote(up_buf.at[0], up_in.at[p], up_core, up_core_in, p, twin)

    def up_to_beside(p):
        return remote(up_in.at[p, :, 1 - near], up_y.at[p], up_far, up_far_in, p, beside)

    def down_to_twin(u, slot):
        return remote(down_send.at[slot], down_in.at[lax.rem(u, 4)], down_core, down_core_in, u, twin)

    def down_to_other(u):
        return remote(down_keep.at[u, 1 - chip], down_x.at[u], down_far, down_far_in, u, other)

    def up_result(p):
        if fold:
            return pltpu.make_async_copy(up_y.at[p, line], up_out.at[p], up_done.at[p])
        return pltpu.make_async_copy(up_y.at[p], up_out.at[:, p], up_done.at[p])

    def up_to_line(p, k):
        ahead = lax.rem(line + k, 4)
        return remote(up_y.at[p, ahead], up_z.at[k - 1, p], line_sends, line_recvs, 3 * p + k - 1, {"dp": 2 * ahead + near})

    def join_line(p):
        total = up_y[p, line].astype(f32)
        for k in range(1, 4):
            up_to_line(p, k).wait_recv()
            total += up_z[k - 1, p].astype(f32)
        up_y[p, line] = total.astype(bf16)
        up_result(p).start()

    def down_result(u):
        tile = 4 * (u // 4) + 2 * lax.rem(u, 2) + lax.rem(u // 2, 2)
        return pltpu.make_async_copy(down_x.at[u], down_out.at[tile], down_done.at[u])

    def saved(i):
        pairs = ((mid_hbm, gmid_ref), (n_hbm, low), (cot_hbm, cot_ref), (att_hbm, att_ref), (wo_hbm, wo_ref), (turned_hbm, turned_ref), (second_hbm, second_t))
        return pltpu.make_async_copy(*pairs[i], save_sems.at[i])

    def out_line_result():
        return pltpu.make_async_copy(up_y.at[half], out_line, own_sems.at[0])

    def out_result(i):
        return pltpu.make_async_copy(up_buf.at[i], out_out.at[i], own_sems.at[2 + i])

    def columns_to(i):
        target = (last, other, twin)[i]
        block = target["blk"]
        src = gatt.at[:, pl.ds(pl.multiple_of(block * own, own), own)]
        dst = gown_out.at[pl.ds(pl.multiple_of(me * rows, rows), rows), :]
        return remote(src, dst, gatt_sends, gatt_recvs, i, target)

    def columns_here():
        src = gatt.at[:, pl.ds(pl.multiple_of(me * own, own), own)]
        return pltpu.make_async_copy(src, gown_out.at[pl.ds(pl.multiple_of(me * rows, rows), rows), :], own_sems.at[4])

    def join_up(p):
        up_to_twin(p).wait_recv()
        up_in[p] = (up_in[p].astype(f32) + up_buf[1].astype(f32)).astype(bf16)
        up_to_beside(p).start()

    def join_far_up(p):
        up_to_beside(p).wait_recv()
        up_y[p] = (up_y[p].astype(f32) + up_in[p, :, near].astype(f32)).astype(bf16)
        if fold:
            for k in range(1, 4):
                up_to_line(p, k).start()
        else:
            up_result(p).start()

    def join_down(u):
        down_to_twin(u, 0).wait_recv()
        down_keep[u] = (down_keep[u].astype(f32) + down_in[lax.rem(u, 4)].astype(f32)).astype(bf16)
        down_to_other(u).start()

    def join_far_down(u):
        down_to_other(u).wait_recv()
        down_x[u] = (down_x[u].astype(f32) + down_keep[u, chip].astype(f32)).astype(bf16)
        down_result(u).start()

    @pl.when(s == 0)
    def _():
        barrier = pltpu.get_barrier_semaphore()
        for target in (twin, other, beside, last):
            pl.semaphore_signal(barrier, inc=1, device_id=target, device_id_type=mesh_ids)
        sums[...] = jnp.zeros_like(sums)
        for i in (5, 6, 0, 1, 2, 3, 4):
            saved(i).start()
        for i in range(1, 4 if fold else 1):
            ahead = lax.rem(line + i, 4)
            pl.semaphore_signal(barrier, inc=1, device_id={"dp": 2 * ahead + near}, device_id_type=mesh_ids)
        pl.semaphore_wait(barrier, 7 if fold else 4)

    @pl.when(s > 0)
    def _():
        join_down(s - 1)

    @pl.when((side == 0) & (s > 0))
    def _():
        join_up(pair - 1)

    @pl.when(s >= 3)
    def _():
        join_far_down(s - 3)

    @pl.when((s == 5) | (s == 7))
    def _():
        join_far_up((s - 5) // 2)

    g = lax.dot_general(low_ref[...], down_ref[...], NT, preferred_element_type=f32) * slope_ref[...].astype(f32)
    g = g.astype(bf16)
    pre[...] = g
    hid_ref[pl.ds(s, 1)] = jnp.sum(g.astype(f32), 0, keepdims=True)[None]
    part = lax.dot_general(g, up_ref[...], NT, preferred_element_type=f32)

    @pl.when(s == 0)
    def _():
        gs[...] = part

    @pl.when(s > 0)
    def _():
        gs[...] += part

    @pl.when(s == 0)
    def _():
        saved(5).wait()
        saved(6).wait()

    down_grad = jnp.dot(turned_ref[...], act_ref[...], preferred_element_type=f32).astype(bf16)

    @pl.when(s >= 2)
    def _():
        down_to_twin(s - 2, side).wait_send()

    down_send[side] = down_grad[: width // 2].reshape(2, own, -1)
    down_to_twin(s, side).start()
    down_keep[s] = down_grad[width // 2 :].reshape(2, own, -1)
    up_grad = jnp.dot(second_t[...], pre[...], preferred_element_type=f32).astype(bf16).reshape(up_buf.shape[1:])

    @pl.when(side == core)
    def _():
        up_buf[1] = up_grad

    @pl.when(side != core)
    def _():
        @pl.when(pair > 0)
        def _():
            up_to_twin(pair - 1).wait_send()

        up_buf[0] = up_grad
        up_to_twin(pair).start()

    @pl.when(s == tiles - 1)
    def _():
        def normed(at):
            n, r = _stats(gmid_ref[at, :])
            y = gs[at, :]
            gm = cot_ref[at, :].astype(f32) + _pull(n, r, y * _row(gain_ref, 2))
            gmid_ref[at, :] = gm
            sums[pl.ds(8, 8), :] += _fold(y * n)
            sums[pl.ds(24, 8), :] += _fold(y)
            n, r = low[at, :].astype(f32), r_ref[at, :]
            g = _pull(n, r, gm * _row(gain_ref, 1)).astype(bf16)
            low[at, :] = g
            sums[pl.ds(0, 8), :] += _fold(gm * n)
            sums[pl.ds(16, 8), :] += _fold(gm)
            sums[pl.ds(32, 8), :] += _fold(g.astype(f32))

        join_down(tiles - 1)
        join_up(half - 1)
        for i in range(5):
            saved(i).wait()
        _each(rows, strip, normed)
        gatt[...] = lax.dot_general(low[...], wo_ref[...], NT, preferred_element_type=f32).astype(bf16)
        for i in range(3):
            columns_to(i).start()
        columns_here().start()
        join_far_up(2)
        _turn_blocks(turned, low[...], core)
        grad = jnp.dot(turned[...], att_ref[...], preferred_element_type=f32).astype(bf16)
        up_to_twin(half - 1).wait_send()
        if fold:
            thin = width // 8
            for d in range(8):
                for b in range(8):
                    piece = grad[b * thin : (b + 1) * thin, d * thin : (d + 1) * thin]
                    up_buf[b // 4, d // 2, d % 2, :, pl.ds(b % 4 * thin, thin)] = piece
            up_to_twin(half).start()
        else:
            for i in range(2):
                up_buf[i] = grad[:, i * width // 2 : (i + 1) * width // 2].reshape(up_buf.shape[1:])
                out_result(i).start()
        for i in range(5):
            small_ref[pl.ds(i, 1), :] = jnp.sum(sums[pl.ds(8 * i, 8), :], 0, keepdims=True)
        if fold:
            join_up(half)
        join_far_up(3)
        for u in range(tiles - 3, tiles):
            join_far_down(u)
        if fold:
            for p in range(half):
                join_line(p)
            up_to_beside(half).wait_recv()
            up_y[half] = (up_y[half].astype(f32) + up_in[half, :, near].astype(f32)).astype(bf16)
            out_line_result().start()
            out_line_result().wait()
        down_to_twin(tiles - 2, 0).wait_send()
        down_to_twin(tiles - 1, 1).wait_send()
        if fold:
            up_to_twin(half).wait_send()
        else:
            out_result(0).wait()
            out_result(1).wait()
        for p in range(half + fold):
            up_to_beside(p).wait_send()
        for p in range(half):
            up_result(p).wait()
            for i in range(1, 4 if fold else 1):
                up_to_line(p, i).wait_send()
        for u in range(tiles):
            down_to_other(u).wait_send()
            down_result(u).wait()
        for i in range(3):
            columns_to(i).wait_send()
            columns_to(i).wait_recv()
        columns_here().wait()


def ffn_backward(parts, low, turned, second_t, act, slope, up_weight, down_weight, mid, n_one, r_one, cotangent, attended, out_weight, norm_gain):
    rows, width = low.shape
    hidden = up_weight.shape[1]
    tiles, own = 8, width // 4
    hid = hidden // tiles
    bf16, f32 = jnp.bfloat16, jnp.float32
    shape = jax.ShapeDtypeStruct
    tile_of = lambda s: 4 * (s // 4) + 2 * lax.rem(s, 2) + lax.rem(s // 2, 2)
    thin = (parts // 2, 2, width // parts, hid)
    dma = pltpu.SemaphoreType.DMA
    half = tiles // 2
    fold = int(parts == 8)
    return pl.pallas_call(
        functools.partial(grads_kernel, tiles=tiles, strip=rows // 4, fold=fold),
        grid=(tiles,),
        in_specs=[
            _once(rows, width), pl.BlockSpec(memory_space=pl.ANY), pl.BlockSpec(memory_space=pl.ANY),
            pl.BlockSpec((rows, hid), lambda s: (0, tile_of(s))), pl.BlockSpec((rows, hid), lambda s: (0, tile_of(s))),
            pl.BlockSpec((width, hid), lambda s: (0, tile_of(s))), pl.BlockSpec((hid, width), lambda s: (tile_of(s), 0)),
            pl.BlockSpec(memory_space=pl.ANY), pl.BlockSpec(memory_space=pl.ANY), _once(rows, 1), *[pl.BlockSpec(memory_space=pl.ANY)] * 3, _once(4, width),
        ],
        out_specs=[
            _once(rows, width), _once(8, width), _once(tiles, 1, hid),
            *[pl.BlockSpec(memory_space=pl.ANY)] * 5,
        ],
        out_shape=[
            shape((rows, width), f32),
            shape((8, width), f32), shape((tiles, 1, hid), f32),
            shape((half, width // parts, hid) if fold else (parts // 2, half, width // parts, hid), bf16), shape((tiles, own, hid), bf16), shape((2,) + thin, bf16),
            shape((4 * rows, own), bf16), shape((parts // 2, width // parts, hid), bf16),
        ],
        scratch_shapes=[
            pltpu.VMEM((width, rows), bf16), pltpu.VMEM((width, rows), bf16), pltpu.VMEM((rows, width), bf16), pltpu.VMEM((rows, width), bf16),
            pltpu.VMEM((width, width), bf16), pltpu.VMEM((rows, hid), bf16), pltpu.VMEM((rows, width), f32), pltpu.VMEM((rows, width), bf16), pltpu.VMEM((width, rows), bf16), pltpu.VMEM((rows, width), bf16),
            pltpu.VMEM((40, width), f32),
            pltpu.VMEM((2,) + thin, bf16), pltpu.VMEM((half + fold,) + thin, bf16), pltpu.VMEM((half + fold, parts // 2, width // parts, hid), bf16),
            pltpu.VMEM((2, 2, own, hid), bf16), pltpu.VMEM((tiles, 2, own, hid), bf16), pltpu.VMEM((4, 2, own, hid), bf16),
            pltpu.VMEM((tiles, own, hid), bf16), pltpu.VMEM((3, half, width // parts, hid), bf16),
            *[dma((half + fold,))] * 4, *[dma((tiles,))] * 4, dma((half + fold,)), dma((tiles,)), dma((5,)), dma((3,)), dma((3,)), dma((3 * half,)), dma((3 * half,)), dma((7,)),
        ],
        compiler_params=pltpu.CompilerParams(collective_id=1, has_side_effects=True, vmem_limit_bytes=60 * 2**20),
        name="ffn_backward",
    )(low, turned, second_t, act, slope, up_weight, down_weight, mid, n_one, r_one, cotangent, attended, out_weight, norm_gain)


def project_kernel(
    x_hbm, w_hbm, gain_ref, shift_ref, bias_ref, all_out, qkv_out, w_out, x_ref, all_ref, qkv_ref, w_ref, x_sems, out_sems, w_sems, chip_send, chip_recv, core_send, core_recv, pass_send, pass_recv, *, pieces,
):
    me = lax.axis_index("blk")
    core = lax.rem(me, 2)
    twin, other, last = me + 1 - 2 * core, lax.rem(me + 2, 4), 3 - me
    rows, width = x_ref.shape
    own = width // 4
    size = rows // pieces
    fetch = [pltpu.make_async_copy(x_hbm.at[pl.ds(i * size, size), :], x_ref.at[pl.ds(i * size, size), :], x_sems.at[i]) for i in range(pieces)]
    for copy in fetch:
        copy.start()
    barrier = pltpu.get_barrier_semaphore()
    for target in (twin, other):
        pl.semaphore_signal(barrier, inc=1, device_id={"blk": target}, device_id_type=pl.DeviceIdType.MESH)
    loads = []
    for third in range(3):
        columns = pl.ds(pl.multiple_of(third * width + me * own, own), own)
        load = pltpu.make_async_copy(w_hbm.at[:, columns], w_ref.at[:, pl.ds(third * own, own)], w_sems.at[third])
        load.start()
        loads.append(load)

    def at(block, i):
        return pl.ds(pl.multiple_of(block * rows + i * size, size), size)

    def send(block, i, target, sends, recvs):
        piece = all_ref.at[at(block, i), :]
        copy = pltpu.make_async_remote_copy(
            src_ref=piece, dst_ref=piece, send_sem=sends.at[i], recv_sem=recvs.at[i],
            device_id={"blk": target}, device_id_type=pl.DeviceIdType.MESH,
        )
        return copy

    def project(block, i):
        where = at(block, i)
        got = jnp.dot(all_ref[where, :], w_ref[...], preferred_element_type=jnp.float32)
        for third in range(3):
            part = got[:, third * own : (third + 1) * own]
            if third != 1:
                part = part + bias_ref[pl.ds(third // 2, 1), pl.ds(pl.multiple_of(me * own, own), own)]
            qkv_ref[where, pl.ds(third * own, own)] = part.astype(jnp.bfloat16)
        for src, dst in ((all_ref, all_out), (qkv_ref, qkv_out)):
            copy = pltpu.make_async_copy(src.at[where, :], dst.at[where, :], out_sems.at[len(saved)])
            copy.start()
            saved.append(copy)

    sent, saved = [], []
    for i in range(pieces):
        fetch[i].wait()
        n, _ = _stats(x_ref[pl.ds(i * size, size), :].astype(jnp.float32))
        all_ref[at(me, i), :] = (n * gain_ref[pl.ds(0, 1), :] + shift_ref[pl.ds(0, 1), :]).astype(jnp.bfloat16)
        if i == 0:
            pl.semaphore_wait(barrier, 2)
        for target, sends, recvs in ((other, chip_send, chip_recv), (twin, core_send, core_recv)):
            copy = send(me, i, target, sends, recvs)
            copy.start()
            sent.append(copy)
    for load in loads:
        load.wait()
    keep = pltpu.make_async_copy(w_ref, w_out, w_sems.at[3])
    keep.start()
    for i in range(pieces):
        project(me, i)
    for i in range(pieces):
        send(twin, i, twin, core_send, core_recv).wait_recv()
        project(twin, i)
    for i in range(pieces):
        send(other, i, other, chip_send, chip_recv).wait_recv()
        copy = send(other, i, twin, pass_send, pass_recv)
        copy.start()
        sent.append(copy)
        project(other, i)
        if i > 0:
            send(last, i - 1, twin, pass_send, pass_recv).wait_recv()
            project(last, i - 1)
    send(last, pieces - 1, twin, pass_send, pass_recv).wait_recv()
    project(last, pieces - 1)
    for copy in sent:
        copy.wait_send()
    for copy in saved:
        copy.wait()
    keep.wait()


def gather_project(tokens, qkv_weight, norm_gain, norm_bias, proj_bias):
    rows, width = tokens.shape
    pieces = 4
    vmem, hbm = pl.BlockSpec(memory_space=pltpu.VMEM), pl.BlockSpec(memory_space=pl.ANY)
    dma = pltpu.SemaphoreType.DMA((pieces,))
    return pl.pallas_call(
        functools.partial(project_kernel, pieces=pieces),
        in_specs=[hbm, hbm, vmem, vmem, vmem],
        out_specs=[hbm] * 3,
        out_shape=[jax.ShapeDtypeStruct((4 * rows, width), jnp.bfloat16), jax.ShapeDtypeStruct((4 * rows, 3 * width // 4), jnp.bfloat16), jax.ShapeDtypeStruct((width, 3 * width // 4), jnp.bfloat16)],
        scratch_shapes=[
            pltpu.VMEM((rows, width), jnp.bfloat16), pltpu.VMEM((4 * rows, width), jnp.bfloat16),
            pltpu.VMEM((4 * rows, 3 * width // 4), jnp.bfloat16), pltpu.VMEM((width, 3 * width // 4), jnp.bfloat16),
            dma, pltpu.SemaphoreType.DMA((8 * pieces,)), pltpu.SemaphoreType.DMA((4,)),
        ] + [dma] * 6,
        compiler_params=pltpu.CompilerParams(collective_id=0, has_side_effects=True, vmem_limit_bytes=48 * 2**20),
        name="gather_project",
    )(tokens, qkv_weight, norm_gain, norm_bias, proj_bias)


def tail_kernel(
    d_hbm, first_hbm, w_hbm, x_hbm, gmid_hbm, gain_ref, up_ref, out_ref, sums_ref, three_ref, hid_ref,
    token_ref, qkv_ref, up_grad_ref, out_grad_ref, gain_grad_ref, shift_grad_ref, bias_grad_ref, hid_grad_ref,
    d, first, w, x, gmid, turned, core_out, core_in, far_out, far_in, mine, cols, cols_in, line_out, line_in, total, heads_in, part, part_in, both, both_in, sums, up_in, out_in, out_sum, out_far,
    loads, core_send, core_recv, far_send, far_recv, y_send, y_recv, z_send, z_recv, q_send, q_recv, s_send, s_recv, b_send, b_recv, h_send, h_recv, o_send, o_recv, *, pieces,
):
    f32, bf16 = jnp.float32, jnp.bfloat16
    rows, width = x.shape
    own = width // 4
    size = rows // pieces
    thin = width // 8
    me, place = lax.axis_index("blk"), lax.axis_index("dp")
    core, near, line = lax.rem(me, 2), lax.rem(place, 2), place // 2
    twin, other, last = me + 1 - 2 * core, lax.rem(me + 2, 4), 3 - me
    mesh_ids = pl.DeviceIdType.MESH

    def remote(src, dst, sends, recvs, i, target):
        return pltpu.make_async_remote_copy(
            src_ref=src, dst_ref=dst, send_sem=sends.at[i], recv_sem=recvs.at[i], device_id=target, device_id_type=mesh_ids
        )

    def rows_of(block, i):
        return pl.ds(pl.multiple_of(block * rows + i * size, size), size)

    def piece(i):
        return pl.ds(i * size, size)

    barrier = pltpu.get_barrier_semaphore()
    for block in (twin, other, last):
        pl.semaphore_signal(barrier, inc=1, device_id={"blk": block}, device_id_type=mesh_ids)
    for k in range(1, 8):
        pl.semaphore_signal(barrier, inc=1, device_id={"dp": lax.rem(place + k, 8)}, device_id_type=mesh_ids)

    def block_rows(block):
        return pl.ds(pl.multiple_of(block * rows, rows), rows)

    fetch = [pltpu.make_async_copy(w_hbm, w, loads.at[0])]
    for i, block in enumerate((last, other, me, twin)):
        fetch.append(pltpu.make_async_copy(d_hbm.at[block_rows(block), :], d.at[block_rows(block), :], loads.at[1 + i]))
    for i, (src, dst) in enumerate(((first_hbm, first), (x_hbm, x), (gmid_hbm, gmid))):
        fetch.append(pltpu.make_async_copy(src, dst, loads.at[5 + i]))
    for copy in fetch[:3]:
        copy.start()

    def partial(block, i):
        return lax.dot_general(d[rows_of(block, i), :], w[...], NT, preferred_element_type=f32)

    def to_twin(kind, i):
        return remote(core_out.at[kind, piece(i), :], core_in.at[kind, piece(i), :], core_send, core_recv, kind * pieces + i, {"blk": twin})

    def to_other(i):
        return remote(far_out.at[piece(i), :], far_in.at[piece(i), :], far_send, far_recv, i, {"blk": other})

    def to_beside(k):
        return remote(cols.at[k, 1 - near], cols_in.at[k], y_send, y_recv, k, {"dp": place + 1 - 2 * near})

    def to_line(k):
        return remote(line_out.at[k], line_in.at[k], z_send, z_recv, k, {"dp": 2 * lax.rem(line + k, 4) + near})

    pl.semaphore_wait(barrier, 10)
    chip = me // 2
    weights = remote(up_ref.at[pl.ds(2 * (1 - chip), 2)], up_in, h_send, h_recv, 0, {"blk": other})
    weights.start()

    def out_to_line(k):
        ahead = lax.rem(line + k, 4)
        return remote(out_ref.at[ahead], out_in.at[k - 1], o_send, o_recv, k - 1, {"dp": 2 * ahead + near})

    out_to_other = remote(out_sum.at[1 - chip], out_far, h_send, h_recv, 1, {"blk": other})
    for k in range(1, 4):
        out_to_line(k).start()
    fetch[0].wait()
    fetch[1].wait()
    for copy in fetch[3:]:
        copy.start()
    for i in range(pieces):
        core_out[0, piece(i), :] = partial(last, i).astype(bf16)
        to_twin(0, i).start()
    fetch[2].wait()
    for i in range(pieces):
        got = partial(other, i)
        to_twin(0, i).wait_recv()
        far_out[piece(i), :] = (got + core_in[0, piece(i), :].astype(f32)).astype(bf16)
        to_other(i).start()
    fetch[3].wait()
    fetch[4].wait()
    for i in range(d.shape[0] // 256):
        turned[:, pl.ds(i * 256, 256)] = d[pl.ds(i * 256, 256), :].T
    fetch[5].wait()
    for k in (1, 2, 3, 0):
        where = pl.ds(pl.multiple_of(lax.rem(line + k, 4) * 2 * thin, 2 * thin), 2 * thin)
        got = jnp.dot(turned[...], first[:, where], preferred_element_type=f32).astype(bf16)
        cols[k, 0] = got[:, :thin]
        cols[k, 1] = got[:, thin:]
        to_beside(k).start()
    for i in range(pieces):
        core_out[1, piece(i), :] = partial(twin, i).astype(bf16)
        to_twin(1, i).start()
    for i in range(pieces):
        mine[piece(i), :] = partial(me, i)
    ones = jnp.ones((8, d.shape[0]), bf16)
    column = jnp.dot(ones, d[...], preferred_element_type=f32)
    part[...] = jnp.zeros_like(part)
    for k in range(8):
        lanes = pl.ds(k * thin, thin)
        for i, (ref, j) in ((1, (sums_ref, 0)), (2, (sums_ref, 1)), (3, (three_ref, 0)), (5, (sums_ref, 2)), (6, (sums_ref, 3)), (7, (three_ref, 1)), (10, (sums_ref, 4)), (11, (three_ref, 2))):
            part[k, pl.ds(i, 1), :] = ref[pl.ds(j, 1), lanes]
        tile = 4 * (k // 4) + 2 * (k % 2) + k // 2 % 2
        for i in range(4):
            part[tile, pl.ds(12 + i, 1), :] = hid_ref[k, :, pl.ds(i * thin, thin)]
    for h in range(2):
        part[2 * me + h, pl.ds(8, 1), :] = column[:1, h * thin : (h + 1) * thin]
        part[2 * me + h, pl.ds(9, 1), :] = column[:1, 2 * own + h * thin : 2 * own + (h + 1) * thin]
    fetch[6].wait()
    fetch[7].wait()
    sums[...] = jnp.zeros_like(sums)

    def tokens(i):
        at = piece(i)
        to_twin(1, i).wait_recv()
        n, r = _stats(x[at, :].astype(f32))
        got = mine[at, :] + core_in[1, at, :].astype(f32)
        to_other(i).wait_recv()
        y = got + far_in[at, :].astype(f32)
        token_ref[at, :] = (gmid[at, :] + _pull(n, r, y * _row(gain_ref, 0))).astype(bf16)
        sums[pl.ds(0, 8), :] += _fold(y * n)
        sums[pl.ds(8, 8), :] += _fold(y)

    for k in (1, 2, 3):
        to_beside(k).wait_recv()
        line_out[k] = (cols[k, near].astype(f32) + cols_in[k].astype(f32)).astype(bf16)
        to_line(k).start()
    for k in range(1, 4):
        out_to_line(k).wait_recv()
    got = out_ref[line].astype(f32)
    for k in range(3):
        got += out_in[k].astype(f32)
    out_sum[0] = got[:, : 2 * thin].astype(bf16)
    out_sum[1] = got[:, 2 * thin :].astype(bf16)
    out_to_other.start()
    weights.wait_recv()
    for i in range(2):
        up_grad_ref[:, pl.ds(i * 2 * own, 2 * own)] = up_ref[2 * chip + i].astype(f32) + up_in[i].astype(f32)
    for i in range(pieces - 1):
        tokens(i)
    to_beside(0).wait_recv()
    for k in (1, 2, 3):
        to_line(k).wait_recv()
    summed = cols[0, near].astype(f32) + cols_in[0].astype(f32)
    for k in (1, 2, 3):
        summed += line_in[k].astype(f32)
    total[...] = summed.astype(bf16).reshape(total.shape)
    def to_owner(third):
        chunk = 4 * third + me
        return remote(total.at[third], heads_in.at[lax.rem(chunk, 3)], q_send, q_recv, lax.rem(chunk, 3), {"blk": chunk // 3})

    for third in range(3):
        chunk = 4 * third + me

        @pl.when(chunk // 3 != me)
        def _(third=third):
            to_owner(third).start()

        @pl.when(chunk // 3 == me)
        def _(third=third, chunk=chunk):
            heads_in[lax.rem(chunk, 3)] = total[third]

    out_to_other.wait_recv()
    got = out_sum[chip].astype(f32) + out_far[...].astype(f32)
    for i in range(2):
        out_grad_ref[:, pl.ds(i * thin, thin)] = got[:, i * thin : (i + 1) * thin].T
    tokens(pieces - 1)
    for i in range(2):
        line_sum = jnp.sum(sums[pl.ds(8 * i, 8), :], 0, keepdims=True)
        for k in range(8):
            part[k, pl.ds(4 * i, 1), :] = line_sum[:, k * thin : (k + 1) * thin]

    def to_dp(k):
        target = lax.rem(place + k, 8)
        return remote(part.at[target], part_in.at[k], s_send, s_recv, k, {"dp": target})

    def to_blk(k):
        return remote(both, both_in.at[k], b_send, b_recv, k, {"blk": (twin, other, last)[k]})

    for k in range(1, 8):
        to_dp(k).start()
    for s in range(3):
        source = lax.rem(3 * me + s, 4)

        @pl.when(source != me)
        def _(s=s):
            remote(total.at[0], heads_in.at[s], q_send, q_recv, s, {"blk": twin}).wait_recv()

        qkv_ref[:, pl.ds(s * own, own)] = heads_in[s].astype(f32).T
    acc = part[place]
    for k in range(1, 8):
        to_dp(k).wait_recv()
        acc += part_in[k]
    both[...] = acc
    for k in range(3):
        to_blk(k).start()
    for k in range(3):
        to_blk(k).wait_recv()
        acc += both_in[k]
    gain_grad_ref[...] = acc[:4]
    shift_grad_ref[...] = acc[4:8]
    bias_grad_ref[...] = acc[8:12]
    hid_grad_ref[...] = acc[12:]
    for i in range(pieces):
        to_twin(0, i).wait_send()
        to_twin(1, i).wait_send()
        to_other(i).wait_send()
    for k in range(4):
        to_beside(k).wait_send()
    for k in range(1, 4):
        to_line(k).wait_send()
    for third in range(3):

        @pl.when((4 * third + me) // 3 != me)
        def _(third=third):
            to_owner(third).wait_send()

    for k in range(1, 8):
        to_dp(k).wait_send()
    for k in range(3):
        to_blk(k).wait_send()
    weights.wait_send()
    out_to_other.wait_send()
    for k in range(1, 4):
        out_to_line(k).wait_send()


def finish(grads, first_all, own_weight, tokens, grad_middle, norm_gain, up_sum, out_line, sums, sums_three, hidden_bias):
    rows, width = tokens.shape
    total_rows, cols = grads.shape
    own, thin, pieces = width // 4, width // 8, 4
    bf16, f32 = jnp.bfloat16, jnp.float32
    shape, vmem, hbm, dma = jax.ShapeDtypeStruct, pl.BlockSpec(memory_space=pltpu.VMEM), pl.BlockSpec(memory_space=pl.ANY), pltpu.SemaphoreType.DMA
    buffers = [
        ((total_rows, cols), bf16), ((total_rows, width), bf16), ((width, cols), bf16), ((rows, width), bf16), ((rows, width), f32),
        ((cols, total_rows), bf16), ((2, rows, width), bf16), ((2, rows, width), bf16), ((rows, width), bf16), ((rows, width), bf16),
        ((rows, width), f32), ((4, 2, cols, thin), bf16), ((4, cols, thin), bf16), ((4, cols, thin), bf16), ((4, cols, thin), bf16),
        ((3, own, thin), bf16), ((3, own, thin), bf16), ((8, 16, thin), f32), ((8, 16, thin), f32), ((16, thin), f32), ((3, 16, thin), f32),
        ((16, width), f32), ((2,) + up_sum.shape[1:], bf16), ((3,) + out_line.shape[1:], bf16), ((2, thin, own), bf16), ((thin, own), bf16),
    ]
    counts = [8, 2 * pieces, 2 * pieces, pieces, pieces, 4, 4, 4, 4, 3, 3, 8, 8, 3, 3, 2, 2, 3, 3]
    return pl.pallas_call(
        functools.partial(tail_kernel, pieces=pieces),
        in_specs=[hbm] * 5 + [vmem] * 6,
        out_specs=[vmem] * 8,
        out_shape=[shape((rows, width), bf16), shape((thin, 3 * own), f32), shape((thin, width), f32), shape((thin, own), f32)] + [shape((4, thin), f32)] * 4,
        scratch_shapes=[pltpu.VMEM(dims, kind) for dims, kind in buffers] + [dma((n,)) for n in counts],
        compiler_params=pltpu.CompilerParams(collective_id=2, has_side_effects=True, vmem_limit_bytes=58 * 2**20),
        cost_estimate=pl.CostEstimate(flops=60 * rows * width * width, bytes_accessed=2**27, transcendentals=0),
        name="finish",
    )(grads, first_all, own_weight, tokens, grad_middle, norm_gain, up_sum, out_line, sums, sums_three, hidden_bias)


def outer_sum(left, right):
    return lax.dot_general(left, right, (((0,), (0,)), ((), ())), preferred_element_type=jnp.float32)


def times_transposed(left, right):
    return lax.dot_general(left, right, NT, preferred_element_type=jnp.float32)


def column_sums(values):
    return jnp.sum(values.astype(jnp.float32), 0)


def exchange(values, axis, bit):
    return lax.ppermute(values, axis, [(i, i ^ bit) for i in range(lax.axis_size(axis))])


def plus(left, right):
    return (left.astype(jnp.float32) + right.astype(jnp.float32)).astype(jnp.bfloat16)


def pick(values, index, axis):
    return lax.dynamic_index_in_dim(values, index, axis, False)


def sum_everywhere(values):
    for axis in ("blk", "dp"):
        bit = 1
        while bit < lax.axis_size(axis):
            values = values + exchange(values, axis, bit)
            bit *= 2
    return values


def far_sum(half):
    line = lax.axis_index("dp") // 2
    parts = lax.axis_size("dp")
    if parts > 8:
        groups = [[d for d in range(parts) if d % 2 == b] for b in range(2)]
        return jnp.sum(lax.all_to_all(half, "dp", 0, 0, axis_index_groups=groups).astype(jnp.float32), 0)
    got = [exchange(pick(half, line ^ step, 0), "dp", 2 * step) for step in range(1, parts // 2)]
    return pick(half, line, 0).astype(jnp.float32) + sum(piece.astype(jnp.float32) for piece in got)


def far_sums(values):
    groups = [[d for d in range(lax.axis_size("dp")) if d % 2 == b] for b in range(2)]
    return lax.psum_scatter(values, "dp", scatter_dimension=0, axis_index_groups=groups, tiled=False)


def by_chip(up):
    return up.reshape((2, 2) + up.shape[1:]).transpose(0, 2, 1, 3).reshape(2, up.shape[1], -1)


def finish_plain(grads, first_all, own_weight, tokens, grad_middle, norm_gain, early, hidden_bias):
    rows, width = tokens.shape
    blocks, parts, me = lax.axis_size("blk"), lax.axis_size("dp"), lax.axis_index("blk")
    core, chip, own = me % 2, me // 2, width // blocks
    by_block = grads.reshape(2, 2, rows, 3 * own)
    away = times_transposed(pick(by_block, 1 - core, 1).reshape(2 * rows, 3 * own), own_weight).astype(jnp.bfloat16)
    got = exchange(away, "blk", 1)
    stay = times_transposed(pick(by_block, core, 1).reshape(2 * rows, 3 * own), own_weight)
    half = plus(stay, got).reshape(2, rows, width)
    half, grads = lax.optimization_barrier((half, grads))
    far = exchange(pick(half, 1 - chip, 0), "blk", 2)

    term = outer_sum(first_all, grads).astype(jnp.bfloat16).reshape(parts // 2, 2, width // parts, 3 * own)
    near = lax.rem(lax.axis_index("dp"), 2)
    term = plus(pick(term, near, 1), exchange(pick(term, 1 - near, 1), "dp", 1))
    qkv_term = far_sum(term).astype(jnp.bfloat16)
    qkv_blocks = lax.all_gather(qkv_term, "blk", axis=0)
    qkv_rows = qkv_blocks.reshape(blocks, -1, 3, own).transpose(1, 2, 0, 3).reshape(-1, 3 * width)
    qkv_grad = lax.dynamic_slice_in_dim(qkv_rows, me * 3 * own, 3 * own, 1).astype(jnp.float32)

    def spread(values):
        return lax.dynamic_update_slice_in_dim(jnp.zeros((width,), jnp.float32), values, me * own, 0)

    y = pick(half, chip, 0).astype(jnp.float32) + far.astype(jnp.float32)
    n, r = _stats(tokens.astype(jnp.float32))
    token_grad = (grad_middle + _pull(n, r, y * norm_gain[0])).astype(jnp.bfloat16)
    late = {0: jnp.sum(y * n, 0), 4: jnp.sum(y, 0), 8: spread(column_sums(grads[:, :own])), 9: spread(column_sums(grads[:, 2 * own :]))}
    small = jnp.stack([late.get(i, early[i]) for i in range(12)] + list(hidden_bias.reshape(-1, width)))
    small = sum_everywhere(small)
    place = lax.axis_index("dp")
    chunk = width // parts
    small_own = lax.dynamic_slice_in_dim(small[:12], place * chunk, chunk, 1)
    hidden = lax.dynamic_slice_in_dim(small[12:].reshape(-1), place * 4 * chunk, 4 * chunk, 0)
    return token_grad, qkv_grad, small_own, hidden


def local(tokens, cotangent, lengths, qkv_weight, out_weight, up_weight, down_weight, norm_gain, norm_bias, proj_bias, ffn_bias):
    rows, width = tokens.shape
    blocks = lax.axis_size("blk")
    parts = lax.axis_size("dp")
    me = lax.axis_index("blk")
    core, chip = me % 2, me // 2
    own = width // blocks

    first_all, qkv, own_weight = gather_project(tokens, qkv_weight, norm_gain, norm_bias, proj_bias)
    attended_own, log_total = attn_fwd(lengths, qkv)

    mixed, mid, n_one, r_one, low, turned, second_t, act, slope, sums_three, attended = ffn_forward(
        tokens, cotangent, attended_own, out_weight, up_weight, down_weight, norm_gain, norm_bias, proj_bias, ffn_bias
    )
    grad_middle, sums, hidden_bias, up_sum, down_sum, out_term, grad_own, out_line = ffn_backward(
        parts, low, turned, second_t, act, slope, up_weight, down_weight, mid, n_one, r_one, cotangent, attended, out_weight, norm_gain
    )
    grads = attn_bwd(lengths, qkv, grad_own, attended_own, log_total)

    if parts == 8:
        down_grad = lax.psum_scatter(down_sum, "dp", scatter_dimension=0, tiled=False).astype(jnp.float32).T
        token_grad, qkv_grad, up_grad, out_grad, gains, shifts, biases, hidden = finish(
            grads, first_all, own_weight, tokens, grad_middle, norm_gain, up_sum, out_line, sums, sums_three, hidden_bias
        )
        return (mixed, token_grad, qkv_grad, out_grad, up_grad, down_grad, gains, shifts, biases, hidden.reshape(-1))
    early = [None, sums[0], sums[1], sums_three[0], None, sums[2], sums[3], sums_three[1], None, None, sums[4], sums_three[2]]
    hidden_bias = hidden_bias.reshape(2, 2, 2, -1).transpose(0, 2, 1, 3)
    thin = width // parts
    halves = by_chip(far_sums(up_sum))
    up_grad = pick(halves, chip, 0).astype(jnp.float32) + exchange(pick(halves, 1 - chip, 0), "blk", 2).astype(jnp.float32)
    out_term = out_term.reshape(2, 2, width // 2, width // 2).transpose(1, 2, 0, 3).reshape(2, 2, own, width)
    out_half = plus(out_term[1], exchange(out_term[0], "blk", 1))
    out_sum = plus(pick(out_half, chip, 0), exchange(pick(out_half, 1 - chip, 0), "blk", 2))
    down = down_sum.transpose(1, 0, 2).reshape(own, parts, -1).transpose(1, 0, 2)
    out = out_sum.reshape(own, parts, thin).transpose(1, 0, 2)
    both = lax.psum_scatter(jnp.concatenate([down, out], 2), "dp", scatter_dimension=0, tiled=False).astype(jnp.float32)
    down_grad, out_grad = both[:, : down.shape[2]].T, both[:, down.shape[2] :].T
    token_grad, qkv_grad, small, hidden = finish_plain(grads, first_all, own_weight, tokens, grad_middle, norm_gain, early, hidden_bias)
    return (mixed, token_grad, qkv_grad, out_grad, up_grad, down_grad, small[:4], small[4:8], small[8:], hidden)


def solution(mesh):
    return jax.shard_map(
        local,
        mesh=mesh,
        in_specs=(P(("dp", "blk"), None), P(("dp", "blk"), None), P("dp", None)) + (P(),) * 8,
        out_specs=(P(("dp", "blk"), None), P(("dp", "blk"), None))
        + (P("dp", "blk"),) * 4
        + (P(None, "dp"),) * 3
        + (P("dp"),),
        check_vma=False,
    )
```

```python
import functools

import jax
import jax.numpy as jnp
from jax import lax
from jax.experimental import pallas as pl
from jax.experimental.pallas import tpu as pltpu
from jax.sharding import PartitionSpec as P

epsilon = 1e-05
HD = 64
NT = (((1,), (1,)), ((), ()))
NEG = -1e30
TILE = 256


def _bounds(len_ref, qb):
    l0 = len_ref[0, 0]
    e1 = l0 + len_ref[0, 1]

    def start_of(r):
        return jnp.where(r >= e1, e1, jnp.where(r >= l0, l0, 0))

    first = qb * TILE
    s_first, s_last = start_of(first), start_of(first + TILE - 1)
    kmin = s_first // TILE
    kmid = jnp.maximum(kmin, jnp.minimum(qb, (s_last + TILE - 1) // TILE))
    rows = first + lax.broadcasted_iota(jnp.int32, (1, TILE), 1)
    return kmin, kmid, rows, start_of(rows)


def _walk(len_ref, qb, step, carry, wide):
    kmin, kmid, rows, starts = _bounds(len_ref, qb)

    def masked(kb, carry):
        at = pl.multiple_of(kb * TILE, TILE)
        kpos = at + lax.broadcasted_iota(jnp.int32, (TILE, TILE), 0)
        return step(at, TILE, (kpos >= starts) & (kpos <= rows), carry)

    def plain(size):
        def run(kb, carry):
            return step(pl.multiple_of(kb * TILE, TILE), size * TILE, None, carry)

        return run

    carry = lax.fori_loop(kmin, kmid, masked, carry)
    at, left = kmid, qb - kmid
    for size in wide:
        count = left // size
        base = at
        carry = lax.fori_loop(0, count, lambda i, c, base=base, size=size: plain(size)(base + i * size, c), carry)
        at, left = at + count * size, left - count * size
    return masked(qb, carry)


def _fill_masked(dst, value, heads):
    lane = lax.broadcasted_iota(jnp.int32, value.shape, 1) // HD
    for h in range(heads):
        dst[pl.ds(h * TILE, TILE), :] = jnp.where(lane == h, value, jnp.zeros_like(value))


def fwd_kernel(len_ref, q_ref, k_ref, v_ref, o_ref, lse_ref, qm, acc, ps, vt, *, heads, wide):
    qb = pl.program_id(0)

    @pl.when(qb == 0)
    def _():
        vt[...] = v_ref[...].T

    _fill_masked(qm, q_ref[...] * jnp.bfloat16(0.125), heads)
    acc[...] = jnp.zeros_like(acc)

    def step(at, size, mask, carry):
        keys = pl.ds(at, size)
        scores = [
            lax.dot_general(k_ref[keys, :], qm[pl.ds(h * TILE, TILE), :], NT, preferred_element_type=jnp.float32)
            for h in range(heads)
        ]
        out, fades = [], []
        for h in range(heads):
            m, l = carry[h]
            s = scores[h]
            if mask is not None:
                s = jnp.where(mask, s, NEG)
            top = jnp.maximum(m, jnp.max(s, 0, keepdims=True))
            p = jnp.exp(s - top)
            if mask is not None:
                p = jnp.where(mask, p, 0.0)
            fade = jnp.exp(m - top)
            ps[pl.ds(0, size), pl.ds(h * TILE, TILE)] = p.astype(jnp.bfloat16)
            out.append((top, l * fade + jnp.sum(p, 0, keepdims=True)))
            fades.append(fade)
        for h in range(heads):
            lanes = pl.ds(h * HD, HD)
            part = jnp.dot(vt[lanes, keys], ps[pl.ds(0, size), pl.ds(h * TILE, TILE)], preferred_element_type=jnp.float32)
            acc[lanes, :] = acc[lanes, :] * fades[h] + part
        return tuple(out)

    carry = tuple((jnp.full((1, TILE), NEG, jnp.float32), jnp.zeros((1, TILE), jnp.float32)) for _ in range(heads))
    carry = _walk(len_ref, qb, step, carry, wide)
    for h in range(heads):
        m, l = carry[h]
        lse_ref[pl.ds(h, 1), :] = m + jnp.log(l)
        acc[pl.ds(h * HD, HD), :] = acc[pl.ds(h * HD, HD), :] / l
    o_ref[...] = acc[...].T.astype(jnp.bfloat16)


def attn_fwd(lengths, qkv, pair=0, lane=256, wide=(1,)):
    n = qkv.shape[0]
    heads = lane // HD
    return pl.pallas_call(
        functools.partial(fwd_kernel, heads=heads, wide=wide),
        grid_spec=pltpu.PrefetchScalarGridSpec(
            num_scalar_prefetch=1,
            grid=(n // TILE,),
            in_specs=[
                pl.BlockSpec((TILE, lane), lambda i, L: (i, 3 * pair)),
                pl.BlockSpec((n, lane), lambda i, L: (0, 3 * pair + 1)),
                pl.BlockSpec((n, lane), lambda i, L: (0, 3 * pair + 2)),
            ],
            out_specs=[pl.BlockSpec((TILE, lane), lambda i, L: (i, 0)), pl.BlockSpec((heads, TILE), lambda i, L: (0, i))],
            scratch_shapes=[
                pltpu.VMEM((heads * TILE, lane), jnp.bfloat16),
                pltpu.VMEM((lane, TILE), jnp.float32),
                pltpu.VMEM((wide[0] * TILE, heads * TILE), jnp.bfloat16),
                pltpu.VMEM((lane, n), jnp.bfloat16),
            ],
        ),
        out_shape=[jax.ShapeDtypeStruct((n, lane), jnp.bfloat16), jax.ShapeDtypeStruct((heads, n), jnp.float32)],
        compiler_params=pltpu.CompilerParams(vmem_limit_bytes=58 * 2**20),
        cost_estimate=pl.CostEstimate(flops=n * n * lane * 9, bytes_accessed=10 * n * lane, transcendentals=n * n * heads // 2),
        name="attn_fwd",
    )(lengths, qkv, qkv, qkv)


def bwd_kernel(len_ref, q_ref, do_ref, o_ref, lse_ref, k_ref, v_ref, d_ref, qm, dom, ps, ds, dqt, dk, dv, kt, *, heads, wide):
    qb = pl.program_id(0)
    c = heads * HD

    @pl.when(qb == 0)
    def _():
        dk[...] = jnp.zeros_like(dk)
        dv[...] = jnp.zeros_like(dv)
        kt[...] = k_ref[...].T

    _fill_masked(qm, q_ref[...] * jnp.bfloat16(0.125), heads)
    _fill_masked(dom, do_ref[...], heads)
    prod = (do_ref[...].astype(jnp.float32) * o_ref[...].astype(jnp.float32)).T
    delta = [jnp.sum(prod[h * HD : (h + 1) * HD], 0, keepdims=True) for h in range(heads)]
    dqt[...] = jnp.zeros_like(dqt)

    def step(at, size, mask, carry):
        keys = pl.ds(at, size)
        used = pl.ds(0, size)
        for h in range(heads):
            mine = pl.ds(h * TILE, TILE)
            s = lax.dot_general(k_ref[keys, :], qm[mine, :], NT, preferred_element_type=jnp.float32)
            p = jnp.exp(s - lse_ref[pl.ds(h, 1), :])
            if mask is not None:
                p = jnp.where(mask, p, 0.0)
            dp = lax.dot_general(v_ref[keys, :], dom[mine, :], NT, preferred_element_type=jnp.float32)
            ps[used, mine] = p.astype(jnp.bfloat16)
            ds[used, mine] = (p * (dp - delta[h])).astype(jnp.bfloat16)
        dv[keys, :] += jnp.dot(ps[used, :], dom[...], preferred_element_type=jnp.float32)
        dk[keys, :] += jnp.dot(ds[used, :], qm[...], preferred_element_type=jnp.float32)
        for h in range(heads):
            lanes = pl.ds(h * HD, HD)
            dqt[lanes, :] += jnp.dot(kt[lanes, keys], ds[used, pl.ds(h * TILE, TILE)], preferred_element_type=jnp.float32)
        return carry

    _walk(len_ref, qb, step, 0, wide)
    d_ref[pl.ds(pl.multiple_of(qb * TILE, TILE), TILE), pl.ds(0, c)] = (dqt[...] * 0.125).T.astype(jnp.bfloat16)

    @pl.when(qb == pl.num_programs(0) - 1)
    def _():
        d_ref[:, pl.ds(c, c)] = dk[...].astype(jnp.bfloat16)
        d_ref[:, pl.ds(2 * c, c)] = dv[...].astype(jnp.bfloat16)


def attn_bwd(lengths, qkv, do, o, lse, pair=0, lane=256, wide=(1,)):
    n = qkv.shape[0]
    heads = lane // HD
    row = lambda col: pl.BlockSpec((TILE, lane), lambda i, L: (i, col))
    whole = lambda col: pl.BlockSpec((n, lane), lambda i, L: (0, col))
    return pl.pallas_call(
        functools.partial(bwd_kernel, heads=heads, wide=wide),
        grid_spec=pltpu.PrefetchScalarGridSpec(
            num_scalar_prefetch=1,
            grid=(n // TILE,),
            in_specs=[
                row(3 * pair), row(pair), row(0), pl.BlockSpec((heads, TILE), lambda i, L: (0, i)),
                whole(3 * pair + 1), whole(3 * pair + 2),
            ],
            out_specs=pl.BlockSpec((n, 3 * lane), lambda i, L: (0, pair)),
            scratch_shapes=[
                pltpu.VMEM((heads * TILE, lane), jnp.bfloat16),
                pltpu.VMEM((heads * TILE, lane), jnp.bfloat16),
                pltpu.VMEM((wide[0] * TILE, heads * TILE), jnp.bfloat16),
                pltpu.VMEM((wide[0] * TILE, heads * TILE), jnp.bfloat16),
                pltpu.VMEM((lane, TILE), jnp.float32),
                pltpu.VMEM((n, lane), jnp.float32),
                pltpu.VMEM((n, lane), jnp.float32),
                pltpu.VMEM((lane, n), jnp.bfloat16),
            ],
        ),
        out_shape=jax.ShapeDtypeStruct(qkv.shape, jnp.bfloat16),
        compiler_params=pltpu.CompilerParams(vmem_limit_bytes=58 * 2**20),
        cost_estimate=pl.CostEstimate(flops=n * n * lane * 11, bytes_accessed=20 * n * lane, transcendentals=n * n * heads // 2),
        name="attn_bwd",
    )(lengths, qkv, do, o, lse, qkv, qkv)


def _stats(v):
    c = v - jnp.mean(v, -1, keepdims=True)
    r = lax.rsqrt(jnp.mean(c * c, -1, keepdims=True) + epsilon)
    return c * r, r


def _pull(n, r, e):
    return r * (e - jnp.mean(e, -1, keepdims=True) - n * jnp.mean(e * n, -1, keepdims=True))


def _fold(v):
    return jnp.sum(v.reshape(-1, 8, v.shape[-1]), 0)


def _row(ref, i):
    return ref[pl.ds(i, 1), :]


def _each(total, size, fn):
    def body(i, carry):
        fn(pl.ds(pl.multiple_of(i * size, size), size))
        return carry

    lax.fori_loop(0, total // size, body, 0)


def _turn_blocks(dst, value, core):
    own = dst.shape[0] // 4
    flipped = value.T
    for b in range(4):
        stays = 1 - lax.rem(core + b % 2, 2)
        dst[pl.ds(pl.multiple_of((2 * stays + b // 2) * own, own), own), :] = flipped[b * own : (b + 1) * own, :]


def ffn_kernel(
    x_hbm, cot_hbm, own_hbm, wo_hbm, up_ref, down_ref, gain_ref, shift_ref, bias_ref, fb_ref,
    mixed_ref, mid_out, n_out, r_ref, low_ref, turned_ref, second_out, act_ref, slope_ref, small_ref, att_out,
    x_ref, cot_ref, wo_ref, mid_ref, n_ref, second_t, att_ref, second, branch, ffn, sums, sends, recvs, own_sem, load_sems, save_sems, *, tiles, strip,
):
    s = pl.program_id(0)
    rows, width = x_ref.shape
    f32 = jnp.float32

    def loaded(i):
        return pltpu.make_async_copy((x_hbm, cot_hbm, wo_hbm)[i], (x_ref, cot_ref, wo_ref)[i], load_sems.at[i])

    def saved(i):
        pairs = ((mid_ref, mid_out), (n_ref, n_out), (second_t, second_out), (att_ref, att_out))
        return pltpu.make_async_copy(*pairs[i], save_sems.at[i])

    @pl.when(s == 0)
    def _():
        me = lax.axis_index("blk")
        own = width // 4
        peers = (me + 1 - 2 * lax.rem(me, 2), lax.rem(me + 2, 4), 3 - me)
        mesh_ids = pl.DeviceIdType.MESH
        barrier = pltpu.get_barrier_semaphore()
        for block in peers:
            pl.semaphore_signal(barrier, inc=1, device_id={"blk": block}, device_id_type=mesh_ids)
        pl.semaphore_wait(barrier, 3)

        def rows_of(block):
            return own_hbm.at[pl.ds(pl.multiple_of(block * rows, rows), rows), :]

        here = att_ref.at[:, pl.ds(pl.multiple_of(me * own, own), own)]
        copies = [
            pltpu.make_async_remote_copy(
                src_ref=rows_of(block), dst_ref=here, send_sem=sends.at[i], recv_sem=recvs.at[i],
                device_id={"blk": block}, device_id_type=mesh_ids,
            )
            for i, block in enumerate(peers)
        ]
        for copy in copies[::-1]:
            copy.start()
        mine = pltpu.make_async_copy(rows_of(me), here, own_sem)
        mine.start()
        for i in (2, 0, 1):
            loaded(i).start()
        sums[...] = jnp.zeros_like(sums)
        mine.wait()
        for i in range(3):
            loaded(i).wait()
        for copy in copies:
            copy.wait_send()
            copy.wait_recv()
        saved(3).start()
        branch[...] = jnp.dot(att_ref[...], wo_ref[...], preferred_element_type=f32) + _row(bias_ref, 2)

        def normed(at):
            n, r = _stats(branch[at, :])
            n_ref[at, :] = n.astype(jnp.bfloat16)
            r_ref[at, :] = r
            m = x_ref[at, :].astype(f32) + n * _row(gain_ref, 1) + _row(shift_ref, 1)
            mid_ref[at, :] = m
            n, _ = _stats(m)
            second[at, :] = (n * _row(gain_ref, 2) + _row(shift_ref, 2)).astype(jnp.bfloat16)

        _each(rows, strip, normed)
        second_t[...] = second[...].T
        for i in range(3):
            saved(i).start()

    u = jnp.dot(second[...], up_ref[...], preferred_element_type=f32) + fb_ref[...]
    c1, c3 = 0.7978845608028654, 0.7978845608028654 * 0.044715
    sq = u * u
    t = jnp.tanh(u * (c1 + c3 * sq))
    half = 0.5 + 0.5 * t
    a = (u * half).astype(jnp.bfloat16)
    act_ref[...] = a
    slope_ref[...] = (half + (0.5 * u) * (1.0 - t * t) * (c1 + 3.0 * c3 * sq)).astype(jnp.bfloat16)
    part = jnp.dot(a, down_ref[...], preferred_element_type=f32)

    @pl.when(s == 0)
    def _():
        ffn[...] = part + _row(bias_ref, 3)

    @pl.when(s > 0)
    def _():
        ffn[...] += part

    @pl.when(s == tiles - 1)
    def _():
        def normed(at):
            n, r = _stats(ffn[at, :])
            y = cot_ref[at, :].astype(f32)
            mixed_ref[at, :] = (mid_ref[at, :] + n * _row(gain_ref, 3) + _row(shift_ref, 3)).astype(jnp.bfloat16)
            g = _pull(n, r, y * _row(gain_ref, 3)).astype(jnp.bfloat16)
            low_ref[at, :] = g
            sums[pl.ds(0, 8), :] += _fold(y * n)
            sums[pl.ds(8, 8), :] += _fold(y)
            sums[pl.ds(16, 8), :] += _fold(g.astype(f32))

        _each(rows, strip, normed)
        _turn_blocks(turned_ref, low_ref[...], lax.rem(lax.axis_index("blk"), 2))
        for i in range(4):
            saved(i).wait()
        for i in range(3):
            small_ref[pl.ds(i, 1), :] = jnp.sum(sums[pl.ds(8 * i, 8), :], 0, keepdims=True)


def _once(*shape):
    return pl.BlockSpec(shape, lambda s: (0,) * len(shape), pipeline_mode=pl.Buffered(1))


def ffn_forward(tokens, cotangent, attended, out_weight, up_weight, down_weight, norm_gain, norm_bias, proj_bias, ffn_bias):
    rows, width = tokens.shape
    hidden = up_weight.shape[1]
    tiles = 8
    hid = hidden // tiles
    bf16, f32 = jnp.bfloat16, jnp.float32
    shape = jax.ShapeDtypeStruct
    return pl.pallas_call(
        functools.partial(ffn_kernel, tiles=tiles, strip=rows // 4),
        grid=(tiles,),
        in_specs=[
            *[pl.BlockSpec(memory_space=pl.ANY)] * 4,
            pl.BlockSpec((width, hid), lambda s: (0, s)), pl.BlockSpec((hid, width), lambda s: (s, 0)),
            _once(4, width), _once(4, width), _once(4, width), pl.BlockSpec((1, hid), lambda s: (0, s)),
        ],
        out_specs=[
            _once(rows, width), *[pl.BlockSpec(memory_space=pl.ANY)] * 2, _once(rows, 1), _once(rows, width),
            _once(width, rows), pl.BlockSpec(memory_space=pl.ANY),
            pl.BlockSpec((rows, hid), lambda s: (0, s)), pl.BlockSpec((rows, hid), lambda s: (0, s)), _once(8, width), pl.BlockSpec(memory_space=pl.ANY),
        ],
        out_shape=[
            shape((rows, width), bf16), shape((rows, width), f32), shape((rows, width), bf16), shape((rows, 1), f32),
            shape((rows, width), bf16), shape((width, rows), bf16), shape((width, rows), bf16),
            shape((rows, hidden), bf16), shape((rows, hidden), bf16), shape((8, width), f32), shape((rows, width), bf16),
        ],
        scratch_shapes=[
            pltpu.VMEM((rows, width), bf16), pltpu.VMEM((rows, width), bf16), pltpu.VMEM((width, width), bf16), pltpu.VMEM((rows, width), f32),
            pltpu.VMEM((rows, width), bf16), pltpu.VMEM((width, rows), bf16), pltpu.VMEM((rows, width), bf16),
            pltpu.VMEM((rows, width), bf16), pltpu.VMEM((rows, width), f32), pltpu.VMEM((rows, width), f32), pltpu.VMEM((24, width), f32), pltpu.SemaphoreType.DMA((3,)), pltpu.SemaphoreType.DMA((3,)), pltpu.SemaphoreType.DMA(()),
            pltpu.SemaphoreType.DMA((3,)), pltpu.SemaphoreType.DMA((4,)),
        ],
        compiler_params=pltpu.CompilerParams(collective_id=3, has_side_effects=True, vmem_limit_bytes=56 * 2**20),
        cost_estimate=pl.CostEstimate(flops=18 * rows * width * width, bytes_accessed=50 * 2**20, transcendentals=rows * hidden),
        name="ffn_forward",
    )(tokens, cotangent, attended, out_weight, up_weight, down_weight, norm_gain, norm_bias, proj_bias, ffn_bias.reshape(1, -1))


def grads_kernel(
    low_ref, turned_hbm, second_hbm, act_ref, slope_ref, up_ref, down_ref, mid_hbm, n_hbm, r_ref, cot_hbm, att_hbm, wo_hbm, gain_ref,
    gmid_ref, small_ref, hid_ref, up_out, down_out, out_out, gown_out, out_line,
    turned_ref, second_t, cot_ref, att_ref, wo_ref, pre, gs, low, turned, gatt, sums, up_buf, up_in, up_y, down_send, down_keep, down_in, down_x, up_z,
    up_core, up_core_in, up_far, up_far_in, down_core, down_core_in, down_far, down_far_in, up_done, down_done, own_sems, gatt_sends, gatt_recvs, line_sends, line_recvs, save_sems, *, tiles, strip, fold,
):
    s = pl.program_id(0)
    rows, width = low_ref.shape
    own = width // 4
    f32, bf16 = jnp.float32, jnp.bfloat16
    pair, side = s // 2, lax.rem(s, 2)
    me, place = lax.axis_index("blk"), lax.axis_index("dp")
    core, chip, near = lax.rem(me, 2), me // 2, lax.rem(place, 2)
    line = place // 2
    twin, other, beside = {"blk": me + 1 - 2 * core}, {"blk": lax.rem(me + 2, 4)}, {"dp": place + 1 - 2 * near}
    last = {"blk": 3 - me}
    half = tiles // 2
    mesh_ids = pl.DeviceIdType.MESH

    def remote(src, dst, sends, recvs, i, target):
        return pltpu.make_async_remote_copy(
            src_ref=src, dst_ref=dst, send_sem=sends.at[i], recv_sem=recvs.at[i], device_id=target, device_id_type=mesh_ids
        )

    def up_to_twin(p):
        return remote(up_buf.at[0], up_in.at[p], up_core, up_core_in, p, twin)

    def up_to_beside(p):
        return remote(up_in.at[p, :, 1 - near], up_y.at[p], up_far, up_far_in, p, beside)

    def down_to_twin(u, slot):
        return remote(down_send.at[slot], down_in.at[lax.rem(u, 4)], down_core, down_core_in, u, twin)

    def down_to_other(u):
        return remote(down_keep.at[u, 1 - chip], down_x.at[u], down_far, down_far_in, u, other)

    def up_result(p):
        if fold:
            return pltpu.make_async_copy(up_y.at[p, line], up_out.at[p], up_done.at[p])
        return pltpu.make_async_copy(up_y.at[p], up_out.at[:, p], up_done.at[p])

    def up_to_line(p, k):
        ahead = lax.rem(line + k, 4)
        return remote(up_y.at[p, ahead], up_z.at[k - 1, p], line_sends, line_recvs, 3 * p + k - 1, {"dp": 2 * ahead + near})

    def join_line(p):
        total = up_y[p, line].astype(f32)
        for k in range(1, 4):
            up_to_line(p, k).wait_recv()
            total += up_z[k - 1, p].astype(f32)
        up_y[p, line] = total.astype(bf16)
        up_result(p).start()

    def down_result(u):
        tile = 4 * (u // 4) + 2 * lax.rem(u, 2) + lax.rem(u // 2, 2)
        return pltpu.make_async_copy(down_x.at[u], down_out.at[tile], down_done.at[u])

    def saved(i):
        pairs = ((mid_hbm, gmid_ref), (n_hbm, low), (cot_hbm, cot_ref), (att_hbm, att_ref), (wo_hbm, wo_ref), (turned_hbm, turned_ref), (second_hbm, second_t))
        return pltpu.make_async_copy(*pairs[i], save_sems.at[i])

    def out_line_result():
        return pltpu.make_async_copy(up_y.at[half], out_line, own_sems.at[0])

    def out_result(i):
        return pltpu.make_async_copy(up_buf.at[i], out_out.at[i], own_sems.at[2 + i])

    def columns_to(i):
        target = (last, other, twin)[i]
        block = target["blk"]
        src = gatt.at[:, pl.ds(pl.multiple_of(block * own, own), own)]
        dst = gown_out.at[pl.ds(pl.multiple_of(me * rows, rows), rows), :]
        return remote(src, dst, gatt_sends, gatt_recvs, i, target)

    def columns_here():
        src = gatt.at[:, pl.ds(pl.multiple_of(me * own, own), own)]
        return pltpu.make_async_copy(src, gown_out.at[pl.ds(pl.multiple_of(me * rows, rows), rows), :], own_sems.at[4])

    def join_up(p):
        up_to_twin(p).wait_recv()
        up_in[p] = (up_in[p].astype(f32) + up_buf[1].astype(f32)).astype(bf16)
        up_to_beside(p).start()

    def join_far_up(p):
        up_to_beside(p).wait_recv()
        up_y[p] = (up_y[p].astype(f32) + up_in[p, :, near].astype(f32)).astype(bf16)
        if fold:
            for k in range(1, 4):
                up_to_line(p, k).start()
        else:
            up_result(p).start()

    def join_down(u):
        down_to_twin(u, 0).wait_recv()
        down_keep[u] = (down_keep[u].astype(f32) + down_in[lax.rem(u, 4)].astype(f32)).astype(bf16)
        down_to_other(u).start()

    def join_far_down(u):
        down_to_other(u).wait_recv()
        down_x[u] = (down_x[u].astype(f32) + down_keep[u, chip].astype(f32)).astype(bf16)
        down_result(u).start()

    @pl.when(s == 0)
    def _():
        barrier = pltpu.get_barrier_semaphore()
        for target in (twin, other, beside, last):
            pl.semaphore_signal(barrier, inc=1, device_id=target, device_id_type=mesh_ids)
        sums[...] = jnp.zeros_like(sums)
        for i in (5, 6, 0, 1, 2, 3, 4):
            saved(i).start()
        for i in range(1, 4 if fold else 1):
            ahead = lax.rem(line + i, 4)
            pl.semaphore_signal(barrier, inc=1, device_id={"dp": 2 * ahead + near}, device_id_type=mesh_ids)
        pl.semaphore_wait(barrier, 7 if fold else 4)

    @pl.when(s >= 3)
    def _():
        join_far_down(s - 3)

    @pl.when((s == 5) | (s == 7))
    def _():
        join_far_up((s - 5) // 2)

    g = lax.dot_general(low_ref[...], down_ref[...], NT, preferred_element_type=f32) * slope_ref[...].astype(f32)
    g = g.astype(bf16)
    pre[...] = g
    hid_ref[pl.ds(s, 1)] = jnp.sum(g.astype(f32), 0, keepdims=True)[None]
    part = lax.dot_general(g, up_ref[...], NT, preferred_element_type=f32)

    @pl.when(s == 0)
    def _():
        gs[...] = part

    @pl.when(s > 0)
    def _():
        gs[...] += part

    @pl.when(s == 0)
    def _():
        saved(5).wait()
        saved(6).wait()

    down_grad = jnp.dot(turned_ref[...], act_ref[...], preferred_element_type=f32).astype(bf16)

    @pl.when(s >= 2)
    def _():
        down_to_twin(s - 2, side).wait_send()

    down_send[side] = down_grad[: width // 2].reshape(2, own, -1)
    down_to_twin(s, side).start()
    down_keep[s] = down_grad[width // 2 :].reshape(2, own, -1)

    @pl.when(s > 0)
    def _():
        join_down(s - 1)

    @pl.when((side == 0) & (s > 0))
    def _():
        join_up(pair - 1)

    up_grad = jnp.dot(second_t[...], pre[...], preferred_element_type=f32).astype(bf16).reshape(up_buf.shape[1:])

    @pl.when(side == core)
    def _():
        up_buf[1] = up_grad

    @pl.when(side != core)
    def _():
        @pl.when(pair > 0)
        def _():
            up_to_twin(pair - 1).wait_send()

        up_buf[0] = up_grad
        up_to_twin(pair).start()

    @pl.when(s == tiles - 1)
    def _():
        def normed(at):
            n, r = _stats(gmid_ref[at, :])
            y = gs[at, :]
            gm = cot_ref[at, :].astype(f32) + _pull(n, r, y * _row(gain_ref, 2))
            gmid_ref[at, :] = gm
            sums[pl.ds(8, 8), :] += _fold(y * n)
            sums[pl.ds(24, 8), :] += _fold(y)
            n, r = low[at, :].astype(f32), r_ref[at, :]
            g = _pull(n, r, gm * _row(gain_ref, 1)).astype(bf16)
            low[at, :] = g
            sums[pl.ds(0, 8), :] += _fold(gm * n)
            sums[pl.ds(16, 8), :] += _fold(gm)
            sums[pl.ds(32, 8), :] += _fold(g.astype(f32))

        for i in range(5):
            saved(i).wait()
        _each(rows, strip, normed)
        join_down(tiles - 1)
        join_up(half - 1)
        gatt[...] = lax.dot_general(low[...], wo_ref[...], NT, preferred_element_type=f32).astype(bf16)
        for i in range(3):
            columns_to(i).start()
        columns_here().start()
        join_far_up(2)
        _turn_blocks(turned, low[...], core)
        grad = jnp.dot(turned[...], att_ref[...], preferred_element_type=f32).astype(bf16)
        up_to_twin(half - 1).wait_send()
        if fold:
            thin = width // 8
            for d in range(8):
                for b in range(8):
                    piece = grad[b * thin : (b + 1) * thin, d * thin : (d + 1) * thin]
                    up_buf[b // 4, d // 2, d % 2, :, pl.ds(b % 4 * thin, thin)] = piece
            up_to_twin(half).start()
        else:
            for i in range(2):
                up_buf[i] = grad[:, i * width // 2 : (i + 1) * width // 2].reshape(up_buf.shape[1:])
                out_result(i).start()
        for i in range(5):
            small_ref[pl.ds(i, 1), :] = jnp.sum(sums[pl.ds(8 * i, 8), :], 0, keepdims=True)
        if fold:
            join_up(half)
        join_far_up(3)
        for u in range(tiles - 3, tiles):
            join_far_down(u)
        if fold:
            for p in range(half):
                join_line(p)
            up_to_beside(half).wait_recv()
            up_y[half] = (up_y[half].astype(f32) + up_in[half, :, near].astype(f32)).astype(bf16)
            out_line_result().start()
            out_line_result().wait()
        down_to_twin(tiles - 2, 0).wait_send()
        down_to_twin(tiles - 1, 1).wait_send()
        if fold:
            up_to_twin(half).wait_send()
        else:
            out_result(0).wait()
            out_result(1).wait()
        for p in range(half + fold):
            up_to_beside(p).wait_send()
        for p in range(half):
            up_result(p).wait()
            for i in range(1, 4 if fold else 1):
                up_to_line(p, i).wait_send()
        for u in range(tiles):
            down_to_other(u).wait_send()
            down_result(u).wait()
        for i in range(3):
            columns_to(i).wait_send()
            columns_to(i).wait_recv()
        columns_here().wait()


def ffn_backward(parts, low, turned, second_t, act, slope, up_weight, down_weight, mid, n_one, r_one, cotangent, attended, out_weight, norm_gain):
    rows, width = low.shape
    hidden = up_weight.shape[1]
    tiles, own = 8, width // 4
    hid = hidden // tiles
    bf16, f32 = jnp.bfloat16, jnp.float32
    shape = jax.ShapeDtypeStruct
    tile_of = lambda s: 4 * (s // 4) + 2 * lax.rem(s, 2) + lax.rem(s // 2, 2)
    thin = (parts // 2, 2, width // parts, hid)
    dma = pltpu.SemaphoreType.DMA
    half = tiles // 2
    fold = int(parts == 8)
    return pl.pallas_call(
        functools.partial(grads_kernel, tiles=tiles, strip=rows // 4, fold=fold),
        grid=(tiles,),
        in_specs=[
            _once(rows, width), pl.BlockSpec(memory_space=pl.ANY), pl.BlockSpec(memory_space=pl.ANY),
            pl.BlockSpec((rows, hid), lambda s: (0, tile_of(s))), pl.BlockSpec((rows, hid), lambda s: (0, tile_of(s))),
            pl.BlockSpec((width, hid), lambda s: (0, tile_of(s))), pl.BlockSpec((hid, width), lambda s: (tile_of(s), 0)),
            pl.BlockSpec(memory_space=pl.ANY), pl.BlockSpec(memory_space=pl.ANY), _once(rows, 1), *[pl.BlockSpec(memory_space=pl.ANY)] * 3, _once(4, width),
        ],
        out_specs=[
            _once(rows, width), _once(8, width), _once(tiles, 1, hid),
            *[pl.BlockSpec(memory_space=pl.ANY)] * 5,
        ],
        out_shape=[
            shape((rows, width), f32),
            shape((8, width), f32), shape((tiles, 1, hid), f32),
            shape((half, width // parts, hid) if fold else (parts // 2, half, width // parts, hid), bf16), shape((tiles, own, hid), bf16), shape((2,) + thin, bf16),
            shape((4 * rows, own), bf16), shape((parts // 2, width // parts, hid), bf16),
        ],
        scratch_shapes=[
            pltpu.VMEM((width, rows), bf16), pltpu.VMEM((width, rows), bf16), pltpu.VMEM((rows, width), bf16), pltpu.VMEM((rows, width), bf16),
            pltpu.VMEM((width, width), bf16), pltpu.VMEM((rows, hid), bf16), pltpu.VMEM((rows, width), f32), pltpu.VMEM((rows, width), bf16), pltpu.VMEM((width, rows), bf16), pltpu.VMEM((rows, width), bf16),
            pltpu.VMEM((40, width), f32),
            pltpu.VMEM((2,) + thin, bf16), pltpu.VMEM((half + fold,) + thin, bf16), pltpu.VMEM((half + fold, parts // 2, width // parts, hid), bf16),
            pltpu.VMEM((2, 2, own, hid), bf16), pltpu.VMEM((tiles, 2, own, hid), bf16), pltpu.VMEM((4, 2, own, hid), bf16),
            pltpu.VMEM((tiles, own, hid), bf16), pltpu.VMEM((3, half, width // parts, hid), bf16),
            *[dma((half + fold,))] * 4, *[dma((tiles,))] * 4, dma((half + fold,)), dma((tiles,)), dma((5,)), dma((3,)), dma((3,)), dma((3 * half,)), dma((3 * half,)), dma((7,)),
        ],
        compiler_params=pltpu.CompilerParams(collective_id=1, has_side_effects=True, vmem_limit_bytes=60 * 2**20),
        name="ffn_backward",
    )(low, turned, second_t, act, slope, up_weight, down_weight, mid, n_one, r_one, cotangent, attended, out_weight, norm_gain)


def project_kernel(
    x_hbm, w_hbm, gain_ref, shift_ref, bias_ref, all_out, qkv_out, w_out, x_ref, all_ref, qkv_ref, w_ref, x_sems, out_sems, w_sems, chip_send, chip_recv, core_send, core_recv, pass_send, pass_recv, *, pieces,
):
    me = lax.axis_index("blk")
    core = lax.rem(me, 2)
    twin, other, last = me + 1 - 2 * core, lax.rem(me + 2, 4), 3 - me
    rows, width = x_ref.shape
    own = width // 4
    size = rows // pieces
    fetch = [pltpu.make_async_copy(x_hbm.at[pl.ds(i * size, size), :], x_ref.at[pl.ds(i * size, size), :], x_sems.at[i]) for i in range(pieces)]
    for copy in fetch:
        copy.start()
    barrier = pltpu.get_barrier_semaphore()
    for target in (twin, other):
        pl.semaphore_signal(barrier, inc=1, device_id={"blk": target}, device_id_type=pl.DeviceIdType.MESH)
    loads = []
    for third in range(3):
        columns = pl.ds(pl.multiple_of(third * width + me * own, own), own)
        load = pltpu.make_async_copy(w_hbm.at[:, columns], w_ref.at[:, pl.ds(third * own, own)], w_sems.at[third])
        load.start()
        loads.append(load)

    def at(block, i):
        return pl.ds(pl.multiple_of(block * rows + i * size, size), size)

    def send(block, i, target, sends, recvs):
        piece = all_ref.at[at(block, i), :]
        copy = pltpu.make_async_remote_copy(
            src_ref=piece, dst_ref=piece, send_sem=sends.at[i], recv_sem=recvs.at[i],
            device_id={"blk": target}, device_id_type=pl.DeviceIdType.MESH,
        )
        return copy

    def project(block, i):
        where = at(block, i)
        got = jnp.dot(all_ref[where, :], w_ref[...], preferred_element_type=jnp.float32)
        for third in range(3):
            part = got[:, third * own : (third + 1) * own]
            if third != 1:
                part = part + bias_ref[pl.ds(third // 2, 1), pl.ds(pl.multiple_of(me * own, own), own)]
            qkv_ref[where, pl.ds(third * own, own)] = part.astype(jnp.bfloat16)
        for src, dst in ((all_ref, all_out), (qkv_ref, qkv_out)):
            copy = pltpu.make_async_copy(src.at[where, :], dst.at[where, :], out_sems.at[len(saved)])
            copy.start()
            saved.append(copy)

    sent, saved = [], []
    for i in range(pieces):
        fetch[i].wait()
        n, _ = _stats(x_ref[pl.ds(i * size, size), :].astype(jnp.float32))
        all_ref[at(me, i), :] = (n * gain_ref[pl.ds(0, 1), :] + shift_ref[pl.ds(0, 1), :]).astype(jnp.bfloat16)
        if i == 0:
            pl.semaphore_wait(barrier, 2)
        for target, sends, recvs in ((other, chip_send, chip_recv), (twin, core_send, core_recv)):
            copy = send(me, i, target, sends, recvs)
            copy.start()
            sent.append(copy)
    for load in loads:
        load.wait()
    keep = pltpu.make_async_copy(w_ref, w_out, w_sems.at[3])
    keep.start()
    for i in range(pieces):
        project(me, i)
    for i in range(pieces):
        send(twin, i, twin, core_send, core_recv).wait_recv()
        project(twin, i)
    for i in range(pieces):
        send(other, i, other, chip_send, chip_recv).wait_recv()
        copy = send(other, i, twin, pass_send, pass_recv)
        copy.start()
        sent.append(copy)
        project(other, i)
        if i > 0:
            send(last, i - 1, twin, pass_send, pass_recv).wait_recv()
            project(last, i - 1)
    send(last, pieces - 1, twin, pass_send, pass_recv).wait_recv()
    project(last, pieces - 1)
    for copy in sent:
        copy.wait_send()
    for copy in saved:
        copy.wait()
    keep.wait()


def gather_project(tokens, qkv_weight, norm_gain, norm_bias, proj_bias):
    rows, width = tokens.shape
    pieces = 4
    vmem, hbm = pl.BlockSpec(memory_space=pltpu.VMEM), pl.BlockSpec(memory_space=pl.ANY)
    dma = pltpu.SemaphoreType.DMA((pieces,))
    return pl.pallas_call(
        functools.partial(project_kernel, pieces=pieces),
        in_specs=[hbm, hbm, vmem, vmem, vmem],
        out_specs=[hbm] * 3,
        out_shape=[jax.ShapeDtypeStruct((4 * rows, width), jnp.bfloat16), jax.ShapeDtypeStruct((4 * rows, 3 * width // 4), jnp.bfloat16), jax.ShapeDtypeStruct((width, 3 * width // 4), jnp.bfloat16)],
        scratch_shapes=[
            pltpu.VMEM((rows, width), jnp.bfloat16), pltpu.VMEM((4 * rows, width), jnp.bfloat16),
            pltpu.VMEM((4 * rows, 3 * width // 4), jnp.bfloat16), pltpu.VMEM((width, 3 * width // 4), jnp.bfloat16),
            dma, pltpu.SemaphoreType.DMA((8 * pieces,)), pltpu.SemaphoreType.DMA((4,)),
        ] + [dma] * 6,
        compiler_params=pltpu.CompilerParams(collective_id=0, has_side_effects=True, vmem_limit_bytes=60 * 2**20),
        name="gather_project",
    )(tokens, qkv_weight, norm_gain, norm_bias, proj_bias)


def tail_kernel(
    d_hbm, first_hbm, w_hbm, x_hbm, gmid_hbm, gain_ref, up_ref, out_ref, sums_ref, three_ref, hid_ref,
    token_ref, qkv_ref, up_grad_ref, out_grad_ref, gain_grad_ref, shift_grad_ref, bias_grad_ref, hid_grad_ref,
    d, first, w, x, gmid, turned, core_out, core_in, far_out, far_in, mine, cols, cols_in, line_out, line_in, total, heads_in, part, part_in, both, both_in, sums, up_in, out_in, out_sum, out_far,
    loads, core_send, core_recv, far_send, far_recv, y_send, y_recv, z_send, z_recv, q_send, q_recv, s_send, s_recv, b_send, b_recv, h_send, h_recv, o_send, o_recv, *, pieces,
):
    f32, bf16 = jnp.float32, jnp.bfloat16
    rows, width = x.shape
    own = width // 4
    size = rows // pieces
    thin = width // 8
    me, place = lax.axis_index("blk"), lax.axis_index("dp")
    core, near, line = lax.rem(me, 2), lax.rem(place, 2), place // 2
    twin, other, last = me + 1 - 2 * core, lax.rem(me + 2, 4), 3 - me
    mesh_ids = pl.DeviceIdType.MESH

    def remote(src, dst, sends, recvs, i, target):
        return pltpu.make_async_remote_copy(
            src_ref=src, dst_ref=dst, send_sem=sends.at[i], recv_sem=recvs.at[i], device_id=target, device_id_type=mesh_ids
        )

    def rows_of(block, i):
        return pl.ds(pl.multiple_of(block * rows + i * size, size), size)

    def piece(i):
        return pl.ds(i * size, size)

    barrier = pltpu.get_barrier_semaphore()
    for block in (twin, other, last):
        pl.semaphore_signal(barrier, inc=1, device_id={"blk": block}, device_id_type=mesh_ids)
    for k in range(1, 8):
        pl.semaphore_signal(barrier, inc=1, device_id={"dp": lax.rem(place + k, 8)}, device_id_type=mesh_ids)

    def block_rows(block):
        return pl.ds(pl.multiple_of(block * rows, rows), rows)

    fetch = [pltpu.make_async_copy(w_hbm, w, loads.at[0])]
    for i, block in enumerate((last, other, me, twin)):
        fetch.append(pltpu.make_async_copy(d_hbm.at[block_rows(block), :], d.at[block_rows(block), :], loads.at[1 + i]))
    for i, (src, dst) in enumerate(((first_hbm, first), (x_hbm, x), (gmid_hbm, gmid))):
        fetch.append(pltpu.make_async_copy(src, dst, loads.at[5 + i]))
    for copy in fetch[:3]:
        copy.start()

    def partial(block, i):
        return lax.dot_general(d[rows_of(block, i), :], w[...], NT, preferred_element_type=f32)

    def to_twin(kind, i):
        return remote(core_out.at[kind, piece(i), :], core_in.at[kind, piece(i), :], core_send, core_recv, kind * pieces + i, {"blk": twin})

    def to_other(i):
        return remote(far_out.at[piece(i), :], far_in.at[piece(i), :], far_send, far_recv, i, {"blk": other})

    def to_beside(k):
        return remote(cols.at[k, 1 - near], cols_in.at[k], y_send, y_recv, k, {"dp": place + 1 - 2 * near})

    def to_line(k):
        return remote(line_out.at[k], line_in.at[k], z_send, z_recv, k, {"dp": 2 * lax.rem(line + k, 4) + near})

    pl.semaphore_wait(barrier, 10)
    chip = me // 2
    weights = remote(up_ref.at[pl.ds(2 * (1 - chip), 2)], up_in, h_send, h_recv, 0, {"blk": other})
    weights.start()

    def out_to_line(k):
        ahead = lax.rem(line + k, 4)
        return remote(out_ref.at[ahead], out_in.at[k - 1], o_send, o_recv, k - 1, {"dp": 2 * ahead + near})

    out_to_other = remote(out_sum.at[1 - chip], out_far, h_send, h_recv, 1, {"blk": other})
    for k in range(1, 4):
        out_to_line(k).start()
    fetch[0].wait()
    fetch[1].wait()
    for copy in fetch[3:]:
        copy.start()
    for i in range(pieces):
        core_out[0, piece(i), :] = partial(last, i).astype(bf16)
        to_twin(0, i).start()
    fetch[2].wait()
    for i in range(pieces):
        got = partial(other, i)
        to_twin(0, i).wait_recv()
        far_out[piece(i), :] = (got + core_in[0, piece(i), :].astype(f32)).astype(bf16)
        to_other(i).start()
    fetch[3].wait()
    fetch[4].wait()
    for i in range(d.shape[0] // 256):
        turned[:, pl.ds(i * 256, 256)] = d[pl.ds(i * 256, 256), :].T
    fetch[5].wait()
    for k in (1, 2, 3, 0):
        where = pl.ds(pl.multiple_of(lax.rem(line + k, 4) * 2 * thin, 2 * thin), 2 * thin)
        got = jnp.dot(turned[...], first[:, where], preferred_element_type=f32).astype(bf16)
        cols[k, 0] = got[:, :thin]
        cols[k, 1] = got[:, thin:]
        to_beside(k).start()
    for i in range(pieces):
        core_out[1, piece(i), :] = partial(twin, i).astype(bf16)
        to_twin(1, i).start()
    for i in range(pieces):
        mine[piece(i), :] = partial(me, i)
    ones = jnp.ones((8, d.shape[0]), bf16)
    column = jnp.dot(ones, d[...], preferred_element_type=f32)
    part[...] = jnp.zeros_like(part)
    for k in range(8):
        lanes = pl.ds(k * thin, thin)
        for i, (ref, j) in ((1, (sums_ref, 0)), (2, (sums_ref, 1)), (3, (three_ref, 0)), (5, (sums_ref, 2)), (6, (sums_ref, 3)), (7, (three_ref, 1)), (10, (sums_ref, 4)), (11, (three_ref, 2))):
            part[k, pl.ds(i, 1), :] = ref[pl.ds(j, 1), lanes]
        tile = 4 * (k // 4) + 2 * (k % 2) + k // 2 % 2
        for i in range(4):
            part[tile, pl.ds(12 + i, 1), :] = hid_ref[k, :, pl.ds(i * thin, thin)]
    for h in range(2):
        part[2 * me + h, pl.ds(8, 1), :] = column[:1, h * thin : (h + 1) * thin]
        part[2 * me + h, pl.ds(9, 1), :] = column[:1, 2 * own + h * thin : 2 * own + (h + 1) * thin]
    fetch[6].wait()
    fetch[7].wait()
    sums[...] = jnp.zeros_like(sums)

    def tokens(i):
        at = piece(i)
        to_twin(1, i).wait_recv()
        n, r = _stats(x[at, :].astype(f32))
        got = mine[at, :] + core_in[1, at, :].astype(f32)
        to_other(i).wait_recv()
        y = got + far_in[at, :].astype(f32)
        token_ref[at, :] = (gmid[at, :] + _pull(n, r, y * _row(gain_ref, 0))).astype(bf16)
        sums[pl.ds(0, 8), :] += _fold(y * n)
        sums[pl.ds(8, 8), :] += _fold(y)

    for k in (1, 2, 3):
        to_beside(k).wait_recv()
        line_out[k] = (cols[k, near].astype(f32) + cols_in[k].astype(f32)).astype(bf16)
        to_line(k).start()
    for k in range(1, 4):
        out_to_line(k).wait_recv()
    got = out_ref[line].astype(f32)
    for k in range(3):
        got += out_in[k].astype(f32)
    out_sum[0] = got[:, : 2 * thin].astype(bf16)
    out_sum[1] = got[:, 2 * thin :].astype(bf16)
    out_to_other.start()
    weights.wait_recv()
    for i in range(2):
        up_grad_ref[:, pl.ds(i * 2 * own, 2 * own)] = up_ref[2 * chip + i].astype(f32) + up_in[i].astype(f32)
    for i in range(pieces - 1):
        tokens(i)
    to_beside(0).wait_recv()
    for k in (1, 2, 3):
        to_line(k).wait_recv()
    summed = cols[0, near].astype(f32) + cols_in[0].astype(f32)
    for k in (1, 2, 3):
        summed += line_in[k].astype(f32)
    total[...] = summed.astype(bf16).reshape(total.shape)
    def to_owner(third):
        chunk = 4 * third + me
        return remote(total.at[third], heads_in.at[lax.rem(chunk, 3)], q_send, q_recv, lax.rem(chunk, 3), {"blk": chunk // 3})

    for third in range(3):
        chunk = 4 * third + me

        @pl.when(chunk // 3 != me)
        def _(third=third):
            to_owner(third).start()

        @pl.when(chunk // 3 == me)
        def _(third=third, chunk=chunk):
            heads_in[lax.rem(chunk, 3)] = total[third]

    out_to_other.wait_recv()
    got = out_sum[chip].astype(f32) + out_far[...].astype(f32)
    for i in range(2):
        out_grad_ref[:, pl.ds(i * thin, thin)] = got[:, i * thin : (i + 1) * thin].T
    tokens(pieces - 1)
    for i in range(2):
        line_sum = jnp.sum(sums[pl.ds(8 * i, 8), :], 0, keepdims=True)
        for k in range(8):
            part[k, pl.ds(4 * i, 1), :] = line_sum[:, k * thin : (k + 1) * thin]

    def to_dp(k):
        target = lax.rem(place + k, 8)
        return remote(part.at[target], part_in.at[k], s_send, s_recv, k, {"dp": target})

    def to_blk(k):
        return remote(both, both_in.at[k], b_send, b_recv, k, {"blk": (twin, other, last)[k]})

    for k in range(1, 8):
        to_dp(k).start()
    for s in range(3):
        source = lax.rem(3 * me + s, 4)

        @pl.when(source != me)
        def _(s=s):
            remote(total.at[0], heads_in.at[s], q_send, q_recv, s, {"blk": twin}).wait_recv()

        qkv_ref[:, pl.ds(s * own, own)] = heads_in[s].astype(f32).T
    acc = part[place]
    for k in range(1, 8):
        to_dp(k).wait_recv()
        acc += part_in[k]
    both[...] = acc
    for k in range(3):
        to_blk(k).start()
    for k in range(3):
        to_blk(k).wait_recv()
        acc += both_in[k]
    gain_grad_ref[...] = acc[:4]
    shift_grad_ref[...] = acc[4:8]
    bias_grad_ref[...] = acc[8:12]
    hid_grad_ref[...] = acc[12:]
    for i in range(pieces):
        to_twin(0, i).wait_send()
        to_twin(1, i).wait_send()
        to_other(i).wait_send()
    for k in range(4):
        to_beside(k).wait_send()
    for k in range(1, 4):
        to_line(k).wait_send()
    for third in range(3):

        @pl.when((4 * third + me) // 3 != me)
        def _(third=third):
            to_owner(third).wait_send()

    for k in range(1, 8):
        to_dp(k).wait_send()
    for k in range(3):
        to_blk(k).wait_send()
    weights.wait_send()
    out_to_other.wait_send()
    for k in range(1, 4):
        out_to_line(k).wait_send()


def finish(grads, first_all, own_weight, tokens, grad_middle, norm_gain, up_sum, out_line, sums, sums_three, hidden_bias):
    rows, width = tokens.shape
    total_rows, cols = grads.shape
    own, thin, pieces = width // 4, width // 8, 4
    bf16, f32 = jnp.bfloat16, jnp.float32
    shape, vmem, hbm, dma = jax.ShapeDtypeStruct, pl.BlockSpec(memory_space=pltpu.VMEM), pl.BlockSpec(memory_space=pl.ANY), pltpu.SemaphoreType.DMA
    buffers = [
        ((total_rows, cols), bf16), ((total_rows, width), bf16), ((width, cols), bf16), ((rows, width), bf16), ((rows, width), f32),
        ((cols, total_rows), bf16), ((2, rows, width), bf16), ((2, rows, width), bf16), ((rows, width), bf16), ((rows, width), bf16),
        ((rows, width), f32), ((4, 2, cols, thin), bf16), ((4, cols, thin), bf16), ((4, cols, thin), bf16), ((4, cols, thin), bf16),
        ((3, own, thin), bf16), ((3, own, thin), bf16), ((8, 16, thin), f32), ((8, 16, thin), f32), ((16, thin), f32), ((3, 16, thin), f32),
        ((16, width), f32), ((2,) + up_sum.shape[1:], bf16), ((3,) + out_line.shape[1:], bf16), ((2, thin, own), bf16), ((thin, own), bf16),
    ]
    counts = [8, 2 * pieces, 2 * pieces, pieces, pieces, 4, 4, 4, 4, 3, 3, 8, 8, 3, 3, 2, 2, 3, 3]
    return pl.pallas_call(
        functools.partial(tail_kernel, pieces=pieces),
        in_specs=[hbm] * 5 + [vmem] * 6,
        out_specs=[vmem] * 8,
        out_shape=[shape((rows, width), bf16), shape((thin, 3 * own), f32), shape((thin, width), f32), shape((thin, own), f32)] + [shape((4, thin), f32)] * 4,
        scratch_shapes=[pltpu.VMEM(dims, kind) for dims, kind in buffers] + [dma((n,)) for n in counts],
        compiler_params=pltpu.CompilerParams(collective_id=2, has_side_effects=True, vmem_limit_bytes=58 * 2**20),
        cost_estimate=pl.CostEstimate(flops=60 * rows * width * width, bytes_accessed=2**27, transcendentals=0),
        name="finish",
    )(grads, first_all, own_weight, tokens, grad_middle, norm_gain, up_sum, out_line, sums, sums_three, hidden_bias)


def emit_kernel(token_in, qkv_in, up_in, out_in, down_in, gain_in, shift_in, bias_in, hid_in, token_ref, qkv_ref, up_ref, out_ref, down_ref, gain_ref, shift_ref, bias_ref, hid_ref):
    for src, dst in (
        (token_in, token_ref), (qkv_in, qkv_ref), (up_in, up_ref), (out_in, out_ref),
        (gain_in, gain_ref), (shift_in, shift_ref), (bias_in, bias_ref), (hid_in, hid_ref),
    ):
        dst[...] = src[...]
    down_ref[...] = down_in[...].astype(jnp.float32).T


def emit(token_grad, qkv_grad, up_grad, out_grad, down_grad, gains, shifts, biases, hidden):
    arrays = (token_grad, qkv_grad, up_grad, out_grad, down_grad, gains, shifts, biases, hidden)
    shapes = [jax.ShapeDtypeStruct(a.shape, a.dtype) for a in arrays]
    shapes[4] = jax.ShapeDtypeStruct(down_grad.shape[::-1], jnp.float32)
    return pl.pallas_call(
        emit_kernel,
        in_specs=[pl.BlockSpec(memory_space=pltpu.VMEM)] * 9,
        out_specs=[pl.BlockSpec(memory_space=pltpu.VMEM)] * 9,
        out_shape=shapes,
        compiler_params=pltpu.CompilerParams(vmem_limit_bytes=60 * 2**20),
        name="emit",
    )(*arrays)


def outer_sum(left, right):
    return lax.dot_general(left, right, (((0,), (0,)), ((), ())), preferred_element_type=jnp.float32)


def times_transposed(left, right):
    return lax.dot_general(left, right, NT, preferred_element_type=jnp.float32)


def column_sums(values):
    return jnp.sum(values.astype(jnp.float32), 0)


def exchange(values, axis, bit):
    return lax.ppermute(values, axis, [(i, i ^ bit) for i in range(lax.axis_size(axis))])


def plus(left, right):
    return (left.astype(jnp.float32) + right.astype(jnp.float32)).astype(jnp.bfloat16)


def pick(values, index, axis):
    return lax.dynamic_index_in_dim(values, index, axis, False)


def sum_everywhere(values):
    for axis in ("blk", "dp"):
        bit = 1
        while bit < lax.axis_size(axis):
            values = values + exchange(values, axis, bit)
            bit *= 2
    return values


def far_sum(half):
    line = lax.axis_index("dp") // 2
    parts = lax.axis_size("dp")
    if parts > 8:
        groups = [[d for d in range(parts) if d % 2 == b] for b in range(2)]
        return jnp.sum(lax.all_to_all(half, "dp", 0, 0, axis_index_groups=groups).astype(jnp.float32), 0)
    got = [exchange(pick(half, line ^ step, 0), "dp", 2 * step) for step in range(1, parts // 2)]
    return pick(half, line, 0).astype(jnp.float32) + sum(piece.astype(jnp.float32) for piece in got)


def far_sums(values):
    groups = [[d for d in range(lax.axis_size("dp")) if d % 2 == b] for b in range(2)]
    return lax.psum_scatter(values, "dp", scatter_dimension=0, axis_index_groups=groups, tiled=False)


def by_chip(up):
    return up.reshape((2, 2) + up.shape[1:]).transpose(0, 2, 1, 3).reshape(2, up.shape[1], -1)


def finish_plain(grads, first_all, own_weight, tokens, grad_middle, norm_gain, early, hidden_bias):
    rows, width = tokens.shape
    blocks, parts, me = lax.axis_size("blk"), lax.axis_size("dp"), lax.axis_index("blk")
    core, chip, own = me % 2, me // 2, width // blocks
    by_block = grads.reshape(2, 2, rows, 3 * own)
    away = times_transposed(pick(by_block, 1 - core, 1).reshape(2 * rows, 3 * own), own_weight).astype(jnp.bfloat16)
    got = exchange(away, "blk", 1)
    stay = times_transposed(pick(by_block, core, 1).reshape(2 * rows, 3 * own), own_weight)
    half = plus(stay, got).reshape(2, rows, width)
    half, grads = lax.optimization_barrier((half, grads))
    far = exchange(pick(half, 1 - chip, 0), "blk", 2)

    term = outer_sum(first_all, grads).astype(jnp.bfloat16).reshape(parts // 2, 2, width // parts, 3 * own)
    near = lax.rem(lax.axis_index("dp"), 2)
    term = plus(pick(term, near, 1), exchange(pick(term, 1 - near, 1), "dp", 1))
    qkv_term = far_sum(term).astype(jnp.bfloat16)
    qkv_blocks = lax.all_gather(qkv_term, "blk", axis=0)
    qkv_rows = qkv_blocks.reshape(blocks, -1, 3, own).transpose(1, 2, 0, 3).reshape(-1, 3 * width)
    qkv_grad = lax.dynamic_slice_in_dim(qkv_rows, me * 3 * own, 3 * own, 1).astype(jnp.float32)

    def spread(values):
        return lax.dynamic_update_slice_in_dim(jnp.zeros((width,), jnp.float32), values, me * own, 0)

    y = pick(half, chip, 0).astype(jnp.float32) + far.astype(jnp.float32)
    n, r = _stats(tokens.astype(jnp.float32))
    token_grad = (grad_middle + _pull(n, r, y * norm_gain[0])).astype(jnp.bfloat16)
    late = {0: jnp.sum(y * n, 0), 4: jnp.sum(y, 0), 8: spread(column_sums(grads[:, :own])), 9: spread(column_sums(grads[:, 2 * own :]))}
    small = jnp.stack([late.get(i, early[i]) for i in range(12)] + list(hidden_bias.reshape(-1, width)))
    small = sum_everywhere(small)
    place = lax.axis_index("dp")
    chunk = width // parts
    small_own = lax.dynamic_slice_in_dim(small[:12], place * chunk, chunk, 1)
    hidden = lax.dynamic_slice_in_dim(small[12:].reshape(-1), place * 4 * chunk, 4 * chunk, 0)
    return token_grad, qkv_grad, small_own, hidden


def local(tokens, cotangent, lengths, qkv_weight, out_weight, up_weight, down_weight, norm_gain, norm_bias, proj_bias, ffn_bias):
    rows, width = tokens.shape
    blocks = lax.axis_size("blk")
    parts = lax.axis_size("dp")
    me = lax.axis_index("blk")
    core, chip = me % 2, me // 2
    own = width // blocks

    first_all, qkv, own_weight = gather_project(tokens, qkv_weight, norm_gain, norm_bias, proj_bias)
    attended_own, log_total = attn_fwd(lengths, qkv)

    mixed, mid, n_one, r_one, low, turned, second_t, act, slope, sums_three, attended = ffn_forward(
        tokens, cotangent, attended_own, out_weight, up_weight, down_weight, norm_gain, norm_bias, proj_bias, ffn_bias
    )
    grad_middle, sums, hidden_bias, up_sum, down_sum, out_term, grad_own, out_line = ffn_backward(
        parts, low, turned, second_t, act, slope, up_weight, down_weight, mid, n_one, r_one, cotangent, attended, out_weight, norm_gain
    )
    grads = attn_bwd(lengths, qkv, grad_own, attended_own, log_total)

    if parts == 8:
        down_grad = lax.psum_scatter(down_sum, "dp", scatter_dimension=0, tiled=False)
        token_grad, qkv_grad, up_grad, out_grad, gains, shifts, biases, hidden = finish(
            grads, first_all, own_weight, tokens, grad_middle, norm_gain, up_sum, out_line, sums, sums_three, hidden_bias
        )
        token_grad, qkv_grad, up_grad, out_grad, down_grad, gains, shifts, biases, hidden = emit(
            token_grad, qkv_grad, up_grad, out_grad, down_grad, gains, shifts, biases, hidden
        )
        return (mixed, token_grad, qkv_grad, out_grad, up_grad, down_grad, gains, shifts, biases, hidden.reshape(-1))
    early = [None, sums[0], sums[1], sums_three[0], None, sums[2], sums[3], sums_three[1], None, None, sums[4], sums_three[2]]
    hidden_bias = hidden_bias.reshape(2, 2, 2, -1).transpose(0, 2, 1, 3)
    thin = width // parts
    halves = by_chip(far_sums(up_sum))
    up_grad = pick(halves, chip, 0).astype(jnp.float32) + exchange(pick(halves, 1 - chip, 0), "blk", 2).astype(jnp.float32)
    out_term = out_term.reshape(2, 2, width // 2, width // 2).transpose(1, 2, 0, 3).reshape(2, 2, own, width)
    out_half = plus(out_term[1], exchange(out_term[0], "blk", 1))
    out_sum = plus(pick(out_half, chip, 0), exchange(pick(out_half, 1 - chip, 0), "blk", 2))
    down = down_sum.transpose(1, 0, 2).reshape(own, parts, -1).transpose(1, 0, 2)
    out = out_sum.reshape(own, parts, thin).transpose(1, 0, 2)
    both = lax.psum_scatter(jnp.concatenate([down, out], 2), "dp", scatter_dimension=0, tiled=False).astype(jnp.float32)
    down_grad, out_grad = both[:, : down.shape[2]].T, both[:, down.shape[2] :].T
    token_grad, qkv_grad, small, hidden = finish_plain(grads, first_all, own_weight, tokens, grad_middle, norm_gain, early, hidden_bias)
    return (mixed, token_grad, qkv_grad, out_grad, up_grad, down_grad, small[:4], small[4:8], small[8:], hidden)


def solution(mesh):
    return jax.shard_map(
        local,
        mesh=mesh,
        in_specs=(P(("dp", "blk"), None), P(("dp", "blk"), None), P("dp", None)) + (P(),) * 8,
        out_specs=(P(("dp", "blk"), None), P(("dp", "blk"), None))
        + (P("dp", "blk"),) * 4
        + (P(None, "dp"),) * 3
        + (P("dp"),),
        check_vma=False,
    )
```

```python
import functools

import jax
import jax.numpy as jnp
from jax import lax
from jax.experimental import pallas as pl
from jax.experimental.pallas import tpu as pltpu
from jax.sharding import PartitionSpec as P

epsilon = 1e-05
HD = 64
NT = (((1,), (1,)), ((), ()))
NEG = -1e30
TILE = 256


def _bounds(len_ref, qb):
    l0 = len_ref[0, 0]
    e1 = l0 + len_ref[0, 1]

    def start_of(r):
        return jnp.where(r >= e1, e1, jnp.where(r >= l0, l0, 0))

    first = qb * TILE
    s_first, s_last = start_of(first), start_of(first + TILE - 1)
    kmin = s_first // TILE
    kmid = jnp.maximum(kmin, jnp.minimum(qb, (s_last + TILE - 1) // TILE))
    rows = first + lax.broadcasted_iota(jnp.int32, (1, TILE), 1)
    return kmin, kmid, rows, start_of(rows)


def _walk(len_ref, qb, step, carry, wide):
    kmin, kmid, rows, starts = _bounds(len_ref, qb)

    def run(masked, size):
        def body(kb, carry):
            at = pl.multiple_of(kb * TILE, TILE)
            mask = None
            if masked:
                kpos = at + lax.broadcasted_iota(jnp.int32, (size * TILE, TILE), 0)
                mask = (kpos >= starts) & (kpos <= rows)
            return step(at, size * TILE, mask, carry)

        return body

    for masked, at, left in ((True, kmin, kmid - kmin), (False, kmid, qb - kmid)):
        for size in wide:
            count, body = left // size, run(masked, size)
            carry = lax.fori_loop(0, count, lambda i, c, at=at, size=size, body=body: body(at + i * size, c), carry)
            at, left = at + count * size, left - count * size
    return run(True, 1)(qb, carry)


def _fill_masked(dst, value, heads):
    lane = lax.broadcasted_iota(jnp.int32, value.shape, 1) // HD
    for h in range(heads):
        dst[pl.ds(h * TILE, TILE), :] = jnp.where(lane == h, value, jnp.zeros_like(value))


def fwd_kernel(len_ref, q_ref, k_ref, v_ref, o_ref, lse_ref, qm, acc, ps, vt, *, heads, wide):
    qb = pl.program_id(0)

    @pl.when(qb == 0)
    def _():
        vt[...] = v_ref[...].T

    _fill_masked(qm, q_ref[...] * jnp.bfloat16(0.125), heads)
    acc[...] = jnp.zeros_like(acc)

    def step(at, size, mask, carry):
        keys = pl.ds(at, size)
        scores = [
            lax.dot_general(k_ref[keys, :], qm[pl.ds(h * TILE, TILE), :], NT, preferred_element_type=jnp.float32)
            for h in range(heads)
        ]
        out, fades = [], []
        for h in range(heads):
            m, l = carry[h]
            s = scores[h]
            if mask is not None:
                s = jnp.where(mask, s, NEG)
            top = jnp.maximum(m, jnp.max(s, 0, keepdims=True))
            p = jnp.exp(s - top)
            fade = jnp.exp(m - top)
            ps[pl.ds(0, size), pl.ds(h * TILE, TILE)] = p.astype(jnp.bfloat16)
            out.append((top, l * fade + jnp.sum(p, 0, keepdims=True)))
            fades.append(fade)
        for h in range(heads):
            lanes = pl.ds(h * HD, HD)
            part = jnp.dot(vt[lanes, keys], ps[pl.ds(0, size), pl.ds(h * TILE, TILE)], preferred_element_type=jnp.float32)
            acc[lanes, :] = acc[lanes, :] * fades[h] + part
        return tuple(out)

    carry = tuple((jnp.full((1, TILE), 0.1 * NEG, jnp.float32), jnp.zeros((1, TILE), jnp.float32)) for _ in range(heads))
    carry = _walk(len_ref, qb, step, carry, wide)
    for h in range(heads):
        m, l = carry[h]
        lse_ref[pl.ds(h, 1), :] = m + jnp.log(l)
        acc[pl.ds(h * HD, HD), :] = acc[pl.ds(h * HD, HD), :] / l
    o_ref[...] = acc[...].T.astype(jnp.bfloat16)


def attn_fwd(lengths, qkv, pair=0, lane=256, wide=(2, 1)):
    n = qkv.shape[0]
    heads = lane // HD
    return pl.pallas_call(
        functools.partial(fwd_kernel, heads=heads, wide=wide),
        grid_spec=pltpu.PrefetchScalarGridSpec(
            num_scalar_prefetch=1,
            grid=(n // TILE,),
            in_specs=[
                pl.BlockSpec((TILE, lane), lambda i, L: (i, 3 * pair)),
                pl.BlockSpec((n, lane), lambda i, L: (0, 3 * pair + 1)),
                pl.BlockSpec((n, lane), lambda i, L: (0, 3 * pair + 2)),
            ],
            out_specs=[pl.BlockSpec((TILE, lane), lambda i, L: (i, 0)), pl.BlockSpec((heads, TILE), lambda i, L: (0, i))],
            scratch_shapes=[
                pltpu.VMEM((heads * TILE, lane), jnp.bfloat16),
                pltpu.VMEM((lane, TILE), jnp.float32),
                pltpu.VMEM((wide[0] * TILE, heads * TILE), jnp.bfloat16),
                pltpu.VMEM((lane, n), jnp.bfloat16),
            ],
        ),
        out_shape=[jax.ShapeDtypeStruct((n, lane), jnp.bfloat16), jax.ShapeDtypeStruct((heads, n), jnp.float32)],
        compiler_params=pltpu.CompilerParams(vmem_limit_bytes=58 * 2**20),
        cost_estimate=pl.CostEstimate(flops=n * n * lane * 9, bytes_accessed=10 * n * lane, transcendentals=n * n * heads // 2),
        name="attn_fwd",
    )(lengths, qkv, qkv, qkv)


def bwd_kernel(len_ref, q_ref, do_ref, o_ref, lse_ref, k_ref, v_ref, d_ref, qm, dom, ps, ds, dqt, dk, dv, kt, *, heads, wide):
    qb = pl.program_id(0)
    c = heads * HD

    @pl.when(qb == 0)
    def _():
        dk[...] = jnp.zeros_like(dk)
        dv[...] = jnp.zeros_like(dv)
        kt[...] = k_ref[...].T

    _fill_masked(qm, q_ref[...] * jnp.bfloat16(0.125), heads)
    _fill_masked(dom, do_ref[...], heads)
    prod = (do_ref[...].astype(jnp.float32) * o_ref[...].astype(jnp.float32)).T
    delta = [jnp.sum(prod[h * HD : (h + 1) * HD], 0, keepdims=True) for h in range(heads)]
    dqt[...] = jnp.zeros_like(dqt)

    def step(at, size, mask, carry):
        keys = pl.ds(at, size)
        used = pl.ds(0, size)
        for h in range(heads):
            mine = pl.ds(h * TILE, TILE)
            s = lax.dot_general(k_ref[keys, :], qm[mine, :], NT, preferred_element_type=jnp.float32)
            p = jnp.exp(s - lse_ref[pl.ds(h, 1), :])
            if mask is not None:
                p = jnp.where(mask, p, 0.0)
            dp = lax.dot_general(v_ref[keys, :], dom[mine, :], NT, preferred_element_type=jnp.float32)
            ps[used, mine] = p.astype(jnp.bfloat16)
            ds[used, mine] = (p * (dp - delta[h])).astype(jnp.bfloat16)
        dv[keys, :] += jnp.dot(ps[used, :], dom[...], preferred_element_type=jnp.float32)
        dk[keys, :] += jnp.dot(ds[used, :], qm[...], preferred_element_type=jnp.float32)
        for h in range(heads):
            lanes = pl.ds(h * HD, HD)
            dqt[lanes, :] += jnp.dot(kt[lanes, keys], ds[used, pl.ds(h * TILE, TILE)], preferred_element_type=jnp.float32)
        return carry

    _walk(len_ref, qb, step, 0, wide)
    d_ref[pl.ds(pl.multiple_of(qb * TILE, TILE), TILE), pl.ds(0, c)] = (dqt[...] * 0.125).T.astype(jnp.bfloat16)

    @pl.when(qb == pl.num_programs(0) - 1)
    def _():
        d_ref[:, pl.ds(c, c)] = dk[...].astype(jnp.bfloat16)
        d_ref[:, pl.ds(2 * c, c)] = dv[...].astype(jnp.bfloat16)


def attn_bwd(lengths, qkv, do, o, lse, pair=0, lane=256, wide=(2, 1)):
    n = qkv.shape[0]
    heads = lane // HD
    row = lambda col: pl.BlockSpec((TILE, lane), lambda i, L: (i, col))
    whole = lambda col: pl.BlockSpec((n, lane), lambda i, L: (0, col))
    return pl.pallas_call(
        functools.partial(bwd_kernel, heads=heads, wide=wide),
        grid_spec=pltpu.PrefetchScalarGridSpec(
            num_scalar_prefetch=1,
            grid=(n // TILE,),
            in_specs=[
                row(3 * pair), row(pair), row(0), pl.BlockSpec((heads, TILE), lambda i, L: (0, i)),
                whole(3 * pair + 1), whole(3 * pair + 2),
            ],
            out_specs=pl.BlockSpec((n, 3 * lane), lambda i, L: (0, pair)),
            scratch_shapes=[
                pltpu.VMEM((heads * TILE, lane), jnp.bfloat16),
                pltpu.VMEM((heads * TILE, lane), jnp.bfloat16),
                pltpu.VMEM((wide[0] * TILE, heads * TILE), jnp.bfloat16),
                pltpu.VMEM((wide[0] * TILE, heads * TILE), jnp.bfloat16),
                pltpu.VMEM((lane, TILE), jnp.float32),
                pltpu.VMEM((n, lane), jnp.float32),
                pltpu.VMEM((n, lane), jnp.float32),
                pltpu.VMEM((lane, n), jnp.bfloat16),
            ],
        ),
        out_shape=jax.ShapeDtypeStruct(qkv.shape, jnp.bfloat16),
        compiler_params=pltpu.CompilerParams(vmem_limit_bytes=58 * 2**20),
        cost_estimate=pl.CostEstimate(flops=n * n * lane * 11, bytes_accessed=20 * n * lane, transcendentals=n * n * heads // 2),
        name="attn_bwd",
    )(lengths, qkv, do, o, lse, qkv, qkv)


def _stats(v):
    c = v - jnp.mean(v, -1, keepdims=True)
    r = lax.rsqrt(jnp.mean(c * c, -1, keepdims=True) + epsilon)
    return c * r, r


def _pull(n, r, e):
    return r * (e - jnp.mean(e, -1, keepdims=True) - n * jnp.mean(e * n, -1, keepdims=True))


def _fold(v):
    return jnp.sum(v.reshape(-1, 8, v.shape[-1]), 0)


def _row(ref, i):
    return ref[pl.ds(i, 1), :]


def _each(total, size, fn):
    def body(i, carry):
        fn(pl.ds(pl.multiple_of(i * size, size), size))
        return carry

    lax.fori_loop(0, total // size, body, 0)


def _turn_blocks(dst, value, core):
    own = dst.shape[0] // 4
    flipped = value.T
    for b in range(4):
        stays = 1 - lax.rem(core + b % 2, 2)
        dst[pl.ds(pl.multiple_of((2 * stays + b // 2) * own, own), own), :] = flipped[b * own : (b + 1) * own, :]


def ffn_kernel(
    x_hbm, cot_hbm, own_hbm, wo_hbm, up_ref, down_ref, gain_ref, shift_ref, bias_ref, fb_ref,
    mixed_ref, mid_out, n_out, r_ref, low_ref, turned_ref, second_out, act_ref, slope_ref, small_ref, att_out,
    x_ref, cot_ref, wo_ref, mid_ref, n_ref, second_t, att_ref, second, branch, ffn, sums, sends, recvs, own_sem, load_sems, save_sems, *, tiles, strip,
):
    s = pl.program_id(0)
    rows, width = x_ref.shape
    f32 = jnp.float32

    def loaded(i):
        return pltpu.make_async_copy((x_hbm, cot_hbm, wo_hbm)[i], (x_ref, cot_ref, wo_ref)[i], load_sems.at[i])

    def saved(i):
        pairs = ((mid_ref, mid_out), (n_ref, n_out), (second_t, second_out), (att_ref, att_out))
        return pltpu.make_async_copy(*pairs[i], save_sems.at[i])

    @pl.when(s == 0)
    def _():
        me = lax.axis_index("blk")
        own = width // 4
        peers = (me + 1 - 2 * lax.rem(me, 2), lax.rem(me + 2, 4), 3 - me)
        mesh_ids = pl.DeviceIdType.MESH
        barrier = pltpu.get_barrier_semaphore()
        for block in peers:
            pl.semaphore_signal(barrier, inc=1, device_id={"blk": block}, device_id_type=mesh_ids)
        pl.semaphore_wait(barrier, 3)

        def rows_of(block):
            return own_hbm.at[pl.ds(pl.multiple_of(block * rows, rows), rows), :]

        here = att_ref.at[:, pl.ds(pl.multiple_of(me * own, own), own)]
        copies = [
            pltpu.make_async_remote_copy(
                src_ref=rows_of(block), dst_ref=here, send_sem=sends.at[i], recv_sem=recvs.at[i],
                device_id={"blk": block}, device_id_type=mesh_ids,
            )
            for i, block in enumerate(peers)
        ]
        for copy in copies[::-1]:
            copy.start()
        mine = pltpu.make_async_copy(rows_of(me), here, own_sem)
        mine.start()
        for i in (2, 0, 1):
            loaded(i).start()
        sums[...] = jnp.zeros_like(sums)
        mine.wait()
        for i in range(3):
            loaded(i).wait()
        for copy in copies:
            copy.wait_send()
            copy.wait_recv()
        saved(3).start()
        branch[...] = jnp.dot(att_ref[...], wo_ref[...], preferred_element_type=f32) + _row(bias_ref, 2)

        def normed(at):
            n, r = _stats(branch[at, :])
            n_ref[at, :] = n.astype(jnp.bfloat16)
            r_ref[at, :] = r
            m = x_ref[at, :].astype(f32) + n * _row(gain_ref, 1) + _row(shift_ref, 1)
            mid_ref[at, :] = m
            n, _ = _stats(m)
            second[at, :] = (n * _row(gain_ref, 2) + _row(shift_ref, 2)).astype(jnp.bfloat16)

        _each(rows, strip, normed)
        second_t[...] = second[...].T
        for i in range(3):
            saved(i).start()

    c1, c3 = 0.7978845608028654, 0.7978845608028654 * 0.044715
    strips = [pl.ds(i * (rows // 2), rows // 2) for i in range(2)]
    us = [jnp.dot(second[at, :], up_ref[...], preferred_element_type=f32) + fb_ref[...] for at in strips]
    parts = []
    for at, u in zip(strips, us):
        sq = u * u
        t = jnp.tanh(u * (c1 + c3 * sq))
        half = 0.5 + 0.5 * t
        a = (u * half).astype(jnp.bfloat16)
        act_ref[at, :] = a
        slope_ref[at, :] = (half + (0.5 * u) * (1.0 - t * t) * (c1 + 3.0 * c3 * sq)).astype(jnp.bfloat16)
        parts.append(jnp.dot(a, down_ref[...], preferred_element_type=f32))

    @pl.when(s == 0)
    def _():
        for at in strips:
            ffn[at, :] = jnp.zeros((rows // 2, width), f32) + _row(bias_ref, 3)

    for at, part in zip(strips, parts):
        ffn[at, :] += part

    @pl.when(s == tiles - 1)
    def _():
        def normed(at):
            n, r = _stats(ffn[at, :])
            y = cot_ref[at, :].astype(f32)
            mixed_ref[at, :] = (mid_ref[at, :] + n * _row(gain_ref, 3) + _row(shift_ref, 3)).astype(jnp.bfloat16)
            g = _pull(n, r, y * _row(gain_ref, 3)).astype(jnp.bfloat16)
            low_ref[at, :] = g
            sums[pl.ds(0, 8), :] += _fold(y * n)
            sums[pl.ds(8, 8), :] += _fold(y)
            sums[pl.ds(16, 8), :] += _fold(g.astype(f32))

        _each(rows, strip, normed)
        _turn_blocks(turned_ref, low_ref[...], lax.rem(lax.axis_index("blk"), 2))
        for i in range(4):
            saved(i).wait()
        for i in range(3):
            small_ref[pl.ds(i, 1), :] = jnp.sum(sums[pl.ds(8 * i, 8), :], 0, keepdims=True)


def _once(*shape):
    return pl.BlockSpec(shape, lambda s: (0,) * len(shape), pipeline_mode=pl.Buffered(1))


def ffn_forward(tokens, cotangent, attended, out_weight, up_weight, down_weight, norm_gain, norm_bias, proj_bias, ffn_bias):
    rows, width = tokens.shape
    hidden = up_weight.shape[1]
    tiles = 8
    hid = hidden // tiles
    bf16, f32 = jnp.bfloat16, jnp.float32
    shape = jax.ShapeDtypeStruct
    return pl.pallas_call(
        functools.partial(ffn_kernel, tiles=tiles, strip=rows // 4),
        grid=(tiles,),
        in_specs=[
            *[pl.BlockSpec(memory_space=pl.ANY)] * 4,
            pl.BlockSpec((width, hid), lambda s: (0, s)), pl.BlockSpec((hid, width), lambda s: (s, 0)),
            _once(4, width), _once(4, width), _once(4, width), pl.BlockSpec((1, hid), lambda s: (0, s)),
        ],
        out_specs=[
            _once(rows, width), *[pl.BlockSpec(memory_space=pl.ANY)] * 2, _once(rows, 1), _once(rows, width),
            _once(width, rows), pl.BlockSpec(memory_space=pl.ANY),
            pl.BlockSpec((rows, hid), lambda s: (0, s)), pl.BlockSpec((rows, hid), lambda s: (0, s)), _once(8, width), pl.BlockSpec(memory_space=pl.ANY),
        ],
        out_shape=[
            shape((rows, width), bf16), shape((rows, width), f32), shape((rows, width), bf16), shape((rows, 1), f32),
            shape((rows, width), bf16), shape((width, rows), bf16), shape((width, rows), bf16),
            shape((rows, hidden), bf16), shape((rows, hidden), bf16), shape((8, width), f32), shape((rows, width), bf16),
        ],
        scratch_shapes=[
            pltpu.VMEM((rows, width), bf16), pltpu.VMEM((rows, width), bf16), pltpu.VMEM((width, width), bf16), pltpu.VMEM((rows, width), f32),
            pltpu.VMEM((rows, width), bf16), pltpu.VMEM((width, rows), bf16), pltpu.VMEM((rows, width), bf16),
            pltpu.VMEM((rows, width), bf16), pltpu.VMEM((rows, width), f32), pltpu.VMEM((rows, width), f32), pltpu.VMEM((24, width), f32), pltpu.SemaphoreType.DMA((3,)), pltpu.SemaphoreType.DMA((3,)), pltpu.SemaphoreType.DMA(()),
            pltpu.SemaphoreType.DMA((3,)), pltpu.SemaphoreType.DMA((4,)),
        ],
        compiler_params=pltpu.CompilerParams(collective_id=3, has_side_effects=True, vmem_limit_bytes=56 * 2**20),
        cost_estimate=pl.CostEstimate(flops=18 * rows * width * width, bytes_accessed=50 * 2**20, transcendentals=rows * hidden),
        name="ffn_forward",
    )(tokens, cotangent, attended, out_weight, up_weight, down_weight, norm_gain, norm_bias, proj_bias, ffn_bias.reshape(1, -1))


def grads_kernel(
    low_ref, turned_hbm, second_hbm, act_ref, slope_ref, up_ref, down_ref, mid_hbm, n_hbm, r_ref, cot_hbm, att_hbm, wo_hbm, gain_ref,
    gmid_ref, small_ref, hid_ref, up_out, down_out, out_out, gown_out, out_line,
    turned_ref, second_t, cot_ref, att_ref, wo_ref, pre, gs, low, turned, gatt, sums, up_buf, up_in, up_y, down_send, down_keep, down_in, down_x, up_z,
    up_core, up_core_in, up_far, up_far_in, down_core, down_core_in, down_far, down_far_in, up_done, down_done, own_sems, gatt_sends, gatt_recvs, line_sends, line_recvs, save_sems, *, tiles, strip, fold,
):
    s = pl.program_id(0)
    rows, width = low_ref.shape
    own = width // 4
    f32, bf16 = jnp.float32, jnp.bfloat16
    pair, side = s // 2, lax.rem(s, 2)
    me, place = lax.axis_index("blk"), lax.axis_index("dp")
    core, chip, near = lax.rem(me, 2), me // 2, lax.rem(place, 2)
    line = place // 2
    twin, other, beside = {"blk": me + 1 - 2 * core}, {"blk": lax.rem(me + 2, 4)}, {"dp": place + 1 - 2 * near}
    last = {"blk": 3 - me}
    half = tiles // 2
    mesh_ids = pl.DeviceIdType.MESH

    def remote(src, dst, sends, recvs, i, target):
        return pltpu.make_async_remote_copy(
            src_ref=src, dst_ref=dst, send_sem=sends.at[i], recv_sem=recvs.at[i], device_id=target, device_id_type=mesh_ids
        )

    def up_to_twin(p):
        return remote(up_buf.at[0], up_in.at[p], up_core, up_core_in, p, twin)

    def up_to_beside(p):
        return remote(up_in.at[p, :, 1 - near], up_y.at[p], up_far, up_far_in, p, beside)

    def down_to_twin(u, slot):
        return remote(down_send.at[slot], down_in.at[lax.rem(u, 4)], down_core, down_core_in, u, twin)

    def down_to_other(u):
        return remote(down_keep.at[u, 1 - chip], down_x.at[u], down_far, down_far_in, u, other)

    def up_result(p):
        if fold:
            return pltpu.make_async_copy(up_y.at[p, line], up_out.at[p], up_done.at[p])
        return pltpu.make_async_copy(up_y.at[p], up_out.at[:, p], up_done.at[p])

    def up_to_line(p, k):
        ahead = lax.rem(line + k, 4)
        return remote(up_y.at[p, ahead], up_z.at[k - 1, p], line_sends, line_recvs, 3 * p + k - 1, {"dp": 2 * ahead + near})

    def join_line(p):
        total = up_y[p, line].astype(f32)
        for k in range(1, 4):
            up_to_line(p, k).wait_recv()
            total += up_z[k - 1, p].astype(f32)
        up_y[p, line] = total.astype(bf16)
        up_result(p).start()

    def down_result(u):
        tile = 4 * (u // 4) + 2 * lax.rem(u, 2) + lax.rem(u // 2, 2)
        return pltpu.make_async_copy(down_x.at[u], down_out.at[tile], down_done.at[u])

    def saved(i):
        pairs = ((mid_hbm, gmid_ref), (n_hbm, low), (cot_hbm, cot_ref), (att_hbm, att_ref), (wo_hbm, wo_ref), (turned_hbm, turned_ref), (second_hbm, second_t))
        return pltpu.make_async_copy(*pairs[i], save_sems.at[i])

    def out_line_result():
        return pltpu.make_async_copy(up_y.at[half], out_line, own_sems.at[0])

    def out_result(i):
        return pltpu.make_async_copy(up_buf.at[i], out_out.at[i], own_sems.at[2 + i])

    def columns_to(i):
        target = (last, other, twin)[i]
        block = target["blk"]
        src = gatt.at[:, pl.ds(pl.multiple_of(block * own, own), own)]
        dst = gown_out.at[pl.ds(pl.multiple_of(me * rows, rows), rows), :]
        return remote(src, dst, gatt_sends, gatt_recvs, i, target)

    def columns_here():
        src = gatt.at[:, pl.ds(pl.multiple_of(me * own, own), own)]
        return pltpu.make_async_copy(src, gown_out.at[pl.ds(pl.multiple_of(me * rows, rows), rows), :], own_sems.at[4])

    def join_up(p):
        up_to_twin(p).wait_recv()
        up_in[p] = (up_in[p].astype(f32) + up_buf[1].astype(f32)).astype(bf16)
        up_to_beside(p).start()

    def join_far_up(p):
        up_to_beside(p).wait_recv()
        up_y[p] = (up_y[p].astype(f32) + up_in[p, :, near].astype(f32)).astype(bf16)
        if fold:
            for k in range(1, 4):
                up_to_line(p, k).start()
        else:
            up_result(p).start()

    def join_down(u):
        down_to_twin(u, 0).wait_recv()
        down_keep[u] = (down_keep[u].astype(f32) + down_in[lax.rem(u, 4)].astype(f32)).astype(bf16)
        down_to_other(u).start()

    def join_far_down(u):
        down_to_other(u).wait_recv()
        down_x[u] = (down_x[u].astype(f32) + down_keep[u, chip].astype(f32)).astype(bf16)
        down_result(u).start()

    @pl.when(s == 0)
    def _():
        barrier = pltpu.get_barrier_semaphore()
        for target in (twin, other, beside, last):
            pl.semaphore_signal(barrier, inc=1, device_id=target, device_id_type=mesh_ids)
        sums[...] = jnp.zeros_like(sums)
        for i in (5, 6, 0, 1, 2, 3, 4):
            saved(i).start()
        for i in range(1, 4 if fold else 1):
            ahead = lax.rem(line + i, 4)
            pl.semaphore_signal(barrier, inc=1, device_id={"dp": 2 * ahead + near}, device_id_type=mesh_ids)
        pl.semaphore_wait(barrier, 7 if fold else 4)

    @pl.when(s >= 3)
    def _():
        join_far_down(s - 3)

    @pl.when((s == 5) | (s == 7))
    def _():
        join_far_up((s - 5) // 2)

    g = lax.dot_general(low_ref[...], down_ref[...], NT, preferred_element_type=f32) * slope_ref[...].astype(f32)
    g = g.astype(bf16)
    pre[...] = g
    hid_ref[pl.ds(s, 1)] = jnp.sum(g.astype(f32), 0, keepdims=True)[None]
    part = lax.dot_general(g, up_ref[...], NT, preferred_element_type=f32)

    @pl.when(s == 0)
    def _():
        gs[...] = part

    @pl.when(s > 0)
    def _():
        gs[...] += part

    @pl.when(s == 0)
    def _():
        saved(5).wait()
        saved(6).wait()

    down_grad = jnp.dot(turned_ref[...], act_ref[...], preferred_element_type=f32).astype(bf16)

    @pl.when(s >= 2)
    def _():
        down_to_twin(s - 2, side).wait_send()

    down_send[side] = down_grad[: width // 2].reshape(2, own, -1)
    down_to_twin(s, side).start()
    down_keep[s] = down_grad[width // 2 :].reshape(2, own, -1)

    @pl.when(s > 0)
    def _():
        join_down(s - 1)

    @pl.when((side == 0) & (s > 0))
    def _():
        join_up(pair - 1)

    up_grad = jnp.dot(second_t[...], pre[...], preferred_element_type=f32).astype(bf16).reshape(up_buf.shape[1:])

    @pl.when(side == core)
    def _():
        up_buf[1] = up_grad

    @pl.when(side != core)
    def _():
        @pl.when(pair > 0)
        def _():
            up_to_twin(pair - 1).wait_send()

        up_buf[0] = up_grad
        up_to_twin(pair).start()

    @pl.when(s == tiles - 1)
    def _():
        def normed(at):
            n, r = _stats(gmid_ref[at, :])
            y = gs[at, :]
            gm = cot_ref[at, :].astype(f32) + _pull(n, r, y * _row(gain_ref, 2))
            gmid_ref[at, :] = gm
            sums[pl.ds(8, 8), :] += _fold(y * n)
            sums[pl.ds(24, 8), :] += _fold(y)
            n, r = low[at, :].astype(f32), r_ref[at, :]
            g = _pull(n, r, gm * _row(gain_ref, 1)).astype(bf16)
            low[at, :] = g
            sums[pl.ds(0, 8), :] += _fold(gm * n)
            sums[pl.ds(16, 8), :] += _fold(gm)
            sums[pl.ds(32, 8), :] += _fold(g.astype(f32))

        for i in range(5):
            saved(i).wait()
        _each(rows, strip, normed)
        join_down(tiles - 1)
        join_up(half - 1)
        gatt[...] = lax.dot_general(low[...], wo_ref[...], NT, preferred_element_type=f32).astype(bf16)
        for i in range(3):
            columns_to(i).start()
        columns_here().start()
        join_far_up(2)
        _turn_blocks(turned, low[...], core)
        grad = jnp.dot(turned[...], att_ref[...], preferred_element_type=f32).astype(bf16)
        up_to_twin(half - 1).wait_send()
        if fold:
            thin = width // 8
            for d in range(8):
                for b in range(8):
                    piece = grad[b * thin : (b + 1) * thin, d * thin : (d + 1) * thin]
                    up_buf[b // 4, d // 2, d % 2, :, pl.ds(b % 4 * thin, thin)] = piece
            up_to_twin(half).start()
        else:
            for i in range(2):
                up_buf[i] = grad[:, i * width // 2 : (i + 1) * width // 2].reshape(up_buf.shape[1:])
                out_result(i).start()
        for i in range(5):
            small_ref[pl.ds(i, 1), :] = jnp.sum(sums[pl.ds(8 * i, 8), :], 0, keepdims=True)
        if fold:
            join_up(half)
        join_far_up(3)
        for u in range(tiles - 3, tiles):
            join_far_down(u)
        if fold:
            for p in range(half):
                join_line(p)
            up_to_beside(half).wait_recv()
            up_y[half] = (up_y[half].astype(f32) + up_in[half, :, near].astype(f32)).astype(bf16)
            out_line_result().start()
            out_line_result().wait()
        down_to_twin(tiles - 2, 0).wait_send()
        down_to_twin(tiles - 1, 1).wait_send()
        if fold:
            up_to_twin(half).wait_send()
        else:
            out_result(0).wait()
            out_result(1).wait()
        for p in range(half + fold):
            up_to_beside(p).wait_send()
        for p in range(half):
            up_result(p).wait()
            for i in range(1, 4 if fold else 1):
                up_to_line(p, i).wait_send()
        for u in range(tiles):
            down_to_other(u).wait_send()
            down_result(u).wait()
        for i in range(3):
            columns_to(i).wait_send()
            columns_to(i).wait_recv()
        columns_here().wait()


def ffn_backward(parts, low, turned, second_t, act, slope, up_weight, down_weight, mid, n_one, r_one, cotangent, attended, out_weight, norm_gain):
    rows, width = low.shape
    hidden = up_weight.shape[1]
    tiles, own = 8, width // 4
    hid = hidden // tiles
    bf16, f32 = jnp.bfloat16, jnp.float32
    shape = jax.ShapeDtypeStruct
    tile_of = lambda s: 4 * (s // 4) + 2 * lax.rem(s, 2) + lax.rem(s // 2, 2)
    thin = (parts // 2, 2, width // parts, hid)
    dma = pltpu.SemaphoreType.DMA
    half = tiles // 2
    fold = int(parts == 8)
    return pl.pallas_call(
        functools.partial(grads_kernel, tiles=tiles, strip=rows // 4, fold=fold),
        grid=(tiles,),
        in_specs=[
            _once(rows, width), pl.BlockSpec(memory_space=pl.ANY), pl.BlockSpec(memory_space=pl.ANY),
            pl.BlockSpec((rows, hid), lambda s: (0, tile_of(s))), pl.BlockSpec((rows, hid), lambda s: (0, tile_of(s))),
            pl.BlockSpec((width, hid), lambda s: (0, tile_of(s))), pl.BlockSpec((hid, width), lambda s: (tile_of(s), 0)),
            pl.BlockSpec(memory_space=pl.ANY), pl.BlockSpec(memory_space=pl.ANY), _once(rows, 1), *[pl.BlockSpec(memory_space=pl.ANY)] * 3, _once(4, width),
        ],
        out_specs=[
            _once(rows, width), _once(8, width), _once(tiles, 1, hid),
            *[pl.BlockSpec(memory_space=pl.ANY)] * 5,
        ],
        out_shape=[
            shape((rows, width), f32),
            shape((8, width), f32), shape((tiles, 1, hid), f32),
            shape((half, width // parts, hid) if fold else (parts // 2, half, width // parts, hid), bf16), shape((tiles, own, hid), bf16), shape((2,) + thin, bf16),
            shape((4 * rows, own), bf16), shape((parts // 2, width // parts, hid), bf16),
        ],
        scratch_shapes=[
            pltpu.VMEM((width, rows), bf16), pltpu.VMEM((width, rows), bf16), pltpu.VMEM((rows, width), bf16), pltpu.VMEM((rows, width), bf16),
            pltpu.VMEM((width, width), bf16), pltpu.VMEM((rows, hid), bf16), pltpu.VMEM((rows, width), f32), pltpu.VMEM((rows, width), bf16), pltpu.VMEM((width, rows), bf16), pltpu.VMEM((rows, width), bf16),
            pltpu.VMEM((40, width), f32),
            pltpu.VMEM((2,) + thin, bf16), pltpu.VMEM((half + fold,) + thin, bf16), pltpu.VMEM((half + fold, parts // 2, width // parts, hid), bf16),
            pltpu.VMEM((2, 2, own, hid), bf16), pltpu.VMEM((tiles, 2, own, hid), bf16), pltpu.VMEM((4, 2, own, hid), bf16),
            pltpu.VMEM((tiles, own, hid), bf16), pltpu.VMEM((3, half, width // parts, hid), bf16),
            *[dma((half + fold,))] * 4, *[dma((tiles,))] * 4, dma((half + fold,)), dma((tiles,)), dma((5,)), dma((3,)), dma((3,)), dma((3 * half,)), dma((3 * half,)), dma((7,)),
        ],
        compiler_params=pltpu.CompilerParams(collective_id=1, has_side_effects=True, vmem_limit_bytes=60 * 2**20),
        name="ffn_backward",
    )(low, turned, second_t, act, slope, up_weight, down_weight, mid, n_one, r_one, cotangent, attended, out_weight, norm_gain)


def project_kernel(
    x_hbm, w_hbm, gain_ref, shift_ref, bias_ref, all_out, qkv_out, w_out, x_ref, all_ref, qkv_ref, w_ref, x_sems, out_sems, w_sems, chip_send, chip_recv, core_send, core_recv, pass_send, pass_recv, *, pieces,
):
    me = lax.axis_index("blk")
    core = lax.rem(me, 2)
    twin, other, last = me + 1 - 2 * core, lax.rem(me + 2, 4), 3 - me
    rows, width = x_ref.shape
    own = width // 4
    size = rows // pieces
    fetch = [pltpu.make_async_copy(x_hbm.at[pl.ds(i * size, size), :], x_ref.at[pl.ds(i * size, size), :], x_sems.at[i]) for i in range(pieces)]
    for copy in fetch:
        copy.start()
    barrier = pltpu.get_barrier_semaphore()
    for target in (twin, other):
        pl.semaphore_signal(barrier, inc=1, device_id={"blk": target}, device_id_type=pl.DeviceIdType.MESH)
    loads = []
    for third in range(3):
        columns = pl.ds(pl.multiple_of(third * width + me * own, own), own)
        load = pltpu.make_async_copy(w_hbm.at[:, columns], w_ref.at[:, pl.ds(third * own, own)], w_sems.at[third])
        load.start()
        loads.append(load)

    def at(block, i):
        return pl.ds(pl.multiple_of(block * rows + i * size, size), size)

    def send(block, i, target, sends, recvs):
        piece = all_ref.at[at(block, i), :]
        copy = pltpu.make_async_remote_copy(
            src_ref=piece, dst_ref=piece, send_sem=sends.at[i], recv_sem=recvs.at[i],
            device_id={"blk": target}, device_id_type=pl.DeviceIdType.MESH,
        )
        return copy

    def project(block, i):
        where = at(block, i)
        got = jnp.dot(all_ref[where, :], w_ref[...], preferred_element_type=jnp.float32)
        for third in range(3):
            part = got[:, third * own : (third + 1) * own]
            if third != 1:
                part = part + bias_ref[pl.ds(third // 2, 1), pl.ds(pl.multiple_of(me * own, own), own)]
            qkv_ref[where, pl.ds(third * own, own)] = part.astype(jnp.bfloat16)
        for src, dst in ((all_ref, all_out), (qkv_ref, qkv_out)):
            copy = pltpu.make_async_copy(src.at[where, :], dst.at[where, :], out_sems.at[len(saved)])
            copy.start()
            saved.append(copy)

    sent, saved = [], []
    for i in range(pieces):
        fetch[i].wait()
        n, _ = _stats(x_ref[pl.ds(i * size, size), :].astype(jnp.float32))
        all_ref[at(me, i), :] = (n * gain_ref[pl.ds(0, 1), :] + shift_ref[pl.ds(0, 1), :]).astype(jnp.bfloat16)
        if i == 0:
            pl.semaphore_wait(barrier, 2)
        for target, sends, recvs in ((other, chip_send, chip_recv), (twin, core_send, core_recv)):
            copy = send(me, i, target, sends, recvs)
            copy.start()
            sent.append(copy)
    for load in loads:
        load.wait()
    keep = pltpu.make_async_copy(w_ref, w_out, w_sems.at[3])
    keep.start()
    for i in range(pieces):
        project(me, i)
    for i in range(pieces):
        send(twin, i, twin, core_send, core_recv).wait_recv()
        project(twin, i)
    for i in range(pieces):
        send(other, i, other, chip_send, chip_recv).wait_recv()
        copy = send(other, i, twin, pass_send, pass_recv)
        copy.start()
        sent.append(copy)
        project(other, i)
        if i > 0:
            send(last, i - 1, twin, pass_send, pass_recv).wait_recv()
            project(last, i - 1)
    send(last, pieces - 1, twin, pass_send, pass_recv).wait_recv()
    project(last, pieces - 1)
    for copy in sent:
        copy.wait_send()
    for copy in saved:
        copy.wait()
    keep.wait()


def gather_project(tokens, qkv_weight, norm_gain, norm_bias, proj_bias):
    rows, width = tokens.shape
    pieces = 4
    vmem, hbm = pl.BlockSpec(memory_space=pltpu.VMEM), pl.BlockSpec(memory_space=pl.ANY)
    dma = pltpu.SemaphoreType.DMA((pieces,))
    return pl.pallas_call(
        functools.partial(project_kernel, pieces=pieces),
        in_specs=[hbm, hbm, vmem, vmem, vmem],
        out_specs=[hbm] * 3,
        out_shape=[jax.ShapeDtypeStruct((4 * rows, width), jnp.bfloat16), jax.ShapeDtypeStruct((4 * rows, 3 * width // 4), jnp.bfloat16), jax.ShapeDtypeStruct((width, 3 * width // 4), jnp.bfloat16)],
        scratch_shapes=[
            pltpu.VMEM((rows, width), jnp.bfloat16), pltpu.VMEM((4 * rows, width), jnp.bfloat16),
            pltpu.VMEM((4 * rows, 3 * width // 4), jnp.bfloat16), pltpu.VMEM((width, 3 * width // 4), jnp.bfloat16),
            dma, pltpu.SemaphoreType.DMA((8 * pieces,)), pltpu.SemaphoreType.DMA((4,)),
        ] + [dma] * 6,
        compiler_params=pltpu.CompilerParams(collective_id=0, has_side_effects=True, vmem_limit_bytes=60 * 2**20),
        name="gather_project",
    )(tokens, qkv_weight, norm_gain, norm_bias, proj_bias)


def tail_kernel(
    d_hbm, first_hbm, w_hbm, x_hbm, gmid_hbm, gain_ref, up_ref, out_ref, sums_ref, three_ref, hid_ref,
    token_ref, qkv_ref, up_grad_ref, out_grad_ref, gain_grad_ref, shift_grad_ref, bias_grad_ref, hid_grad_ref,
    d, first, w, x, gmid, turned, core_out, core_in, far_out, far_in, mine, cols, cols_in, line_out, line_in, total, heads_in, part, part_in, both, both_in, sums, up_in, out_in, out_sum, out_far,
    loads, core_send, core_recv, far_send, far_recv, y_send, y_recv, z_send, z_recv, q_send, q_recv, s_send, s_recv, b_send, b_recv, h_send, h_recv, o_send, o_recv, *, pieces,
):
    f32, bf16 = jnp.float32, jnp.bfloat16
    rows, width = x.shape
    own = width // 4
    size = rows // pieces
    thin = width // 8
    me, place = lax.axis_index("blk"), lax.axis_index("dp")
    core, near, line = lax.rem(me, 2), lax.rem(place, 2), place // 2
    twin, other, last = me + 1 - 2 * core, lax.rem(me + 2, 4), 3 - me
    mesh_ids = pl.DeviceIdType.MESH

    def remote(src, dst, sends, recvs, i, target):
        return pltpu.make_async_remote_copy(
            src_ref=src, dst_ref=dst, send_sem=sends.at[i], recv_sem=recvs.at[i], device_id=target, device_id_type=mesh_ids
        )

    def rows_of(block, i):
        return pl.ds(pl.multiple_of(block * rows + i * size, size), size)

    def piece(i):
        return pl.ds(i * size, size)

    barrier = pltpu.get_barrier_semaphore()
    for block in (twin, other, last):
        pl.semaphore_signal(barrier, inc=1, device_id={"blk": block}, device_id_type=mesh_ids)
    for k in range(1, 8):
        pl.semaphore_signal(barrier, inc=1, device_id={"dp": lax.rem(place + k, 8)}, device_id_type=mesh_ids)

    def block_rows(block):
        return pl.ds(pl.multiple_of(block * rows, rows), rows)

    fetch = [pltpu.make_async_copy(w_hbm, w, loads.at[0])]
    for i, block in enumerate((last, other, me, twin)):
        fetch.append(pltpu.make_async_copy(d_hbm.at[block_rows(block), :], d.at[block_rows(block), :], loads.at[1 + i]))
    for i, (src, dst) in enumerate(((first_hbm, first), (x_hbm, x), (gmid_hbm, gmid))):
        fetch.append(pltpu.make_async_copy(src, dst, loads.at[5 + i]))
    for copy in fetch[:3]:
        copy.start()

    def partial(block, i):
        return lax.dot_general(d[rows_of(block, i), :], w[...], NT, preferred_element_type=f32)

    def to_twin(kind, i):
        return remote(core_out.at[kind, piece(i), :], core_in.at[kind, piece(i), :], core_send, core_recv, kind * pieces + i, {"blk": twin})

    def to_other(i):
        return remote(far_out.at[piece(i), :], far_in.at[piece(i), :], far_send, far_recv, i, {"blk": other})

    def to_beside(k):
        return remote(cols.at[k, 1 - near], cols_in.at[k], y_send, y_recv, k, {"dp": place + 1 - 2 * near})

    def to_line(k):
        return remote(line_out.at[k], line_in.at[k], z_send, z_recv, k, {"dp": 2 * lax.rem(line + k, 4) + near})

    pl.semaphore_wait(barrier, 10)
    chip = me // 2
    weights = remote(up_ref.at[pl.ds(2 * (1 - chip), 2)], up_in, h_send, h_recv, 0, {"blk": other})
    weights.start()

    def out_to_line(k):
        ahead = lax.rem(line + k, 4)
        return remote(out_ref.at[ahead], out_in.at[k - 1], o_send, o_recv, k - 1, {"dp": 2 * ahead + near})

    out_to_other = remote(out_sum.at[1 - chip], out_far, h_send, h_recv, 1, {"blk": other})
    for k in range(1, 4):
        out_to_line(k).start()
    fetch[0].wait()
    fetch[1].wait()
    for copy in fetch[3:]:
        copy.start()
    for i in range(pieces):
        core_out[0, piece(i), :] = partial(last, i).astype(bf16)
        to_twin(0, i).start()
    fetch[2].wait()
    for i in range(pieces):
        got = partial(other, i)
        to_twin(0, i).wait_recv()
        far_out[piece(i), :] = (got + core_in[0, piece(i), :].astype(f32)).astype(bf16)
        to_other(i).start()
    fetch[3].wait()
    fetch[4].wait()
    for i in range(d.shape[0] // 256):
        turned[:, pl.ds(i * 256, 256)] = d[pl.ds(i * 256, 256), :].T
    fetch[5].wait()
    for k in (1, 2, 3, 0):
        where = pl.ds(pl.multiple_of(lax.rem(line + k, 4) * 2 * thin, 2 * thin), 2 * thin)
        got = jnp.dot(turned[...], first[:, where], preferred_element_type=f32).astype(bf16)
        cols[k, 0] = got[:, :thin]
        cols[k, 1] = got[:, thin:]
        to_beside(k).start()
    for i in range(pieces):
        core_out[1, piece(i), :] = partial(twin, i).astype(bf16)
        to_twin(1, i).start()
    for i in range(pieces):
        mine[piece(i), :] = partial(me, i)
    ones = jnp.ones((8, d.shape[0]), bf16)
    column = jnp.dot(ones, d[...], preferred_element_type=f32)
    part[...] = jnp.zeros_like(part)
    for k in range(8):
        lanes = pl.ds(k * thin, thin)
        for i, (ref, j) in ((1, (sums_ref, 0)), (2, (sums_ref, 1)), (3, (three_ref, 0)), (5, (sums_ref, 2)), (6, (sums_ref, 3)), (7, (three_ref, 1)), (10, (sums_ref, 4)), (11, (three_ref, 2))):
            part[k, pl.ds(i, 1), :] = ref[pl.ds(j, 1), lanes]
        tile = 4 * (k // 4) + 2 * (k % 2) + k // 2 % 2
        for i in range(4):
            part[tile, pl.ds(12 + i, 1), :] = hid_ref[k, :, pl.ds(i * thin, thin)]
    for h in range(2):
        part[2 * me + h, pl.ds(8, 1), :] = column[:1, h * thin : (h + 1) * thin]
        part[2 * me + h, pl.ds(9, 1), :] = column[:1, 2 * own + h * thin : 2 * own + (h + 1) * thin]
    fetch[6].wait()
    fetch[7].wait()
    sums[...] = jnp.zeros_like(sums)

    def tokens(i):
        at = piece(i)
        to_twin(1, i).wait_recv()
        n, r = _stats(x[at, :].astype(f32))
        got = mine[at, :] + core_in[1, at, :].astype(f32)
        to_other(i).wait_recv()
        y = got + far_in[at, :].astype(f32)
        token_ref[at, :] = (gmid[at, :] + _pull(n, r, y * _row(gain_ref, 0))).astype(bf16)
        sums[pl.ds(0, 8), :] += _fold(y * n)
        sums[pl.ds(8, 8), :] += _fold(y)

    for k in (1, 2, 3):
        to_beside(k).wait_recv()
        line_out[k] = (cols[k, near].astype(f32) + cols_in[k].astype(f32)).astype(bf16)
        to_line(k).start()
    for k in range(1, 4):
        out_to_line(k).wait_recv()
    got = out_ref[line].astype(f32)
    for k in range(3):
        got += out_in[k].astype(f32)
    out_sum[0] = got[:, : 2 * thin].astype(bf16)
    out_sum[1] = got[:, 2 * thin :].astype(bf16)
    out_to_other.start()
    weights.wait_recv()
    for i in range(2):
        up_grad_ref[:, pl.ds(i * 2 * own, 2 * own)] = up_ref[2 * chip + i].astype(f32) + up_in[i].astype(f32)
    for i in range(pieces - 1):
        tokens(i)
    to_beside(0).wait_recv()
    for k in (1, 2, 3):
        to_line(k).wait_recv()
    summed = cols[0, near].astype(f32) + cols_in[0].astype(f32)
    for k in (1, 2, 3):
        summed += line_in[k].astype(f32)
    total[...] = summed.astype(bf16).reshape(total.shape)
    def to_owner(third):
        chunk = 4 * third + me
        return remote(total.at[third], heads_in.at[lax.rem(chunk, 3)], q_send, q_recv, lax.rem(chunk, 3), {"blk": chunk // 3})

    for third in range(3):
        chunk = 4 * third + me

        @pl.when(chunk // 3 != me)
        def _(third=third):
            to_owner(third).start()

        @pl.when(chunk // 3 == me)
        def _(third=third, chunk=chunk):
            heads_in[lax.rem(chunk, 3)] = total[third]

    out_to_other.wait_recv()
    got = out_sum[chip].astype(f32) + out_far[...].astype(f32)
    for i in range(2):
        out_grad_ref[:, pl.ds(i * thin, thin)] = got[:, i * thin : (i + 1) * thin].T
    tokens(pieces - 1)
    for i in range(2):
        line_sum = jnp.sum(sums[pl.ds(8 * i, 8), :], 0, keepdims=True)
        for k in range(8):
            part[k, pl.ds(4 * i, 1), :] = line_sum[:, k * thin : (k + 1) * thin]

    def to_dp(k):
        target = lax.rem(place + k, 8)
        return remote(part.at[target], part_in.at[k], s_send, s_recv, k, {"dp": target})

    def to_blk(k):
        return remote(both, both_in.at[k], b_send, b_recv, k, {"blk": (twin, other, last)[k]})

    for k in range(1, 8):
        to_dp(k).start()
    for s in range(3):
        source = lax.rem(3 * me + s, 4)

        @pl.when(source != me)
        def _(s=s):
            remote(total.at[0], heads_in.at[s], q_send, q_recv, s, {"blk": twin}).wait_recv()

        qkv_ref[:, pl.ds(s * own, own)] = heads_in[s].astype(f32).T
    acc = part[place]
    for k in range(1, 8):
        to_dp(k).wait_recv()
        acc += part_in[k]
    both[...] = acc
    for k in range(3):
        to_blk(k).start()
    for k in range(3):
        to_blk(k).wait_recv()
        acc += both_in[k]
    gain_grad_ref[...] = acc[:4]
    shift_grad_ref[...] = acc[4:8]
    bias_grad_ref[...] = acc[8:12]
    hid_grad_ref[...] = acc[12:]
    for i in range(pieces):
        to_twin(0, i).wait_send()
        to_twin(1, i).wait_send()
        to_other(i).wait_send()
    for k in range(4):
        to_beside(k).wait_send()
    for k in range(1, 4):
        to_line(k).wait_send()
    for third in range(3):

        @pl.when((4 * third + me) // 3 != me)
        def _(third=third):
            to_owner(third).wait_send()

    for k in range(1, 8):
        to_dp(k).wait_send()
    for k in range(3):
        to_blk(k).wait_send()
    weights.wait_send()
    out_to_other.wait_send()
    for k in range(1, 4):
        out_to_line(k).wait_send()


def finish(grads, first_all, own_weight, tokens, grad_middle, norm_gain, up_sum, out_line, sums, sums_three, hidden_bias):
    rows, width = tokens.shape
    total_rows, cols = grads.shape
    own, thin, pieces = width // 4, width // 8, 4
    bf16, f32 = jnp.bfloat16, jnp.float32
    shape, vmem, hbm, dma = jax.ShapeDtypeStruct, pl.BlockSpec(memory_space=pltpu.VMEM), pl.BlockSpec(memory_space=pl.ANY), pltpu.SemaphoreType.DMA
    buffers = [
        ((total_rows, cols), bf16), ((total_rows, width), bf16), ((width, cols), bf16), ((rows, width), bf16), ((rows, width), f32),
        ((cols, total_rows), bf16), ((2, rows, width), bf16), ((2, rows, width), bf16), ((rows, width), bf16), ((rows, width), bf16),
        ((rows, width), f32), ((4, 2, cols, thin), bf16), ((4, cols, thin), bf16), ((4, cols, thin), bf16), ((4, cols, thin), bf16),
        ((3, own, thin), bf16), ((3, own, thin), bf16), ((8, 16, thin), f32), ((8, 16, thin), f32), ((16, thin), f32), ((3, 16, thin), f32),
        ((16, width), f32), ((2,) + up_sum.shape[1:], bf16), ((3,) + out_line.shape[1:], bf16), ((2, thin, own), bf16), ((thin, own), bf16),
    ]
    counts = [8, 2 * pieces, 2 * pieces, pieces, pieces, 4, 4, 4, 4, 3, 3, 8, 8, 3, 3, 2, 2, 3, 3]
    return pl.pallas_call(
        functools.partial(tail_kernel, pieces=pieces),
        in_specs=[hbm] * 5 + [vmem] * 6,
        out_specs=[vmem] * 8,
        out_shape=[shape((rows, width), bf16), shape((thin, 3 * own), f32), shape((thin, width), f32), shape((thin, own), f32)] + [shape((4, thin), f32)] * 4,
        scratch_shapes=[pltpu.VMEM(dims, kind) for dims, kind in buffers] + [dma((n,)) for n in counts],
        compiler_params=pltpu.CompilerParams(collective_id=2, has_side_effects=True, vmem_limit_bytes=58 * 2**20),
        cost_estimate=pl.CostEstimate(flops=60 * rows * width * width, bytes_accessed=2**27, transcendentals=0),
        name="finish",
    )(grads, first_all, own_weight, tokens, grad_middle, norm_gain, up_sum, out_line, sums, sums_three, hidden_bias)


def emit_kernel(token_in, qkv_in, up_in, out_in, down_in, gain_in, shift_in, bias_in, hid_in, token_ref, qkv_ref, up_ref, out_ref, down_ref, gain_ref, shift_ref, bias_ref, hid_ref):
    for src, dst in (
        (token_in, token_ref), (qkv_in, qkv_ref), (up_in, up_ref), (out_in, out_ref),
        (gain_in, gain_ref), (shift_in, shift_ref), (bias_in, bias_ref), (hid_in, hid_ref),
    ):
        dst[...] = src[...]
    down_ref[...] = down_in[...].astype(jnp.float32).T


def emit(token_grad, qkv_grad, up_grad, out_grad, down_grad, gains, shifts, biases, hidden):
    arrays = (token_grad, qkv_grad, up_grad, out_grad, down_grad, gains, shifts, biases, hidden)
    shapes = [jax.ShapeDtypeStruct(a.shape, a.dtype) for a in arrays]
    shapes[4] = jax.ShapeDtypeStruct(down_grad.shape[::-1], jnp.float32)
    return pl.pallas_call(
        emit_kernel,
        in_specs=[pl.BlockSpec(memory_space=pltpu.VMEM)] * 9,
        out_specs=[pl.BlockSpec(memory_space=pltpu.VMEM)] * 9,
        out_shape=shapes,
        compiler_params=pltpu.CompilerParams(vmem_limit_bytes=60 * 2**20),
        name="emit",
    )(*arrays)


def outer_sum(left, right):
    return lax.dot_general(left, right, (((0,), (0,)), ((), ())), preferred_element_type=jnp.float32)


def times_transposed(left, right):
    return lax.dot_general(left, right, NT, preferred_element_type=jnp.float32)


def column_sums(values):
    return jnp.sum(values.astype(jnp.float32), 0)


def exchange(values, axis, bit):
    return lax.ppermute(values, axis, [(i, i ^ bit) for i in range(lax.axis_size(axis))])


def plus(left, right):
    return (left.astype(jnp.float32) + right.astype(jnp.float32)).astype(jnp.bfloat16)


def pick(values, index, axis):
    return lax.dynamic_index_in_dim(values, index, axis, False)


def sum_everywhere(values):
    for axis in ("blk", "dp"):
        bit = 1
        while bit < lax.axis_size(axis):
            values = values + exchange(values, axis, bit)
            bit *= 2
    return values


def far_sum(half):
    line = lax.axis_index("dp") // 2
    parts = lax.axis_size("dp")
    if parts > 8:
        groups = [[d for d in range(parts) if d % 2 == b] for b in range(2)]
        return jnp.sum(lax.all_to_all(half, "dp", 0, 0, axis_index_groups=groups).astype(jnp.float32), 0)
    got = [exchange(pick(half, line ^ step, 0), "dp", 2 * step) for step in range(1, parts // 2)]
    return pick(half, line, 0).astype(jnp.float32) + sum(piece.astype(jnp.float32) for piece in got)


def far_sums(values):
    groups = [[d for d in range(lax.axis_size("dp")) if d % 2 == b] for b in range(2)]
    return lax.psum_scatter(values, "dp", scatter_dimension=0, axis_index_groups=groups, tiled=False)


def by_chip(up):
    return up.reshape((2, 2) + up.shape[1:]).transpose(0, 2, 1, 3).reshape(2, up.shape[1], -1)


def finish_plain(grads, first_all, own_weight, tokens, grad_middle, norm_gain, early, hidden_bias):
    rows, width = tokens.shape
    blocks, parts, me = lax.axis_size("blk"), lax.axis_size("dp"), lax.axis_index("blk")
    core, chip, own = me % 2, me // 2, width // blocks
    by_block = grads.reshape(2, 2, rows, 3 * own)
    away = times_transposed(pick(by_block, 1 - core, 1).reshape(2 * rows, 3 * own), own_weight).astype(jnp.bfloat16)
    got = exchange(away, "blk", 1)
    stay = times_transposed(pick(by_block, core, 1).reshape(2 * rows, 3 * own), own_weight)
    half = plus(stay, got).reshape(2, rows, width)
    half, grads = lax.optimization_barrier((half, grads))
    far = exchange(pick(half, 1 - chip, 0), "blk", 2)

    term = outer_sum(first_all, grads).astype(jnp.bfloat16).reshape(parts // 2, 2, width // parts, 3 * own)
    near = lax.rem(lax.axis_index("dp"), 2)
    term = plus(pick(term, near, 1), exchange(pick(term, 1 - near, 1), "dp", 1))
    qkv_term = far_sum(term).astype(jnp.bfloat16)
    qkv_blocks = lax.all_gather(qkv_term, "blk", axis=0)
    qkv_rows = qkv_blocks.reshape(blocks, -1, 3, own).transpose(1, 2, 0, 3).reshape(-1, 3 * width)
    qkv_grad = lax.dynamic_slice_in_dim(qkv_rows, me * 3 * own, 3 * own, 1).astype(jnp.float32)

    def spread(values):
        return lax.dynamic_update_slice_in_dim(jnp.zeros((width,), jnp.float32), values, me * own, 0)

    y = pick(half, chip, 0).astype(jnp.float32) + far.astype(jnp.float32)
    n, r = _stats(tokens.astype(jnp.float32))
    token_grad = (grad_middle + _pull(n, r, y * norm_gain[0])).astype(jnp.bfloat16)
    late = {0: jnp.sum(y * n, 0), 4: jnp.sum(y, 0), 8: spread(column_sums(grads[:, :own])), 9: spread(column_sums(grads[:, 2 * own :]))}
    small = jnp.stack([late.get(i, early[i]) for i in range(12)] + list(hidden_bias.reshape(-1, width)))
    small = sum_everywhere(small)
    place = lax.axis_index("dp")
    chunk = width // parts
    small_own = lax.dynamic_slice_in_dim(small[:12], place * chunk, chunk, 1)
    hidden = lax.dynamic_slice_in_dim(small[12:].reshape(-1), place * 4 * chunk, 4 * chunk, 0)
    return token_grad, qkv_grad, small_own, hidden


def local(tokens, cotangent, lengths, qkv_weight, out_weight, up_weight, down_weight, norm_gain, norm_bias, proj_bias, ffn_bias):
    rows, width = tokens.shape
    blocks = lax.axis_size("blk")
    parts = lax.axis_size("dp")
    me = lax.axis_index("blk")
    core, chip = me % 2, me // 2
    own = width // blocks

    first_all, qkv, own_weight = gather_project(tokens, qkv_weight, norm_gain, norm_bias, proj_bias)
    attended_own, log_total = attn_fwd(lengths, qkv)

    mixed, mid, n_one, r_one, low, turned, second_t, act, slope, sums_three, attended = ffn_forward(
        tokens, cotangent, attended_own, out_weight, up_weight, down_weight, norm_gain, norm_bias, proj_bias, ffn_bias
    )
    grad_middle, sums, hidden_bias, up_sum, down_sum, out_term, grad_own, out_line = ffn_backward(
        parts, low, turned, second_t, act, slope, up_weight, down_weight, mid, n_one, r_one, cotangent, attended, out_weight, norm_gain
    )
    grads = attn_bwd(lengths, qkv, grad_own, attended_own, log_total)

    if parts == 8:
        down_grad = lax.psum_scatter(down_sum, "dp", scatter_dimension=0, tiled=False)
        token_grad, qkv_grad, up_grad, out_grad, gains, shifts, biases, hidden = finish(
            grads, first_all, own_weight, tokens, grad_middle, norm_gain, up_sum, out_line, sums, sums_three, hidden_bias
        )
        token_grad, qkv_grad, up_grad, out_grad, down_grad, gains, shifts, biases, hidden = emit(
            token_grad, qkv_grad, up_grad, out_grad, down_grad, gains, shifts, biases, hidden
        )
        return (mixed, token_grad, qkv_grad, out_grad, up_grad, down_grad, gains, shifts, biases, hidden.reshape(-1))
    early = [None, sums[0], sums[1], sums_three[0], None, sums[2], sums[3], sums_three[1], None, None, sums[4], sums_three[2]]
    hidden_bias = hidden_bias.reshape(2, 2, 2, -1).transpose(0, 2, 1, 3)
    thin = width // parts
    halves = by_chip(far_sums(up_sum))
    up_grad = pick(halves, chip, 0).astype(jnp.float32) + exchange(pick(halves, 1 - chip, 0), "blk", 2).astype(jnp.float32)
    out_term = out_term.reshape(2, 2, width // 2, width // 2).transpose(1, 2, 0, 3).reshape(2, 2, own, width)
    out_half = plus(out_term[1], exchange(out_term[0], "blk", 1))
    out_sum = plus(pick(out_half, chip, 0), exchange(pick(out_half, 1 - chip, 0), "blk", 2))
    down = down_sum.transpose(1, 0, 2).reshape(own, parts, -1).transpose(1, 0, 2)
    out = out_sum.reshape(own, parts, thin).transpose(1, 0, 2)
    both = lax.psum_scatter(jnp.concatenate([down, out], 2), "dp", scatter_dimension=0, tiled=False).astype(jnp.float32)
    down_grad, out_grad = both[:, : down.shape[2]].T, both[:, down.shape[2] :].T
    token_grad, qkv_grad, small, hidden = finish_plain(grads, first_all, own_weight, tokens, grad_middle, norm_gain, early, hidden_bias)
    return (mixed, token_grad, qkv_grad, out_grad, up_grad, down_grad, small[:4], small[4:8], small[8:], hidden)


def solution(mesh):
    return jax.shard_map(
        local,
        mesh=mesh,
        in_specs=(P(("dp", "blk"), None), P(("dp", "blk"), None), P("dp", None)) + (P(),) * 8,
        out_specs=(P(("dp", "blk"), None), P(("dp", "blk"), None))
        + (P("dp", "blk"),) * 4
        + (P(None, "dp"),) * 3
        + (P("dp"),),
        check_vma=False,
    )
```

```python
import functools

import jax
import jax.numpy as jnp
from jax import lax
from jax.experimental import pallas as pl
from jax.experimental.pallas import tpu as pltpu
from jax.sharding import PartitionSpec as P

epsilon = 1e-05
HD = 64
NT = (((1,), (1,)), ((), ()))
NEG = -1e30
TILE = 256


def _bounds(len_ref, qb):
    l0 = len_ref[0, 0]
    e1 = l0 + len_ref[0, 1]

    def start_of(r):
        return jnp.where(r >= e1, e1, jnp.where(r >= l0, l0, 0))

    first = qb * TILE
    s_first, s_last = start_of(first), start_of(first + TILE - 1)
    kmin = s_first // TILE
    kmid = jnp.maximum(kmin, jnp.minimum(qb, (s_last + TILE - 1) // TILE))
    rows = first + lax.broadcasted_iota(jnp.int32, (1, TILE), 1)
    return kmin, kmid, rows, start_of(rows)


def _walk(len_ref, qb, step, carry, wide):
    kmin, kmid, rows, starts = _bounds(len_ref, qb)

    def run(masked, size):
        def body(kb, carry):
            at = pl.multiple_of(kb * TILE, TILE)
            mask = None
            if masked:
                kpos = at + lax.broadcasted_iota(jnp.int32, (size * TILE, TILE), 0)
                mask = (kpos >= starts) & (kpos <= rows)
            return step(at, size * TILE, mask, carry)

        return body

    for masked, at, left in ((True, kmin, kmid - kmin), (False, kmid, qb - kmid)):
        for size in wide:
            count, body = left // size, run(masked, size)
            carry = lax.fori_loop(0, count, lambda i, c, at=at, size=size, body=body: body(at + i * size, c), carry)
            at, left = at + count * size, left - count * size
    return run(True, 1)(qb, carry)


def _fill_masked(dst, value, heads):
    lane = lax.broadcasted_iota(jnp.int32, value.shape, 1) // HD
    for h in range(heads):
        dst[pl.ds(h * TILE, TILE), :] = jnp.where(lane == h, value, jnp.zeros_like(value))


def fwd_kernel(len_ref, q_ref, k_ref, v_ref, o_ref, lse_ref, qm, acc, ps, vt, *, heads, wide):
    qb = pl.program_id(0)

    @pl.when(qb == 0)
    def _():
        vt[...] = v_ref[...].T

    _fill_masked(qm, q_ref[...] * jnp.bfloat16(0.125), heads)
    acc[...] = jnp.zeros_like(acc)

    def step(at, size, mask, carry):
        keys = pl.ds(at, size)
        scores = [
            lax.dot_general(k_ref[keys, :], qm[pl.ds(h * TILE, TILE), :], NT, preferred_element_type=jnp.float32)
            for h in range(heads)
        ]
        out, fades = [], []
        for h in range(heads):
            m, l = carry[h]
            s = scores[h]
            if mask is not None:
                s = jnp.where(mask, s, NEG)
            top = jnp.maximum(m, jnp.max(s, 0, keepdims=True))
            p = jnp.exp(s - top)
            fade = jnp.exp(m - top)
            ps[pl.ds(0, size), pl.ds(h * TILE, TILE)] = p.astype(jnp.bfloat16)
            out.append((top, l * fade + jnp.sum(p, 0, keepdims=True)))
            fades.append(fade)
        for h in range(heads):
            lanes = pl.ds(h * HD, HD)
            part = jnp.dot(vt[lanes, keys], ps[pl.ds(0, size), pl.ds(h * TILE, TILE)], preferred_element_type=jnp.float32)
            acc[lanes, :] = acc[lanes, :] * fades[h] + part
        return tuple(out)

    carry = tuple((jnp.full((1, TILE), 0.1 * NEG, jnp.float32), jnp.zeros((1, TILE), jnp.float32)) for _ in range(heads))
    carry = _walk(len_ref, qb, step, carry, wide)
    for h in range(heads):
        m, l = carry[h]
        lse_ref[pl.ds(h, 1), :] = m + jnp.log(l)
        acc[pl.ds(h * HD, HD), :] = acc[pl.ds(h * HD, HD), :] / l
    o_ref[...] = acc[...].T.astype(jnp.bfloat16)


def attn_fwd(lengths, qkv, pair=0, lane=256, wide=(2, 1)):
    n = qkv.shape[0]
    heads = lane // HD
    return pl.pallas_call(
        functools.partial(fwd_kernel, heads=heads, wide=wide),
        grid_spec=pltpu.PrefetchScalarGridSpec(
            num_scalar_prefetch=1,
            grid=(n // TILE,),
            in_specs=[
                pl.BlockSpec((TILE, lane), lambda i, L: (i, 3 * pair)),
                pl.BlockSpec((n, lane), lambda i, L: (0, 3 * pair + 1)),
                pl.BlockSpec((n, lane), lambda i, L: (0, 3 * pair + 2)),
            ],
            out_specs=[pl.BlockSpec((TILE, lane), lambda i, L: (i, 0)), pl.BlockSpec((heads, TILE), lambda i, L: (0, i))],
            scratch_shapes=[
                pltpu.VMEM((heads * TILE, lane), jnp.bfloat16),
                pltpu.VMEM((lane, TILE), jnp.float32),
                pltpu.VMEM((wide[0] * TILE, heads * TILE), jnp.bfloat16),
                pltpu.VMEM((lane, n), jnp.bfloat16),
            ],
        ),
        out_shape=[jax.ShapeDtypeStruct((n, lane), jnp.bfloat16), jax.ShapeDtypeStruct((heads, n), jnp.float32)],
        compiler_params=pltpu.CompilerParams(vmem_limit_bytes=58 * 2**20),
        cost_estimate=pl.CostEstimate(flops=n * n * lane * 9, bytes_accessed=10 * n * lane, transcendentals=n * n * heads // 2),
        name="attn_fwd",
    )(lengths, qkv, qkv, qkv)


def bwd_kernel(len_ref, q_ref, do_ref, o_ref, lse_ref, k_ref, v_ref, d_ref, qm, dom, ps, ds, dqt, dk, dv, kt, *, heads, wide):
    qb = pl.program_id(0)
    c = heads * HD

    @pl.when(qb == 0)
    def _():
        dk[...] = jnp.zeros_like(dk)
        dv[...] = jnp.zeros_like(dv)
        kt[...] = k_ref[...].T

    _fill_masked(qm, q_ref[...] * jnp.bfloat16(0.125), heads)
    _fill_masked(dom, do_ref[...], heads)
    prod = (do_ref[...].astype(jnp.float32) * o_ref[...].astype(jnp.float32)).T
    delta = [jnp.sum(prod[h * HD : (h + 1) * HD], 0, keepdims=True) for h in range(heads)]
    dqt[...] = jnp.zeros_like(dqt)

    def step(at, size, mask, carry):
        keys = pl.ds(at, size)
        used = pl.ds(0, size)
        for h in range(heads):
            mine = pl.ds(h * TILE, TILE)
            s = lax.dot_general(k_ref[keys, :], qm[mine, :], NT, preferred_element_type=jnp.float32)
            p = jnp.exp(s - lse_ref[pl.ds(h, 1), :])
            if mask is not None:
                p = jnp.where(mask, p, 0.0)
            dp = lax.dot_general(v_ref[keys, :], dom[mine, :], NT, preferred_element_type=jnp.float32)
            ps[used, mine] = p.astype(jnp.bfloat16)
            ds[used, mine] = (p * (dp - delta[h])).astype(jnp.bfloat16)
        dv[keys, :] += jnp.dot(ps[used, :], dom[...], preferred_element_type=jnp.float32)
        dk[keys, :] += jnp.dot(ds[used, :], qm[...], preferred_element_type=jnp.float32)
        for h in range(heads):
            lanes = pl.ds(h * HD, HD)
            dqt[lanes, :] += jnp.dot(kt[lanes, keys], ds[used, pl.ds(h * TILE, TILE)], preferred_element_type=jnp.float32)
        return carry

    _walk(len_ref, qb, step, 0, wide)
    d_ref[pl.ds(pl.multiple_of(qb * TILE, TILE), TILE), pl.ds(0, c)] = (dqt[...] * 0.125).T.astype(jnp.bfloat16)

    @pl.when(qb == pl.num_programs(0) - 1)
    def _():
        d_ref[:, pl.ds(c, c)] = dk[...].astype(jnp.bfloat16)
        d_ref[:, pl.ds(2 * c, c)] = dv[...].astype(jnp.bfloat16)


def attn_bwd(lengths, qkv, do, o, lse, pair=0, lane=256, wide=(2, 1)):
    n = qkv.shape[0]
    heads = lane // HD
    row = lambda col: pl.BlockSpec((TILE, lane), lambda i, L: (i, col))
    whole = lambda col: pl.BlockSpec((n, lane), lambda i, L: (0, col))
    return pl.pallas_call(
        functools.partial(bwd_kernel, heads=heads, wide=wide),
        grid_spec=pltpu.PrefetchScalarGridSpec(
            num_scalar_prefetch=1,
            grid=(n // TILE,),
            in_specs=[
                row(3 * pair), row(pair), row(0), pl.BlockSpec((heads, TILE), lambda i, L: (0, i)),
                whole(3 * pair + 1), whole(3 * pair + 2),
            ],
            out_specs=pl.BlockSpec((n, 3 * lane), lambda i, L: (0, pair)),
            scratch_shapes=[
                pltpu.VMEM((heads * TILE, lane), jnp.bfloat16),
                pltpu.VMEM((heads * TILE, lane), jnp.bfloat16),
                pltpu.VMEM((wide[0] * TILE, heads * TILE), jnp.bfloat16),
                pltpu.VMEM((wide[0] * TILE, heads * TILE), jnp.bfloat16),
                pltpu.VMEM((lane, TILE), jnp.float32),
                pltpu.VMEM((n, lane), jnp.float32),
                pltpu.VMEM((n, lane), jnp.float32),
                pltpu.VMEM((lane, n), jnp.bfloat16),
            ],
        ),
        out_shape=jax.ShapeDtypeStruct(qkv.shape, jnp.bfloat16),
        compiler_params=pltpu.CompilerParams(vmem_limit_bytes=58 * 2**20),
        cost_estimate=pl.CostEstimate(flops=n * n * lane * 11, bytes_accessed=20 * n * lane, transcendentals=n * n * heads // 2),
        name="attn_bwd",
    )(lengths, qkv, do, o, lse, qkv, qkv)


def _stats(v):
    c = v - jnp.mean(v, -1, keepdims=True)
    r = lax.rsqrt(jnp.mean(c * c, -1, keepdims=True) + epsilon)
    return c * r, r


def _pull(n, r, e):
    return r * (e - jnp.mean(e, -1, keepdims=True) - n * jnp.mean(e * n, -1, keepdims=True))


def _fold(v):
    return jnp.sum(v.reshape(-1, 8, v.shape[-1]), 0)


def _row(ref, i):
    return ref[pl.ds(i, 1), :]


def _each(total, size, fn):
    def body(i, carry):
        fn(pl.ds(pl.multiple_of(i * size, size), size))
        return carry

    lax.fori_loop(0, total // size, body, 0)


def _turn_blocks(dst, value, core):
    own = dst.shape[0] // 4
    flipped = value.T
    for b in range(4):
        stays = 1 - lax.rem(core + b % 2, 2)
        dst[pl.ds(pl.multiple_of((2 * stays + b // 2) * own, own), own), :] = flipped[b * own : (b + 1) * own, :]


def ffn_kernel(
    x_hbm, cot_hbm, own_hbm, wo_hbm, up_ref, down_ref, gain_ref, shift_ref, bias_ref, fb_ref,
    mixed_ref, mid_out, n_out, r_ref, low_ref, turned_ref, second_out, act_ref, slope_ref, small_ref, att_out,
    x_ref, cot_ref, wo_ref, mid_ref, n_ref, second_t, att_ref, second, branch, ffn, sums, sends, recvs, own_sem, load_sems, save_sems, *, tiles, strip,
):
    s = pl.program_id(0)
    rows, width = x_ref.shape
    f32 = jnp.float32

    def loaded(i):
        return pltpu.make_async_copy((x_hbm, cot_hbm, wo_hbm)[i], (x_ref, cot_ref, wo_ref)[i], load_sems.at[i])

    def saved(i):
        pairs = ((mid_ref, mid_out), (n_ref, n_out), (second_t, second_out), (att_ref, att_out))
        return pltpu.make_async_copy(*pairs[i], save_sems.at[i])

    @pl.when(s == 0)
    def _():
        me = lax.axis_index("blk")
        own = width // 4
        peers = (me + 1 - 2 * lax.rem(me, 2), lax.rem(me + 2, 4), 3 - me)
        mesh_ids = pl.DeviceIdType.MESH
        barrier = pltpu.get_barrier_semaphore()
        for block in peers:
            pl.semaphore_signal(barrier, inc=1, device_id={"blk": block}, device_id_type=mesh_ids)
        pl.semaphore_wait(barrier, 3)

        def rows_of(block):
            return own_hbm.at[pl.ds(pl.multiple_of(block * rows, rows), rows), :]

        here = att_ref.at[:, pl.ds(pl.multiple_of(me * own, own), own)]
        copies = [
            pltpu.make_async_remote_copy(
                src_ref=rows_of(block), dst_ref=here, send_sem=sends.at[i], recv_sem=recvs.at[i],
                device_id={"blk": block}, device_id_type=mesh_ids,
            )
            for i, block in enumerate(peers)
        ]
        for copy in copies[::-1]:
            copy.start()
        mine = pltpu.make_async_copy(rows_of(me), here, own_sem)
        mine.start()
        for i in (2, 0, 1):
            loaded(i).start()
        sums[...] = jnp.zeros_like(sums)
        mine.wait()
        for i in range(3):
            loaded(i).wait()
        for copy in copies:
            copy.wait_send()
            copy.wait_recv()
        saved(3).start()
        branch[...] = jnp.dot(att_ref[...], wo_ref[...], preferred_element_type=f32) + _row(bias_ref, 2)

        def normed(at):
            n, r = _stats(branch[at, :])
            n_ref[at, :] = n.astype(jnp.bfloat16)
            r_ref[at, :] = r
            m = x_ref[at, :].astype(f32) + n * _row(gain_ref, 1) + _row(shift_ref, 1)
            mid_ref[at, :] = m
            n, _ = _stats(m)
            second[at, :] = (n * _row(gain_ref, 2) + _row(shift_ref, 2)).astype(jnp.bfloat16)

        _each(rows, strip, normed)
        second_t[...] = second[...].T
        for i in range(3):
            saved(i).start()

    c1, c3 = 0.7978845608028654, 0.7978845608028654 * 0.044715
    strips = [pl.ds(i * (rows // 2), rows // 2) for i in range(2)]
    us = [jnp.dot(second[at, :], up_ref[...], preferred_element_type=f32) + fb_ref[...] for at in strips]
    parts = []
    for at, u in zip(strips, us):
        sq = u * u
        t = jnp.tanh(u * (c1 + c3 * sq))
        half = 0.5 + 0.5 * t
        a = (u * half).astype(jnp.bfloat16)
        act_ref[at, :] = a
        slope_ref[at, :] = (half + (0.5 * u) * (1.0 - t * t) * (c1 + 3.0 * c3 * sq)).astype(jnp.bfloat16)
        parts.append(jnp.dot(a, down_ref[...], preferred_element_type=f32))

    @pl.when(s == 0)
    def _():
        for at in strips:
            ffn[at, :] = jnp.zeros((rows // 2, width), f32) + _row(bias_ref, 3)

    for at, part in zip(strips, parts):
        ffn[at, :] += part

    @pl.when(s == tiles - 1)
    def _():
        def normed(at):
            n, r = _stats(ffn[at, :])
            y = cot_ref[at, :].astype(f32)
            mixed_ref[at, :] = (mid_ref[at, :] + n * _row(gain_ref, 3) + _row(shift_ref, 3)).astype(jnp.bfloat16)
            g = _pull(n, r, y * _row(gain_ref, 3)).astype(jnp.bfloat16)
            low_ref[at, :] = g
            sums[pl.ds(0, 8), :] += _fold(y * n)
            sums[pl.ds(8, 8), :] += _fold(y)
            sums[pl.ds(16, 8), :] += _fold(g.astype(f32))

        _each(rows, strip, normed)
        _turn_blocks(turned_ref, low_ref[...], lax.rem(lax.axis_index("blk"), 2))
        for i in range(4):
            saved(i).wait()
        for i in range(3):
            small_ref[pl.ds(i, 1), :] = jnp.sum(sums[pl.ds(8 * i, 8), :], 0, keepdims=True)


def _once(*shape):
    return pl.BlockSpec(shape, lambda s: (0,) * len(shape), pipeline_mode=pl.Buffered(1))


def ffn_forward(tokens, cotangent, attended, out_weight, up_weight, down_weight, norm_gain, norm_bias, proj_bias, ffn_bias):
    rows, width = tokens.shape
    hidden = up_weight.shape[1]
    tiles = 8
    hid = hidden // tiles
    bf16, f32 = jnp.bfloat16, jnp.float32
    shape = jax.ShapeDtypeStruct
    return pl.pallas_call(
        functools.partial(ffn_kernel, tiles=tiles, strip=rows // 4),
        grid=(tiles,),
        in_specs=[
            *[pl.BlockSpec(memory_space=pl.ANY)] * 4,
            pl.BlockSpec((width, hid), lambda s: (0, s)), pl.BlockSpec((hid, width), lambda s: (s, 0)),
            _once(4, width), _once(4, width), _once(4, width), pl.BlockSpec((1, hid), lambda s: (0, s)),
        ],
        out_specs=[
            _once(rows, width), *[pl.BlockSpec(memory_space=pl.ANY)] * 2, _once(rows, 1), _once(rows, width),
            _once(width, rows), pl.BlockSpec(memory_space=pl.ANY),
            pl.BlockSpec((rows, hid), lambda s: (0, s)), pl.BlockSpec((rows, hid), lambda s: (0, s)), _once(8, width), pl.BlockSpec(memory_space=pl.ANY),
        ],
        out_shape=[
            shape((rows, width), bf16), shape((rows, width), f32), shape((rows, width), bf16), shape((rows, 1), f32),
            shape((rows, width), bf16), shape((width, rows), bf16), shape((width, rows), bf16),
            shape((rows, hidden), bf16), shape((rows, hidden), bf16), shape((8, width), f32), shape((rows, width), bf16),
        ],
        scratch_shapes=[
            pltpu.VMEM((rows, width), bf16), pltpu.VMEM((rows, width), bf16), pltpu.VMEM((width, width), bf16), pltpu.VMEM((rows, width), f32),
            pltpu.VMEM((rows, width), bf16), pltpu.VMEM((width, rows), bf16), pltpu.VMEM((rows, width), bf16),
            pltpu.VMEM((rows, width), bf16), pltpu.VMEM((rows, width), f32), pltpu.VMEM((rows, width), f32), pltpu.VMEM((24, width), f32), pltpu.SemaphoreType.DMA((3,)), pltpu.SemaphoreType.DMA((3,)), pltpu.SemaphoreType.DMA(()),
            pltpu.SemaphoreType.DMA((3,)), pltpu.SemaphoreType.DMA((4,)),
        ],
        compiler_params=pltpu.CompilerParams(collective_id=3, has_side_effects=True, vmem_limit_bytes=56 * 2**20),
        cost_estimate=pl.CostEstimate(flops=18 * rows * width * width, bytes_accessed=50 * 2**20, transcendentals=rows * hidden),
        name="ffn_forward",
    )(tokens, cotangent, attended, out_weight, up_weight, down_weight, norm_gain, norm_bias, proj_bias, ffn_bias.reshape(1, -1))


def grads_kernel(
    low_ref, turned_hbm, second_hbm, act_ref, slope_ref, up_ref, down_ref, mid_hbm, n_hbm, r_ref, cot_hbm, att_hbm, wo_hbm, gain_ref,
    gmid_ref, small_ref, hid_ref, up_out, down_out, out_out, gown_out, out_line,
    turned_ref, second_t, cot_ref, att_ref, wo_ref, pre, gs, low, turned, gatt, sums, up_buf, up_in, up_y, down_send, down_keep, down_in, down_x, up_z,
    up_core, up_core_in, up_far, up_far_in, down_core, down_core_in, down_far, down_far_in, up_done, down_done, own_sems, gatt_sends, gatt_recvs, line_sends, line_recvs, save_sems, *, tiles, strip, fold,
):
    s = pl.program_id(0)
    rows, width = low_ref.shape
    own = width // 4
    f32, bf16 = jnp.float32, jnp.bfloat16
    pair, side = s // 2, lax.rem(s, 2)
    me, place = lax.axis_index("blk"), lax.axis_index("dp")
    core, chip, near = lax.rem(me, 2), me // 2, lax.rem(place, 2)
    line = place // 2
    twin, other, beside = {"blk": me + 1 - 2 * core}, {"blk": lax.rem(me + 2, 4)}, {"dp": place + 1 - 2 * near}
    last = {"blk": 3 - me}
    half = tiles // 2
    mesh_ids = pl.DeviceIdType.MESH

    def remote(src, dst, sends, recvs, i, target):
        return pltpu.make_async_remote_copy(
            src_ref=src, dst_ref=dst, send_sem=sends.at[i], recv_sem=recvs.at[i], device_id=target, device_id_type=mesh_ids
        )

    def up_to_twin(p):
        return remote(up_buf.at[0], up_in.at[p], up_core, up_core_in, p, twin)

    def up_to_beside(p):
        return remote(up_in.at[p, :, 1 - near], up_y.at[p], up_far, up_far_in, p, beside)

    def down_to_twin(u, slot):
        return remote(down_send.at[slot], down_in.at[lax.rem(u, 4)], down_core, down_core_in, u, twin)

    def down_to_other(u):
        return remote(down_keep.at[u, 1 - chip], down_x.at[u], down_far, down_far_in, u, other)

    def up_result(p):
        if fold:
            return pltpu.make_async_copy(up_y.at[p, line], up_out.at[p], up_done.at[p])
        return pltpu.make_async_copy(up_y.at[p], up_out.at[:, p], up_done.at[p])

    def up_to_line(p, k):
        ahead = lax.rem(line + k, 4)
        return remote(up_y.at[p, ahead], up_z.at[k - 1, p], line_sends, line_recvs, 3 * p + k - 1, {"dp": 2 * ahead + near})

    def join_line(p):
        total = up_y[p, line].astype(f32)
        for k in range(1, 4):
            up_to_line(p, k).wait_recv()
            total += up_z[k - 1, p].astype(f32)
        up_y[p, line] = total.astype(bf16)
        up_result(p).start()

    def down_result(u):
        tile = 4 * (u // 4) + 2 * lax.rem(u, 2) + lax.rem(u // 2, 2)
        return pltpu.make_async_copy(down_x.at[u], down_out.at[tile], down_done.at[u])

    def saved(i):
        pairs = ((mid_hbm, gmid_ref), (n_hbm, low), (cot_hbm, cot_ref), (att_hbm, att_ref), (wo_hbm, wo_ref), (turned_hbm, turned_ref), (second_hbm, second_t))
        return pltpu.make_async_copy(*pairs[i], save_sems.at[i])

    def out_line_result():
        return pltpu.make_async_copy(up_y.at[half], out_line, own_sems.at[0])

    def out_result(i):
        return pltpu.make_async_copy(up_buf.at[i], out_out.at[i], own_sems.at[2 + i])

    def columns_to(i):
        target = (last, other, twin)[i]
        block = target["blk"]
        src = gatt.at[:, pl.ds(pl.multiple_of(block * own, own), own)]
        dst = gown_out.at[pl.ds(pl.multiple_of(me * rows, rows), rows), :]
        return remote(src, dst, gatt_sends, gatt_recvs, i, target)

    def columns_here():
        src = gatt.at[:, pl.ds(pl.multiple_of(me * own, own), own)]
        return pltpu.make_async_copy(src, gown_out.at[pl.ds(pl.multiple_of(me * rows, rows), rows), :], own_sems.at[4])

    def join_up(p):
        up_to_twin(p).wait_recv()
        up_in[p] = (up_in[p].astype(f32) + up_buf[1].astype(f32)).astype(bf16)
        up_to_beside(p).start()

    def join_far_up(p):
        up_to_beside(p).wait_recv()
        up_y[p] = (up_y[p].astype(f32) + up_in[p, :, near].astype(f32)).astype(bf16)
        if fold:
            for k in range(1, 4):
                up_to_line(p, k).start()
        else:
            up_result(p).start()

    def join_down(u):
        down_to_twin(u, 0).wait_recv()
        down_keep[u] = (down_keep[u].astype(f32) + down_in[lax.rem(u, 4)].astype(f32)).astype(bf16)
        down_to_other(u).start()

    def join_far_down(u):
        down_to_other(u).wait_recv()
        down_x[u] = (down_x[u].astype(f32) + down_keep[u, chip].astype(f32)).astype(bf16)
        down_result(u).start()

    @pl.when(s == 0)
    def _():
        barrier = pltpu.get_barrier_semaphore()
        for target in (twin, other, beside, last):
            pl.semaphore_signal(barrier, inc=1, device_id=target, device_id_type=mesh_ids)
        sums[...] = jnp.zeros_like(sums)
        for i in (5, 6, 0, 1, 2, 3, 4):
            saved(i).start()
        for i in range(1, 4 if fold else 1):
            ahead = lax.rem(line + i, 4)
            pl.semaphore_signal(barrier, inc=1, device_id={"dp": 2 * ahead + near}, device_id_type=mesh_ids)
        pl.semaphore_wait(barrier, 7 if fold else 4)

    @pl.when(s >= 4)
    def _():
        join_far_down(s - 4)

    @pl.when((s == 5) | (s == 7))
    def _():
        join_far_up((s - 5) // 2)

    g = lax.dot_general(low_ref[...], down_ref[...], NT, preferred_element_type=f32) * slope_ref[...].astype(f32)
    g = g.astype(bf16)
    pre[...] = g
    hid_ref[pl.ds(s, 1)] = jnp.sum(g.astype(f32), 0, keepdims=True)[None]
    part = lax.dot_general(g, up_ref[...], NT, preferred_element_type=f32)

    @pl.when(s == 0)
    def _():
        gs[...] = part

    @pl.when(s > 0)
    def _():
        gs[...] += part

    @pl.when(s == 0)
    def _():
        saved(5).wait()
        saved(6).wait()

    down_grad = jnp.dot(turned_ref[...], act_ref[...], preferred_element_type=f32).astype(bf16)

    @pl.when(s >= 2)
    def _():
        down_to_twin(s - 2, side).wait_send()

    down_send[side] = down_grad[: width // 2].reshape(2, own, -1)
    down_to_twin(s, side).start()
    down_keep[s] = down_grad[width // 2 :].reshape(2, own, -1)

    @pl.when(s > 0)
    def _():
        join_down(s - 1)

    @pl.when((side == 0) & (s > 0))
    def _():
        join_up(pair - 1)

    up_grad = jnp.dot(second_t[...], pre[...], preferred_element_type=f32).astype(bf16).reshape(up_buf.shape[1:])

    @pl.when(side == core)
    def _():
        up_buf[1] = up_grad

    @pl.when(side != core)
    def _():
        @pl.when(pair > 0)
        def _():
            up_to_twin(pair - 1).wait_send()

        up_buf[0] = up_grad
        up_to_twin(pair).start()

    @pl.when(s == tiles - 1)
    def _():
        def normed(at):
            n, r = _stats(gmid_ref[at, :])
            y = gs[at, :]
            gm = cot_ref[at, :].astype(f32) + _pull(n, r, y * _row(gain_ref, 2))
            gmid_ref[at, :] = gm
            sums[pl.ds(8, 8), :] += _fold(y * n)
            sums[pl.ds(24, 8), :] += _fold(y)
            n, r = low[at, :].astype(f32), r_ref[at, :]
            g = _pull(n, r, gm * _row(gain_ref, 1)).astype(bf16)
            low[at, :] = g
            sums[pl.ds(0, 8), :] += _fold(gm * n)
            sums[pl.ds(16, 8), :] += _fold(gm)
            sums[pl.ds(32, 8), :] += _fold(g.astype(f32))

        for i in range(5):
            saved(i).wait()
        _each(rows, strip, normed)
        join_down(tiles - 1)
        join_up(half - 1)
        gatt[...] = lax.dot_general(low[...], wo_ref[...], NT, preferred_element_type=f32).astype(bf16)
        for i in range(3):
            columns_to(i).start()
        columns_here().start()
        join_far_up(2)
        _turn_blocks(turned, low[...], core)
        grad = jnp.dot(turned[...], att_ref[...], preferred_element_type=f32).astype(bf16)
        up_to_twin(half - 1).wait_send()
        if fold:
            thin = width // 8
            for d in range(8):
                for b in range(8):
                    piece = grad[b * thin : (b + 1) * thin, d * thin : (d + 1) * thin]
                    up_buf[b // 4, d // 2, d % 2, :, pl.ds(b % 4 * thin, thin)] = piece
            up_to_twin(half).start()
        else:
            for i in range(2):
                up_buf[i] = grad[:, i * width // 2 : (i + 1) * width // 2].reshape(up_buf.shape[1:])
                out_result(i).start()
        for i in range(5):
            small_ref[pl.ds(i, 1), :] = jnp.sum(sums[pl.ds(8 * i, 8), :], 0, keepdims=True)
        if fold:
            join_up(half)
        join_far_up(3)
        for u in range(tiles - 4, tiles):
            join_far_down(u)
        if fold:
            for p in range(half):
                join_line(p)
            up_to_beside(half).wait_recv()
            up_y[half] = (up_y[half].astype(f32) + up_in[half, :, near].astype(f32)).astype(bf16)
            out_line_result().start()
            out_line_result().wait()
        down_to_twin(tiles - 2, 0).wait_send()
        down_to_twin(tiles - 1, 1).wait_send()
        if fold:
            up_to_twin(half).wait_send()
        else:
            out_result(0).wait()
            out_result(1).wait()
        for p in range(half + fold):
            up_to_beside(p).wait_send()
        for p in range(half):
            up_result(p).wait()
            for i in range(1, 4 if fold else 1):
                up_to_line(p, i).wait_send()
        for u in range(tiles):
            down_to_other(u).wait_send()
            down_result(u).wait()
        for i in range(3):
            columns_to(i).wait_send()
            columns_to(i).wait_recv()
        columns_here().wait()


def ffn_backward(parts, low, turned, second_t, act, slope, up_weight, down_weight, mid, n_one, r_one, cotangent, attended, out_weight, norm_gain):
    rows, width = low.shape
    hidden = up_weight.shape[1]
    tiles, own = 8, width // 4
    hid = hidden // tiles
    bf16, f32 = jnp.bfloat16, jnp.float32
    shape = jax.ShapeDtypeStruct
    tile_of = lambda s: 4 * (s // 4) + 2 * lax.rem(s, 2) + lax.rem(s // 2, 2)
    thin = (parts // 2, 2, width // parts, hid)
    dma = pltpu.SemaphoreType.DMA
    half = tiles // 2
    fold = int(parts == 8)
    return pl.pallas_call(
        functools.partial(grads_kernel, tiles=tiles, strip=rows // 4, fold=fold),
        grid=(tiles,),
        in_specs=[
            _once(rows, width), pl.BlockSpec(memory_space=pl.ANY), pl.BlockSpec(memory_space=pl.ANY),
            pl.BlockSpec((rows, hid), lambda s: (0, tile_of(s))), pl.BlockSpec((rows, hid), lambda s: (0, tile_of(s))),
            pl.BlockSpec((width, hid), lambda s: (0, tile_of(s))), pl.BlockSpec((hid, width), lambda s: (tile_of(s), 0)),
            pl.BlockSpec(memory_space=pl.ANY), pl.BlockSpec(memory_space=pl.ANY), _once(rows, 1), *[pl.BlockSpec(memory_space=pl.ANY)] * 3, _once(4, width),
        ],
        out_specs=[
            _once(rows, width), _once(8, width), _once(tiles, 1, hid),
            *[pl.BlockSpec(memory_space=pl.ANY)] * 5,
        ],
        out_shape=[
            shape((rows, width), f32),
            shape((8, width), f32), shape((tiles, 1, hid), f32),
            shape((half, width // parts, hid) if fold else (parts // 2, half, width // parts, hid), bf16), shape((tiles, own, hid), bf16), shape((2,) + thin, bf16),
            shape((4 * rows, own), bf16), shape((parts // 2, width // parts, hid), bf16),
        ],
        scratch_shapes=[
            pltpu.VMEM((width, rows), bf16), pltpu.VMEM((width, rows), bf16), pltpu.VMEM((rows, width), bf16), pltpu.VMEM((rows, width), bf16),
            pltpu.VMEM((width, width), bf16), pltpu.VMEM((rows, hid), bf16), pltpu.VMEM((rows, width), f32), pltpu.VMEM((rows, width), bf16), pltpu.VMEM((width, rows), bf16), pltpu.VMEM((rows, width), bf16),
            pltpu.VMEM((40, width), f32),
            pltpu.VMEM((2,) + thin, bf16), pltpu.VMEM((half + fold,) + thin, bf16), pltpu.VMEM((half + fold, parts // 2, width // parts, hid), bf16),
            pltpu.VMEM((2, 2, own, hid), bf16), pltpu.VMEM((tiles, 2, own, hid), bf16), pltpu.VMEM((4, 2, own, hid), bf16),
            pltpu.VMEM((tiles, own, hid), bf16), pltpu.VMEM((3, half, width // parts, hid), bf16),
            *[dma((half + fold,))] * 4, *[dma((tiles,))] * 4, dma((half + fold,)), dma((tiles,)), dma((5,)), dma((3,)), dma((3,)), dma((3 * half,)), dma((3 * half,)), dma((7,)),
        ],
        compiler_params=pltpu.CompilerParams(collective_id=1, has_side_effects=True, vmem_limit_bytes=60 * 2**20),
        name="ffn_backward",
    )(low, turned, second_t, act, slope, up_weight, down_weight, mid, n_one, r_one, cotangent, attended, out_weight, norm_gain)


def project_kernel(
    x_hbm, w_hbm, gain_ref, shift_ref, bias_ref, all_out, qkv_out, w_out, x_ref, all_ref, qkv_ref, w_ref, x_sems, out_sems, w_sems, chip_send, chip_recv, core_send, core_recv, pass_send, pass_recv, *, pieces,
):
    me = lax.axis_index("blk")
    core = lax.rem(me, 2)
    twin, other, last = me + 1 - 2 * core, lax.rem(me + 2, 4), 3 - me
    rows, width = x_ref.shape
    own = width // 4
    size = rows // pieces
    fetch = [pltpu.make_async_copy(x_hbm.at[pl.ds(i * size, size), :], x_ref.at[pl.ds(i * size, size), :], x_sems.at[i]) for i in range(pieces)]
    for copy in fetch:
        copy.start()
    barrier = pltpu.get_barrier_semaphore()
    for target in (twin, other):
        pl.semaphore_signal(barrier, inc=1, device_id={"blk": target}, device_id_type=pl.DeviceIdType.MESH)
    loads = []
    for third in range(3):
        columns = pl.ds(pl.multiple_of(third * width + me * own, own), own)
        load = pltpu.make_async_copy(w_hbm.at[:, columns], w_ref.at[:, pl.ds(third * own, own)], w_sems.at[third])
        load.start()
        loads.append(load)

    def at(block, i):
        return pl.ds(pl.multiple_of(block * rows + i * size, size), size)

    def send(block, i, target, sends, recvs):
        piece = all_ref.at[at(block, i), :]
        copy = pltpu.make_async_remote_copy(
            src_ref=piece, dst_ref=piece, send_sem=sends.at[i], recv_sem=recvs.at[i],
            device_id={"blk": target}, device_id_type=pl.DeviceIdType.MESH,
        )
        return copy

    def project(block, i):
        where = at(block, i)
        got = jnp.dot(all_ref[where, :], w_ref[...], preferred_element_type=jnp.float32)
        for third in range(3):
            part = got[:, third * own : (third + 1) * own]
            if third != 1:
                part = part + bias_ref[pl.ds(third // 2, 1), pl.ds(pl.multiple_of(me * own, own), own)]
            qkv_ref[where, pl.ds(third * own, own)] = part.astype(jnp.bfloat16)
        for src, dst in ((all_ref, all_out), (qkv_ref, qkv_out)):
            copy = pltpu.make_async_copy(src.at[where, :], dst.at[where, :], out_sems.at[len(saved)])
            copy.start()
            saved.append(copy)

    sent, saved = [], []
    for i in range(pieces):
        fetch[i].wait()
        n, _ = _stats(x_ref[pl.ds(i * size, size), :].astype(jnp.float32))
        all_ref[at(me, i), :] = (n * gain_ref[pl.ds(0, 1), :] + shift_ref[pl.ds(0, 1), :]).astype(jnp.bfloat16)
        if i == 0:
            pl.semaphore_wait(barrier, 2)
        for target, sends, recvs in ((other, chip_send, chip_recv), (twin, core_send, core_recv)):
            copy = send(me, i, target, sends, recvs)
            copy.start()
            sent.append(copy)
    for load in loads:
        load.wait()
    keep = pltpu.make_async_copy(w_ref, w_out, w_sems.at[3])
    keep.start()
    for i in range(pieces):
        project(me, i)
    for i in range(pieces):
        send(twin, i, twin, core_send, core_recv).wait_recv()
        project(twin, i)
    for i in range(pieces):
        send(other, i, other, chip_send, chip_recv).wait_recv()
        copy = send(other, i, twin, pass_send, pass_recv)
        copy.start()
        sent.append(copy)
        project(other, i)
        if i > 0:
            send(last, i - 1, twin, pass_send, pass_recv).wait_recv()
            project(last, i - 1)
    send(last, pieces - 1, twin, pass_send, pass_recv).wait_recv()
    project(last, pieces - 1)
    for copy in sent:
        copy.wait_send()
    for copy in saved:
        copy.wait()
    keep.wait()


def gather_project(tokens, qkv_weight, norm_gain, norm_bias, proj_bias):
    rows, width = tokens.shape
    pieces = 4
    vmem, hbm = pl.BlockSpec(memory_space=pltpu.VMEM), pl.BlockSpec(memory_space=pl.ANY)
    dma = pltpu.SemaphoreType.DMA((pieces,))
    return pl.pallas_call(
        functools.partial(project_kernel, pieces=pieces),
        in_specs=[hbm, hbm, vmem, vmem, vmem],
        out_specs=[hbm] * 3,
        out_shape=[jax.ShapeDtypeStruct((4 * rows, width), jnp.bfloat16), jax.ShapeDtypeStruct((4 * rows, 3 * width // 4), jnp.bfloat16), jax.ShapeDtypeStruct((width, 3 * width // 4), jnp.bfloat16)],
        scratch_shapes=[
            pltpu.VMEM((rows, width), jnp.bfloat16), pltpu.VMEM((4 * rows, width), jnp.bfloat16),
            pltpu.VMEM((4 * rows, 3 * width // 4), jnp.bfloat16), pltpu.VMEM((width, 3 * width // 4), jnp.bfloat16),
            dma, pltpu.SemaphoreType.DMA((8 * pieces,)), pltpu.SemaphoreType.DMA((4,)),
        ] + [dma] * 6,
        compiler_params=pltpu.CompilerParams(collective_id=0, has_side_effects=True, vmem_limit_bytes=60 * 2**20),
        name="gather_project",
    )(tokens, qkv_weight, norm_gain, norm_bias, proj_bias)


def tail_kernel(
    d_hbm, first_hbm, w_hbm, x_hbm, gmid_hbm, gain_ref, up_ref, out_ref, sums_ref, three_ref, hid_ref,
    token_ref, qkv_ref, up_grad_ref, out_grad_ref, gain_grad_ref, shift_grad_ref, bias_grad_ref, hid_grad_ref,
    d, first, w, x, gmid, turned, core_out, core_in, far_out, far_in, mine, cols, cols_in, line_out, line_in, total, heads_in, part, part_in, both, both_in, sums, up_in, out_in, out_sum, out_far,
    loads, core_send, core_recv, far_send, far_recv, y_send, y_recv, z_send, z_recv, q_send, q_recv, s_send, s_recv, b_send, b_recv, h_send, h_recv, o_send, o_recv, *, pieces,
):
    f32, bf16 = jnp.float32, jnp.bfloat16
    rows, width = x.shape
    own = width // 4
    size = rows // pieces
    thin = width // 8
    me, place = lax.axis_index("blk"), lax.axis_index("dp")
    core, near, line = lax.rem(me, 2), lax.rem(place, 2), place // 2
    twin, other, last = me + 1 - 2 * core, lax.rem(me + 2, 4), 3 - me
    mesh_ids = pl.DeviceIdType.MESH

    def remote(src, dst, sends, recvs, i, target):
        return pltpu.make_async_remote_copy(
            src_ref=src, dst_ref=dst, send_sem=sends.at[i], recv_sem=recvs.at[i], device_id=target, device_id_type=mesh_ids
        )

    def rows_of(block, i):
        return pl.ds(pl.multiple_of(block * rows + i * size, size), size)

    def piece(i):
        return pl.ds(i * size, size)

    barrier = pltpu.get_barrier_semaphore()
    for block in (twin, other, last):
        pl.semaphore_signal(barrier, inc=1, device_id={"blk": block}, device_id_type=mesh_ids)
    for k in range(1, 8):
        pl.semaphore_signal(barrier, inc=1, device_id={"dp": lax.rem(place + k, 8)}, device_id_type=mesh_ids)

    def block_rows(block):
        return pl.ds(pl.multiple_of(block * rows, rows), rows)

    fetch = [pltpu.make_async_copy(w_hbm, w, loads.at[0])]
    for i, block in enumerate((last, other, me, twin)):
        fetch.append(pltpu.make_async_copy(d_hbm.at[block_rows(block), :], d.at[block_rows(block), :], loads.at[1 + i]))
    for i, (src, dst) in enumerate(((first_hbm, first), (x_hbm, x), (gmid_hbm, gmid))):
        fetch.append(pltpu.make_async_copy(src, dst, loads.at[5 + i]))
    for copy in fetch[:3]:
        copy.start()

    def partial(block, i):
        return lax.dot_general(d[rows_of(block, i), :], w[...], NT, preferred_element_type=f32)

    def to_twin(kind, i):
        return remote(core_out.at[kind, piece(i), :], core_in.at[kind, piece(i), :], core_send, core_recv, kind * pieces + i, {"blk": twin})

    def to_other(i):
        return remote(far_out.at[piece(i), :], far_in.at[piece(i), :], far_send, far_recv, i, {"blk": other})

    def to_beside(k):
        return remote(cols.at[k, 1 - near], cols_in.at[k], y_send, y_recv, k, {"dp": place + 1 - 2 * near})

    def to_line(k):
        return remote(line_out.at[k], line_in.at[k], z_send, z_recv, k, {"dp": 2 * lax.rem(line + k, 4) + near})

    pl.semaphore_wait(barrier, 10)
    chip = me // 2
    weights = remote(up_ref.at[pl.ds(2 * (1 - chip), 2)], up_in, h_send, h_recv, 0, {"blk": other})
    weights.start()

    def out_to_line(k):
        ahead = lax.rem(line + k, 4)
        return remote(out_ref.at[ahead], out_in.at[k - 1], o_send, o_recv, k - 1, {"dp": 2 * ahead + near})

    out_to_other = remote(out_sum.at[1 - chip], out_far, h_send, h_recv, 1, {"blk": other})
    for k in range(1, 4):
        out_to_line(k).start()
    fetch[0].wait()
    fetch[1].wait()
    for copy in fetch[3:]:
        copy.start()
    for i in range(pieces):
        core_out[0, piece(i), :] = partial(last, i).astype(bf16)
        to_twin(0, i).start()
    fetch[2].wait()
    for i in range(pieces):
        got = partial(other, i)
        to_twin(0, i).wait_recv()
        far_out[piece(i), :] = (got + core_in[0, piece(i), :].astype(f32)).astype(bf16)
        to_other(i).start()
    fetch[3].wait()
    fetch[4].wait()
    for i in range(d.shape[0] // 256):
        turned[:, pl.ds(i * 256, 256)] = d[pl.ds(i * 256, 256), :].T
    fetch[5].wait()
    for k in (1, 2, 3, 0):
        where = pl.ds(pl.multiple_of(lax.rem(line + k, 4) * 2 * thin, 2 * thin), 2 * thin)
        got = jnp.dot(turned[...], first[:, where], preferred_element_type=f32).astype(bf16)
        cols[k, 0] = got[:, :thin]
        cols[k, 1] = got[:, thin:]
        to_beside(k).start()
    for i in range(pieces):
        core_out[1, piece(i), :] = partial(twin, i).astype(bf16)
        to_twin(1, i).start()
    for i in range(pieces):
        mine[piece(i), :] = partial(me, i)
    ones = jnp.ones((8, d.shape[0]), bf16)
    column = jnp.dot(ones, d[...], preferred_element_type=f32)
    part[...] = jnp.zeros_like(part)
    for k in range(8):
        lanes = pl.ds(k * thin, thin)
        for i, (ref, j) in ((1, (sums_ref, 0)), (2, (sums_ref, 1)), (3, (three_ref, 0)), (5, (sums_ref, 2)), (6, (sums_ref, 3)), (7, (three_ref, 1)), (10, (sums_ref, 4)), (11, (three_ref, 2))):
            part[k, pl.ds(i, 1), :] = ref[pl.ds(j, 1), lanes]
        tile = 4 * (k // 4) + 2 * (k % 2) + k // 2 % 2
        for i in range(4):
            part[tile, pl.ds(12 + i, 1), :] = hid_ref[k, :, pl.ds(i * thin, thin)]
    for h in range(2):
        part[2 * me + h, pl.ds(8, 1), :] = column[:1, h * thin : (h + 1) * thin]
        part[2 * me + h, pl.ds(9, 1), :] = column[:1, 2 * own + h * thin : 2 * own + (h + 1) * thin]
    fetch[6].wait()
    fetch[7].wait()
    sums[...] = jnp.zeros_like(sums)

    def tokens(i):
        at = piece(i)
        to_twin(1, i).wait_recv()
        n, r = _stats(x[at, :].astype(f32))
        got = mine[at, :] + core_in[1, at, :].astype(f32)
        to_other(i).wait_recv()
        y = got + far_in[at, :].astype(f32)
        token_ref[at, :] = (gmid[at, :] + _pull(n, r, y * _row(gain_ref, 0))).astype(bf16)
        sums[pl.ds(0, 8), :] += _fold(y * n)
        sums[pl.ds(8, 8), :] += _fold(y)

    for k in (1, 2, 3):
        to_beside(k).wait_recv()
        line_out[k] = (cols[k, near].astype(f32) + cols_in[k].astype(f32)).astype(bf16)
        to_line(k).start()
    for k in range(1, 4):
        out_to_line(k).wait_recv()
    got = out_ref[line].astype(f32)
    for k in range(3):
        got += out_in[k].astype(f32)
    out_sum[0] = got[:, : 2 * thin].astype(bf16)
    out_sum[1] = got[:, 2 * thin :].astype(bf16)
    out_to_other.start()
    weights.wait_recv()
    for i in range(2):
        up_grad_ref[:, pl.ds(i * 2 * own, 2 * own)] = up_ref[2 * chip + i].astype(f32) + up_in[i].astype(f32)
    for i in range(pieces - 1):
        tokens(i)
    to_beside(0).wait_recv()
    for k in (1, 2, 3):
        to_line(k).wait_recv()
    summed = cols[0, near].astype(f32) + cols_in[0].astype(f32)
    for k in (1, 2, 3):
        summed += line_in[k].astype(f32)
    total[...] = summed.astype(bf16).reshape(total.shape)
    def to_owner(third):
        chunk = 4 * third + me
        return remote(total.at[third], heads_in.at[lax.rem(chunk, 3)], q_send, q_recv, lax.rem(chunk, 3), {"blk": chunk // 3})

    for third in range(3):
        chunk = 4 * third + me

        @pl.when(chunk // 3 != me)
        def _(third=third):
            to_owner(third).start()

        @pl.when(chunk // 3 == me)
        def _(third=third, chunk=chunk):
            heads_in[lax.rem(chunk, 3)] = total[third]

    out_to_other.wait_recv()
    got = out_sum[chip].astype(f32) + out_far[...].astype(f32)
    for i in range(2):
        out_grad_ref[:, pl.ds(i * thin, thin)] = got[:, i * thin : (i + 1) * thin].T
    tokens(pieces - 1)
    for i in range(2):
        line_sum = jnp.sum(sums[pl.ds(8 * i, 8), :], 0, keepdims=True)
        for k in range(8):
            part[k, pl.ds(4 * i, 1), :] = line_sum[:, k * thin : (k + 1) * thin]

    def to_dp(k):
        target = lax.rem(place + k, 8)
        return remote(part.at[target], part_in.at[k], s_send, s_recv, k, {"dp": target})

    def to_blk(k):
        return remote(both, both_in.at[k], b_send, b_recv, k, {"blk": (twin, other, last)[k]})

    for k in range(1, 8):
        to_dp(k).start()
    for s in range(3):
        source = lax.rem(3 * me + s, 4)

        @pl.when(source != me)
        def _(s=s):
            remote(total.at[0], heads_in.at[s], q_send, q_recv, s, {"blk": twin}).wait_recv()

        qkv_ref[:, pl.ds(s * own, own)] = heads_in[s].astype(f32).T
    acc = part[place]
    for k in range(1, 8):
        to_dp(k).wait_recv()
        acc += part_in[k]
    both[...] = acc
    for k in range(3):
        to_blk(k).start()
    for k in range(3):
        to_blk(k).wait_recv()
        acc += both_in[k]
    gain_grad_ref[...] = acc[:4]
    shift_grad_ref[...] = acc[4:8]
    bias_grad_ref[...] = acc[8:12]
    hid_grad_ref[...] = acc[12:]
    for i in range(pieces):
        to_twin(0, i).wait_send()
        to_twin(1, i).wait_send()
        to_other(i).wait_send()
    for k in range(4):
        to_beside(k).wait_send()
    for k in range(1, 4):
        to_line(k).wait_send()
    for third in range(3):

        @pl.when((4 * third + me) // 3 != me)
        def _(third=third):
            to_owner(third).wait_send()

    for k in range(1, 8):
        to_dp(k).wait_send()
    for k in range(3):
        to_blk(k).wait_send()
    weights.wait_send()
    out_to_other.wait_send()
    for k in range(1, 4):
        out_to_line(k).wait_send()


def finish(grads, first_all, own_weight, tokens, grad_middle, norm_gain, up_sum, out_line, sums, sums_three, hidden_bias):
    rows, width = tokens.shape
    total_rows, cols = grads.shape
    own, thin, pieces = width // 4, width // 8, 4
    bf16, f32 = jnp.bfloat16, jnp.float32
    shape, vmem, hbm, dma = jax.ShapeDtypeStruct, pl.BlockSpec(memory_space=pltpu.VMEM), pl.BlockSpec(memory_space=pl.ANY), pltpu.SemaphoreType.DMA
    buffers = [
        ((total_rows, cols), bf16), ((total_rows, width), bf16), ((width, cols), bf16), ((rows, width), bf16), ((rows, width), f32),
        ((cols, total_rows), bf16), ((2, rows, width), bf16), ((2, rows, width), bf16), ((rows, width), bf16), ((rows, width), bf16),
        ((rows, width), f32), ((4, 2, cols, thin), bf16), ((4, cols, thin), bf16), ((4, cols, thin), bf16), ((4, cols, thin), bf16),
        ((3, own, thin), bf16), ((3, own, thin), bf16), ((8, 16, thin), f32), ((8, 16, thin), f32), ((16, thin), f32), ((3, 16, thin), f32),
        ((16, width), f32), ((2,) + up_sum.shape[1:], bf16), ((3,) + out_line.shape[1:], bf16), ((2, thin, own), bf16), ((thin, own), bf16),
    ]
    counts = [8, 2 * pieces, 2 * pieces, pieces, pieces, 4, 4, 4, 4, 3, 3, 8, 8, 3, 3, 2, 2, 3, 3]
    return pl.pallas_call(
        functools.partial(tail_kernel, pieces=pieces),
        in_specs=[hbm] * 5 + [vmem] * 6,
        out_specs=[vmem] * 8,
        out_shape=[shape((rows, width), bf16), shape((thin, 3 * own), f32), shape((thin, width), f32), shape((thin, own), f32)] + [shape((4, thin), f32)] * 4,
        scratch_shapes=[pltpu.VMEM(dims, kind) for dims, kind in buffers] + [dma((n,)) for n in counts],
        compiler_params=pltpu.CompilerParams(collective_id=2, has_side_effects=True, vmem_limit_bytes=58 * 2**20),
        cost_estimate=pl.CostEstimate(flops=60 * rows * width * width, bytes_accessed=2**27, transcendentals=0),
        name="finish",
    )(grads, first_all, own_weight, tokens, grad_middle, norm_gain, up_sum, out_line, sums, sums_three, hidden_bias)


def emit_kernel(token_in, qkv_in, up_in, out_in, down_in, gain_in, shift_in, bias_in, hid_in, token_ref, qkv_ref, up_ref, out_ref, down_ref, gain_ref, shift_ref, bias_ref, hid_ref):
    for src, dst in (
        (token_in, token_ref), (qkv_in, qkv_ref), (up_in, up_ref), (out_in, out_ref),
        (gain_in, gain_ref), (shift_in, shift_ref), (bias_in, bias_ref), (hid_in, hid_ref),
    ):
        dst[...] = src[...]
    down_ref[...] = down_in[...].astype(jnp.float32).T


def emit(token_grad, qkv_grad, up_grad, out_grad, down_grad, gains, shifts, biases, hidden):
    arrays = (token_grad, qkv_grad, up_grad, out_grad, down_grad, gains, shifts, biases, hidden)
    shapes = [jax.ShapeDtypeStruct(a.shape, a.dtype) for a in arrays]
    shapes[4] = jax.ShapeDtypeStruct(down_grad.shape[::-1], jnp.float32)
    return pl.pallas_call(
        emit_kernel,
        in_specs=[pl.BlockSpec(memory_space=pltpu.VMEM)] * 9,
        out_specs=[pl.BlockSpec(memory_space=pltpu.VMEM)] * 9,
        out_shape=shapes,
        compiler_params=pltpu.CompilerParams(vmem_limit_bytes=60 * 2**20),
        name="emit",
    )(*arrays)


def outer_sum(left, right):
    return lax.dot_general(left, right, (((0,), (0,)), ((), ())), preferred_element_type=jnp.float32)


def times_transposed(left, right):
    return lax.dot_general(left, right, NT, preferred_element_type=jnp.float32)


def column_sums(values):
    return jnp.sum(values.astype(jnp.float32), 0)


def exchange(values, axis, bit):
    return lax.ppermute(values, axis, [(i, i ^ bit) for i in range(lax.axis_size(axis))])


def plus(left, right):
    return (left.astype(jnp.float32) + right.astype(jnp.float32)).astype(jnp.bfloat16)


def pick(values, index, axis):
    return lax.dynamic_index_in_dim(values, index, axis, False)


def sum_everywhere(values):
    for axis in ("blk", "dp"):
        bit = 1
        while bit < lax.axis_size(axis):
            values = values + exchange(values, axis, bit)
            bit *= 2
    return values


def far_sum(half):
    line = lax.axis_index("dp") // 2
    parts = lax.axis_size("dp")
    if parts > 8:
        groups = [[d for d in range(parts) if d % 2 == b] for b in range(2)]
        return jnp.sum(lax.all_to_all(half, "dp", 0, 0, axis_index_groups=groups).astype(jnp.float32), 0)
    got = [exchange(pick(half, line ^ step, 0), "dp", 2 * step) for step in range(1, parts // 2)]
    return pick(half, line, 0).astype(jnp.float32) + sum(piece.astype(jnp.float32) for piece in got)


def far_sums(values):
    groups = [[d for d in range(lax.axis_size("dp")) if d % 2 == b] for b in range(2)]
    return lax.psum_scatter(values, "dp", scatter_dimension=0, axis_index_groups=groups, tiled=False)


def by_chip(up):
    return up.reshape((2, 2) + up.shape[1:]).transpose(0, 2, 1, 3).reshape(2, up.shape[1], -1)


def finish_plain(grads, first_all, own_weight, tokens, grad_middle, norm_gain, early, hidden_bias):
    rows, width = tokens.shape
    blocks, parts, me = lax.axis_size("blk"), lax.axis_size("dp"), lax.axis_index("blk")
    core, chip, own = me % 2, me // 2, width // blocks
    by_block = grads.reshape(2, 2, rows, 3 * own)
    away = times_transposed(pick(by_block, 1 - core, 1).reshape(2 * rows, 3 * own), own_weight).astype(jnp.bfloat16)
    got = exchange(away, "blk", 1)
    stay = times_transposed(pick(by_block, core, 1).reshape(2 * rows, 3 * own), own_weight)
    half = plus(stay, got).reshape(2, rows, width)
    half, grads = lax.optimization_barrier((half, grads))
    far = exchange(pick(half, 1 - chip, 0), "blk", 2)

    term = outer_sum(first_all, grads).astype(jnp.bfloat16).reshape(parts // 2, 2, width // parts, 3 * own)
    near = lax.rem(lax.axis_index("dp"), 2)
    term = plus(pick(term, near, 1), exchange(pick(term, 1 - near, 1), "dp", 1))
    qkv_term = far_sum(term).astype(jnp.bfloat16)
    qkv_blocks = lax.all_gather(qkv_term, "blk", axis=0)
    qkv_rows = qkv_blocks.reshape(blocks, -1, 3, own).transpose(1, 2, 0, 3).reshape(-1, 3 * width)
    qkv_grad = lax.dynamic_slice_in_dim(qkv_rows, me * 3 * own, 3 * own, 1).astype(jnp.float32)

    def spread(values):
        return lax.dynamic_update_slice_in_dim(jnp.zeros((width,), jnp.float32), values, me * own, 0)

    y = pick(half, chip, 0).astype(jnp.float32) + far.astype(jnp.float32)
    n, r = _stats(tokens.astype(jnp.float32))
    token_grad = (grad_middle + _pull(n, r, y * norm_gain[0])).astype(jnp.bfloat16)
    late = {0: jnp.sum(y * n, 0), 4: jnp.sum(y, 0), 8: spread(column_sums(grads[:, :own])), 9: spread(column_sums(grads[:, 2 * own :]))}
    small = jnp.stack([late.get(i, early[i]) for i in range(12)] + list(hidden_bias.reshape(-1, width)))
    small = sum_everywhere(small)
    place = lax.axis_index("dp")
    chunk = width // parts
    small_own = lax.dynamic_slice_in_dim(small[:12], place * chunk, chunk, 1)
    hidden = lax.dynamic_slice_in_dim(small[12:].reshape(-1), place * 4 * chunk, 4 * chunk, 0)
    return token_grad, qkv_grad, small_own, hidden


def local(tokens, cotangent, lengths, qkv_weight, out_weight, up_weight, down_weight, norm_gain, norm_bias, proj_bias, ffn_bias):
    rows, width = tokens.shape
    blocks = lax.axis_size("blk")
    parts = lax.axis_size("dp")
    me = lax.axis_index("blk")
    core, chip = me % 2, me // 2
    own = width // blocks

    first_all, qkv, own_weight = gather_project(tokens, qkv_weight, norm_gain, norm_bias, proj_bias)
    attended_own, log_total = attn_fwd(lengths, qkv)

    mixed, mid, n_one, r_one, low, turned, second_t, act, slope, sums_three, attended = ffn_forward(
        tokens, cotangent, attended_own, out_weight, up_weight, down_weight, norm_gain, norm_bias, proj_bias, ffn_bias
    )
    grad_middle, sums, hidden_bias, up_sum, down_sum, out_term, grad_own, out_line = ffn_backward(
        parts, low, turned, second_t, act, slope, up_weight, down_weight, mid, n_one, r_one, cotangent, attended, out_weight, norm_gain
    )
    grads = attn_bwd(lengths, qkv, grad_own, attended_own, log_total)

    if parts == 8:
        down_grad = lax.psum_scatter(down_sum, "dp", scatter_dimension=0, tiled=False)
        token_grad, qkv_grad, up_grad, out_grad, gains, shifts, biases, hidden = finish(
            grads, first_all, own_weight, tokens, grad_middle, norm_gain, up_sum, out_line, sums, sums_three, hidden_bias
        )
        token_grad, qkv_grad, up_grad, out_grad, down_grad, gains, shifts, biases, hidden = emit(
            token_grad, qkv_grad, up_grad, out_grad, down_grad, gains, shifts, biases, hidden
        )
        return (mixed, token_grad, qkv_grad, out_grad, up_grad, down_grad, gains, shifts, biases, hidden.reshape(-1))
    early = [None, sums[0], sums[1], sums_three[0], None, sums[2], sums[3], sums_three[1], None, None, sums[4], sums_three[2]]
    hidden_bias = hidden_bias.reshape(2, 2, 2, -1).transpose(0, 2, 1, 3)
    thin = width // parts
    halves = by_chip(far_sums(up_sum))
    up_grad = pick(halves, chip, 0).astype(jnp.float32) + exchange(pick(halves, 1 - chip, 0), "blk", 2).astype(jnp.float32)
    out_term = out_term.reshape(2, 2, width // 2, width // 2).transpose(1, 2, 0, 3).reshape(2, 2, own, width)
    out_half = plus(out_term[1], exchange(out_term[0], "blk", 1))
    out_sum = plus(pick(out_half, chip, 0), exchange(pick(out_half, 1 - chip, 0), "blk", 2))
    down = down_sum.transpose(1, 0, 2).reshape(own, parts, -1).transpose(1, 0, 2)
    out = out_sum.reshape(own, parts, thin).transpose(1, 0, 2)
    both = lax.psum_scatter(jnp.concatenate([down, out], 2), "dp", scatter_dimension=0, tiled=False).astype(jnp.float32)
    down_grad, out_grad = both[:, : down.shape[2]].T, both[:, down.shape[2] :].T
    token_grad, qkv_grad, small, hidden = finish_plain(grads, first_all, own_weight, tokens, grad_middle, norm_gain, early, hidden_bias)
    return (mixed, token_grad, qkv_grad, out_grad, up_grad, down_grad, small[:4], small[4:8], small[8:], hidden)


def solution(mesh):
    return jax.shard_map(
        local,
        mesh=mesh,
        in_specs=(P(("dp", "blk"), None), P(("dp", "blk"), None), P("dp", None)) + (P(),) * 8,
        out_specs=(P(("dp", "blk"), None), P(("dp", "blk"), None))
        + (P("dp", "blk"),) * 4
        + (P(None, "dp"),) * 3
        + (P("dp"),),
        check_vma=False,
    )
```

```python
import functools

import jax
import jax.numpy as jnp
from jax import lax
from jax.experimental import pallas as pl
from jax.experimental.pallas import tpu as pltpu
from jax.sharding import PartitionSpec as P

epsilon = 1e-05
HD = 64
NT = (((1,), (1,)), ((), ()))
NEG = -1e30
TILE = 256


def _bounds(len_ref, qb):
    l0 = len_ref[0, 0]
    e1 = l0 + len_ref[0, 1]

    def start_of(r):
        return jnp.where(r >= e1, e1, jnp.where(r >= l0, l0, 0))

    first = qb * TILE
    s_first, s_last = start_of(first), start_of(first + TILE - 1)
    kmin = s_first // TILE
    kmid = jnp.maximum(kmin, jnp.minimum(qb, (s_last + TILE - 1) // TILE))
    rows = first + lax.broadcasted_iota(jnp.int32, (1, TILE), 1)
    return kmin, kmid, rows, start_of(rows)


def _walk(len_ref, qb, step, carry, wide):
    kmin, kmid, rows, starts = _bounds(len_ref, qb)

    def run(masked, size):
        def body(kb, carry):
            at = pl.multiple_of(kb * TILE, TILE)
            mask = None
            if masked:
                kpos = at + lax.broadcasted_iota(jnp.int32, (size * TILE, TILE), 0)
                mask = (kpos >= starts) & (kpos <= rows)
            return step(at, size * TILE, mask, carry)

        return body

    for masked, at, left in ((True, kmin, kmid - kmin), (False, kmid, qb - kmid)):
        for size in wide:
            count, body = left // size, run(masked, size)
            carry = lax.fori_loop(0, count, lambda i, c, at=at, size=size, body=body: body(at + i * size, c), carry)
            at, left = at + count * size, left - count * size
    return run(True, 1)(qb, carry)


def _fill_masked(dst, value, heads):
    lane = lax.broadcasted_iota(jnp.int32, value.shape, 1) // HD
    for h in range(heads):
        dst[pl.ds(h * TILE, TILE), :] = jnp.where(lane == h, value, jnp.zeros_like(value))


def fwd_kernel(len_ref, q_ref, k_ref, v_ref, o_ref, lse_ref, qm, acc, ps, vt, *, heads, wide):
    qb = pl.program_id(0)

    @pl.when(qb == 0)
    def _():
        vt[...] = v_ref[...].T

    _fill_masked(qm, q_ref[...] * jnp.bfloat16(0.125), heads)
    acc[...] = jnp.zeros_like(acc)

    def step(at, size, mask, carry):
        keys = pl.ds(at, size)
        scores = [
            lax.dot_general(k_ref[keys, :], qm[pl.ds(h * TILE, TILE), :], NT, preferred_element_type=jnp.float32)
            for h in range(heads)
        ]
        out, fades = [], []
        for h in range(heads):
            m, l = carry[h]
            s = scores[h]
            if mask is not None:
                s = jnp.where(mask, s, NEG)
            top = jnp.maximum(m, jnp.max(s, 0, keepdims=True))
            p = jnp.exp(s - top)
            fade = jnp.exp(m - top)
            ps[pl.ds(0, size), pl.ds(h * TILE, TILE)] = p.astype(jnp.bfloat16)
            out.append((top, l * fade + jnp.sum(p, 0, keepdims=True)))
            fades.append(fade)
        for h in range(heads):
            lanes = pl.ds(h * HD, HD)
            part = jnp.dot(vt[lanes, keys], ps[pl.ds(0, size), pl.ds(h * TILE, TILE)], preferred_element_type=jnp.float32)
            acc[lanes, :] = acc[lanes, :] * fades[h] + part
        return tuple(out)

    carry = tuple((jnp.full((1, TILE), 0.1 * NEG, jnp.float32), jnp.zeros((1, TILE), jnp.float32)) for _ in range(heads))
    carry = _walk(len_ref, qb, step, carry, wide)
    for h in range(heads):
        m, l = carry[h]
        lse_ref[pl.ds(h, 1), :] = m + jnp.log(l)
        acc[pl.ds(h * HD, HD), :] = acc[pl.ds(h * HD, HD), :] / l
    o_ref[...] = acc[...].T.astype(jnp.bfloat16)


def attn_fwd(lengths, qkv, pair=0, lane=256, wide=(2, 1)):
    n = qkv.shape[0]
    heads = lane // HD
    return pl.pallas_call(
        functools.partial(fwd_kernel, heads=heads, wide=wide),
        grid_spec=pltpu.PrefetchScalarGridSpec(
            num_scalar_prefetch=1,
            grid=(n // TILE,),
            in_specs=[
                pl.BlockSpec((TILE, lane), lambda i, L: (i, 3 * pair)),
                pl.BlockSpec((n, lane), lambda i, L: (0, 3 * pair + 1)),
                pl.BlockSpec((n, lane), lambda i, L: (0, 3 * pair + 2)),
            ],
            out_specs=[pl.BlockSpec((TILE, lane), lambda i, L: (i, 0)), pl.BlockSpec((heads, TILE), lambda i, L: (0, i))],
            scratch_shapes=[
                pltpu.VMEM((heads * TILE, lane), jnp.bfloat16),
                pltpu.VMEM((lane, TILE), jnp.float32),
                pltpu.VMEM((wide[0] * TILE, heads * TILE), jnp.bfloat16),
                pltpu.VMEM((lane, n), jnp.bfloat16),
            ],
        ),
        out_shape=[jax.ShapeDtypeStruct((n, lane), jnp.bfloat16), jax.ShapeDtypeStruct((heads, n), jnp.float32)],
        compiler_params=pltpu.CompilerParams(vmem_limit_bytes=58 * 2**20),
        cost_estimate=pl.CostEstimate(flops=n * n * lane * 9, bytes_accessed=10 * n * lane, transcendentals=n * n * heads // 2),
        name="attn_fwd",
    )(lengths, qkv, qkv, qkv)


def bwd_kernel(len_ref, q_ref, do_ref, o_ref, lse_ref, k_ref, v_ref, d_ref, qm, dom, ps, ds, dqt, dk, dv, kt, *, heads, wide):
    qb = pl.program_id(0)
    c = heads * HD

    @pl.when(qb == 0)
    def _():
        dk[...] = jnp.zeros_like(dk)
        dv[...] = jnp.zeros_like(dv)
        kt[...] = k_ref[...].T

    _fill_masked(qm, q_ref[...] * jnp.bfloat16(0.125), heads)
    _fill_masked(dom, do_ref[...], heads)
    prod = (do_ref[...].astype(jnp.float32) * o_ref[...].astype(jnp.float32)).T
    delta = [jnp.sum(prod[h * HD : (h + 1) * HD], 0, keepdims=True) for h in range(heads)]
    dqt[...] = jnp.zeros_like(dqt)

    def step(at, size, mask, carry):
        keys = pl.ds(at, size)
        used = pl.ds(0, size)
        for h in range(heads):
            mine = pl.ds(h * TILE, TILE)
            s = lax.dot_general(k_ref[keys, :], qm[mine, :], NT, preferred_element_type=jnp.float32)
            p = jnp.exp(s - lse_ref[pl.ds(h, 1), :])
            if mask is not None:
                p = jnp.where(mask, p, 0.0)
            dp = lax.dot_general(v_ref[keys, :], dom[mine, :], NT, preferred_element_type=jnp.float32)
            ps[used, mine] = p.astype(jnp.bfloat16)
            ds[used, mine] = (p * (dp - delta[h])).astype(jnp.bfloat16)
        dv[keys, :] += jnp.dot(ps[used, :], dom[...], preferred_element_type=jnp.float32)
        dk[keys, :] += jnp.dot(ds[used, :], qm[...], preferred_element_type=jnp.float32)
        for h in range(heads):
            lanes = pl.ds(h * HD, HD)
            dqt[lanes, :] += jnp.dot(kt[lanes, keys], ds[used, pl.ds(h * TILE, TILE)], preferred_element_type=jnp.float32)
        return carry

    _walk(len_ref, qb, step, 0, wide)
    d_ref[pl.ds(pl.multiple_of(qb * TILE, TILE), TILE), pl.ds(0, c)] = (dqt[...] * 0.125).T.astype(jnp.bfloat16)

    @pl.when(qb == pl.num_programs(0) - 1)
    def _():
        d_ref[:, pl.ds(c, c)] = dk[...].astype(jnp.bfloat16)
        d_ref[:, pl.ds(2 * c, c)] = dv[...].astype(jnp.bfloat16)


def attn_bwd(lengths, qkv, do, o, lse, pair=0, lane=256, wide=(2, 1)):
    n = qkv.shape[0]
    heads = lane // HD
    row = lambda col: pl.BlockSpec((TILE, lane), lambda i, L: (i, col))
    whole = lambda col: pl.BlockSpec((n, lane), lambda i, L: (0, col))
    return pl.pallas_call(
        functools.partial(bwd_kernel, heads=heads, wide=wide),
        grid_spec=pltpu.PrefetchScalarGridSpec(
            num_scalar_prefetch=1,
            grid=(n // TILE,),
            in_specs=[
                row(3 * pair), row(pair), row(0), pl.BlockSpec((heads, TILE), lambda i, L: (0, i)),
                whole(3 * pair + 1), whole(3 * pair + 2),
            ],
            out_specs=pl.BlockSpec((n, 3 * lane), lambda i, L: (0, pair)),
            scratch_shapes=[
                pltpu.VMEM((heads * TILE, lane), jnp.bfloat16),
                pltpu.VMEM((heads * TILE, lane), jnp.bfloat16),
                pltpu.VMEM((wide[0] * TILE, heads * TILE), jnp.bfloat16),
                pltpu.VMEM((wide[0] * TILE, heads * TILE), jnp.bfloat16),
                pltpu.VMEM((lane, TILE), jnp.float32),
                pltpu.VMEM((n, lane), jnp.float32),
                pltpu.VMEM((n, lane), jnp.float32),
                pltpu.VMEM((lane, n), jnp.bfloat16),
            ],
        ),
        out_shape=jax.ShapeDtypeStruct(qkv.shape, jnp.bfloat16),
        compiler_params=pltpu.CompilerParams(vmem_limit_bytes=58 * 2**20),
        cost_estimate=pl.CostEstimate(flops=n * n * lane * 11, bytes_accessed=20 * n * lane, transcendentals=n * n * heads // 2),
        name="attn_bwd",
    )(lengths, qkv, do, o, lse, qkv, qkv)


def _stats(v):
    c = v - jnp.mean(v, -1, keepdims=True)
    r = lax.rsqrt(jnp.mean(c * c, -1, keepdims=True) + epsilon)
    return c * r, r


def _pull(n, r, e):
    return r * (e - jnp.mean(e, -1, keepdims=True) - n * jnp.mean(e * n, -1, keepdims=True))


def _fold(v):
    return jnp.sum(v.reshape(-1, 8, v.shape[-1]), 0)


def _row(ref, i):
    return ref[pl.ds(i, 1), :]


def _each(total, size, fn):
    def body(i, carry):
        fn(pl.ds(pl.multiple_of(i * size, size), size))
        return carry

    lax.fori_loop(0, total // size, body, 0)


def _turn_blocks(dst, value, core):
    own = dst.shape[0] // 4
    flipped = value.T
    for b in range(4):
        stays = 1 - lax.rem(core + b % 2, 2)
        dst[pl.ds(pl.multiple_of((2 * stays + b // 2) * own, own), own), :] = flipped[b * own : (b + 1) * own, :]


def ffn_kernel(
    x_hbm, cot_hbm, own_hbm, wo_hbm, up_ref, down_ref, gain_ref, shift_ref, bias_ref, fb_ref,
    mixed_ref, mid_out, n_out, r_ref, low_ref, turned_ref, second_out, act_ref, slope_ref, small_ref, att_out,
    x_ref, cot_ref, wo_ref, mid_ref, n_ref, second_t, att_ref, second, branch, ffn, sums, sends, recvs, own_sem, load_sems, save_sems, *, tiles, strip,
):
    s = pl.program_id(0)
    rows, width = x_ref.shape
    f32 = jnp.float32

    def loaded(i):
        return pltpu.make_async_copy((x_hbm, cot_hbm, wo_hbm)[i], (x_ref, cot_ref, wo_ref)[i], load_sems.at[i])

    def saved(i):
        pairs = ((mid_ref, mid_out), (n_ref, n_out), (second_t, second_out), (att_ref, att_out))
        return pltpu.make_async_copy(*pairs[i], save_sems.at[i])

    @pl.when(s == 0)
    def _():
        me = lax.axis_index("blk")
        own = width // 4
        peers = (me + 1 - 2 * lax.rem(me, 2), lax.rem(me + 2, 4), 3 - me)
        mesh_ids = pl.DeviceIdType.MESH
        barrier = pltpu.get_barrier_semaphore()
        for block in peers:
            pl.semaphore_signal(barrier, inc=1, device_id={"blk": block}, device_id_type=mesh_ids)
        pl.semaphore_wait(barrier, 3)

        def rows_of(block):
            return own_hbm.at[pl.ds(pl.multiple_of(block * rows, rows), rows), :]

        here = att_ref.at[:, pl.ds(pl.multiple_of(me * own, own), own)]
        copies = [
            pltpu.make_async_remote_copy(
                src_ref=rows_of(block), dst_ref=here, send_sem=sends.at[i], recv_sem=recvs.at[i],
                device_id={"blk": block}, device_id_type=mesh_ids,
            )
            for i, block in enumerate(peers)
        ]
        for copy in copies[::-1]:
            copy.start()
        mine = pltpu.make_async_copy(rows_of(me), here, own_sem)
        mine.start()
        for i in (2, 0, 1):
            loaded(i).start()
        sums[...] = jnp.zeros_like(sums)
        mine.wait()
        for i in range(3):
            loaded(i).wait()
        for copy in copies:
            copy.wait_send()
            copy.wait_recv()
        saved(3).start()
        branch[...] = jnp.dot(att_ref[...], wo_ref[...], preferred_element_type=f32) + _row(bias_ref, 2)

        def normed(at):
            n, r = _stats(branch[at, :])
            n_ref[at, :] = n.astype(jnp.bfloat16)
            r_ref[at, :] = r
            m = x_ref[at, :].astype(f32) + n * _row(gain_ref, 1) + _row(shift_ref, 1)
            mid_ref[at, :] = m
            n, _ = _stats(m)
            second[at, :] = (n * _row(gain_ref, 2) + _row(shift_ref, 2)).astype(jnp.bfloat16)

        _each(rows, strip, normed)
        second_t[...] = second[...].T
        for i in range(3):
            saved(i).start()

    c1, c3 = 0.7978845608028654, 0.7978845608028654 * 0.044715
    strips = [pl.ds(i * (rows // 2), rows // 2) for i in range(2)]
    us = [jnp.dot(second[at, :], up_ref[...], preferred_element_type=f32) + fb_ref[...] for at in strips]
    parts = []
    for at, u in zip(strips, us):
        sq = u * u
        t = jnp.tanh(u * (c1 + c3 * sq))
        half = 0.5 + 0.5 * t
        a = (u * half).astype(jnp.bfloat16)
        act_ref[at, :] = a
        slope_ref[at, :] = (half + (0.5 * u) * (1.0 - t * t) * (c1 + 3.0 * c3 * sq)).astype(jnp.bfloat16)
        parts.append(jnp.dot(a, down_ref[...], preferred_element_type=f32))

    @pl.when(s == 0)
    def _():
        for at in strips:
            ffn[at, :] = jnp.zeros((rows // 2, width), f32) + _row(bias_ref, 3)

    for at, part in zip(strips, parts):
        ffn[at, :] += part

    @pl.when(s == tiles - 1)
    def _():
        def normed(at):
            n, r = _stats(ffn[at, :])
            y = cot_ref[at, :].astype(f32)
            mixed_ref[at, :] = (mid_ref[at, :] + n * _row(gain_ref, 3) + _row(shift_ref, 3)).astype(jnp.bfloat16)
            g = _pull(n, r, y * _row(gain_ref, 3)).astype(jnp.bfloat16)
            low_ref[at, :] = g
            sums[pl.ds(0, 8), :] += _fold(y * n)
            sums[pl.ds(8, 8), :] += _fold(y)
            sums[pl.ds(16, 8), :] += _fold(g.astype(f32))

        _each(rows, strip, normed)
        _turn_blocks(turned_ref, low_ref[...], lax.rem(lax.axis_index("blk"), 2))
        for i in range(4):
            saved(i).wait()
        for i in range(3):
            small_ref[pl.ds(i, 1), :] = jnp.sum(sums[pl.ds(8 * i, 8), :], 0, keepdims=True)


def _once(*shape):
    return pl.BlockSpec(shape, lambda s: (0,) * len(shape), pipeline_mode=pl.Buffered(1))


def ffn_forward(tokens, cotangent, attended, out_weight, up_weight, down_weight, norm_gain, norm_bias, proj_bias, ffn_bias):
    rows, width = tokens.shape
    hidden = up_weight.shape[1]
    tiles = 8
    hid = hidden // tiles
    bf16, f32 = jnp.bfloat16, jnp.float32
    shape = jax.ShapeDtypeStruct
    return pl.pallas_call(
        functools.partial(ffn_kernel, tiles=tiles, strip=rows // 4),
        grid=(tiles,),
        in_specs=[
            *[pl.BlockSpec(memory_space=pl.ANY)] * 4,
            pl.BlockSpec((width, hid), lambda s: (0, s)), pl.BlockSpec((hid, width), lambda s: (s, 0)),
            _once(4, width), _once(4, width), _once(4, width), pl.BlockSpec((1, hid), lambda s: (0, s)),
        ],
        out_specs=[
            _once(rows, width), *[pl.BlockSpec(memory_space=pl.ANY)] * 2, _once(rows, 1), _once(rows, width),
            _once(width, rows), pl.BlockSpec(memory_space=pl.ANY),
            pl.BlockSpec((rows, hid), lambda s: (0, s)), pl.BlockSpec((rows, hid), lambda s: (0, s)), _once(8, width), pl.BlockSpec(memory_space=pl.ANY),
        ],
        out_shape=[
            shape((rows, width), bf16), shape((rows, width), f32), shape((rows, width), bf16), shape((rows, 1), f32),
            shape((rows, width), bf16), shape((width, rows), bf16), shape((width, rows), bf16),
            shape((rows, hidden), bf16), shape((rows, hidden), bf16), shape((8, width), f32), shape((rows, width), bf16),
        ],
        scratch_shapes=[
            pltpu.VMEM((rows, width), bf16), pltpu.VMEM((rows, width), bf16), pltpu.VMEM((width, width), bf16), pltpu.VMEM((rows, width), f32),
            pltpu.VMEM((rows, width), bf16), pltpu.VMEM((width, rows), bf16), pltpu.VMEM((rows, width), bf16),
            pltpu.VMEM((rows, width), bf16), pltpu.VMEM((rows, width), f32), pltpu.VMEM((rows, width), f32), pltpu.VMEM((24, width), f32), pltpu.SemaphoreType.DMA((3,)), pltpu.SemaphoreType.DMA((3,)), pltpu.SemaphoreType.DMA(()),
            pltpu.SemaphoreType.DMA((3,)), pltpu.SemaphoreType.DMA((4,)),
        ],
        compiler_params=pltpu.CompilerParams(collective_id=3, has_side_effects=True, vmem_limit_bytes=56 * 2**20),
        cost_estimate=pl.CostEstimate(flops=18 * rows * width * width, bytes_accessed=50 * 2**20, transcendentals=rows * hidden),
        name="ffn_forward",
    )(tokens, cotangent, attended, out_weight, up_weight, down_weight, norm_gain, norm_bias, proj_bias, ffn_bias.reshape(1, -1))


def grads_kernel(
    low_ref, turned_hbm, second_hbm, act_ref, slope_ref, up_ref, down_ref, mid_hbm, n_hbm, r_ref, cot_hbm, att_hbm, wo_hbm, gain_ref,
    gmid_ref, small_ref, hid_ref, up_out, down_out, out_out, gown_out, out_line,
    turned_ref, second_t, cot_ref, att_ref, wo_ref, pre, gs, low, turned, gatt, sums, up_buf, up_in, up_y, down_send, down_keep, down_in, down_x, up_z,
    up_core, up_core_in, up_far, up_far_in, down_core, down_core_in, down_far, down_far_in, up_done, down_done, own_sems, gatt_sends, gatt_recvs, line_sends, line_recvs, save_sems, *, tiles, strip, fold,
):
    s = pl.program_id(0)
    rows, width = low_ref.shape
    own = width // 4
    f32, bf16 = jnp.float32, jnp.bfloat16
    pair, side = s // 2, lax.rem(s, 2)
    me, place = lax.axis_index("blk"), lax.axis_index("dp")
    core, chip, near = lax.rem(me, 2), me // 2, lax.rem(place, 2)
    line = place // 2
    twin, other, beside = {"blk": me + 1 - 2 * core}, {"blk": lax.rem(me + 2, 4)}, {"dp": place + 1 - 2 * near}
    last = {"blk": 3 - me}
    half = tiles // 2
    mesh_ids = pl.DeviceIdType.MESH

    def remote(src, dst, sends, recvs, i, target):
        return pltpu.make_async_remote_copy(
            src_ref=src, dst_ref=dst, send_sem=sends.at[i], recv_sem=recvs.at[i], device_id=target, device_id_type=mesh_ids
        )

    def up_to_twin(p):
        return remote(up_buf.at[0], up_in.at[p], up_core, up_core_in, p, twin)

    def up_to_beside(p):
        return remote(up_in.at[p, :, 1 - near], up_y.at[p], up_far, up_far_in, p, beside)

    def down_to_twin(u, slot):
        return remote(down_send.at[slot], down_in.at[lax.rem(u, 4)], down_core, down_core_in, u, twin)

    def down_to_other(u):
        return remote(down_keep.at[u, 1 - chip], down_x.at[u], down_far, down_far_in, u, other)

    def up_result(p):
        if fold:
            return pltpu.make_async_copy(up_y.at[p, line], up_out.at[p], up_done.at[p])
        return pltpu.make_async_copy(up_y.at[p], up_out.at[:, p], up_done.at[p])

    def up_to_line(p, k):
        ahead = lax.rem(line + k, 4)
        return remote(up_y.at[p, ahead], up_z.at[k - 1, p], line_sends, line_recvs, 3 * p + k - 1, {"dp": 2 * ahead + near})

    def join_line(p):
        total = up_y[p, line].astype(f32)
        for k in range(1, 4):
            up_to_line(p, k).wait_recv()
            total += up_z[k - 1, p].astype(f32)
        up_y[p, line] = total.astype(bf16)
        up_result(p).start()

    def down_result(u):
        tile = 4 * (u // 4) + 2 * lax.rem(u, 2) + lax.rem(u // 2, 2)
        return pltpu.make_async_copy(down_x.at[u], down_out.at[tile], down_done.at[u])

    def saved(i):
        pairs = ((mid_hbm, gmid_ref), (n_hbm, low), (cot_hbm, cot_ref), (att_hbm, att_ref), (wo_hbm, wo_ref), (turned_hbm, turned_ref), (second_hbm, second_t))
        return pltpu.make_async_copy(*pairs[i], save_sems.at[i])

    def out_line_result():
        return pltpu.make_async_copy(up_y.at[half], out_line, own_sems.at[0])

    def out_result(i):
        return pltpu.make_async_copy(up_buf.at[i], out_out.at[i], own_sems.at[2 + i])

    def columns_to(i):
        target = (last, other, twin)[i]
        block = target["blk"]
        src = gatt.at[:, pl.ds(pl.multiple_of(block * own, own), own)]
        dst = gown_out.at[pl.ds(pl.multiple_of(me * rows, rows), rows), :]
        return remote(src, dst, gatt_sends, gatt_recvs, i, target)

    def columns_here():
        src = gatt.at[:, pl.ds(pl.multiple_of(me * own, own), own)]
        return pltpu.make_async_copy(src, gown_out.at[pl.ds(pl.multiple_of(me * rows, rows), rows), :], own_sems.at[4])

    def join_up(p):
        up_to_twin(p).wait_recv()
        up_in[p] = (up_in[p].astype(f32) + up_buf[1].astype(f32)).astype(bf16)
        up_to_beside(p).start()

    def join_far_up(p):
        up_to_beside(p).wait_recv()
        up_y[p] = (up_y[p].astype(f32) + up_in[p, :, near].astype(f32)).astype(bf16)
        if fold:
            for k in range(1, 4):
                up_to_line(p, k).start()
        else:
            up_result(p).start()

    def join_down(u):
        down_to_twin(u, 0).wait_recv()
        down_keep[u] = (down_keep[u].astype(f32) + down_in[lax.rem(u, 4)].astype(f32)).astype(bf16)
        down_to_other(u).start()

    def join_far_down(u):
        down_to_other(u).wait_recv()
        down_x[u] = (down_x[u].astype(f32) + down_keep[u, chip].astype(f32)).astype(bf16)
        down_result(u).start()

    @pl.when(s == 0)
    def _():
        barrier = pltpu.get_barrier_semaphore()
        for target in (twin, other, beside, last):
            pl.semaphore_signal(barrier, inc=1, device_id=target, device_id_type=mesh_ids)
        sums[...] = jnp.zeros_like(sums)
        for i in (5, 6, 0, 1, 2, 3, 4):
            saved(i).start()
        for i in range(1, 4 if fold else 1):
            ahead = lax.rem(line + i, 4)
            pl.semaphore_signal(barrier, inc=1, device_id={"dp": 2 * ahead + near}, device_id_type=mesh_ids)
        pl.semaphore_wait(barrier, 7 if fold else 4)

    @pl.when(s >= 4)
    def _():
        join_far_down(s - 4)

    g = lax.dot_general(low_ref[...], down_ref[...], NT, preferred_element_type=f32) * slope_ref[...].astype(f32)
    g = g.astype(bf16)
    pre[...] = g
    hid_ref[pl.ds(s, 1)] = jnp.sum(g.astype(f32), 0, keepdims=True)[None]
    part = lax.dot_general(g, up_ref[...], NT, preferred_element_type=f32)

    @pl.when(s == 0)
    def _():
        gs[...] = part

    @pl.when(s > 0)
    def _():
        gs[...] += part

    @pl.when(s == 0)
    def _():
        saved(5).wait()
        saved(6).wait()

    down_grad = jnp.dot(turned_ref[...], act_ref[...], preferred_element_type=f32).astype(bf16)

    @pl.when(s >= 2)
    def _():
        down_to_twin(s - 2, side).wait_send()

    down_send[side] = down_grad[: width // 2].reshape(2, own, -1)
    down_to_twin(s, side).start()
    down_keep[s] = down_grad[width // 2 :].reshape(2, own, -1)

    @pl.when(s > 0)
    def _():
        join_down(s - 1)

    @pl.when((side == 0) & (s > 0))
    def _():
        join_up(pair - 1)

    @pl.when((s == 5) | (s == 7))
    def _():
        join_far_up((s - 5) // 2)

    up_grad = jnp.dot(second_t[...], pre[...], preferred_element_type=f32).astype(bf16).reshape(up_buf.shape[1:])

    @pl.when(side == core)
    def _():
        up_buf[1] = up_grad

    @pl.when(side != core)
    def _():
        @pl.when(pair > 0)
        def _():
            up_to_twin(pair - 1).wait_send()

        up_buf[0] = up_grad
        up_to_twin(pair).start()

    @pl.when(s == tiles - 1)
    def _():
        def normed(at):
            n, r = _stats(gmid_ref[at, :])
            y = gs[at, :]
            gm = cot_ref[at, :].astype(f32) + _pull(n, r, y * _row(gain_ref, 2))
            gmid_ref[at, :] = gm
            sums[pl.ds(8, 8), :] += _fold(y * n)
            sums[pl.ds(24, 8), :] += _fold(y)
            n, r = low[at, :].astype(f32), r_ref[at, :]
            g = _pull(n, r, gm * _row(gain_ref, 1)).astype(bf16)
            low[at, :] = g
            sums[pl.ds(0, 8), :] += _fold(gm * n)
            sums[pl.ds(16, 8), :] += _fold(gm)
            sums[pl.ds(32, 8), :] += _fold(g.astype(f32))

        for i in range(5):
            saved(i).wait()
        _each(rows, strip, normed)
        join_down(tiles - 1)
        join_up(half - 1)
        gatt[...] = lax.dot_general(low[...], wo_ref[...], NT, preferred_element_type=f32).astype(bf16)
        for i in range(3):
            columns_to(i).start()
        columns_here().start()
        join_far_up(2)
        _turn_blocks(turned, low[...], core)
        grad = jnp.dot(turned[...], att_ref[...], preferred_element_type=f32).astype(bf16)
        up_to_twin(half - 1).wait_send()
        if fold:
            thin = width // 8
            for d in range(8):
                for b in range(8):
                    piece = grad[b * thin : (b + 1) * thin, d * thin : (d + 1) * thin]
                    up_buf[b // 4, d // 2, d % 2, :, pl.ds(b % 4 * thin, thin)] = piece
            up_to_twin(half).start()
        else:
            for i in range(2):
                up_buf[i] = grad[:, i * width // 2 : (i + 1) * width // 2].reshape(up_buf.shape[1:])
                out_result(i).start()
        for i in range(5):
            small_ref[pl.ds(i, 1), :] = jnp.sum(sums[pl.ds(8 * i, 8), :], 0, keepdims=True)
        if fold:
            join_up(half)
        join_far_up(3)
        for u in range(tiles - 4, tiles):
            join_far_down(u)
        if fold:
            for p in range(half):
                join_line(p)
            up_to_beside(half).wait_recv()
            up_y[half] = (up_y[half].astype(f32) + up_in[half, :, near].astype(f32)).astype(bf16)
            out_line_result().start()
            out_line_result().wait()
        down_to_twin(tiles - 2, 0).wait_send()
        down_to_twin(tiles - 1, 1).wait_send()
        if fold:
            up_to_twin(half).wait_send()
        else:
            out_result(0).wait()
            out_result(1).wait()
        for p in range(half + fold):
            up_to_beside(p).wait_send()
        for p in range(half):
            up_result(p).wait()
            for i in range(1, 4 if fold else 1):
                up_to_line(p, i).wait_send()
        for u in range(tiles):
            down_to_other(u).wait_send()
            down_result(u).wait()
        for i in range(3):
            columns_to(i).wait_send()
            columns_to(i).wait_recv()
        columns_here().wait()


def ffn_backward(parts, low, turned, second_t, act, slope, up_weight, down_weight, mid, n_one, r_one, cotangent, attended, out_weight, norm_gain):
    rows, width = low.shape
    hidden = up_weight.shape[1]
    tiles, own = 8, width // 4
    hid = hidden // tiles
    bf16, f32 = jnp.bfloat16, jnp.float32
    shape = jax.ShapeDtypeStruct
    tile_of = lambda s: 4 * (s // 4) + 2 * lax.rem(s, 2) + lax.rem(s // 2, 2)
    thin = (parts // 2, 2, width // parts, hid)
    dma = pltpu.SemaphoreType.DMA
    half = tiles // 2
    fold = int(parts == 8)
    return pl.pallas_call(
        functools.partial(grads_kernel, tiles=tiles, strip=rows // 4, fold=fold),
        grid=(tiles,),
        in_specs=[
            _once(rows, width), pl.BlockSpec(memory_space=pl.ANY), pl.BlockSpec(memory_space=pl.ANY),
            pl.BlockSpec((rows, hid), lambda s: (0, tile_of(s))), pl.BlockSpec((rows, hid), lambda s: (0, tile_of(s))),
            pl.BlockSpec((width, hid), lambda s: (0, tile_of(s))), pl.BlockSpec((hid, width), lambda s: (tile_of(s), 0)),
            pl.BlockSpec(memory_space=pl.ANY), pl.BlockSpec(memory_space=pl.ANY), _once(rows, 1), *[pl.BlockSpec(memory_space=pl.ANY)] * 3, _once(4, width),
        ],
        out_specs=[
            _once(rows, width), _once(8, width), _once(tiles, 1, hid),
            *[pl.BlockSpec(memory_space=pl.ANY)] * 5,
        ],
        out_shape=[
            shape((rows, width), f32),
            shape((8, width), f32), shape((tiles, 1, hid), f32),
            shape((half, width // parts, hid) if fold else (parts // 2, half, width // parts, hid), bf16), shape((tiles, own, hid), bf16), shape((2,) + thin, bf16),
            shape((4 * rows, own), bf16), shape((parts // 2, width // parts, hid), bf16),
        ],
        scratch_shapes=[
            pltpu.VMEM((width, rows), bf16), pltpu.VMEM((width, rows), bf16), pltpu.VMEM((rows, width), bf16), pltpu.VMEM((rows, width), bf16),
            pltpu.VMEM((width, width), bf16), pltpu.VMEM((rows, hid), bf16), pltpu.VMEM((rows, width), f32), pltpu.VMEM((rows, width), bf16), pltpu.VMEM((width, rows), bf16), pltpu.VMEM((rows, width), bf16),
            pltpu.VMEM((40, width), f32),
            pltpu.VMEM((2,) + thin, bf16), pltpu.VMEM((half + fold,) + thin, bf16), pltpu.VMEM((half + fold, parts // 2, width // parts, hid), bf16),
            pltpu.VMEM((2, 2, own, hid), bf16), pltpu.VMEM((tiles, 2, own, hid), bf16), pltpu.VMEM((4, 2, own, hid), bf16),
            pltpu.VMEM((tiles, own, hid), bf16), pltpu.VMEM((3, half, width // parts, hid), bf16),
            *[dma((half + fold,))] * 4, *[dma((tiles,))] * 4, dma((half + fold,)), dma((tiles,)), dma((5,)), dma((3,)), dma((3,)), dma((3 * half,)), dma((3 * half,)), dma((7,)),
        ],
        compiler_params=pltpu.CompilerParams(collective_id=1, has_side_effects=True, vmem_limit_bytes=60 * 2**20),
        name="ffn_backward",
    )(low, turned, second_t, act, slope, up_weight, down_weight, mid, n_one, r_one, cotangent, attended, out_weight, norm_gain)


def project_kernel(
    x_hbm, w_hbm, gain_ref, shift_ref, bias_ref, all_out, qkv_out, w_out, x_ref, all_ref, qkv_ref, w_ref, x_sems, out_sems, w_sems, chip_send, chip_recv, core_send, core_recv, pass_send, pass_recv, *, pieces,
):
    me = lax.axis_index("blk")
    core = lax.rem(me, 2)
    twin, other, last = me + 1 - 2 * core, lax.rem(me + 2, 4), 3 - me
    rows, width = x_ref.shape
    own = width // 4
    size = rows // pieces
    fetch = [pltpu.make_async_copy(x_hbm.at[pl.ds(i * size, size), :], x_ref.at[pl.ds(i * size, size), :], x_sems.at[i]) for i in range(pieces)]
    for copy in fetch:
        copy.start()
    barrier = pltpu.get_barrier_semaphore()
    for target in (twin, other):
        pl.semaphore_signal(barrier, inc=1, device_id={"blk": target}, device_id_type=pl.DeviceIdType.MESH)
    loads = []
    for third in range(3):
        columns = pl.ds(pl.multiple_of(third * width + me * own, own), own)
        load = pltpu.make_async_copy(w_hbm.at[:, columns], w_ref.at[:, pl.ds(third * own, own)], w_sems.at[third])
        load.start()
        loads.append(load)

    def at(block, i):
        return pl.ds(pl.multiple_of(block * rows + i * size, size), size)

    def send(block, i, target, sends, recvs):
        piece = all_ref.at[at(block, i), :]
        copy = pltpu.make_async_remote_copy(
            src_ref=piece, dst_ref=piece, send_sem=sends.at[i], recv_sem=recvs.at[i],
            device_id={"blk": target}, device_id_type=pl.DeviceIdType.MESH,
        )
        return copy

    def project(block, i):
        where = at(block, i)
        got = jnp.dot(all_ref[where, :], w_ref[...], preferred_element_type=jnp.float32)
        for third in range(3):
            part = got[:, third * own : (third + 1) * own]
            if third != 1:
                part = part + bias_ref[pl.ds(third // 2, 1), pl.ds(pl.multiple_of(me * own, own), own)]
            qkv_ref[where, pl.ds(third * own, own)] = part.astype(jnp.bfloat16)
        for src, dst in ((all_ref, all_out), (qkv_ref, qkv_out)):
            copy = pltpu.make_async_copy(src.at[where, :], dst.at[where, :], out_sems.at[len(saved)])
            copy.start()
            saved.append(copy)

    sent, saved = [], []
    for i in range(pieces):
        fetch[i].wait()
        n, _ = _stats(x_ref[pl.ds(i * size, size), :].astype(jnp.float32))
        all_ref[at(me, i), :] = (n * gain_ref[pl.ds(0, 1), :] + shift_ref[pl.ds(0, 1), :]).astype(jnp.bfloat16)
        if i == 0:
            pl.semaphore_wait(barrier, 2)
        for target, sends, recvs in ((other, chip_send, chip_recv), (twin, core_send, core_recv)):
            copy = send(me, i, target, sends, recvs)
            copy.start()
            sent.append(copy)
    for load in loads:
        load.wait()
    keep = pltpu.make_async_copy(w_ref, w_out, w_sems.at[3])
    keep.start()
    for i in range(pieces):
        project(me, i)
    for i in range(pieces):
        send(twin, i, twin, core_send, core_recv).wait_recv()
        project(twin, i)
    for i in range(pieces):
        send(other, i, other, chip_send, chip_recv).wait_recv()
        copy = send(other, i, twin, pass_send, pass_recv)
        copy.start()
        sent.append(copy)
        project(other, i)
        if i > 0:
            send(last, i - 1, twin, pass_send, pass_recv).wait_recv()
            project(last, i - 1)
    send(last, pieces - 1, twin, pass_send, pass_recv).wait_recv()
    project(last, pieces - 1)
    for copy in sent:
        copy.wait_send()
    for copy in saved:
        copy.wait()
    keep.wait()


def gather_project(tokens, qkv_weight, norm_gain, norm_bias, proj_bias):
    rows, width = tokens.shape
    pieces = 4
    vmem, hbm = pl.BlockSpec(memory_space=pltpu.VMEM), pl.BlockSpec(memory_space=pl.ANY)
    dma = pltpu.SemaphoreType.DMA((pieces,))
    return pl.pallas_call(
        functools.partial(project_kernel, pieces=pieces),
        in_specs=[hbm, hbm, vmem, vmem, vmem],
        out_specs=[hbm] * 3,
        out_shape=[jax.ShapeDtypeStruct((4 * rows, width), jnp.bfloat16), jax.ShapeDtypeStruct((4 * rows, 3 * width // 4), jnp.bfloat16), jax.ShapeDtypeStruct((width, 3 * width // 4), jnp.bfloat16)],
        scratch_shapes=[
            pltpu.VMEM((rows, width), jnp.bfloat16), pltpu.VMEM((4 * rows, width), jnp.bfloat16),
            pltpu.VMEM((4 * rows, 3 * width // 4), jnp.bfloat16), pltpu.VMEM((width, 3 * width // 4), jnp.bfloat16),
            dma, pltpu.SemaphoreType.DMA((8 * pieces,)), pltpu.SemaphoreType.DMA((4,)),
        ] + [dma] * 6,
        compiler_params=pltpu.CompilerParams(collective_id=0, has_side_effects=True, vmem_limit_bytes=60 * 2**20),
        name="gather_project",
    )(tokens, qkv_weight, norm_gain, norm_bias, proj_bias)


def tail_kernel(
    d_hbm, first_hbm, w_hbm, x_hbm, gmid_hbm, gain_ref, up_ref, out_ref, sums_ref, three_ref, hid_ref,
    token_ref, qkv_ref, up_grad_ref, out_grad_ref, gain_grad_ref, shift_grad_ref, bias_grad_ref, hid_grad_ref,
    d, first, w, x, gmid, turned, core_out, core_in, far_out, far_in, mine, cols, cols_in, line_out, line_in, total, heads_in, part, part_in, both, both_in, sums, up_in, out_in, out_sum, out_far,
    loads, core_send, core_recv, far_send, far_recv, y_send, y_recv, z_send, z_recv, q_send, q_recv, s_send, s_recv, b_send, b_recv, h_send, h_recv, o_send, o_recv, *, pieces,
):
    f32, bf16 = jnp.float32, jnp.bfloat16
    rows, width = x.shape
    own = width // 4
    size = rows // pieces
    thin = width // 8
    me, place = lax.axis_index("blk"), lax.axis_index("dp")
    core, near, line = lax.rem(me, 2), lax.rem(place, 2), place // 2
    twin, other, last = me + 1 - 2 * core, lax.rem(me + 2, 4), 3 - me
    mesh_ids = pl.DeviceIdType.MESH

    def remote(src, dst, sends, recvs, i, target):
        return pltpu.make_async_remote_copy(
            src_ref=src, dst_ref=dst, send_sem=sends.at[i], recv_sem=recvs.at[i], device_id=target, device_id_type=mesh_ids
        )

    def rows_of(block, i):
        return pl.ds(pl.multiple_of(block * rows + i * size, size), size)

    def piece(i):
        return pl.ds(i * size, size)

    barrier = pltpu.get_barrier_semaphore()
    for block in (twin, other, last):
        pl.semaphore_signal(barrier, inc=1, device_id={"blk": block}, device_id_type=mesh_ids)
    for k in range(1, 8):
        pl.semaphore_signal(barrier, inc=1, device_id={"dp": lax.rem(place + k, 8)}, device_id_type=mesh_ids)

    def block_rows(block):
        return pl.ds(pl.multiple_of(block * rows, rows), rows)

    fetch = [pltpu.make_async_copy(w_hbm, w, loads.at[0])]
    for i, block in enumerate((last, other, me, twin)):
        fetch.append(pltpu.make_async_copy(d_hbm.at[block_rows(block), :], d.at[block_rows(block), :], loads.at[1 + i]))
    for i, (src, dst) in enumerate(((first_hbm, first), (x_hbm, x), (gmid_hbm, gmid))):
        fetch.append(pltpu.make_async_copy(src, dst, loads.at[5 + i]))
    for copy in fetch[:3]:
        copy.start()

    def partial(block, i):
        return lax.dot_general(d[rows_of(block, i), :], w[...], NT, preferred_element_type=f32)

    def to_twin(kind, i):
        return remote(core_out.at[kind, piece(i), :], core_in.at[kind, piece(i), :], core_send, core_recv, kind * pieces + i, {"blk": twin})

    def to_other(i):
        return remote(far_out.at[piece(i), :], far_in.at[piece(i), :], far_send, far_recv, i, {"blk": other})

    def to_beside(k):
        return remote(cols.at[k, 1 - near], cols_in.at[k], y_send, y_recv, k, {"dp": place + 1 - 2 * near})

    def to_line(k):
        return remote(line_out.at[k], line_in.at[k], z_send, z_recv, k, {"dp": 2 * lax.rem(line + k, 4) + near})

    pl.semaphore_wait(barrier, 10)
    chip = me // 2
    weights = remote(up_ref.at[pl.ds(2 * (1 - chip), 2)], up_in, h_send, h_recv, 0, {"blk": other})
    weights.start()

    def out_to_line(k):
        ahead = lax.rem(line + k, 4)
        return remote(out_ref.at[ahead], out_in.at[k - 1], o_send, o_recv, k - 1, {"dp": 2 * ahead + near})

    out_to_other = remote(out_sum.at[1 - chip], out_far, h_send, h_recv, 1, {"blk": other})
    for k in range(1, 4):
        out_to_line(k).start()
    fetch[0].wait()
    fetch[1].wait()
    for copy in fetch[3:]:
        copy.start()
    for i in range(pieces):
        core_out[0, piece(i), :] = partial(last, i).astype(bf16)
        to_twin(0, i).start()
    fetch[2].wait()
    for i in range(pieces):
        got = partial(other, i)
        to_twin(0, i).wait_recv()
        far_out[piece(i), :] = (got + core_in[0, piece(i), :].astype(f32)).astype(bf16)
        to_other(i).start()
    fetch[3].wait()
    fetch[4].wait()
    for i in range(d.shape[0] // 256):
        turned[:, pl.ds(i * 256, 256)] = d[pl.ds(i * 256, 256), :].T
    fetch[5].wait()
    for k in (1, 2, 3, 0):
        where = pl.ds(pl.multiple_of(lax.rem(line + k, 4) * 2 * thin, 2 * thin), 2 * thin)
        got = jnp.dot(turned[...], first[:, where], preferred_element_type=f32).astype(bf16)
        cols[k, 0] = got[:, :thin]
        cols[k, 1] = got[:, thin:]
        to_beside(k).start()
    for i in range(pieces):
        core_out[1, piece(i), :] = partial(twin, i).astype(bf16)
        to_twin(1, i).start()
    for i in range(pieces):
        mine[piece(i), :] = partial(me, i)
    ones = jnp.ones((8, d.shape[0]), bf16)
    column = jnp.dot(ones, d[...], preferred_element_type=f32)
    part[...] = jnp.zeros_like(part)
    for k in range(8):
        lanes = pl.ds(k * thin, thin)
        for i, (ref, j) in ((1, (sums_ref, 0)), (2, (sums_ref, 1)), (3, (three_ref, 0)), (5, (sums_ref, 2)), (6, (sums_ref, 3)), (7, (three_ref, 1)), (10, (sums_ref, 4)), (11, (three_ref, 2))):
            part[k, pl.ds(i, 1), :] = ref[pl.ds(j, 1), lanes]
        tile = 4 * (k // 4) + 2 * (k % 2) + k // 2 % 2
        for i in range(4):
            part[tile, pl.ds(12 + i, 1), :] = hid_ref[k, :, pl.ds(i * thin, thin)]
    for h in range(2):
        part[2 * me + h, pl.ds(8, 1), :] = column[:1, h * thin : (h + 1) * thin]
        part[2 * me + h, pl.ds(9, 1), :] = column[:1, 2 * own + h * thin : 2 * own + (h + 1) * thin]
    fetch[6].wait()
    fetch[7].wait()
    sums[...] = jnp.zeros_like(sums)

    def tokens(i):
        at = piece(i)
        to_twin(1, i).wait_recv()
        n, r = _stats(x[at, :].astype(f32))
        got = mine[at, :] + core_in[1, at, :].astype(f32)
        to_other(i).wait_recv()
        y = got + far_in[at, :].astype(f32)
        token_ref[at, :] = (gmid[at, :] + _pull(n, r, y * _row(gain_ref, 0))).astype(bf16)
        sums[pl.ds(0, 8), :] += _fold(y * n)
        sums[pl.ds(8, 8), :] += _fold(y)

    for k in (1, 2, 3):
        to_beside(k).wait_recv()
        line_out[k] = (cols[k, near].astype(f32) + cols_in[k].astype(f32)).astype(bf16)
        to_line(k).start()
    for k in range(1, 4):
        out_to_line(k).wait_recv()
    got = out_ref[line].astype(f32)
    for k in range(3):
        got += out_in[k].astype(f32)
    out_sum[0] = got[:, : 2 * thin].astype(bf16)
    out_sum[1] = got[:, 2 * thin :].astype(bf16)
    out_to_other.start()
    weights.wait_recv()
    for i in range(2):
        up_grad_ref[:, pl.ds(i * 2 * own, 2 * own)] = up_ref[2 * chip + i].astype(f32) + up_in[i].astype(f32)
    for i in range(pieces - 1):
        tokens(i)
    to_beside(0).wait_recv()
    for k in (1, 2, 3):
        to_line(k).wait_recv()
    summed = cols[0, near].astype(f32) + cols_in[0].astype(f32)
    for k in (1, 2, 3):
        summed += line_in[k].astype(f32)
    total[...] = summed.astype(bf16).reshape(total.shape)
    def to_owner(third):
        chunk = 4 * third + me
        return remote(total.at[third], heads_in.at[lax.rem(chunk, 3)], q_send, q_recv, lax.rem(chunk, 3), {"blk": chunk // 3})

    for third in range(3):
        chunk = 4 * third + me

        @pl.when(chunk // 3 != me)
        def _(third=third):
            to_owner(third).start()

        @pl.when(chunk // 3 == me)
        def _(third=third, chunk=chunk):
            heads_in[lax.rem(chunk, 3)] = total[third]

    out_to_other.wait_recv()
    got = out_sum[chip].astype(f32) + out_far[...].astype(f32)
    for i in range(2):
        out_grad_ref[:, pl.ds(i * thin, thin)] = got[:, i * thin : (i + 1) * thin].T
    tokens(pieces - 1)
    for i in range(2):
        line_sum = jnp.sum(sums[pl.ds(8 * i, 8), :], 0, keepdims=True)
        for k in range(8):
            part[k, pl.ds(4 * i, 1), :] = line_sum[:, k * thin : (k + 1) * thin]

    def to_dp(k):
        target = lax.rem(place + k, 8)
        return remote(part.at[target], part_in.at[k], s_send, s_recv, k, {"dp": target})

    def to_blk(k):
        return remote(both, both_in.at[k], b_send, b_recv, k, {"blk": (twin, other, last)[k]})

    for k in range(1, 8):
        to_dp(k).start()
    for s in range(3):
        source = lax.rem(3 * me + s, 4)

        @pl.when(source != me)
        def _(s=s):
            remote(total.at[0], heads_in.at[s], q_send, q_recv, s, {"blk": twin}).wait_recv()

        qkv_ref[:, pl.ds(s * own, own)] = heads_in[s].astype(f32).T
    acc = part[place]
    for k in range(1, 8):
        to_dp(k).wait_recv()
        acc += part_in[k]
    both[...] = acc
    for k in range(3):
        to_blk(k).start()
    for k in range(3):
        to_blk(k).wait_recv()
        acc += both_in[k]
    gain_grad_ref[...] = acc[:4]
    shift_grad_ref[...] = acc[4:8]
    bias_grad_ref[...] = acc[8:12]
    hid_grad_ref[...] = acc[12:]
    for i in range(pieces):
        to_twin(0, i).wait_send()
        to_twin(1, i).wait_send()
        to_other(i).wait_send()
    for k in range(4):
        to_beside(k).wait_send()
    for k in range(1, 4):
        to_line(k).wait_send()
    for third in range(3):

        @pl.when((4 * third + me) // 3 != me)
        def _(third=third):
            to_owner(third).wait_send()

    for k in range(1, 8):
        to_dp(k).wait_send()
    for k in range(3):
        to_blk(k).wait_send()
    weights.wait_send()
    out_to_other.wait_send()
    for k in range(1, 4):
        out_to_line(k).wait_send()


def finish(grads, first_all, own_weight, tokens, grad_middle, norm_gain, up_sum, out_line, sums, sums_three, hidden_bias):
    rows, width = tokens.shape
    total_rows, cols = grads.shape
    own, thin, pieces = width // 4, width // 8, 4
    bf16, f32 = jnp.bfloat16, jnp.float32
    shape, vmem, hbm, dma = jax.ShapeDtypeStruct, pl.BlockSpec(memory_space=pltpu.VMEM), pl.BlockSpec(memory_space=pl.ANY), pltpu.SemaphoreType.DMA
    buffers = [
        ((total_rows, cols), bf16), ((total_rows, width), bf16), ((width, cols), bf16), ((rows, width), bf16), ((rows, width), f32),
        ((cols, total_rows), bf16), ((2, rows, width), bf16), ((2, rows, width), bf16), ((rows, width), bf16), ((rows, width), bf16),
        ((rows, width), f32), ((4, 2, cols, thin), bf16), ((4, cols, thin), bf16), ((4, cols, thin), bf16), ((4, cols, thin), bf16),
        ((3, own, thin), bf16), ((3, own, thin), bf16), ((8, 16, thin), f32), ((8, 16, thin), f32), ((16, thin), f32), ((3, 16, thin), f32),
        ((16, width), f32), ((2,) + up_sum.shape[1:], bf16), ((3,) + out_line.shape[1:], bf16), ((2, thin, own), bf16), ((thin, own), bf16),
    ]
    counts = [8, 2 * pieces, 2 * pieces, pieces, pieces, 4, 4, 4, 4, 3, 3, 8, 8, 3, 3, 2, 2, 3, 3]
    return pl.pallas_call(
        functools.partial(tail_kernel, pieces=pieces),
        in_specs=[hbm] * 5 + [vmem] * 6,
        out_specs=[vmem] * 8,
        out_shape=[shape((rows, width), bf16), shape((thin, 3 * own), f32), shape((thin, width), f32), shape((thin, own), f32)] + [shape((4, thin), f32)] * 4,
        scratch_shapes=[pltpu.VMEM(dims, kind) for dims, kind in buffers] + [dma((n,)) for n in counts],
        compiler_params=pltpu.CompilerParams(collective_id=2, has_side_effects=True, vmem_limit_bytes=58 * 2**20),
        cost_estimate=pl.CostEstimate(flops=60 * rows * width * width, bytes_accessed=2**27, transcendentals=0),
        name="finish",
    )(grads, first_all, own_weight, tokens, grad_middle, norm_gain, up_sum, out_line, sums, sums_three, hidden_bias)


def emit_kernel(token_in, qkv_in, up_in, out_in, down_in, gain_in, shift_in, bias_in, hid_in, token_ref, qkv_ref, up_ref, out_ref, down_ref, gain_ref, shift_ref, bias_ref, hid_ref):
    for src, dst in (
        (token_in, token_ref), (qkv_in, qkv_ref), (up_in, up_ref), (out_in, out_ref),
        (gain_in, gain_ref), (shift_in, shift_ref), (bias_in, bias_ref), (hid_in, hid_ref),
    ):
        dst[...] = src[...]
    down_ref[...] = down_in[...].astype(jnp.float32).T


def emit(token_grad, qkv_grad, up_grad, out_grad, down_grad, gains, shifts, biases, hidden):
    arrays = (token_grad, qkv_grad, up_grad, out_grad, down_grad, gains, shifts, biases, hidden)
    shapes = [jax.ShapeDtypeStruct(a.shape, a.dtype) for a in arrays]
    shapes[4] = jax.ShapeDtypeStruct(down_grad.shape[::-1], jnp.float32)
    return pl.pallas_call(
        emit_kernel,
        in_specs=[pl.BlockSpec(memory_space=pltpu.VMEM)] * 9,
        out_specs=[pl.BlockSpec(memory_space=pltpu.VMEM)] * 9,
        out_shape=shapes,
        compiler_params=pltpu.CompilerParams(vmem_limit_bytes=60 * 2**20),
        name="emit",
    )(*arrays)


def outer_sum(left, right):
    return lax.dot_general(left, right, (((0,), (0,)), ((), ())), preferred_element_type=jnp.float32)


def times_transposed(left, right):
    return lax.dot_general(left, right, NT, preferred_element_type=jnp.float32)


def column_sums(values):
    return jnp.sum(values.astype(jnp.float32), 0)


def exchange(values, axis, bit):
    return lax.ppermute(values, axis, [(i, i ^ bit) for i in range(lax.axis_size(axis))])


def plus(left, right):
    return (left.astype(jnp.float32) + right.astype(jnp.float32)).astype(jnp.bfloat16)


def pick(values, index, axis):
    return lax.dynamic_index_in_dim(values, index, axis, False)


def sum_everywhere(values):
    for axis in ("blk", "dp"):
        bit = 1
        while bit < lax.axis_size(axis):
            values = values + exchange(values, axis, bit)
            bit *= 2
    return values


def far_sum(half):
    line = lax.axis_index("dp") // 2
    parts = lax.axis_size("dp")
    if parts > 8:
        groups = [[d for d in range(parts) if d % 2 == b] for b in range(2)]
        return jnp.sum(lax.all_to_all(half, "dp", 0, 0, axis_index_groups=groups).astype(jnp.float32), 0)
    got = [exchange(pick(half, line ^ step, 0), "dp", 2 * step) for step in range(1, parts // 2)]
    return pick(half, line, 0).astype(jnp.float32) + sum(piece.astype(jnp.float32) for piece in got)


def far_sums(values):
    groups = [[d for d in range(lax.axis_size("dp")) if d % 2 == b] for b in range(2)]
    return lax.psum_scatter(values, "dp", scatter_dimension=0, axis_index_groups=groups, tiled=False)


def by_chip(up):
    return up.reshape((2, 2) + up.shape[1:]).transpose(0, 2, 1, 3).reshape(2, up.shape[1], -1)


def finish_plain(grads, first_all, own_weight, tokens, grad_middle, norm_gain, early, hidden_bias):
    rows, width = tokens.shape
    blocks, parts, me = lax.axis_size("blk"), lax.axis_size("dp"), lax.axis_index("blk")
    core, chip, own = me % 2, me // 2, width // blocks
    by_block = grads.reshape(2, 2, rows, 3 * own)
    away = times_transposed(pick(by_block, 1 - core, 1).reshape(2 * rows, 3 * own), own_weight).astype(jnp.bfloat16)
    got = exchange(away, "blk", 1)
    stay = times_transposed(pick(by_block, core, 1).reshape(2 * rows, 3 * own), own_weight)
    half = plus(stay, got).reshape(2, rows, width)
    half, grads = lax.optimization_barrier((half, grads))
    far = exchange(pick(half, 1 - chip, 0), "blk", 2)

    term = outer_sum(first_all, grads).astype(jnp.bfloat16).reshape(parts // 2, 2, width // parts, 3 * own)
    near = lax.rem(lax.axis_index("dp"), 2)
    term = plus(pick(term, near, 1), exchange(pick(term, 1 - near, 1), "dp", 1))
    qkv_term = far_sum(term).astype(jnp.bfloat16)
    qkv_blocks = lax.all_gather(qkv_term, "blk", axis=0)
    qkv_rows = qkv_blocks.reshape(blocks, -1, 3, own).transpose(1, 2, 0, 3).reshape(-1, 3 * width)
    qkv_grad = lax.dynamic_slice_in_dim(qkv_rows, me * 3 * own, 3 * own, 1).astype(jnp.float32)

    def spread(values):
        return lax.dynamic_update_slice_in_dim(jnp.zeros((width,), jnp.float32), values, me * own, 0)

    y = pick(half, chip, 0).astype(jnp.float32) + far.astype(jnp.float32)
    n, r = _stats(tokens.astype(jnp.float32))
    token_grad = (grad_middle + _pull(n, r, y * norm_gain[0])).astype(jnp.bfloat16)
    late = {0: jnp.sum(y * n, 0), 4: jnp.sum(y, 0), 8: spread(column_sums(grads[:, :own])), 9: spread(column_sums(grads[:, 2 * own :]))}
    small = jnp.stack([late.get(i, early[i]) for i in range(12)] + list(hidden_bias.reshape(-1, width)))
    small = sum_everywhere(small)
    place = lax.axis_index("dp")
    chunk = width // parts
    small_own = lax.dynamic_slice_in_dim(small[:12], place * chunk, chunk, 1)
    hidden = lax.dynamic_slice_in_dim(small[12:].reshape(-1), place * 4 * chunk, 4 * chunk, 0)
    return token_grad, qkv_grad, small_own, hidden


def local(tokens, cotangent, lengths, qkv_weight, out_weight, up_weight, down_weight, norm_gain, norm_bias, proj_bias, ffn_bias):
    rows, width = tokens.shape
    blocks = lax.axis_size("blk")
    parts = lax.axis_size("dp")
    me = lax.axis_index("blk")
    core, chip = me % 2, me // 2
    own = width // blocks

    first_all, qkv, own_weight = gather_project(tokens, qkv_weight, norm_gain, norm_bias, proj_bias)
    attended_own, log_total = attn_fwd(lengths, qkv)

    mixed, mid, n_one, r_one, low, turned, second_t, act, slope, sums_three, attended = ffn_forward(
        tokens, cotangent, attended_own, out_weight, up_weight, down_weight, norm_gain, norm_bias, proj_bias, ffn_bias
    )
    grad_middle, sums, hidden_bias, up_sum, down_sum, out_term, grad_own, out_line = ffn_backward(
        parts, low, turned, second_t, act, slope, up_weight, down_weight, mid, n_one, r_one, cotangent, attended, out_weight, norm_gain
    )
    grads = attn_bwd(lengths, qkv, grad_own, attended_own, log_total)

    if parts == 8:
        down_grad = lax.psum_scatter(down_sum, "dp", scatter_dimension=0, tiled=False)
        token_grad, qkv_grad, up_grad, out_grad, gains, shifts, biases, hidden = finish(
            grads, first_all, own_weight, tokens, grad_middle, norm_gain, up_sum, out_line, sums, sums_three, hidden_bias
        )
        token_grad, qkv_grad, up_grad, out_grad, down_grad, gains, shifts, biases, hidden = emit(
            token_grad, qkv_grad, up_grad, out_grad, down_grad, gains, shifts, biases, hidden
        )
        return (mixed, token_grad, qkv_grad, out_grad, up_grad, down_grad, gains, shifts, biases, hidden.reshape(-1))
    early = [None, sums[0], sums[1], sums_three[0], None, sums[2], sums[3], sums_three[1], None, None, sums[4], sums_three[2]]
    hidden_bias = hidden_bias.reshape(2, 2, 2, -1).transpose(0, 2, 1, 3)
    thin = width // parts
    halves = by_chip(far_sums(up_sum))
    up_grad = pick(halves, chip, 0).astype(jnp.float32) + exchange(pick(halves, 1 - chip, 0), "blk", 2).astype(jnp.float32)
    out_term = out_term.reshape(2, 2, width // 2, width // 2).transpose(1, 2, 0, 3).reshape(2, 2, own, width)
    out_half = plus(out_term[1], exchange(out_term[0], "blk", 1))
    out_sum = plus(pick(out_half, chip, 0), exchange(pick(out_half, 1 - chip, 0), "blk", 2))
    down = down_sum.transpose(1, 0, 2).reshape(own, parts, -1).transpose(1, 0, 2)
    out = out_sum.reshape(own, parts, thin).transpose(1, 0, 2)
    both = lax.psum_scatter(jnp.concatenate([down, out], 2), "dp", scatter_dimension=0, tiled=False).astype(jnp.float32)
    down_grad, out_grad = both[:, : down.shape[2]].T, both[:, down.shape[2] :].T
    token_grad, qkv_grad, small, hidden = finish_plain(grads, first_all, own_weight, tokens, grad_middle, norm_gain, early, hidden_bias)
    return (mixed, token_grad, qkv_grad, out_grad, up_grad, down_grad, small[:4], small[4:8], small[8:], hidden)


def solution(mesh):
    return jax.shard_map(
        local,
        mesh=mesh,
        in_specs=(P(("dp", "blk"), None), P(("dp", "blk"), None), P("dp", None)) + (P(),) * 8,
        out_specs=(P(("dp", "blk"), None), P(("dp", "blk"), None))
        + (P("dp", "blk"),) * 4
        + (P(None, "dp"),) * 3
        + (P("dp"),),
        check_vma=False,
    )
```
